32 devices in a mesh: dp: 8 (over z, core), fsdp: 4 (over y, x).
Axes of the slice: x: 2, y: 2, z: 4, core: 2. Of those that a mesh axis runs over, the one named last changes fastest.
Arguments:
- tokens: bfloat16 [16384, 1024], P(('dp', 'fsdp')), may hold values from -6 to 6
- cotangent: bfloat16 [16384, 1024], P(('dp', 'fsdp')), may hold values from -6 to 6
- doc_ids: int32 [8, 8], P('dp'), may hold values from 0 to 2, as said below
- norm1_gain: bfloat16 [1024], P(('dp', 'fsdp')), may hold values from 0.099609375 to 1.8984375
- norm1_bias: bfloat16 [1024], P(('dp', 'fsdp')), may hold values from -1.75 to 1.75
- norm2_gain: bfloat16 [1024], P(('dp', 'fsdp')), may hold values from 0.099609375 to 1.8984375
- norm2_bias: bfloat16 [1024], P(('dp', 'fsdp')), may hold values from -1.75 to 1.75
- qkv_weight: bfloat16 [1024, 3072], P(('dp', 'fsdp')), may hold values from -0.25 to 0.25
- qkv_bias: bfloat16 [3072], P(('dp', 'fsdp')), may hold values from -3 to 3
- out_weight: bfloat16 [1024, 1024], P(('dp', 'fsdp')), may hold values from -0.5 to 0.5
- out_bias: bfloat16 [1024], P(('dp', 'fsdp')), may hold values from -3 to 3
- up_weight: bfloat16 [1024, 4096], P(('dp', 'fsdp')), may hold values from -0.1875 to 0.1875
- up_bias: bfloat16 [4096], P(('dp', 'fsdp')), may hold values from -3 to 3
- down_weight: bfloat16 [4096, 1024], P(('dp', 'fsdp')), may hold values from -0.09375 to 0.09375
- down_bias: bfloat16 [1024], P(('dp', 'fsdp')), may hold values from -3 to 3
Outputs:
- output: bfloat16 [16384, 1024], P(('dp', 'fsdp'))
- grad_tokens: bfloat16 [16384, 1024], P(('dp', 'fsdp'))
- grad_norm1_gain: float32 [1024], P(('dp', 'fsdp'))
- grad_norm1_bias: float32 [1024], P(('dp', 'fsdp'))
- grad_norm2_gain: float32 [1024], P(('dp', 'fsdp'))
- grad_norm2_bias: float32 [1024], P(('dp', 'fsdp'))
- grad_qkv_weight: float32 [1024, 3072], P(('dp', 'fsdp'))
- grad_qkv_bias: float32 [3072], P(('dp', 'fsdp'))
- grad_out_weight: float32 [1024, 1024], P(('dp', 'fsdp'))
- grad_out_bias: float32 [1024], P(('dp', 'fsdp'))
- grad_up_weight: float32 [1024, 4096], P(('dp', 'fsdp'))
- grad_up_bias: float32 [4096], P(('dp', 'fsdp'))
- grad_down_weight: float32 [4096, 1024], P(('dp', 'fsdp'))
- grad_down_bias: float32 [1024], P(('dp', 'fsdp'))
The draws below stay inside these ranges and needn't reach their ends.
Inputs may be any that keep to these rules, and one draw needn't show every extreme that they name: `doc_ids`: document numbers never fall along a row. In each row one document spans from the block that holds position 511 to the block that holds position (3) * 512.
All inputs are finite; a program needn't handle non-finite values.
Results may differ from the reference program's by a relative error of at most 0.012.
The reference program's roundings to bfloat16 on the way count: a program that leaves them out, or rounds other values in their place, can miss the bound.
Values may be sent and summed in bfloat16 or wider, within the bound.
No kernel may reach another device: no remote copies, remote signals or barrier semaphores. Data moves between devices by JAX's collectives and lax.ppermute only.
A program may use at most 256 MiB of HBM per device.

```python
import jax
import jax.numpy as jnp
from jax import lax

D = 1024
HEADS = 16
HEAD = 64
ROT = 16
FF = 4096
BLOCK = 256
TOK_DEV = 512
STREAM = 2048
BLOCKS = 8
TOKENS = 16384
N_DP = 8
N_FSDP = 4


def draw_doc_ids(key, part):
    key = jax.random.fold_in(key, 7)
    front_key, back_key, pick_key = jax.random.split(key, 3)
    front_end = (TOK_DEV - 1) // BLOCK + 1
    last_start = (N_FSDP - 1) * TOK_DEV // BLOCK
    starts = jax.random.randint(front_key, (N_DP, 1), 0, front_end)
    tail_runs = jax.random.randint(back_key, (N_DP, 1), 0, BLOCKS - last_start)
    chosen = jax.random.randint(pick_key, (), 0, N_DP)
    streams = jnp.arange(N_DP, dtype=jnp.int32)[:, None]
    forced = (streams == chosen).astype(jnp.int32)
    starts = jnp.maximum(starts, jnp.maximum(forced, (tail_runs == 0).astype(jnp.int32)))
    tail_runs = jnp.maximum(tail_runs, forced)
    places = jnp.arange(BLOCKS, dtype=jnp.int32)[None, :]
    return (places >= starts).astype(jnp.int32) + (places >= BLOCKS - tail_runs).astype(jnp.int32)


def spiked(array, rng, source, target, shards_of, factor):
    def block_of(dim):
        return (jnp.arange(array.shape[dim]) // (array.shape[dim] // shards_of)).reshape((-1,) + (1,) * (array.ndim - 1 - dim))

    first = jax.random.permutation(rng, shards_of)[block_of(target)]
    far = (block_of(target) + shards_of // 2) % shards_of
    return jnp.where((block_of(source) == first) | (block_of(source) == far), factor * array, array)


def steps_of(stream_key, extent, pieces, low, largest):
    def one(dim, shards_of):
        steps = jax.random.uniform(jax.random.fold_in(jax.random.fold_in(stream_key, 6), dim), (shards_of,), jnp.float32, low / len(pieces), largest / len(pieces))
        return jnp.repeat(jnp.exp(steps), extent[dim] // shards_of).reshape((-1,) + (1,) * (len(extent) - dim - 1))

    level = one(*pieces[0])
    for cut in pieces[1:]:
        level = level * one(*cut)
    return level


def bell_draw(key, dims, scale, reach, pieces=(), kind=jnp.bfloat16):
    drawn = scale * jax.random.normal(key, dims, jnp.float32)
    if pieces:
        drawn = drawn * steps_of(key, dims, pieces, -0.22, 0.18)
    return jnp.clip(drawn, -reach, reach).astype(kind)


def bell_draw_with(key, extent, scale, reach, shards, heavy, kind=jnp.bfloat16):
    values = scale * jax.random.normal(key, extent, jnp.float32)
    if shards:
        values = values * steps_of(key, extent, shards, -0.22, 0.18)
    return jnp.clip(spiked(values, jax.random.fold_in(key, 3), *heavy), -reach, reach).astype(kind)


def setup_inputs(seed: int = 0) -> dict:
    key_list = jax.random.split(jax.random.key(seed), 16)
    tokens = bell_draw_with(key_list[0], (TOKENS, D), 1.0, 6.0, ((0, 32),), (0, 1, 32, 2.75))
    cotangent = bell_draw_with(key_list[1], (TOKENS, D), 1.0, 6.0, ((0, 32),), (0, 1, 32, 2.75))
    doc_ids = draw_doc_ids(jax.random.fold_in(key_list[15], 71), 0)
    norm1_gain = jnp.clip(1.0 + 0.18 * jax.random.normal(key_list[3], (D,), jnp.float32), 0.099609375, 1.8984375).astype(jnp.bfloat16)
    norm1_bias = bell_draw(key_list[4], (D,), 0.3, 1.75, ((0, 32),))
    norm2_gain = jnp.clip(1.0 + 0.18 * jax.random.normal(key_list[5], (D,), jnp.float32), 0.099609375, 1.8984375).astype(jnp.bfloat16)
    norm2_bias = bell_draw(key_list[6], (D,), 0.3, 1.75, ((0, 32),))
    qkv_weight = bell_draw(key_list[7], (D, 3 * D), (D // 2) ** -0.5, 0.25, ((0, 32),))
    qkv_bias = bell_draw(key_list[8], (3 * D,), 0.5, 3.0, ((0, 32),))
    out_weight = bell_draw(key_list[9], (D, D), (D // 8) ** -0.5, 0.5, ((0, 32),))
    out_bias = bell_draw(key_list[10], (D,), 0.5, 3.0, ((0, 32),))
    up_weight = bell_draw(key_list[11], (D, FF), D ** -0.5, 0.1875, ((0, 32),))
    up_bias = bell_draw(key_list[12], (FF,), 0.5, 3.0, ((0, 32),))
    down_weight = bell_draw(key_list[13], (FF, D), FF ** -0.5, 0.09375, ((0, 32),))
    down_bias = bell_draw(key_list[14], (D,), 0.5, 3.0, ((0, 32),))
    return {"tokens": tokens, "cotangent": cotangent, "doc_ids": doc_ids, "norm1_gain": norm1_gain, "norm1_bias": norm1_bias, "norm2_gain": norm2_gain, "norm2_bias": norm2_bias, "qkv_weight": qkv_weight, "qkv_bias": qkv_bias, "out_weight": out_weight, "out_bias": out_bias, "up_weight": up_weight, "up_bias": up_bias, "down_weight": down_weight, "down_bias": down_bias}


EPS = 1e-05
HIGH = lax.Precision.HIGHEST

@jax.custom_vjp
def low(v):
    return lax.optimization_barrier(v.astype(jnp.bfloat16)).astype(jnp.float32)

@jax.custom_vjp
def low_back(v):
    return v

def low_keep(v):
    return (low(v), None)

def low_pass(kept, grad):
    return (grad,)

def back_keep(v):
    return (v, None)

def back_low(kept, grad):
    return (low(grad),)
low.defvjp(low_keep, low_pass)
low_back.defvjp(back_keep, back_low)

def gelu(values_in):
    return jax.nn.gelu(values_in, approximate=False)

def norm(values_in, gain_vec, bias_vec):
    centre = values_in - lax.optimization_barrier(jnp.mean(values_in, axis=-1, keepdims=True))
    spread = lax.optimization_barrier(jnp.mean(centre * centre, axis=-1, keepdims=True))
    return centre * lax.rsqrt(spread + EPS) * gain_vec + bias_vec

def rotate(matrix, positions):
    row_count = matrix.shape[0]
    by_head = matrix.reshape(row_count, HEADS, HEAD)
    half_rot = ROT // 2
    frequency = 10000.0 ** (-(jnp.arange(half_rot, dtype=jnp.float32) * 2.0) / ROT)
    angles = positions.astype(jnp.float32)[:, None] * frequency[None, :]
    cosine = jnp.cos(angles)[:, None, :]
    sine_vals = jnp.sin(angles)[:, None, :]
    leading = by_head[:, :, :half_rot]
    trailing = by_head[:, :, half_rot:ROT]
    turned = jnp.concatenate([leading * cosine - trailing * sine_vals, trailing * cosine + leading * sine_vals, by_head[:, :, ROT:]], axis=-1)
    return turned.reshape(row_count, HEADS * HEAD)

def layer(x_rows, doc_row, gain_one, bias_one, gain_two, bias_two, w_qkv, b_qkv, w_out, b_out, w_up, b_up, w_down, b_down):
    length = x_rows.shape[0]
    h_one = low(norm(x_rows, gain_one, bias_one))
    h_two = low(norm(x_rows, gain_two, bias_two))
    qkv_rows = low_back(jnp.dot(h_one, w_qkv, precision=HIGH) + b_qkv)
    places = jnp.arange(length, dtype=jnp.int32)
    queries = low(rotate(qkv_rows[:, :D], places) * 0.125)
    keys = low(rotate(qkv_rows[:, D:2 * D], places))
    values = low(qkv_rows[:, 2 * D:])
    blocks = places // BLOCK
    owners = doc_row[blocks]
    key_heads = keys.reshape(length, HEADS, HEAD)
    value_heads = values.reshape(length, HEADS, HEAD)
    block_span = 2 * BLOCK
    block_count = length // block_span

    def attend(piece_in):
        query_block, query_ids, query_docs = piece_in
        scores = low_back(jnp.einsum('qhd,khd->hqk', query_block, key_heads, precision=HIGH))
        allowed = (blocks[None, :] <= query_ids[:, None]) & (owners[None, :] == query_docs[:, None])
        attn_probs = jax.nn.softmax(jnp.where(allowed[None], scores, -1e+30), axis=-1)
        return jnp.einsum('hqk,khd->qhd', low(attn_probs), value_heads, precision=HIGH)
    attended = lax.map(jax.checkpoint(attend), (queries.reshape(block_count, block_span, HEADS, HEAD), blocks.reshape(block_count, block_span), owners.reshape(block_count, block_span)))
    attended = low(low_back(attended.reshape(length, D)))
    up_rows = low_back(jnp.dot(h_two, w_up, precision=HIGH) + b_up)
    active = low(gelu(up_rows))
    return x_rows + jnp.dot(attended, w_out, precision=HIGH) + b_out + jnp.dot(active, w_down, precision=HIGH) + b_down

def reference(tokens, cotangent, doc_ids, norm1_gain, norm1_bias, norm2_gain, norm2_bias, qkv_weight, qkv_bias, out_weight, out_bias, up_weight, up_bias, down_weight, down_bias):
    params = tuple((entry.astype(jnp.float32) for entry in (norm1_gain, norm1_bias, norm2_gain, norm2_bias, qkv_weight, qkv_bias, out_weight, out_bias, up_weight, up_bias, down_weight, down_bias)))
    inputs = tokens.astype(jnp.float32).reshape(N_DP, STREAM, D)
    seeds = cotangent.astype(jnp.float32).reshape(N_DP, STREAM, D)

    def stream_step(totals, inputs_now):
        x_rows, d_rows, doc_row = inputs_now

        def forward(x_in, *weights):
            return layer(x_in, doc_row, *weights)
        result, pull = jax.vjp(forward, x_rows, *params)
        grads = pull(d_rows)
        return (tuple((total + extra for total, extra in zip(totals, grads[1:]))), (result, grads[0]))
    zeros = tuple((jnp.zeros_like(entry) for entry in params))
    totals, (outputs, input_grads) = lax.scan(stream_step, zeros, (inputs, seeds, doc_ids))
    return (outputs.reshape(TOKENS, D).astype(jnp.bfloat16), input_grads.reshape(TOKENS, D).astype(jnp.bfloat16), totals[0], totals[1], totals[2], totals[3], totals[4], totals[5], totals[6], totals[7], totals[8], totals[9], totals[10], totals[11])
```

```python
import functools

import jax
import jax.numpy as jnp
import numpy as np
from jax import lax
from jax.experimental import pallas as pl
from jax.experimental.pallas import tpu as pltpu
from jax.sharding import PartitionSpec as P

HEADS = 16
HEAD = 64
ROT = 16
BLOCK = 256
EPS = 1e-05
VMEM = 60 * 1024 * 1024
ALL = ("dp", "fsdp")
F32 = jnp.float32
LOW = jnp.bfloat16


def dot(left, right, contract=((1,), (0,))):
    return lax.dot_general(left, right, (contract, ((), ())), preferred_element_type=F32)


NT = ((1,), (1,))
TN = ((0,), (0,))


def normed(x_rows):
    centre = x_rows - jnp.mean(x_rows, axis=-1, keepdims=True)
    spread = jnp.mean(centre * centre, axis=-1, keepdims=True)
    scale = lax.rsqrt(spread + EPS)
    return centre * scale, scale


def turned(z, cosine, sine_a, sine_b, sign):
    groups = []
    for start in range(0, z.shape[1], 128):
        part = z[:, start : start + 128]
        ahead = pltpu.roll(part, 128 - ROT // 2, 1)
        behind = pltpu.roll(part, ROT // 2, 1)
        groups.append(part * cosine + sign * (ahead * sine_a + behind * sine_b))
    return groups[0] if len(groups) == 1 else jnp.concatenate(groups, axis=1)


def head_only(array, head):
    lane = lax.broadcasted_iota(jnp.int32, array.shape, 1)
    keep = (lane >= head * HEAD) & (lane < (head + 1) * HEAD)
    return jnp.where(keep, array, jnp.zeros_like(array))


def params(*order):
    return pltpu.CompilerParams(vmem_limit_bytes=VMEM, dimension_semantics=order)


def whole(shape):
    return pl.BlockSpec(shape, lambda *_: (0,) * len(shape))


def qkv_kernel(order, x, gain, bias, weight, shift, cosine, sine_a, sine_b, q, k, v):
    width = q.shape[1]
    n, _ = normed(x[...].astype(F32))
    h = (n * gain[...] + bias[...]).astype(LOW)
    rows = dot(h, weight[...]) + shift[...]
    tables = (cosine[...], sine_a[...], sine_b[...])
    q[...] = (turned(rows[:, :width], *tables, 1.0) * 0.125).astype(LOW)
    k[...] = turned(rows[:, width : 2 * width], *tables, 1.0).astype(LOW)
    v[...] = rows[:, 2 * width :].astype(LOW)


def call_qkv(order, x, gain, bias, weight, shift, tables, span):
    rows, model = x.shape
    width = shift.shape[1] // 3
    here = lambda i, o: (i, 0)
    there = lambda i, o: (o[i], 0)
    return pl.pallas_call(
        qkv_kernel,
        grid_spec=pltpu.PrefetchScalarGridSpec(
            num_scalar_prefetch=1,
            grid=(rows // span,),
            in_specs=[
                pl.BlockSpec((span, model), here),
                whole((1, model)),
                whole((1, model)),
                whole((model, 3 * width)),
                whole((1, 3 * width)),
            ]
            + [pl.BlockSpec((span, 128), there)] * 3,
            out_specs=[pl.BlockSpec((span, width), there)] * 3,
        ),
        out_shape=[jax.ShapeDtypeStruct((rows, width), LOW)] * 3,
        compiler_params=params("arbitrary"),
        cost_estimate=pl.CostEstimate(flops=6 * rows * model * width, bytes_accessed=4 * rows * model, transcendentals=0),
        name="qkv",
    )(order, x, gain, bias, weight, shift, *tables)


def fwd_kernel(first, q, k, v, mixed, low_mixed, lse, keys, values_t, scores, top, total, out_t):
    step = pl.program_id(0)
    width = q.shape[1]
    heads = width // HEAD
    own = pl.ds(pl.multiple_of(step * BLOCK, BLOCK), BLOCK)
    k_own = k[own, :]
    for head in range(heads):
        keys[step, head] = head_only(k_own, head)
    values_t[step] = v[own, :].T
    q_t = q[own, :].T
    top[...] = jnp.full_like(top, -1e30)
    total[...] = jnp.zeros_like(total)
    out_t[...] = jnp.zeros_like(out_t)

    def score(at, _):
        for head in range(heads):
            s = dot(keys[at, head], q_t)
            scores[at, head] = s
            top[head] = jnp.maximum(top[head], jnp.max(s.reshape(BLOCK // 8, 8, BLOCK), axis=0))
        return 0

    lax.fori_loop(first[step], step + 1, score, 0)
    peak = [jnp.max(top[head], axis=0, keepdims=True) for head in range(heads)]

    def mix(at, _):
        for head in range(heads):
            e = jnp.exp(scores[at, head] - peak[head])
            total[head] += jnp.sum(e.reshape(BLOCK // 8, 8, BLOCK), axis=0)
            span = slice(head * HEAD, (head + 1) * HEAD)
            out_t[span, :] += dot(values_t[at, span, :], e.astype(LOW))
        return 0

    lax.fori_loop(first[step], step + 1, mix, 0)
    for head in range(heads):
        sums = jnp.sum(total[head], axis=0, keepdims=True)
        lse[head : head + 1, :] = peak[head] + jnp.log(sums)
        span = slice(head * HEAD, (head + 1) * HEAD)
        out_t[span, :] = out_t[span, :] * (1.0 / sums)
    result = out_t[...].T
    mixed[...] = result
    low_mixed[...] = result.astype(LOW)


def call_fwd(first, q, k, v):
    rows, width = q.shape
    heads = width // HEAD
    blocks = rows // BLOCK
    return pl.pallas_call(
        fwd_kernel,
        grid_spec=pltpu.PrefetchScalarGridSpec(
            num_scalar_prefetch=1,
            grid=(blocks,),
            in_specs=[whole((rows, width))] * 3,
            out_specs=[
                pl.BlockSpec((BLOCK, width), lambda i, o: (i, 0)),
                pl.BlockSpec((BLOCK, width), lambda i, o: (i, 0)),
                pl.BlockSpec((heads, BLOCK), lambda i, o: (0, i)),
            ],
            scratch_shapes=[
                pltpu.VMEM((blocks, heads, BLOCK, width), LOW),
                pltpu.VMEM((blocks, width, BLOCK), LOW),
                pltpu.VMEM((blocks, heads, BLOCK, BLOCK), F32),
                pltpu.VMEM((heads, 8, BLOCK), F32),
                pltpu.VMEM((heads, 8, BLOCK), F32),
                pltpu.VMEM((width, BLOCK), F32),
            ],
        ),
        out_shape=[
            jax.ShapeDtypeStruct((rows, width), F32),
            jax.ShapeDtypeStruct((rows, width), LOW),
            jax.ShapeDtypeStruct((heads, rows), F32),
        ],
        compiler_params=params("arbitrary"),
        cost_estimate=pl.CostEstimate(flops=8 * rows * rows * width, bytes_accessed=16 * rows * width, transcendentals=rows * rows * heads),
        name="attend",
    )(first, q, k, v)


def mlp_kernel(
    order, x, cot, mixed, gain, bias, w_up, b_up, w_down, w_out,
    part, d_mixed, to_norm, g_up, g_down, g_out, sums, acc_up, acc_down, acc_out,
):
    step = pl.program_id(0)

    @pl.when(step == 0)
    def _():
        acc_up[...] = jnp.zeros_like(acc_up)
        acc_down[...] = jnp.zeros_like(acc_down)
        acc_out[...] = jnp.zeros_like(acc_out)
        sums[...] = jnp.zeros_like(sums)

    n, _ = normed(x[...].astype(F32))
    h = (n * gain[...] + bias[...]).astype(LOW)
    u = dot(h, w_up[...]) + b_up[...]
    cdf = 0.5 * (1.0 + lax.erf(u * np.float32(np.sqrt(0.5))))
    slope = cdf + u * (jnp.exp(-0.5 * u * u) * np.float32(1.0 / np.sqrt(2.0 * np.pi)))
    active = (u * cdf).astype(LOW)
    dy = cot[...]
    part[...] = (dot(active, w_down[...]) + dot(mixed[...], w_out[...])).astype(LOW)
    d_mixed[...] = dot(dy, w_out[...], NT).astype(LOW)
    acc_down[...] += dot(active, dy, TN)
    acc_out[...] += dot(mixed[...], dy, TN)
    d_up32 = dot(dy, w_down[...], NT) * slope
    d_up = d_up32.astype(LOW)
    sums[0:1, : d_up.shape[1]] += jnp.sum(d_up.astype(F32), axis=0, keepdims=True)
    acc_up[...] += dot(h, d_up, TN)
    d_h = dot(d_up, w_up[...], NT)
    sums[1:2, : n.shape[1]] += jnp.sum(d_h, axis=0, keepdims=True)
    sums[2:3, : n.shape[1]] += jnp.sum(d_h * n, axis=0, keepdims=True)
    to_norm[...] = d_h * gain[...]

    @pl.when(step == pl.num_programs(0) - 1)
    def _():
        g_up[...] = acc_up[...].astype(LOW)
        g_down[...] = acc_down[...].astype(LOW)
        g_out[...] = acc_out[...].astype(LOW)


def call_mlp(order, x, cot, mixed, gain, bias, w_up, b_up, w_down, w_out, span):
    rows, model = x.shape
    units = w_up.shape[1]
    width = mixed.shape[1]
    here = lambda i, o: (i, 0)
    there = lambda i, o: (o[i], 0)
    return pl.pallas_call(
        mlp_kernel,
        grid_spec=pltpu.PrefetchScalarGridSpec(
            num_scalar_prefetch=1,
            grid=(rows // span,),
            in_specs=[
                pl.BlockSpec((span, model), here),
                pl.BlockSpec((span, model), here),
                pl.BlockSpec((span, width), there),
                whole((1, model)),
                whole((1, model)),
                whole((model, units)),
                whole((1, units)),
                whole((units, model)),
                whole((width, model)),
            ],
            out_specs=[
                pl.BlockSpec((span, model), here),
                pl.BlockSpec((span, width), there),
                pl.BlockSpec((span, model), here),
                whole((model, units)),
                whole((units, model)),
                whole((width, model)),
                whole((8, max(model, units))),
            ],
            scratch_shapes=[
                pltpu.VMEM((model, units), F32),
                pltpu.VMEM((units, model), F32),
                pltpu.VMEM((width, model), F32),
            ],
        ),
        out_shape=[
            jax.ShapeDtypeStruct((rows, model), LOW),
            jax.ShapeDtypeStruct((rows, width), LOW),
            jax.ShapeDtypeStruct((rows, model), F32),
            jax.ShapeDtypeStruct((model, units), LOW),
            jax.ShapeDtypeStruct((units, model), LOW),
            jax.ShapeDtypeStruct((width, model), LOW),
            jax.ShapeDtypeStruct((8, max(model, units)), F32),
        ],
        compiler_params=params("arbitrary"),
        cost_estimate=pl.CostEstimate(flops=12 * rows * model * (units + width // 2), bytes_accessed=12 * rows * model, transcendentals=rows * units * 2),
        name="mlp",
    )(order, x, cot, mixed, gain, bias, w_up, b_up, w_down, w_out)


def bwd_kernel(
    first, q, k, v, d_mixed, mixed, lse, cosine, sine_a, sine_b,
    d_qkv, keys, values, keys_t, d_q_t, d_k, d_v, queries, seeds,
):
    step = pl.program_id(0)
    width = q.shape[1]
    heads = width // HEAD
    own = pl.ds(pl.multiple_of(step * BLOCK, BLOCK), BLOCK)
    k_own = k[own, :]
    v_own = v[own, :]
    q_own = q[own, :]
    s_own = d_mixed[own, :]
    for head in range(heads):
        keys[step, head] = head_only(k_own, head)
        values[step, head] = head_only(v_own, head)
        queries[head] = head_only(q_own, head)
        seeds[head] = head_only(s_own, head)
    keys_t[step] = k_own.T
    q_t = q_own.T
    s_t = s_own.T
    product_t = (s_own.astype(F32) * mixed[own, :]).T
    delta = [
        jnp.sum(product_t[head * HEAD : (head + 1) * HEAD, :], axis=0, keepdims=True) for head in range(heads)
    ]
    log_total = lse[...]
    d_q_t[...] = jnp.zeros_like(d_q_t)
    d_k[own, :] = jnp.zeros((BLOCK, width), F32)
    d_v[own, :] = jnp.zeros((BLOCK, width), F32)

    def body(at, _):
        rows = pl.ds(pl.multiple_of(at * BLOCK, BLOCK), BLOCK)
        low_probs = []
        low_scores = []
        for head in range(heads):
            s = dot(keys[at, head], q_t)
            probs = jnp.exp(s - log_total[head : head + 1, :])
            d_probs = dot(values[at, head], s_t)
            d_scores = (probs * (d_probs - delta[head])).astype(LOW)
            low_probs.append(probs.astype(LOW))
            low_scores.append(d_scores)
            span = slice(head * HEAD, (head + 1) * HEAD)
            d_q_t[span, :] += dot(keys_t[at, span, :], d_scores)
        d_v[rows, :] += dot(jnp.concatenate(low_probs, axis=1), seeds[...].reshape(heads * BLOCK, width))
        d_k[rows, :] += dot(jnp.concatenate(low_scores, axis=1), queries[...].reshape(heads * BLOCK, width))
        return 0

    lax.fori_loop(first[step], step + 1, body, 0)
    d_qkv[own, :width] = (turned(d_q_t[...].T, cosine[own, :], sine_a[own, :], sine_b[own, :], -1.0) * 0.125).astype(LOW)

    @pl.when(step == pl.num_programs(0) - 1)
    def _():
        def close(at, _):
            rows = pl.ds(pl.multiple_of(at * BLOCK, BLOCK), BLOCK)
            d_qkv[rows, width : 2 * width] = turned(d_k[rows, :], cosine[rows, :], sine_a[rows, :], sine_b[rows, :], -1.0).astype(LOW)
            d_qkv[rows, 2 * width :] = d_v[rows, :].astype(LOW)
            return 0

        lax.fori_loop(0, q.shape[0] // BLOCK, close, 0)


def call_bwd(first, q, k, v, d_mixed, mixed, lse, tables):
    rows, width = q.shape
    heads = width // HEAD
    blocks = rows // BLOCK
    return pl.pallas_call(
        bwd_kernel,
        grid_spec=pltpu.PrefetchScalarGridSpec(
            num_scalar_prefetch=1,
            grid=(blocks,),
            in_specs=[whole((rows, width))] * 5
            + [pl.BlockSpec((heads, BLOCK), lambda i, o: (0, i))]
            + [whole((rows, 128))] * 3,
            out_specs=whole((rows, 3 * width)),
            scratch_shapes=[
                pltpu.VMEM((blocks, heads, BLOCK, width), LOW),
                pltpu.VMEM((blocks, heads, BLOCK, width), LOW),
                pltpu.VMEM((blocks, width, BLOCK), LOW),
                pltpu.VMEM((width, BLOCK), F32),
                pltpu.VMEM((rows, width), F32),
                pltpu.VMEM((rows, width), F32),
                pltpu.VMEM((heads, BLOCK, width), LOW),
                pltpu.VMEM((heads, BLOCK, width), LOW),
            ],
        ),
        out_shape=jax.ShapeDtypeStruct((rows, 3 * width), LOW),
        compiler_params=params("arbitrary"),
        cost_estimate=pl.CostEstimate(flops=20 * rows * rows * width, bytes_accessed=24 * rows * width, transcendentals=rows * rows * heads),
        name="attend_back",
    )(first, q, k, v, d_mixed, mixed, lse, *tables)


def close_kernel(order, x, d_qkv, to_norm, gain, bias, weight, part, g_qkv, sums, acc):
    step = pl.program_id(0)

    @pl.when(step == 0)
    def _():
        acc[...] = jnp.zeros_like(acc)
        sums[...] = jnp.zeros_like(sums)

    width3 = d_qkv.shape[1]
    n, scale = normed(x[...].astype(F32))
    h = (n * gain[...] + bias[...]).astype(LOW)
    d_rows = d_qkv[...]
    acc[...] += dot(h, d_rows, TN)
    sums[0:1, :width3] += jnp.sum(d_rows.astype(F32), axis=0, keepdims=True)
    d_h = dot(d_rows, weight[...], NT)
    sums[1:2, : n.shape[1]] += jnp.sum(d_h, axis=0, keepdims=True)
    sums[2:3, : n.shape[1]] += jnp.sum(d_h * n, axis=0, keepdims=True)
    e = d_h * gain[...] + to_norm[...]
    e = e - jnp.mean(e, axis=-1, keepdims=True) - n * jnp.mean(e * n, axis=-1, keepdims=True)
    part[...] = (e * scale).astype(LOW)

    @pl.when(step == pl.num_programs(0) - 1)
    def _():
        g_qkv[...] = acc[...].astype(LOW)


def call_close(order, x, d_qkv, to_norm, gain, bias, weight, span):
    rows, model = x.shape
    width3 = d_qkv.shape[1]
    here = lambda i, o: (i, 0)
    there = lambda i, o: (o[i], 0)
    return pl.pallas_call(
        close_kernel,
        grid_spec=pltpu.PrefetchScalarGridSpec(
            num_scalar_prefetch=1,
            grid=(rows // span,),
            in_specs=[
                pl.BlockSpec((span, model), here),
                pl.BlockSpec((span, width3), there),
                pl.BlockSpec((span, model), here),
                whole((1, model)),
                whole((1, model)),
                whole((model, width3)),
            ],
            out_specs=[
                pl.BlockSpec((span, model), here),
                whole((model, width3)),
                whole((8, max(model, width3))),
            ],
            scratch_shapes=[pltpu.VMEM((model, width3), F32)],
        ),
        out_shape=[
            jax.ShapeDtypeStruct((rows, model), LOW),
            jax.ShapeDtypeStruct((model, width3), LOW),
            jax.ShapeDtypeStruct((8, max(model, width3)), F32),
        ],
        compiler_params=params("arbitrary"),
        cost_estimate=pl.CostEstimate(flops=4 * rows * model * width3, bytes_accessed=10 * rows * model, transcendentals=0),
        name="close",
    )(order, x, d_qkv, to_norm, gain, bias, weight)


def across(array, bit):
    size = lax.axis_size("fsdp")
    return lax.ppermute(array, "fsdp", [(i, i ^ bit) for i in range(size)])


def exchange(pieces):
    size = lax.axis_size("fsdp")
    if size != 4:
        return lax.all_to_all(pieces, "fsdp", split_axis=0, concat_axis=0, tiled=True)
    member = lax.axis_index("fsdp")
    out = pieces
    for bit in range(1, size):
        mine = lax.dynamic_index_in_dim(pieces, member ^ bit, 0, keepdims=False)
        out = lax.dynamic_update_index_in_dim(out, across(mine, bit), member ^ bit, 0)
    return out


def gather_rows(rows):
    if lax.axis_size("fsdp") != 4:
        return lax.all_gather(rows, "fsdp", axis=0, tiled=True)
    half = rows.shape[0] // 2
    one = across(rows, 1)
    two = across(rows, 2)
    low_half = across(one[:half], 2)
    high_half = across(two[half:], 1)
    return jnp.concatenate([rows, one, two, low_half, high_half], axis=0)


def reduce_rows(parts):
    size = lax.axis_size("fsdp")
    if size != 4:
        return lax.psum_scatter(parts, "fsdp", scatter_dimension=0, tiled=True).astype(F32)
    own, one, two, three = jnp.split(parts, 4, axis=0)
    half = own.shape[0] // 2
    from_one = across(three[:half], 1)
    from_two = across(three[half:], 2)
    one = jnp.concatenate([one[:half], (one[half:].astype(F32) + from_two.astype(F32)).astype(LOW)], axis=0)
    two = jnp.concatenate([(two[:half].astype(F32) + from_one.astype(F32)).astype(LOW), two[half:]], axis=0)
    return own.astype(F32) + across(one, 1).astype(F32) + across(two, 2).astype(F32)


def total_over_all(vector):
    count = lax.axis_size("dp") * lax.axis_size("fsdp")
    step = 1
    while step < count:
        vector = vector + lax.ppermute(vector, ALL, [(i, i ^ step) for i in range(count)])
        step *= 2
    return vector


def swap_owner(array, back):
    groups, members = lax.axis_size("dp"), lax.axis_size("fsdp")
    pairs = [(m * groups + g, g * members + m) for g in range(groups) for m in range(members)]
    if back:
        pairs = [(b, a) for a, b in pairs]
    return lax.ppermute(array, ALL, pairs)


def gather_dp(array):
    return lax.all_gather(array, "dp", axis=0, tiled=True)


def scatter_dp(array):
    return lax.psum_scatter(array, "dp", scatter_dimension=0, tiled=True)


def rotary_tables(length):
    half = ROT // 2
    frequency = (np.float32(10000.0) ** (-(np.arange(half, dtype=np.float32) * np.float32(2.0)) / np.float32(ROT))).astype(np.float32)
    angles = (np.arange(length, dtype=np.float32)[:, None] * frequency[None, :]).astype(np.float32)
    cosine = np.cos(angles).astype(np.float32)
    sine = np.sin(angles).astype(np.float32)
    cos_row = np.ones((length, 128), np.float32)
    ahead = np.zeros((length, 128), np.float32)
    behind = np.zeros((length, 128), np.float32)
    for start in range(0, 128, HEAD):
        cos_row[:, start : start + half] = cosine
        cos_row[:, start + half : start + ROT] = cosine
        ahead[:, start : start + half] = -sine
        behind[:, start + half : start + ROT] = sine
    return tuple(jnp.asarray(t) for t in (cos_row, ahead, behind))


def local(
    tokens, cotangent, doc_ids, norm1_gain, norm1_bias, norm2_gain, norm2_bias, qkv_weight, qkv_bias,
    out_weight, out_bias, up_weight, up_bias, down_weight, down_bias,
):
    groups, members = lax.axis_size("dp"), lax.axis_size("fsdp")
    group, member = lax.axis_index("dp"), lax.axis_index("fsdp")
    devices = groups * members
    rows, model = tokens.shape
    stream = rows * members
    shard = qkv_weight.shape[0]
    width = model // members
    units_dev = up_bias.shape[0]
    units = groups * units_dev

    small = jnp.concatenate([norm1_gain, norm1_bias, norm2_gain, norm2_bias, qkv_bias, out_bias, down_bias, up_bias])
    sizes = [norm1_gain.shape[0]] * 4 + [qkv_bias.shape[0], out_bias.shape[0], down_bias.shape[0], units_dev]
    small = jnp.pad(small, (0, shard * 128 - small.shape[0])).reshape(shard, 128)
    qkv_cut = qkv_weight.reshape(shard, 3, members, width).transpose(2, 0, 1, 3).reshape(members, shard, 3 * width)
    up_cut = up_weight.reshape(shard, groups, members, units_dev).transpose(2, 0, 1, 3).reshape(members, shard, units)
    small_cut = jnp.broadcast_to(small[None], (members, shard, 128))
    arrived = exchange(jnp.concatenate([qkv_cut, small_cut, up_cut], axis=2)).reshape(members * shard, -1)
    x_all = gather_rows(tokens)
    qkv_all = gather_dp(arrived[:, : 3 * width + 128])
    up_all = gather_dp(arrived[:, 3 * width + 128 :])
    down_all = gather_dp(down_weight)
    out_all = gather_dp(swap_owner(out_weight, False))
    cot_all = gather_rows(cotangent)

    packed = qkv_all[:, 3 * width :].reshape(devices, shard * 128).astype(F32)
    ends = np.cumsum([0] + sizes)
    gain_one, bias_one, gain_two, bias_two, shift_qkv, shift_out, shift_down, shift_up = (
        packed[:, ends[i] : ends[i + 1]] for i in range(8)
    )
    gain_one, bias_one, gain_two, bias_two = (a.reshape(1, model) for a in (gain_one, bias_one, gain_two, bias_two))
    shift_qkv = lax.dynamic_index_in_dim(shift_qkv.reshape(3, members, width), member, 1, keepdims=False).reshape(1, 3 * width)
    shift_up = lax.dynamic_index_in_dim(shift_up.reshape(groups, members, units_dev), member, 1, keepdims=False).reshape(1, units)

    sources = jnp.arange(members, dtype=jnp.int32)
    order = sources ^ member if members == 4 else sources
    doc_row = doc_ids[0]
    first = jnp.sum((doc_row[None, :] < doc_row[:, None]).astype(jnp.int32), axis=1)
    tables = rotary_tables(stream)

    q, k, v = call_qkv(order, x_all, gain_one, bias_one, qkv_all, shift_qkv, tables, rows)
    mixed, low_mixed, lse = call_fwd(first, q, k, v)
    part, d_mixed, to_norm, g_up, g_down, g_out, sums_two = call_mlp(
        order, x_all, cot_all, low_mixed, gain_two, bias_two, up_all, shift_up, down_all, out_all, rows
    )
    x_rows = tokens.astype(F32)
    d_rows = cotangent.astype(F32)
    output = (
        x_rows + reduce_rows(part) + shift_out.reshape(1, model) + shift_down.reshape(1, model)
    ).astype(LOW)
    g_down = scatter_dp(g_down).astype(F32)
    g_up = exchange(scatter_dp(g_up).reshape(members, shard, units))
    g_up = g_up.reshape(members, shard, groups, units_dev).transpose(1, 2, 0, 3).reshape(shard, -1).astype(F32)
    g_out = swap_owner(scatter_dp(g_out), True).astype(F32)

    d_qkv = call_bwd(first, q, k, v, d_mixed, mixed, lse, tables)
    part, g_qkv, sums_one = call_close(order, x_all, d_qkv, to_norm, gain_one, bias_one, qkv_all, rows)
    grad_tokens = (d_rows + reduce_rows(part)).astype(LOW)
    g_qkv = exchange(scatter_dp(g_qkv).reshape(members, shard, 3 * width))
    g_qkv = g_qkv.reshape(members, shard, 3, width).transpose(1, 2, 0, 3).reshape(shard, -1).astype(F32)

    wide_qkv = lax.dynamic_update_index_in_dim(
        jnp.zeros((3, members, width), F32), sums_one[0, : 3 * width].reshape(3, 1, width), member, 1
    )
    wide_up = lax.dynamic_update_index_in_dim(
        jnp.zeros((groups, members, units_dev), F32), sums_two[0, :units].reshape(groups, 1, units_dev), member, 1
    )
    vectors = [
        sums_one[2, :model], sums_one[1, :model], sums_two[2, :model], sums_two[1, :model],
        jnp.sum(d_rows, axis=0), wide_qkv.reshape(-1), wide_up.reshape(-1),
    ]
    summed = total_over_all(jnp.concatenate(vectors))
    place = group * members + member
    mine = []
    start = 0
    for vector in vectors:
        size = vector.shape[0] // devices
        mine.append(lax.dynamic_slice_in_dim(summed, start + place * size, size))
        start += vector.shape[0]
    gain_1, bias_1, gain_2, bias_2, end_bias, qkv_shift, up_shift = mine
    return (
        output, grad_tokens, gain_1, bias_1, gain_2, bias_2, g_qkv, qkv_shift, g_out, end_bias, g_up, up_shift, g_down, end_bias,
    )


def solution(mesh):
    row, vec = P(ALL, None), P(ALL)
    return jax.shard_map(
        local,
        mesh=mesh,
        in_specs=(row, row, P("dp", None), vec, vec, vec, vec, row, vec, row, vec, row, vec, row, vec),
        out_specs=(row, row, vec, vec, vec, vec, row, vec, row, vec, row, vec, row, vec),
        check_vma=False,
    )
```

```python
import functools

import jax
import jax.numpy as jnp
import numpy as np
from jax import lax
from jax.experimental import pallas as pl
from jax.experimental.pallas import tpu as pltpu
from jax.sharding import PartitionSpec as P

HEADS = 16
HEAD = 64
ROT = 16
BLOCK = 256
EPS = 1e-05
VMEM = 60 * 1024 * 1024
ALL = ("dp", "fsdp")
SHORT = pl.CostEstimate(flops=0, bytes_accessed=0, transcendentals=0)
F32 = jnp.float32
LOW = jnp.bfloat16


def dot(left, right, contract=((1,), (0,))):
    return lax.dot_general(left, right, (contract, ((), ())), preferred_element_type=F32)


NT = ((1,), (1,))
TN = ((0,), (0,))


def normed(x_rows):
    centre = x_rows - jnp.mean(x_rows, axis=-1, keepdims=True)
    spread = jnp.mean(centre * centre, axis=-1, keepdims=True)
    scale = lax.rsqrt(spread + EPS)
    return centre * scale, scale


def turned(z, cosine, sine_a, sine_b, sign):
    groups = []
    for start in range(0, z.shape[1], 128):
        part = z[:, start : start + 128]
        ahead = pltpu.roll(part, 128 - ROT // 2, 1)
        behind = pltpu.roll(part, ROT // 2, 1)
        groups.append(part * cosine + sign * (ahead * sine_a + behind * sine_b))
    return groups[0] if len(groups) == 1 else jnp.concatenate(groups, axis=1)


def head_only(array, head):
    lane = lax.broadcasted_iota(jnp.int32, array.shape, 1)
    keep = (lane >= head * HEAD) & (lane < (head + 1) * HEAD)
    return jnp.where(keep, array, jnp.zeros_like(array))


def params(*order):
    return pltpu.CompilerParams(vmem_limit_bytes=VMEM, dimension_semantics=order)


def whole(shape):
    return pl.BlockSpec(shape, lambda *_: (0,) * len(shape))


HBM = pl.BlockSpec(memory_space=pl.ANY)


def fetch(plan, step, refs, target, sems, begin):
    for at, pieces in enumerate(plan):

        @pl.when(step == at)
        def _():
            for index, (ref, start, put, size) in enumerate(pieces):
                copy = pltpu.make_async_copy(
                    refs[ref].at[pl.ds(start, size)], target.at[pl.ds(put, size)], sems.at[at, index]
                )
                if begin:
                    copy.start()
                else:
                    copy.wait()


def fetch_all(plan, refs, target, sems):
    for at in range(len(plan)):
        fetch(plan, at, refs, target, sems, True)


def plan_of(pieces, span):
    plan, total = [], sum(p.shape[0] for p in pieces)
    for low in range(0, total, span):
        taken, at = [], 0
        for index, piece in enumerate(pieces):
            a, b = max(low, at), min(low + span, at + piece.shape[0])
            if a < b:
                taken.append((index, a - at, a, b - a))
            at += piece.shape[0]
        plan.append(tuple(taken))
    return tuple(plan)


def store(plan, step, source, refs, sems, begin):
    for at, pieces in enumerate(plan):

        @pl.when(step == at)
        def _():
            for index, (ref, start, put, size) in enumerate(pieces):
                copy = pltpu.make_async_copy(
                    source.at[pl.ds(put, size)], refs[ref].at[pl.ds(start, size)], sems.at[at, index]
                )
                if begin:
                    copy.start()
                else:
                    copy.wait()


def pack_kernel(members, member, qkv, up, small, *out):
    width = qkv.shape[1] // 3 // members
    units_dev = 128
    groups = up.shape[1] // units_dev // members
    for bit in range(members):
        to = member[0] ^ bit
        for part in range(3):
            start = pl.multiple_of((part * members + to) * width, 128)
            out[bit][:, part * width : (part + 1) * width] = qkv[:, pl.ds(start, width)]
        out[bit][:, 3 * width : 3 * width + 128] = jnp.zeros((qkv.shape[0], 128), LOW)
        out[bit][0 : small.shape[0], 3 * width : 3 * width + 128] = small[...]
        for group in range(groups):
            start = pl.multiple_of((group * members + to) * units_dev, 128)
            low = 3 * width + 128 + group * units_dev
            out[bit][:, low : low + units_dev] = up[:, pl.ds(start, units_dev)]


def call_pack(member, qkv, up, small, members):
    shard = qkv.shape[0]
    columns = (qkv.shape[1] + up.shape[1]) // members + 128
    return pl.pallas_call(
        functools.partial(pack_kernel, members),
        grid_spec=pltpu.PrefetchScalarGridSpec(
            num_scalar_prefetch=1,
            grid=(1,),
            in_specs=[whole(qkv.shape), whole(up.shape), whole(small.shape)],
            out_specs=[whole((shard, columns))] * members,
        ),
        out_shape=[jax.ShapeDtypeStruct((shard, columns), LOW)] * members,
        compiler_params=params("arbitrary"),
        cost_estimate=SHORT,
        name="pack",
    )(member, qkv, up, small)


def place_kernel(cut, member, *refs):
    *pieces, first, second = refs
    shard = pieces[0].shape[0]
    for bit, piece in enumerate(pieces):
        rows = pl.ds(pl.multiple_of((member[0] ^ bit) * shard, shard), shard)
        first[rows, :] = piece[:, :cut]
        second[rows, :] = piece[:, cut:]


def call_place(member, pieces, cut):
    members, (shard, columns) = len(pieces), pieces[0].shape
    shapes = [(members * shard, cut), (members * shard, columns - cut)]
    return pl.pallas_call(
        functools.partial(place_kernel, cut),
        grid_spec=pltpu.PrefetchScalarGridSpec(
            num_scalar_prefetch=1,
            grid=(1,),
            in_specs=[whole(p.shape) for p in pieces],
            out_specs=[whole(a) for a in shapes],
        ),
        out_shape=[jax.ShapeDtypeStruct(a, LOW) for a in shapes],
        compiler_params=params("arbitrary"),
        cost_estimate=SHORT,
        name="place",
    )(member, *pieces)


def small_block(member, members, vectors, qkv_bias, up_bias):
    size = vectors[0].shape[0]
    wide = 128 // members * (members - 1)
    rows = jnp.pad(jnp.stack(vectors), ((0, 0), (wide, wide)))
    rows = lax.dynamic_slice_in_dim(rows, wide - member * size, 128, 1)
    wide = 3 * wide
    shift = lax.dynamic_slice_in_dim(jnp.pad(qkv_bias, (wide, wide)), wide - member * 3 * size, 384, 0)
    return jnp.concatenate([rows, shift.reshape(3, 128), up_bias[None], jnp.zeros((16 - len(vectors) - 4, 128), LOW)], axis=0)


def vectors_kernel(members, member, gathered, out, wide):
    groups, rows, _ = gathered.shape
    shard = rows // members
    model = groups * 128
    out[...] = jnp.zeros_like(out)
    for group in range(groups):
        blocks = [gathered[group, m * shard : m * shard + 16, :].astype(F32) for m in range(members)]
        block = blocks[0]
        for other in blocks[1:]:
            block = block + other
        lanes = slice(group * 128, (group + 1) * 128)
        for row in range(6):
            out[row : row + 1, lanes] = block[row : row + 1, :]
        for row in range(3):
            low = group * 384 + row * 128
            wide[0:1, low : low + 128] = block[6 + row : 7 + row, :]
        own = jnp.zeros((1, 128), F32)
        for m in range(members):
            own = own + jnp.where(member[0] == m, blocks[m][9:10, :], 0.0)
        out[6:7, lanes] = own
    width = model // members
    for part in range(3):
        start = pl.multiple_of(part * model + member[0] * width, 128)
        out[7 + part : 8 + part, :width] = wide[0:1, pl.ds(start, width)]


def call_vectors(member, gathered, members, cut):
    groups, rows, _ = gathered.shape
    model = groups * 128
    return pl.pallas_call(
        functools.partial(vectors_kernel, members),
        grid_spec=pltpu.PrefetchScalarGridSpec(
            num_scalar_prefetch=1,
            grid=(1,),
            in_specs=[pl.BlockSpec((groups, rows, 128), lambda i, o: (0, 0, cut // 128 - 1))],
            out_specs=whole((16, model)),
            scratch_shapes=[pltpu.VMEM((8, 3 * model), F32)],
        ),
        out_shape=jax.ShapeDtypeStruct((16, model), F32),
        compiler_params=params("arbitrary"),
        cost_estimate=SHORT,
        name="vectors",
    )(member, gathered)


def qkv_kernel(plan, count, order, *refs):
    pieces, rest = refs[:count], refs[count:]
    vectors, weight, cosine, sine_a, sine_b, q, k, v, normal, x, sems = rest
    step = pl.program_id(0)
    width = q.shape[1]
    span = q.shape[0]
    model = x.shape[1]

    @pl.when(step == 0)
    def _():
        fetch_all(plan, pieces, x, sems)

    fetch(plan, step, pieces, x, sems, False)
    n, _ = normed(x[pl.ds(pl.multiple_of(step * span, span), span), :].astype(F32))
    h = (n * vectors[0:1, :] + vectors[1:2, :]).astype(LOW)
    normal[...] = h
    tables = (cosine[...], sine_a[...], sine_b[...])
    rows = dot(h, weight[...].reshape(model, 3 * width))
    q[...] = (turned(rows[:, :width] + vectors[7:8, :width], *tables, 1.0) * 0.125).astype(LOW)
    k[...] = turned(rows[:, width : 2 * width] + vectors[8:9, :width], *tables, 1.0).astype(LOW)
    v[...] = (rows[:, 2 * width :] + vectors[9:10, :width]).astype(LOW)


def call_qkv(order, pieces, vectors, weight, tables, span, width):
    model = pieces[0].shape[1]
    plan = plan_of(pieces, span)
    rows = span * len(plan)
    there = lambda i, o: (o[i], 0)
    return pl.pallas_call(
        functools.partial(qkv_kernel, plan, len(pieces)),
        grid_spec=pltpu.PrefetchScalarGridSpec(
            num_scalar_prefetch=1,
            grid=(rows // span,),
            in_specs=[HBM] * len(pieces)
            + [whole(vectors.shape), whole(weight.shape[:2] + (3 * width,))]
            + [pl.BlockSpec((span, 128), there)] * 3,
            out_specs=[pl.BlockSpec((span, width), there)] * 3 + [pl.BlockSpec((span, model), there)],
            scratch_shapes=[pltpu.VMEM((rows, model), LOW), pltpu.SemaphoreType.DMA((len(plan), 2))],
        ),
        out_shape=[jax.ShapeDtypeStruct((rows, width), LOW)] * 3 + [jax.ShapeDtypeStruct((rows, model), LOW)],
        compiler_params=params("arbitrary"),
        cost_estimate=SHORT,
        name="qkv",
    )(order, *pieces, vectors, weight, *tables)


def masked_rows(target, array):
    for head in range(array.shape[1] // HEAD):
        target[head * BLOCK : (head + 1) * BLOCK, :] = head_only(array, head)


def over_keys(first, step, tiles):
    begin = first[step]
    count = step + 1 - begin

    def pair(i, _):
        tiles(begin + 2 * i, 2)
        return 0

    def single(at, _):
        tiles(at, 1)
        return 0

    lax.fori_loop(0, count // 2, pair, 0)
    lax.fori_loop(step + 1 - count % 2, step + 1, single, 0)


def by_eight(array):
    return array.reshape(BLOCK // 8, 8, BLOCK)


def fwd_kernel(first, q, k, v, mixed, low_mixed, lse, keys, values, scores, top, total, out):
    step = pl.program_id(0)
    width = q.shape[1]
    heads = width // HEAD
    stack = heads * BLOCK
    own = pl.ds(pl.multiple_of(step * BLOCK, BLOCK), BLOCK)
    masked_rows(keys.at[step], k[own, :])
    masked_rows(values.at[step], v[own, :])
    q_t = q[own, :].T
    top[...] = jnp.full_like(top, -1e30)
    total[...] = jnp.zeros_like(total)
    out[...] = jnp.zeros_like(out)

    def score(at, count):
        s = dot(keys[pl.ds(at, count)].reshape(count * stack, width), q_t)
        scores[pl.ds(at, count)] = s.reshape(count, stack, BLOCK)
        for head in range(heads):
            best = top[head]
            for tile in range(count):
                low = tile * stack + head * BLOCK
                best = jnp.maximum(best, jnp.max(by_eight(s[low : low + BLOCK]), axis=0))
            top[head] = best

    over_keys(first, step, score)
    peak = [jnp.max(top[head], axis=0, keepdims=True) for head in range(heads)]

    def mix(at, count):
        grown = []
        for tile in range(count):
            for head in range(heads):
                e = jnp.exp(scores[at + tile, head * BLOCK : (head + 1) * BLOCK] - peak[head])
                total[head] += jnp.sum(by_eight(e), axis=0)
                grown.append(e.astype(LOW))
        out[...] += dot(jnp.concatenate(grown, axis=0), values[pl.ds(at, count)].reshape(count * stack, width), TN)

    over_keys(first, step, mix)
    shares = []
    for head in range(heads):
        sums = jnp.sum(total[head], axis=0, keepdims=True)
        lse[head : head + 1, :] = peak[head] + jnp.log(sums)
        shares.append(jnp.broadcast_to(1.0 / sums, (HEAD, BLOCK)))
    result = out[...] * jnp.concatenate(shares, axis=0).T
    mixed[...] = result
    low_mixed[...] = result.astype(LOW)


def call_fwd(first, q, k, v):
    rows, width = q.shape
    heads = width // HEAD
    blocks = rows // BLOCK
    return pl.pallas_call(
        fwd_kernel,
        grid_spec=pltpu.PrefetchScalarGridSpec(
            num_scalar_prefetch=1,
            grid=(blocks,),
            in_specs=[whole((rows, width))] * 3,
            out_specs=[
                pl.BlockSpec((BLOCK, width), lambda i, o: (i, 0)),
                pl.BlockSpec((BLOCK, width), lambda i, o: (i, 0)),
                pl.BlockSpec((heads, BLOCK), lambda i, o: (0, i)),
            ],
            scratch_shapes=[
                pltpu.VMEM((blocks, heads * BLOCK, width), LOW),
                pltpu.VMEM((blocks, heads * BLOCK, width), LOW),
                pltpu.VMEM((blocks, heads * BLOCK, BLOCK), F32),
                pltpu.VMEM((heads, 8, BLOCK), F32),
                pltpu.VMEM((heads, 8, BLOCK), F32),
                pltpu.VMEM((BLOCK, width), F32),
            ],
        ),
        out_shape=[
            jax.ShapeDtypeStruct((rows, width), F32),
            jax.ShapeDtypeStruct((rows, width), LOW),
            jax.ShapeDtypeStruct((heads, rows), F32),
        ],
        compiler_params=params("arbitrary"),
        cost_estimate=SHORT,
        name="attend",
    )(first, q, k, v)


def bwd_kernel(
    low_head, count_before, first, q, k, v, d_mixed, mixed, lse, cosine, sine_a, sine_b, normal, *rest
):
    before, rest = rest[:count_before], rest[count_before:]
    d_rows, grad, sums, keys, values, sum_q, sum_k, sum_v, queries, seeds, h, sem = rest
    step = pl.program_id(0)
    width = q.shape[1]
    heads = width // HEAD
    stack = heads * BLOCK
    own = pl.ds(pl.multiple_of(step * BLOCK, BLOCK), BLOCK)
    load = pltpu.make_async_copy(normal, h, sem.at[0])

    @pl.when(step == 0)
    def _():
        load.start()

    q_own = q[own, :]
    s_own = d_mixed[own, :]
    masked_rows(keys.at[step], k[own, :])
    masked_rows(values.at[step], v[own, :])
    masked_rows(queries, q_own)
    masked_rows(seeds, s_own)
    q_t = q_own.T
    s_t = s_own.T
    product_t = (s_own.astype(F32) * mixed[own, :]).T
    delta = [jnp.sum(product_t[head * HEAD : (head + 1) * HEAD, :], axis=0, keepdims=True) for head in range(heads)]
    log_total = [lse[low_head + head : low_head + head + 1, :] for head in range(heads)]
    sum_q[...] = jnp.zeros_like(sum_q)
    sum_k[own, :] = jnp.zeros((BLOCK, width), F32)
    sum_v[own, :] = jnp.zeros((BLOCK, width), F32)

    def tiles(at, count):
        key_rows = keys[pl.ds(at, count)].reshape(count * stack, width)
        s = dot(key_rows, q_t)
        d_p = dot(values[pl.ds(at, count)].reshape(count * stack, width), s_t)
        wide_probs, wide_scores, tall_scores = [], [], []
        for tile in range(count):
            low_probs, low_scores = [], []
            for head in range(heads):
                low = tile * stack + head * BLOCK
                probs = jnp.exp(s[low : low + BLOCK] - log_total[head])
                low_scores.append((probs * (d_p[low : low + BLOCK] - delta[head])).astype(LOW))
                low_probs.append(probs.astype(LOW))
            wide_probs.append(jnp.concatenate(low_probs, axis=1))
            wide_scores.append(jnp.concatenate(low_scores, axis=1))
            tall_scores += low_scores
        rows = pl.ds(pl.multiple_of(at * BLOCK, BLOCK), count * BLOCK)
        sum_v[rows, :] += dot(jnp.concatenate(wide_probs, axis=0), seeds[...])
        sum_k[rows, :] += dot(jnp.concatenate(wide_scores, axis=0), queries[...])
        sum_q[...] += dot(jnp.concatenate(tall_scores, axis=0), key_rows, TN)

    over_keys(first, step, tiles)
    d_rows[own, :width] = (turned(sum_q[...], cosine[own, :], sine_a[own, :], sine_b[own, :], -1.0) * 0.125).astype(LOW)

    @pl.when(step == pl.num_programs(0) - 1)
    def _():
        def close(at, _):
            rows = pl.ds(pl.multiple_of(at * BLOCK, BLOCK), BLOCK)
            d_rows[rows, width : 2 * width] = turned(sum_k[rows, :], cosine[rows, :], sine_a[rows, :], sine_b[rows, :], -1.0).astype(LOW)
            d_rows[rows, 2 * width :] = sum_v[rows, :].astype(LOW)
            return 0

        lax.fori_loop(0, q.shape[0] // BLOCK, close, 0)
        low = 0
        for ref in before:
            low = ref.shape[1]
            grad[:, :low] = ref[...]
        load.wait()
        grad[:, low:] = dot(h[...], d_rows[...], TN).astype(LOW)
        sums[0:1, :] = jnp.sum(d_rows[...].astype(F32), axis=0, keepdims=True)


def call_bwd(first, q, k, v, d_mixed, mixed, lse, tables, normal, part, parts, before):
    model = normal.shape[1]
    rows, full = q.shape
    width = full // parts
    heads = width // HEAD
    blocks = rows // BLOCK
    lanes = pl.BlockSpec((rows, width), lambda i, o: (0, part))
    return pl.pallas_call(
        functools.partial(bwd_kernel, part * heads, len(before)),
        grid_spec=pltpu.PrefetchScalarGridSpec(
            num_scalar_prefetch=1,
            grid=(blocks,),
            in_specs=[lanes] * 5
            + [pl.BlockSpec((heads * parts, BLOCK), lambda i, o: (0, i))]
            + [whole((rows, 128))] * 3
            + [HBM]
            + [whole(b.shape) for b in before],
            out_specs=[whole((rows, 3 * width)), whole((model, 3 * width * (part + 1))), whole((8, 3 * width))],
            scratch_shapes=[
                pltpu.VMEM((blocks, heads * BLOCK, width), LOW),
                pltpu.VMEM((blocks, heads * BLOCK, width), LOW),
                pltpu.VMEM((BLOCK, width), F32),
                pltpu.VMEM((rows, width), F32),
                pltpu.VMEM((rows, width), F32),
                pltpu.VMEM((heads * BLOCK, width), LOW),
                pltpu.VMEM((heads * BLOCK, width), LOW),
                pltpu.VMEM((rows, model), LOW),
                pltpu.SemaphoreType.DMA((1,)),
            ],
        ),
        out_shape=[
            jax.ShapeDtypeStruct((rows, 3 * width), LOW),
            jax.ShapeDtypeStruct((model, 3 * width * (part + 1)), LOW),
            jax.ShapeDtypeStruct((8, 3 * width), F32),
        ],
        compiler_params=params("arbitrary"),
        cost_estimate=SHORT,
        name="attend_back",
    )(first, q, k, v, d_mixed, mixed, lse, *tables, normal, *before)


def mlp_kernel(plan, out_plan, count, out_count, joined, chunk, order, *refs):
    x_pieces, cot_pieces, rest = refs[:count], refs[count : 2 * count], refs[2 * count :]
    mixed, vectors, rest = rest[0], rest[1], rest[2:]
    mats, rest = rest[: 1 if joined else 3], rest[1 if joined else 3 :]
    parts, rest = rest[:out_count], rest[out_count:]
    d_mixed, to_norm, rest = rest[0], rest[1], rest[2:]
    grads, rest = rest[: 1 if joined else 3], rest[1 if joined else 3 :]
    sums, normal, cot, active, d_up, own_mixed, g_out, staged, x_sems, cot_sems, out_sems = rest
    step = pl.program_id(0)
    steps = len(plan)
    span, width = own_mixed.shape[0] // steps, own_mixed.shape[1]
    model, units = normal.shape[1], active.shape[1]
    if joined:
        groups = mats[0].shape[0]
        cuts = [0, model // groups, (model + units) // groups, (model + units + width) // groups]
        w_up, w_down, w_out = (mats[0].at[:, pl.ds(cuts[i], cuts[i + 1] - cuts[i]), :] for i in range(3))
    else:
        w_up, w_down, w_out = mats
    as_up = lambda: w_up[...].reshape(model, units)
    as_down = lambda: w_down[...].reshape(units, model)
    as_out = lambda: w_out[...].reshape(width, model)

    @pl.when(step == 0)
    def _():
        fetch_all(plan, x_pieces, normal, x_sems)
        fetch_all(plan, cot_pieces, cot, cot_sems)
        sums[...] = jnp.zeros_like(sums)

    fetch(plan, step, x_pieces, normal, x_sems, False)
    fetch(plan, step, cot_pieces, cot, cot_sems, False)

    @pl.when(step < steps)
    def _():
        here = pl.ds(pl.multiple_of(step * span, span), span)
        n, _ = normed(normal[here, :].astype(F32))
        h = (n * vectors[2:3, :] + vectors[3:4, :]).astype(LOW)
        normal[here, :] = h
        dy = cot[here, :]
        own = mixed[pl.ds(pl.multiple_of(order[step] * span, span), span), :]
        own_mixed[here, :] = own
        d_mixed[...] = dot(dy, as_out(), NT).astype(LOW)
        up, down = as_up(), as_down()
        for low in range(0, units, chunk):
            cols = slice(low, low + chunk)
            u = dot(h, up[:, cols]) + vectors[6:7, cols]
            d_active = dot(dy, down[cols], NT)
            cdf = 0.5 * (1.0 + lax.erf(u * np.float32(np.sqrt(0.5))))
            slope = cdf + u * (jnp.exp(-0.5 * u * u) * np.float32(1.0 / np.sqrt(2.0 * np.pi)))
            active[here, cols] = (u * cdf).astype(LOW)
            back = (d_active * slope).astype(LOW)
            d_up[here, cols] = back
            sums[0:1, cols] += jnp.sum(back.astype(F32), axis=0, keepdims=True)
        staged[here, :] = (dot(active[here, :], down) + dot(own, as_out())).astype(LOW)
        d_h = dot(d_up[here, :], up, NT)
        sums[1:2, :model] += jnp.sum(d_h, axis=0, keepdims=True)
        sums[2:3, :model] += jnp.sum(d_h * n, axis=0, keepdims=True)
        to_norm[...] = d_h * vectors[2:3, :]

        @pl.when(step == 0)
        def _():
            sums[3:4, :model] = jnp.sum(dy.astype(F32), axis=0, keepdims=True)

    store(out_plan, step, staged, parts, out_sems, True)

    @pl.when(step >= steps)
    def _():
        at = step - steps
        many = pl.num_programs(0) - steps

        @pl.when(at == 0)
        def _():
            g_out[...] = dot(own_mixed[...], cot[...], TN).astype(LOW)

        up_cols = pl.ds(pl.multiple_of(at * (model // many), 128), model // many)
        down_cols = pl.ds(pl.multiple_of(at * (units // many), 128), units // many)
        out_rows = pl.ds(pl.multiple_of(at * (width // many), 16), width // many)
        up_grad = dot(normal[:, up_cols], d_up[...], TN).astype(LOW)
        down_grad = dot(active[:, down_cols], cot[...], TN).astype(LOW)
        if joined:
            block = grads[0].shape[0]
            grads[0][:, cuts[0] : cuts[1], :] = up_grad.reshape(block, cuts[1], units)
            grads[0][:, cuts[1] : cuts[2], :] = down_grad.reshape(block, cuts[2] - cuts[1], model)
            grads[0][:, cuts[2] : cuts[3], :] = g_out[out_rows, :].reshape(block, cuts[3] - cuts[2], model)
        else:
            grads[0][...] = up_grad
            grads[1][...] = down_grad
            grads[2][...] = g_out[out_rows, :]

    @pl.when(step == pl.num_programs(0) - 1)
    def _():
        for at in range(steps):
            store(out_plan, at, staged, parts, out_sems, False)


def call_mlp(order, x_pieces, cot_pieces, mixed, vectors, mats, span, units, out_shapes):
    rows, width = mixed.shape
    model = x_pieces[0].shape[1]
    joined = len(mats) == 1
    plan, out_plan = plan_of(x_pieces, span), plan_of(out_shapes, span)
    steps, many = len(plan), 4
    count = len(x_pieces)
    here = lambda i, o: (jnp.minimum(i, steps - 1), 0)
    there = lambda i, o: (o[jnp.minimum(i, steps - 1)], 0)
    later = lambda i, o: (jnp.maximum(i - steps, 0), 0)
    if joined:
        groups = mats[0].shape[0]
        grads = [(groups, (model + units + width) // groups, model)]
        grad_specs = [pl.BlockSpec((groups // many,) + grads[0][1:], lambda i, o: (jnp.maximum(i - steps, 0), 0, 0))]
    else:
        grads = [(model, units), (units, model), (width, model)]
        grad_specs = [pl.BlockSpec((a // many, b), later) for a, b in grads]
    sums = (8, max(model, units))
    return pl.pallas_call(
        functools.partial(mlp_kernel, plan, out_plan, count, len(out_shapes), joined, 256),
        grid_spec=pltpu.PrefetchScalarGridSpec(
            num_scalar_prefetch=1,
            grid=(steps + many,),
            in_specs=[HBM] * (2 * count)
            + [whole((rows, width)), whole(vectors.shape)]
            + [pl.BlockSpec(m.shape, lambda *_: (0, 0, 0), pipeline_mode=pl.Buffered(1)) for m in mats],
            out_specs=[HBM] * len(out_shapes)
            + [pl.BlockSpec((span, width), there), pl.BlockSpec((span, model), here)]
            + grad_specs
            + [whole(sums)],
            scratch_shapes=[
                pltpu.VMEM((rows, model), LOW),
                pltpu.VMEM((rows, model), LOW),
                pltpu.VMEM((rows, units), LOW),
                pltpu.VMEM((rows, units), LOW),
                pltpu.VMEM((rows, width), LOW),
                pltpu.VMEM((width, model), LOW),
                pltpu.VMEM((rows, model), LOW),
                pltpu.SemaphoreType.DMA((steps, 2)),
                pltpu.SemaphoreType.DMA((steps, 2)),
                pltpu.SemaphoreType.DMA((steps, 2)),
            ],
        ),
        out_shape=list(out_shapes)
        + [jax.ShapeDtypeStruct((rows, width), LOW), jax.ShapeDtypeStruct((rows, model), F32)]
        + [jax.ShapeDtypeStruct(g, LOW) for g in grads]
        + [jax.ShapeDtypeStruct(sums, F32)],
        compiler_params=params("arbitrary"),
        cost_estimate=SHORT,
        name="mlp",
    )(order, *x_pieces, *cot_pieces, mixed, vectors, *mats)


def close_kernel(plan, many, parts, order, *refs):
    xs, refs = refs[:many], refs[many:]
    d_rows, (to_norm, vectors, weight), refs = refs[:parts], refs[parts : parts + 3], refs[parts + 3 :]
    outs, (sums, x, e_low) = refs[: len(plan)], refs[len(plan) :]
    step = pl.program_id(0)

    @pl.when(step == 0)
    def _():
        sums[...] = jnp.zeros_like(sums)

    for at, (piece, _, _) in enumerate(plan):

        @pl.when(step == at)
        def _():
            x[...] = xs[piece][...]

    model = x.shape[1]
    n, scale = normed(x[...].astype(F32))
    width = d_rows[0].shape[1] // 3
    rows = jnp.concatenate([d[:, i * width : (i + 1) * width] for i in range(3) for d in d_rows], axis=1)
    d_h = dot(rows, weight[...].reshape(model, 3 * width * parts), NT)
    sums[1:2, :] += jnp.sum(d_h, axis=0, keepdims=True)
    sums[0:1, :] += jnp.sum(d_h * n, axis=0, keepdims=True)
    e = d_h * vectors[0:1, :] + to_norm[...]
    e = e - jnp.mean(e, axis=-1, keepdims=True) - n * jnp.mean(e * n, axis=-1, keepdims=True)
    e_low[...] = (e * scale).astype(LOW)
    for at in range(len(plan)):

        @pl.when(step == at)
        def _():
            outs[at][...] = e_low[...]


def call_close(order, pieces, plan, d_rows, to_norm, vectors, weight, span):
    model = pieces[0].shape[1]
    width3 = sum(d.shape[1] for d in d_rows)
    per = span // BLOCK
    steps = len(plan)

    def pick(values, i):
        value = jnp.int32(values[-1])
        for at in range(len(values) - 1):
            value = jnp.where(i == at, jnp.int32(values[at]), value)
        return value

    def block_of(piece):
        reads = [(at, start // BLOCK) for at, (index, start, _) in enumerate(plan) if index == piece]
        values = [next((b for a, b in reversed(reads) if a <= at), reads[0][1]) for at in range(steps)]
        return lambda i, o: (pick(values, i), 0)

    places = [low // BLOCK for _, _, low in plan]
    here = lambda i, o: (pick(places, i), 0)
    there = lambda i, o: (o[pick(places, i) // per] * per + pick(places, i) % per, 0)
    return pl.pallas_call(
        functools.partial(close_kernel, plan, len(pieces), len(d_rows)),
        grid_spec=pltpu.PrefetchScalarGridSpec(
            num_scalar_prefetch=1,
            grid=(steps,),
            in_specs=[pl.BlockSpec((BLOCK, model), block_of(piece)) for piece in range(len(pieces))]
            + [pl.BlockSpec((BLOCK, d.shape[1]), there) for d in d_rows]
            + [pl.BlockSpec((BLOCK, model), here), whole(vectors.shape), whole(weight.shape[:2] + (width3,))],
            out_specs=[whole((BLOCK, model))] * steps + [whole((8, model))],
            scratch_shapes=[pltpu.VMEM((BLOCK, model), LOW), pltpu.VMEM((BLOCK, model), LOW)],
        ),
        out_shape=[jax.ShapeDtypeStruct((BLOCK, model), LOW)] * steps + [jax.ShapeDtypeStruct((8, model), F32)],
        compiler_params=params("arbitrary"),
        cost_estimate=SHORT,
        name="close",
    )(order, *pieces, *d_rows, to_norm, vectors, weight)


def finish_kernel(halves, base, shift, *refs):
    parts, out = refs[:-1], refs[-1]
    shifts = jnp.sum(shift[...], axis=0, keepdims=True)
    for at in range(2):

        @pl.when(pl.program_id(0) == at)
        def _():
            total = base[...].astype(F32) + shifts
            for part in parts[at::2]:
                total = total + part[...].astype(F32)
            out[...] = total.astype(LOW)


def call_finish(base, shift, low, high):
    rows, model = base.shape
    half = rows // 2
    arrays = [a for pair in zip(low, high) for a in pair]
    return pl.pallas_call(
        functools.partial(finish_kernel, len(low)),
        grid=(2,),
        in_specs=[pl.BlockSpec((half, model), lambda i: (i, 0)), whole(shift.shape)] + [whole((half, model))] * len(arrays),
        out_specs=pl.BlockSpec((half, model), lambda i: (i, 0)),
        out_shape=jax.ShapeDtypeStruct((rows, model), LOW),
        compiler_params=params("arbitrary"),
        cost_estimate=SHORT,
        name="finish",
    )(base, shift, *arrays)


def cut_kernel(count, member, source, *out):
    shard = out[0].shape[0]
    for bit in range(count):
        out[bit][...] = source[pl.ds(pl.multiple_of((member[0] ^ bit) * shard, shard), shard), :]
    low = count * shard
    for ref in out[count:]:
        ref[...] = source[low : low + ref.shape[0], :].astype(ref.dtype)
        low += ref.shape[0]


def call_cut(member, source, count, shard, rest):
    columns = source.shape[1]
    shapes = [jax.ShapeDtypeStruct((shard, columns), LOW)] * count
    shapes += [jax.ShapeDtypeStruct((rows, columns), kind) for rows, kind in rest]
    return pl.pallas_call(
        functools.partial(cut_kernel, count),
        grid_spec=pltpu.PrefetchScalarGridSpec(
            num_scalar_prefetch=1,
            grid=(1,),
            in_specs=[whole(source.shape)],
            out_specs=[whole(a.shape) for a in shapes],
        ),
        out_shape=shapes,
        compiler_params=params("arbitrary"),
        cost_estimate=SHORT,
        name="cut",
    )(member, source)


def join_kernel(places, stride, member, *refs):
    *pieces, out = refs
    for bit, piece in enumerate(pieces):
        for block, place in enumerate(places):
            start = pl.multiple_of(place + (member[0] ^ bit) * stride, 128)
            out[:, pl.ds(start, 128)] = piece[:, block * 128 : (block + 1) * 128].astype(F32)


def call_join(member, pieces, places, stride):
    shard, columns = pieces[0].shape
    shape = (shard, columns * len(pieces))
    return pl.pallas_call(
        functools.partial(join_kernel, tuple(places), stride),
        grid_spec=pltpu.PrefetchScalarGridSpec(
            num_scalar_prefetch=1,
            grid=(1,),
            in_specs=[whole(p.shape) for p in pieces],
            out_specs=whole(shape),
        ),
        out_shape=jax.ShapeDtypeStruct(shape, F32),
        compiler_params=params("arbitrary"),
        cost_estimate=SHORT,
        name="join",
    )(member, *pieces)


def bundle_kernel(members, halves, member, two, *refs):
    *ones, out = refs
    thirds, ones = ones[:halves], ones[halves:]
    out[...] = jnp.zeros_like(out)
    out[0:2, :] = functools.reduce(lambda a, b: a + b, [one[0:2, :] for one in ones])
    out[2:3, :] = two[2:3, :]
    out[3:4, :] = two[1:2, :]
    out[4:5, :] = two[3:4, :]
    model = out.shape[1]
    width = model // members
    size = width // halves
    for half, third in enumerate(thirds):
        lanes = pl.ds(pl.multiple_of(member[0] * width + half * size, 128), size)
        for part in range(3):
            out[5 + part : 6 + part, lanes] = third[0:1, part * size : (part + 1) * size]
    per = model // (128 * members)
    for group in range(two.shape[1] // 128):
        start = pl.multiple_of((group % per * members + member[0]) * 128, 128)
        row = 8 + group // per
        out[row : row + 1, pl.ds(start, 128)] = two[0:1, group * 128 : (group + 1) * 128]


def call_bundle(member, members, two, thirds, ones):
    shape = (16, two.shape[1])
    return pl.pallas_call(
        functools.partial(bundle_kernel, members, len(thirds)),
        grid_spec=pltpu.PrefetchScalarGridSpec(
            num_scalar_prefetch=1,
            grid=(1,),
            in_specs=[whole(a.shape) for a in (two, *thirds, *ones)],
            out_specs=whole(shape),
        ),
        out_shape=jax.ShapeDtypeStruct(shape, F32),
        compiler_params=params("arbitrary"),
        cost_estimate=SHORT,
        name="bundle",
    )(member, two, *thirds, *ones)


def across(array, bit):
    size = lax.axis_size("fsdp")
    return lax.ppermute(array, "fsdp", [(i, i ^ bit) for i in range(size)])


def exchange(pieces):
    size = lax.axis_size("fsdp")
    if size != 4:
        return lax.all_to_all(pieces, "fsdp", split_axis=0, concat_axis=0, tiled=True)
    member = lax.axis_index("fsdp")
    out = pieces
    for bit in range(1, size):
        mine = lax.dynamic_index_in_dim(pieces, member ^ bit, 0, keepdims=False)
        out = lax.dynamic_update_index_in_dim(out, across(mine, bit), member ^ bit, 0)
    return out


def behind(array, *others):
    return lax.optimization_barrier((array, *others))[0]


def behind_all(arrays, *others):
    return tuple(behind(array, *others) for array in arrays)


def gather_rows(rows, near, *others):
    if lax.axis_size("fsdp") != 4:
        return [lax.all_gather(rows, "fsdp", axis=0, tiled=True)]
    half = rows.shape[0] // 2
    one, two = near
    low_half = across(behind(one, *others)[:half], 2)
    high_half = across(behind(two, *others)[half:], 1)
    return [rows, one, two, low_half, high_half]


def reduce_begin(parts):
    if len(parts) == 1:
        return ()
    _, _, one_low, _, _, two_high, three_low, three_high = parts
    return across(three_low, 1), across(three_high, 2), across(one_low, 1), across(two_high, 2)


def reduce_middle(parts, begun):
    if len(parts) == 1:
        return ()
    add = lambda a, b: (a.astype(F32) + b.astype(F32)).astype(LOW)
    return add(parts[3], begun[1]), add(parts[4], begun[0])


def reduce_end(base, shift, parts, begun, middle):
    if len(parts) == 1:
        total = lax.psum_scatter(parts[0], "fsdp", scatter_dimension=0, tiled=True).astype(F32)
        return (base.astype(F32) + total + jnp.sum(shift, axis=0, keepdims=True)).astype(LOW)
    one_high, two_low = across(middle[0], 1), across(middle[1], 2)
    return call_finish(base, shift, (parts[0], begun[2], two_low), (parts[1], one_high, begun[3]))


def total_over_all(vector, between=()):
    count = lax.axis_size("dp") * lax.axis_size("fsdp")
    step = 1
    while step < count:
        radix = 4 if count // step >= 4 else 2
        far = [lax.ppermute(vector, ALL, [(i, i ^ (step * k)) for i in range(count)]) for k in range(1, radix)]
        for other in far:
            vector = vector + other
        if step == 1 and between:
            vector = behind(vector, *between)
        step *= radix
    return vector


def swap_owner(array, back):
    groups, members = lax.axis_size("dp"), lax.axis_size("fsdp")
    pairs = [(m * groups + g, g * members + m) for g in range(groups) for m in range(members)]
    if back:
        pairs = [(b, a) for a, b in pairs]
    return lax.ppermute(array, ALL, pairs)


def gather_dp(array):
    return lax.all_gather(array, "dp", axis=0)


def scatter_dp(array):
    return lax.psum_scatter(array, "dp", scatter_dimension=0, tiled=True)


def rotary_tables(length):
    half = ROT // 2
    frequency = (np.float32(10000.0) ** (-(np.arange(half, dtype=np.float32) * np.float32(2.0)) / np.float32(ROT))).astype(np.float32)
    angles = (np.arange(length, dtype=np.float32)[:, None] * frequency[None, :]).astype(np.float32)
    cosine = np.cos(angles).astype(np.float32)
    sine = np.sin(angles).astype(np.float32)
    cos_row = np.ones((length, 128), np.float32)
    ahead = np.zeros((length, 128), np.float32)
    behind = np.zeros((length, 128), np.float32)
    for start in range(0, 128, HEAD):
        cos_row[:, start : start + half] = cosine
        cos_row[:, start + half : start + ROT] = cosine
        ahead[:, start : start + half] = -sine
        behind[:, start + half : start + ROT] = sine
    return tuple(jnp.asarray(t) for t in (cos_row, ahead, behind))


def local(
    tokens, cotangent, doc_ids, norm1_gain, norm1_bias, norm2_gain, norm2_bias, qkv_weight, qkv_bias,
    out_weight, out_bias, up_weight, up_bias, down_weight, down_bias,
):
    groups, members = lax.axis_size("dp"), lax.axis_size("fsdp")
    group, member = lax.axis_index("dp"), lax.axis_index("fsdp")
    devices = groups * members
    rows, model = tokens.shape
    stream = rows * members
    shard = qkv_weight.shape[0]
    width = model // members
    units_dev = up_bias.shape[0]
    units = groups * units_dev
    paired = members == 4 and units_dev == 128 and units == model
    me = member.astype(jnp.int32).reshape(1)
    vectors_in = [norm1_gain, norm1_bias, norm2_gain, norm2_bias, out_bias, down_bias]

    if paired:
        small = small_block(member, members, vectors_in, qkv_bias, up_bias)
        packed = call_pack(me, qkv_weight, up_weight, small, members)
        arrived = [packed[0]] + [across(packed[bit], bit) for bit in range(1, members)]
        x_in = behind(tokens, *arrived[1:])
        cut = 3 * width + 128
        first_in, up_in = call_place(me, arrived, cut)
        w_first = gather_dp(first_in)
        mats = (gather_dp(jnp.concatenate([up_in, down_weight, swap_owner(out_weight, False)], axis=0)),)
        vectors = call_vectors(me, w_first, members, cut)
    else:
        qkv_cut = qkv_weight.reshape(shard, 3, members, width).transpose(2, 0, 1, 3).reshape(members, shard, 3 * width)
        up_cut = up_weight.reshape(shard, groups, members, units_dev).transpose(2, 0, 1, 3).reshape(members, shard, units)
        arrived = exchange(jnp.concatenate([qkv_cut, up_cut], axis=2)).reshape(members * shard, -1)
        w_first = gather_dp(arrived[:, : 3 * width])
        x_in = tokens
        mats = (gather_dp(arrived[:, 3 * width :]), gather_dp(down_weight), gather_dp(swap_owner(out_weight, False)))
        full = [lax.all_gather(a, ALL, axis=0, tiled=True).astype(F32) for a in vectors_in]
        shift = lax.all_gather(qkv_bias, ALL, axis=0, tiled=True).astype(F32).reshape(3, members, width)
        shift = lax.dynamic_index_in_dim(shift, member, 1, keepdims=False)
        up_all = lax.all_gather(up_bias, "dp", axis=0, tiled=True).astype(F32)
        lines = full + [jnp.pad(a, (0, model - a.shape[0])) for a in (up_all, shift[0], shift[1], shift[2])]
        vectors = jnp.pad(jnp.stack(lines), ((0, 6), (0, 0)))

    x_near = (across(x_in, 1), across(x_in, 2)) if members == 4 else ()
    x_pieces = gather_rows(x_in, x_near)
    sources = jnp.arange(members, dtype=jnp.int32)
    order = sources ^ member if members == 4 else sources
    doc_row = doc_ids[0]
    first = jnp.sum((doc_row[None, :] < doc_row[:, None]).astype(jnp.int32), axis=1)
    tables = rotary_tables(stream)

    q, k, v, normal = call_qkv(order, x_pieces, vectors, w_first, tables, rows, width)
    cot_in = behind(cotangent, *x_pieces[1:])
    cot_near = (across(cot_in, 1), across(cot_in, 2)) if members == 4 else ()
    cot_pieces = gather_rows(cot_in, cot_near, q)
    mixed, low_mixed, lse = call_fwd(first, q, k, v)
    half = rows // 2
    out_sizes = [half] * (2 * members) if members == 4 else [stream]
    out_shapes = [jax.ShapeDtypeStruct((size, model), LOW) for size in out_sizes]
    results = call_mlp(order, x_pieces, cot_pieces, low_mixed, vectors, mats, rows, units, out_shapes)
    count = len(out_shapes)
    parts, (d_mixed, to_norm), grads, sums_two = results[:count], results[count : count + 2], results[count + 2 : -1], results[-1]
    scattered = scatter_dp(grads[0].reshape(-1, model)) if paired else None

    begun = reduce_begin(parts)
    halves = 2 if width % 256 == 0 else 1
    back = [call_bwd(first, q, k, v, d_mixed, mixed, lse, tables, normal, 0, halves, ())]
    middle = reduce_middle(parts, behind_all(begun, back[0][0]))
    output = reduce_end(tokens, vectors[4:6, :], parts, begun, middle)
    for part in range(1, halves):
        q = behind(q, *middle)
        back.append(call_bwd(first, q, k, v, d_mixed, mixed, lse, tables, normal, part, halves, (back[-1][1],)))
    d_qkv = [b[0] for b in back]
    g_qkv = back[-1][1]
    sums_qkv = [b[2] for b in back]
    to_norm = behind(to_norm, output)
    if members == 4:
        plan = [(0, 0, 3 * rows), (1, 0, 3 * rows + half)]
        *three, ones_a = call_close(order, x_pieces[3:], plan, d_qkv, to_norm, vectors, w_first, rows)
        if paired:
            to_norm = behind(to_norm, scattered, *three)
        plan = [(1, 0, rows), (2, half, 2 * rows + half), (1, half, rows + half), (2, 0, 2 * rows), (0, 0, 0), (0, half, half)]
        one_low, two_high, one_high, two_low, own_low, own_high, ones_b = call_close(
            order, x_pieces[:3], plan, d_qkv, to_norm, vectors, w_first, rows
        )
        final = [own_low, own_high, one_low, one_high, two_low, two_high, *three]
        ones = [ones_a, ones_b]
    else:
        plan = [(0, low, low) for low in range(0, stream, BLOCK)]
        *final, ones = call_close(order, x_pieces, plan, d_qkv, to_norm, vectors, w_first, rows)
        final, ones = [jnp.concatenate(final, axis=0)], [ones]
    begun = reduce_begin(final)
    middle = reduce_middle(final, begun)
    grad_tokens = reduce_end(cotangent, jnp.zeros((1, model), F32), final, begun, middle)

    if paired:
        g_qkv = scatter_dp(behind(g_qkv, scattered, *three))
        *g_up, g_down, g_out = call_cut(me, scattered, members, shard, [(down_weight.shape[0], F32), (shard, LOW)])
        places = [b * members * units_dev for b in range(groups)]
        g_up = call_join(me, [g_up[0]] + [across(g_up[bit], bit) for bit in range(1, members)], places, units_dev)
        g_out = swap_owner(g_out, True).astype(F32)
        ready = call_bundle(me, members, sums_two, sums_qkv, [behind(ones[0], g_up, g_out)] + ones[1:])
        g_qkv_pieces = g_qkv = call_cut(me, g_qkv, members, shard, [])
        places = [part * model + half * (width // halves) for half in range(halves) for part in range(3)]
        g_qkv = call_join(me, [g_qkv[0]] + [across(g_qkv[bit], bit) for bit in range(1, members)], places, width)
        summed = total_over_all(ready, g_qkv_pieces).reshape(-1)
    else:
        g_up, g_down, g_out = [scatter_dp(g) for g in grads]
        g_qkv = scatter_dp(g_qkv)
        g_down = g_down.astype(F32)
        g_out = swap_owner(g_out, True).astype(F32)
        g_up = exchange(g_up.reshape(members, shard, units))
        g_up = g_up.reshape(members, shard, groups, units_dev).transpose(1, 2, 0, 3).reshape(shard, -1).astype(F32)
        g_qkv = exchange(g_qkv.reshape(members, shard, 3 * width)).reshape(members, shard, halves, 3, width // halves)
        g_qkv = g_qkv.transpose(1, 3, 0, 2, 4).reshape(shard, -1).astype(F32)
        thirds = jnp.concatenate([a[0].reshape(3, 1, width // halves) for a in sums_qkv], axis=2)
        wide_qkv = lax.dynamic_update_index_in_dim(jnp.zeros((3, members, width), F32), thirds, member, 1)
        wide_up = lax.dynamic_update_index_in_dim(
            jnp.zeros((groups, members, units_dev), F32), sums_two[0, :units].reshape(groups, 1, units_dev), member, 1
        )
        ones = sum(ones)
        summed = total_over_all(jnp.concatenate([
            ones[0], ones[1], sums_two[2], sums_two[1], sums_two[3], wide_qkv.reshape(-1), wide_up.reshape(-1),
        ]))
    place = group * members + member
    mine, start = [], 0
    for size in [model] * 5 + [3 * model, groups * members * units_dev]:
        mine.append(lax.dynamic_slice_in_dim(summed, start + place * (size // devices), size // devices))
        start += size
    gain_1, bias_1, gain_2, bias_2, end_bias, qkv_shift, up_shift = mine
    return (
        output, grad_tokens, gain_1, bias_1, gain_2, bias_2, g_qkv, qkv_shift, g_out, end_bias, g_up, up_shift, g_down, end_bias,
    )


def solution(mesh):
    row, vec = P(ALL, None), P(ALL)
    return jax.shard_map(
        local,
        mesh=mesh,
        in_specs=(row, row, P("dp", None), vec, vec, vec, vec, row, vec, row, vec, row, vec, row, vec),
        out_specs=(row, row, vec, vec, vec, vec, row, vec, row, vec, row, vec, row, vec),
        check_vma=False,
    )
```

```python
import functools

import jax
import jax.numpy as jnp
import numpy as np
from jax import lax
from jax.experimental import pallas as pl
from jax.experimental.pallas import tpu as pltpu
from jax.sharding import PartitionSpec as P

HEADS = 16
HEAD = 64
ROT = 16
BLOCK = 256
EPS = 1e-05
VMEM = 60 * 1024 * 1024
ALL = ("dp", "fsdp")
LONG = pl.CostEstimate(flops=2 * 10**10, bytes_accessed=10**7, transcendentals=0)
SHORT = pl.CostEstimate(flops=0, bytes_accessed=0, transcendentals=0)
F32 = jnp.float32
LOW = jnp.bfloat16


def dot(left, right, contract=((1,), (0,))):
    return lax.dot_general(left, right, (contract, ((), ())), preferred_element_type=F32)


NT = ((1,), (1,))
TN = ((0,), (0,))


def normed(x_rows):
    centre = x_rows - jnp.mean(x_rows, axis=-1, keepdims=True)
    spread = jnp.mean(centre * centre, axis=-1, keepdims=True)
    scale = lax.rsqrt(spread + EPS)
    return centre * scale, scale


def turned(z, cosine, sine_a, sine_b, sign):
    groups = []
    for start in range(0, z.shape[1], 128):
        part = z[:, start : start + 128]
        ahead = pltpu.roll(part, 128 - ROT // 2, 1)
        behind = pltpu.roll(part, ROT // 2, 1)
        groups.append(part * cosine + sign * (ahead * sine_a + behind * sine_b))
    return groups[0] if len(groups) == 1 else jnp.concatenate(groups, axis=1)


def head_only(array, head):
    lane = lax.broadcasted_iota(jnp.int32, array.shape, 1)
    keep = (lane >= head * HEAD) & (lane < (head + 1) * HEAD)
    return jnp.where(keep, array, jnp.zeros_like(array))


def params(*order):
    return pltpu.CompilerParams(vmem_limit_bytes=VMEM, dimension_semantics=order)


def whole(shape):
    return pl.BlockSpec(shape, lambda *_: (0,) * len(shape))


HBM = pl.BlockSpec(memory_space=pl.ANY)


def fetch(plan, step, refs, target, sems, begin):
    for at, pieces in enumerate(plan):

        @pl.when(step == at)
        def _():
            for index, (ref, start, put, size) in enumerate(pieces):
                copy = pltpu.make_async_copy(
                    refs[ref].at[pl.ds(start, size)], target.at[pl.ds(put, size)], sems.at[at, index]
                )
                if begin:
                    copy.start()
                else:
                    copy.wait()


def fetch_all(plan, refs, target, sems):
    for at in range(len(plan)):
        fetch(plan, at, refs, target, sems, True)


def plan_of(pieces, span):
    plan, total = [], sum(p.shape[0] for p in pieces)
    for low in range(0, total, span):
        taken, at = [], 0
        for index, piece in enumerate(pieces):
            a, b = max(low, at), min(low + span, at + piece.shape[0])
            if a < b:
                taken.append((index, a - at, a, b - a))
            at += piece.shape[0]
        plan.append(tuple(taken))
    return tuple(plan)


def store(plan, step, source, refs, sems, begin):
    for at, pieces in enumerate(plan):

        @pl.when(step == at)
        def _():
            for index, (ref, start, put, size) in enumerate(pieces):
                copy = pltpu.make_async_copy(
                    source.at[pl.ds(put, size)], refs[ref].at[pl.ds(start, size)], sems.at[at, index]
                )
                if begin:
                    copy.start()
                else:
                    copy.wait()


def pack_kernel(members, member, qkv, up, small, *out):
    width = qkv.shape[1] // 3 // members
    units_dev = 128
    groups = up.shape[1] // units_dev // members
    for bit in range(members):
        to = member[0] ^ bit
        for part in range(3):
            start = pl.multiple_of((part * members + to) * width, 128)
            out[bit][:, part * width : (part + 1) * width] = qkv[:, pl.ds(start, width)]
        out[bit][:, 3 * width : 3 * width + 128] = jnp.zeros((qkv.shape[0], 128), LOW)
        out[bit][0 : small.shape[0], 3 * width : 3 * width + 128] = small[...]
        for group in range(groups):
            start = pl.multiple_of((group * members + to) * units_dev, 128)
            low = 3 * width + 128 + group * units_dev
            out[bit][:, low : low + units_dev] = up[:, pl.ds(start, units_dev)]


def call_pack(member, qkv, up, small, members):
    shard = qkv.shape[0]
    columns = (qkv.shape[1] + up.shape[1]) // members + 128
    return pl.pallas_call(
        functools.partial(pack_kernel, members),
        grid_spec=pltpu.PrefetchScalarGridSpec(
            num_scalar_prefetch=1,
            grid=(1,),
            in_specs=[whole(qkv.shape), whole(up.shape), whole(small.shape)],
            out_specs=[whole((shard, columns))] * members,
        ),
        out_shape=[jax.ShapeDtypeStruct((shard, columns), LOW)] * members,
        compiler_params=params("arbitrary"),
        cost_estimate=SHORT,
        name="pack",
    )(member, qkv, up, small)


def place_kernel(cut, member, *refs):
    *pieces, first, second = refs
    shard = pieces[0].shape[0]
    for bit, piece in enumerate(pieces):
        rows = pl.ds(pl.multiple_of((member[0] ^ bit) * shard, shard), shard)
        first[rows, :] = piece[:, :cut]
        second[rows, :] = piece[:, cut:]


def call_place(member, pieces, cut):
    members, (shard, columns) = len(pieces), pieces[0].shape
    shapes = [(members * shard, cut), (members * shard, columns - cut)]
    return pl.pallas_call(
        functools.partial(place_kernel, cut),
        grid_spec=pltpu.PrefetchScalarGridSpec(
            num_scalar_prefetch=1,
            grid=(1,),
            in_specs=[whole(p.shape) for p in pieces],
            out_specs=[whole(a) for a in shapes],
        ),
        out_shape=[jax.ShapeDtypeStruct(a, LOW) for a in shapes],
        compiler_params=params("arbitrary"),
        cost_estimate=SHORT,
        name="place",
    )(member, *pieces)


def small_block(member, members, vectors, qkv_bias, up_bias):
    size = vectors[0].shape[0]
    wide = 128 // members * (members - 1)
    rows = jnp.pad(jnp.stack(vectors), ((0, 0), (wide, wide)))
    rows = lax.dynamic_slice_in_dim(rows, wide - member * size, 128, 1)
    wide = 3 * wide
    shift = lax.dynamic_slice_in_dim(jnp.pad(qkv_bias, (wide, wide)), wide - member * 3 * size, 384, 0)
    return jnp.concatenate([rows, shift.reshape(3, 128), up_bias[None], jnp.zeros((16 - len(vectors) - 4, 128), LOW)], axis=0)


def vectors_kernel(members, member, gathered, out, wide):
    groups, rows, _ = gathered.shape
    shard = rows // members
    model = groups * 128
    out[...] = jnp.zeros_like(out)
    for group in range(groups):
        blocks = [gathered[group, m * shard : m * shard + 16, :].astype(F32) for m in range(members)]
        block = blocks[0]
        for other in blocks[1:]:
            block = block + other
        lanes = slice(group * 128, (group + 1) * 128)
        for row in range(6):
            out[row : row + 1, lanes] = block[row : row + 1, :]
        for row in range(3):
            low = group * 384 + row * 128
            wide[0:1, low : low + 128] = block[6 + row : 7 + row, :]
        own = jnp.zeros((1, 128), F32)
        for m in range(members):
            own = own + jnp.where(member[0] == m, blocks[m][9:10, :], 0.0)
        out[6:7, lanes] = own
    width = model // members
    for part in range(3):
        start = pl.multiple_of(part * model + member[0] * width, 128)
        out[7 + part : 8 + part, :width] = wide[0:1, pl.ds(start, width)]


def call_vectors(member, gathered, members, cut):
    groups, rows, _ = gathered.shape
    model = groups * 128
    return pl.pallas_call(
        functools.partial(vectors_kernel, members),
        grid_spec=pltpu.PrefetchScalarGridSpec(
            num_scalar_prefetch=1,
            grid=(1,),
            in_specs=[pl.BlockSpec((groups, rows, 128), lambda i, o: (0, 0, cut // 128 - 1))],
            out_specs=whole((16, model)),
            scratch_shapes=[pltpu.VMEM((8, 3 * model), F32)],
        ),
        out_shape=jax.ShapeDtypeStruct((16, model), F32),
        compiler_params=params("arbitrary"),
        cost_estimate=SHORT,
        name="vectors",
    )(member, gathered)


def qkv_kernel(plan, count, order, *refs):
    pieces, rest = refs[:count], refs[count:]
    vectors, weight, turn, q, k, v, normal, x, sems = rest
    step = pl.program_id(0)
    width = q.shape[1]
    span = q.shape[0]
    model = x.shape[1]

    @pl.when(step == 0)
    def _():
        fetch_all(plan, pieces, x, sems)

    fetch(plan, step, pieces, x, sems, False)
    n, _ = normed(x[pl.ds(pl.multiple_of(step * span, span), span), :].astype(F32))
    h = (n * vectors[0:1, :] + vectors[1:2, :]).astype(LOW)
    normal[...] = h
    tables = (turn[:, :128], turn[:, 128:256], turn[:, 256:])
    rows = dot(h, weight[...].reshape(model, 3 * width))
    q[...] = (turned(rows[:, :width] + vectors[7:8, :width], *tables, 1.0) * 0.125).astype(LOW)
    k[...] = turned(rows[:, width : 2 * width] + vectors[8:9, :width], *tables, 1.0).astype(LOW)
    v[...] = (rows[:, 2 * width :] + vectors[9:10, :width]).astype(LOW)


def call_qkv(order, pieces, vectors, weight, tables, span, width):
    model = pieces[0].shape[1]
    plan = plan_of(pieces, span)
    rows = span * len(plan)
    there = lambda i, o: (o[i], 0)
    return pl.pallas_call(
        functools.partial(qkv_kernel, plan, len(pieces)),
        grid_spec=pltpu.PrefetchScalarGridSpec(
            num_scalar_prefetch=1,
            grid=(rows // span,),
            in_specs=[HBM] * len(pieces)
            + [whole(vectors.shape), whole(weight.shape[:2] + (3 * width,))]
            + [pl.BlockSpec((span, 384), there)],
            out_specs=[pl.BlockSpec((span, width), there)] * 3 + [pl.BlockSpec((span, model), there)],
            scratch_shapes=[pltpu.VMEM((rows, model), LOW), pltpu.SemaphoreType.DMA((len(plan), 2))],
        ),
        out_shape=[jax.ShapeDtypeStruct((rows, width), LOW)] * 3 + [jax.ShapeDtypeStruct((rows, model), LOW)],
        compiler_params=params("arbitrary"),
        cost_estimate=SHORT,
        name="qkv",
    )(order, *pieces, vectors, weight, tables)


def masked_rows(target, array):
    for head in range(array.shape[1] // HEAD):
        target[head * BLOCK : (head + 1) * BLOCK, :] = head_only(array, head)


def over_keys(first, step, tiles):
    begin = first[step]
    count = step + 1 - begin

    def pair(i, _):
        tiles(begin + 2 * i, 2)
        return 0

    def single(at, _):
        tiles(at, 1)
        return 0

    lax.fori_loop(0, count // 2, pair, 0)
    lax.fori_loop(step + 1 - count % 2, step + 1, single, 0)


def by_eight(array):
    return array.reshape(BLOCK // 8, 8, BLOCK)


def fwd_kernel(first, q, k, v, mixed, low_mixed, lse, keys, values, scores, top, total, out):
    step = pl.program_id(0)
    width = q.shape[1]
    heads = width // HEAD
    stack = heads * BLOCK
    own = pl.ds(pl.multiple_of(step * BLOCK, BLOCK), BLOCK)
    masked_rows(keys.at[step], k[own, :])
    masked_rows(values.at[step], v[own, :])
    q_t = q[own, :].T
    top[...] = jnp.full_like(top, -1e30)
    total[...] = jnp.zeros_like(total)
    out[...] = jnp.zeros_like(out)

    def score(at, count):
        s = dot(keys[pl.ds(at, count)].reshape(count * stack, width), q_t)
        scores[pl.ds(at, count)] = s.reshape(count, stack, BLOCK)
        for head in range(heads):
            best = top[head]
            for tile in range(count):
                low = tile * stack + head * BLOCK
                best = jnp.maximum(best, jnp.max(by_eight(s[low : low + BLOCK]), axis=0))
            top[head] = best

    over_keys(first, step, score)
    peak = [jnp.max(top[head], axis=0, keepdims=True) for head in range(heads)]

    def mix(at, count):
        grown = []
        for tile in range(count):
            for head in range(heads):
                e = jnp.exp(scores[at + tile, head * BLOCK : (head + 1) * BLOCK] - peak[head])
                total[head] += jnp.sum(by_eight(e), axis=0)
                grown.append(e.astype(LOW))
        out[...] += dot(jnp.concatenate(grown, axis=0), values[pl.ds(at, count)].reshape(count * stack, width), TN)

    over_keys(first, step, mix)
    shares = []
    for head in range(heads):
        sums = jnp.sum(total[head], axis=0, keepdims=True)
        lse[head : head + 1, :] = peak[head] + jnp.log(sums)
        shares.append(jnp.broadcast_to(1.0 / sums, (HEAD, BLOCK)))
    result = out[...] * jnp.concatenate(shares, axis=0).T
    mixed[...] = result
    low_mixed[...] = result.astype(LOW)


def call_fwd(first, q, k, v):
    rows, width = q.shape
    heads = width // HEAD
    blocks = rows // BLOCK
    return pl.pallas_call(
        fwd_kernel,
        grid_spec=pltpu.PrefetchScalarGridSpec(
            num_scalar_prefetch=1,
            grid=(blocks,),
            in_specs=[whole((rows, width))] * 3,
            out_specs=[
                pl.BlockSpec((BLOCK, width), lambda i, o: (i, 0)),
                pl.BlockSpec((BLOCK, width), lambda i, o: (i, 0)),
                pl.BlockSpec((heads, BLOCK), lambda i, o: (0, i)),
            ],
            scratch_shapes=[
                pltpu.VMEM((blocks, heads * BLOCK, width), LOW),
                pltpu.VMEM((blocks, heads * BLOCK, width), LOW),
                pltpu.VMEM((blocks, heads * BLOCK, BLOCK), F32),
                pltpu.VMEM((heads, 8, BLOCK), F32),
                pltpu.VMEM((heads, 8, BLOCK), F32),
                pltpu.VMEM((BLOCK, width), F32),
            ],
        ),
        out_shape=[
            jax.ShapeDtypeStruct((rows, width), F32),
            jax.ShapeDtypeStruct((rows, width), LOW),
            jax.ShapeDtypeStruct((heads, rows), F32),
        ],
        compiler_params=params("arbitrary"),
        cost_estimate=SHORT,
        name="attend",
    )(first, q, k, v)


def bwd_kernel(low_head, count_before, last, first, q, k, v, d_mixed, mixed, lse, tables, normal, *rest):
    before, rest = rest[:count_before], rest[count_before:]
    d_rows, rest = rest[0], rest[1:]
    grads, rest = rest[: 2 if last else 1], rest[2 if last else 1 :]
    sums, keys, values, sum_q, sum_k, sum_v, queries, seeds, h, turn, sem = rest
    step = pl.program_id(0)
    width = q.shape[1]
    heads = width // HEAD
    stack = heads * BLOCK
    own = pl.ds(pl.multiple_of(step * BLOCK, BLOCK), BLOCK)
    load_turn = pltpu.make_async_copy(tables, turn, sem.at[0])
    load = pltpu.make_async_copy(normal, h, sem.at[1])

    @pl.when(step == 0)
    def _():
        load_turn.start()
        load.start()

    q_own = q[own, :]
    s_own = d_mixed[own, :]
    masked_rows(keys.at[step], k[own, :])
    masked_rows(values.at[step], v[own, :])
    masked_rows(queries, q_own)
    masked_rows(seeds, s_own)
    q_t = q_own.T
    s_t = s_own.T
    product_t = (s_own.astype(F32) * mixed[own, :]).T
    delta = [jnp.sum(product_t[head * HEAD : (head + 1) * HEAD, :], axis=0, keepdims=True) for head in range(heads)]
    log_total = [lse[low_head + head : low_head + head + 1, :] for head in range(heads)]
    sum_q[...] = jnp.zeros_like(sum_q)
    sum_k[own, :] = jnp.zeros((BLOCK, width), F32)
    sum_v[own, :] = jnp.zeros((BLOCK, width), F32)

    def tiles(at, count):
        key_rows = keys[pl.ds(at, count)].reshape(count * stack, width)
        s = dot(key_rows, q_t)
        d_p = dot(values[pl.ds(at, count)].reshape(count * stack, width), s_t)
        wide_probs, wide_scores, tall_scores = [], [], []
        for tile in range(count):
            low_probs, low_scores = [], []
            for head in range(heads):
                low = tile * stack + head * BLOCK
                probs = jnp.exp(s[low : low + BLOCK] - log_total[head])
                low_scores.append((probs * (d_p[low : low + BLOCK] - delta[head])).astype(LOW))
                low_probs.append(probs.astype(LOW))
            wide_probs.append(jnp.concatenate(low_probs, axis=1))
            wide_scores.append(jnp.concatenate(low_scores, axis=1))
            tall_scores += low_scores
        rows = pl.ds(pl.multiple_of(at * BLOCK, BLOCK), count * BLOCK)
        sum_v[rows, :] += dot(jnp.concatenate(wide_probs, axis=0), seeds[...])
        sum_k[rows, :] += dot(jnp.concatenate(wide_scores, axis=0), queries[...])
        sum_q[...] += dot(jnp.concatenate(tall_scores, axis=0), key_rows, TN)

    over_keys(first, step, tiles)

    @pl.when(step == 0)
    def _():
        load_turn.wait()

    def turned_back(array, rows):
        return turned(array, turn[rows, :128], turn[rows, 128:256], turn[rows, 256:], -1.0)

    d_rows[own, :width] = (turned_back(sum_q[...], own) * 0.125).astype(LOW)

    @pl.when(step == pl.num_programs(0) - 1)
    def _():
        def close(at, _):
            rows = pl.ds(pl.multiple_of(at * BLOCK, BLOCK), BLOCK)
            d_rows[rows, width : 2 * width] = turned_back(sum_k[rows, :], rows).astype(LOW)
            d_rows[rows, 2 * width :] = sum_v[rows, :].astype(LOW)
            return 0

        lax.fori_loop(0, q.shape[0] // BLOCK, close, 0)
        load.wait()
        sums[0:1, :] = jnp.sum(d_rows[...].astype(F32), axis=0, keepdims=True)
        if not last:
            grads[0][...] = dot(h[...], d_rows[...], TN).astype(LOW)
        else:
            group = first[first.shape[0] - 1]
            per = grads[0].shape[1]
            own_low = sum(b.shape[1] for b in before)
            for place in range(2 * grads[0].shape[0]):
                to = grads[place % 2].at[place // 2]
                rows = pl.ds(pl.multiple_of((group ^ place) * per, per), per)
                low = 0
                for ref in before:
                    to[:, low : low + ref.shape[1]] = ref[rows, :]
                    low += ref.shape[1]
            grad = dot(h[...], d_rows[...], TN).astype(LOW)
            h[: grad.shape[0], : 3 * width] = grad
            for place in range(2 * grads[0].shape[0]):
                rows = pl.ds(pl.multiple_of((group ^ place) * per, per), per)
                grads[place % 2][place // 2, :, own_low:] = h[rows, : 3 * width]


def call_bwd(first, q, k, v, d_mixed, mixed, lse, tables, normal, part, parts, before, groups):
    rows, full = q.shape
    width = full // parts
    heads = width // HEAD
    blocks = rows // BLOCK
    model = normal.shape[1]
    last = part == parts - 1
    lanes = pl.BlockSpec((rows, width), lambda i, o: (0, part))
    if last:
        grads = [(groups // 2, model // groups, 3 * width * parts)] * 2
    else:
        grads = [(model, 3 * width)]
    return pl.pallas_call(
        functools.partial(bwd_kernel, part * heads, len(before), last),
        grid_spec=pltpu.PrefetchScalarGridSpec(
            num_scalar_prefetch=1,
            grid=(blocks,),
            in_specs=[lanes] * 5
            + [pl.BlockSpec((heads * parts, BLOCK), lambda i, o: (0, i))]
            + [HBM] * 2
            + [whole(b.shape) for b in before],
            out_specs=[whole((rows, 3 * width))] + [whole(g) for g in grads] + [whole((8, 3 * width))],
            scratch_shapes=[
                pltpu.VMEM((blocks, heads * BLOCK, width), LOW),
                pltpu.VMEM((blocks, heads * BLOCK, width), LOW),
                pltpu.VMEM((BLOCK, width), F32),
                pltpu.VMEM((rows, width), F32),
                pltpu.VMEM((rows, width), F32),
                pltpu.VMEM((heads * BLOCK, width), LOW),
                pltpu.VMEM((heads * BLOCK, width), LOW),
                pltpu.VMEM((rows, model), LOW),
                pltpu.VMEM((rows, tables.shape[1]), F32),
                pltpu.SemaphoreType.DMA((2,)),
            ],
        ),
        out_shape=[jax.ShapeDtypeStruct((rows, 3 * width), LOW)]
        + [jax.ShapeDtypeStruct(g, LOW) for g in grads]
        + [jax.ShapeDtypeStruct((8, 3 * width), F32)],
        compiler_params=params("arbitrary"),
        cost_estimate=SHORT,
        name="attend_back",
    )(first, q, k, v, d_mixed, mixed, lse, tables, normal, *before)


def mlp_kernel(plan, out_plan, count, out_count, joined, chunk, order, *refs):
    x_pieces, cot_pieces, rest = refs[:count], refs[count : 2 * count], refs[2 * count :]
    mixed, vectors, rest = rest[0], rest[1], rest[2:]
    mats, rest = rest[: 1 if joined else 3], rest[1 if joined else 3 :]
    parts, rest = rest[:out_count], rest[out_count:]
    d_mixed, to_norm, rest = rest[0], rest[1], rest[2:]
    grads, rest = rest[: 1 if joined else 3], rest[1 if joined else 3 :]
    sums, normal, cot, active, d_up, own_mixed, g_out, staged, x_sems, cot_sems, out_sems = rest
    step = pl.program_id(0)
    steps = len(plan)
    span, width = own_mixed.shape[0] // steps, own_mixed.shape[1]
    model, units = normal.shape[1], active.shape[1]
    if joined:
        groups = mats[0].shape[0]
        cuts = [0, model // groups, (model + units) // groups, (model + units + width) // groups]
        w_up, w_down, w_out = (mats[0].at[:, pl.ds(cuts[i], cuts[i + 1] - cuts[i]), :] for i in range(3))
    else:
        w_up, w_down, w_out = mats
    as_up = lambda: w_up[...].reshape(model, units)
    as_down = lambda: w_down[...].reshape(units, model)
    as_out = lambda: w_out[...].reshape(width, model)

    @pl.when(step == 0)
    def _():
        fetch_all(plan, x_pieces, normal, x_sems)
        fetch_all(plan, cot_pieces, cot, cot_sems)
        sums[...] = jnp.zeros_like(sums)

    fetch(plan, step, x_pieces, normal, x_sems, False)
    fetch(plan, step, cot_pieces, cot, cot_sems, False)

    @pl.when(step < steps)
    def _():
        here = pl.ds(pl.multiple_of(step * span, span), span)
        n, _ = normed(normal[here, :].astype(F32))
        h = (n * vectors[2:3, :] + vectors[3:4, :]).astype(LOW)
        normal[here, :] = h
        dy = cot[here, :]
        own = mixed[pl.ds(pl.multiple_of(order[step] * span, span), span), :]
        own_mixed[here, :] = own
        d_mixed[...] = dot(dy, as_out(), NT).astype(LOW)
        up, down = as_up(), as_down()
        for low in range(0, units, chunk):
            cols = slice(low, low + chunk)
            u = dot(h, up[:, cols]) + vectors[6:7, cols]
            d_active = dot(dy, down[cols], NT)
            cdf = 0.5 * (1.0 + lax.erf(u * np.float32(np.sqrt(0.5))))
            slope = cdf + u * (jnp.exp(-0.5 * u * u) * np.float32(1.0 / np.sqrt(2.0 * np.pi)))
            active[here, cols] = (u * cdf).astype(LOW)
            back = (d_active * slope).astype(LOW)
            d_up[here, cols] = back
            sums[0:1, cols] += jnp.sum(back.astype(F32), axis=0, keepdims=True)
        staged[here, :] = (dot(active[here, :], down) + dot(own, as_out())).astype(LOW)
        d_h = dot(d_up[here, :], up, NT)
        sums[1:2, :model] += jnp.sum(d_h, axis=0, keepdims=True)
        sums[2:3, :model] += jnp.sum(d_h * n, axis=0, keepdims=True)
        to_norm[...] = d_h * vectors[2:3, :]

        @pl.when(step == 0)
        def _():
            sums[3:4, :model] = jnp.sum(dy.astype(F32), axis=0, keepdims=True)

    store(out_plan, step, staged, parts, out_sems, True)

    @pl.when(step >= steps)
    def _():
        at = step - steps
        many = pl.num_programs(0) - steps

        @pl.when(at == 0)
        def _():
            g_out[...] = dot(own_mixed[...], cot[...], TN).astype(LOW)

        up_cols = pl.ds(pl.multiple_of(at * (model // many), 128), model // many)
        down_cols = pl.ds(pl.multiple_of(at * (units // many), 128), units // many)
        out_rows = pl.ds(pl.multiple_of(at * (width // many), 16), width // many)
        up_grad = dot(normal[:, up_cols], d_up[...], TN).astype(LOW)
        down_grad = dot(active[:, down_cols], cot[...], TN).astype(LOW)
        if joined:
            block = grads[0].shape[0]
            grads[0][:, cuts[0] : cuts[1], :] = up_grad.reshape(block, cuts[1], units)
            grads[0][:, cuts[1] : cuts[2], :] = down_grad.reshape(block, cuts[2] - cuts[1], model)
            grads[0][:, cuts[2] : cuts[3], :] = g_out[out_rows, :].reshape(block, cuts[3] - cuts[2], model)
        else:
            grads[0][...] = up_grad
            grads[1][...] = down_grad
            grads[2][...] = g_out[out_rows, :]

    @pl.when(step == pl.num_programs(0) - 1)
    def _():
        for at in range(steps):
            store(out_plan, at, staged, parts, out_sems, False)


def call_mlp(order, x_pieces, cot_pieces, mixed, vectors, mats, span, units, out_shapes):
    rows, width = mixed.shape
    model = x_pieces[0].shape[1]
    joined = len(mats) == 1
    plan, out_plan = plan_of(x_pieces, span), plan_of(out_shapes, span)
    steps, many = len(plan), 4
    count = len(x_pieces)
    here = lambda i, o: (jnp.minimum(i, steps - 1), 0)
    there = lambda i, o: (o[jnp.minimum(i, steps - 1)], 0)
    later = lambda i, o: (jnp.maximum(i - steps, 0), 0)
    if joined:
        groups = mats[0].shape[0]
        grads = [(groups, (model + units + width) // groups, model)]
        grad_specs = [pl.BlockSpec((groups // many,) + grads[0][1:], lambda i, o: (jnp.maximum(i - steps, 0), 0, 0))]
    else:
        grads = [(model, units), (units, model), (width, model)]
        grad_specs = [pl.BlockSpec((a // many, b), later) for a, b in grads]
    sums = (8, max(model, units))
    return pl.pallas_call(
        functools.partial(mlp_kernel, plan, out_plan, count, len(out_shapes), joined, 256),
        grid_spec=pltpu.PrefetchScalarGridSpec(
            num_scalar_prefetch=1,
            grid=(steps + many,),
            in_specs=[HBM] * (2 * count)
            + [whole((rows, width)), whole(vectors.shape)]
            + [pl.BlockSpec(m.shape, lambda *_: (0, 0, 0), pipeline_mode=pl.Buffered(1)) for m in mats],
            out_specs=[HBM] * len(out_shapes)
            + [pl.BlockSpec((span, width), there), pl.BlockSpec((span, model), here)]
            + grad_specs
            + [whole(sums)],
            scratch_shapes=[
                pltpu.VMEM((rows, model), LOW),
                pltpu.VMEM((rows, model), LOW),
                pltpu.VMEM((rows, units), LOW),
                pltpu.VMEM((rows, units), LOW),
                pltpu.VMEM((rows, width), LOW),
                pltpu.VMEM((width, model), LOW),
                pltpu.VMEM((rows, model), LOW),
                pltpu.SemaphoreType.DMA((steps, 2)),
                pltpu.SemaphoreType.DMA((steps, 2)),
                pltpu.SemaphoreType.DMA((steps, 2)),
            ],
        ),
        out_shape=list(out_shapes)
        + [jax.ShapeDtypeStruct((rows, width), LOW), jax.ShapeDtypeStruct((rows, model), F32)]
        + [jax.ShapeDtypeStruct(g, LOW) for g in grads]
        + [jax.ShapeDtypeStruct(sums, F32)],
        compiler_params=params("arbitrary"),
        cost_estimate=SHORT,
        name="mlp",
    )(order, *x_pieces, *cot_pieces, mixed, vectors, *mats)


def close_kernel(plan, many, parts, summed, order, *refs):
    xs, refs = refs[:many], refs[many:]
    d_rows, (to_norm, vectors, weight), refs = refs[:parts], refs[parts : parts + 3], refs[parts + 3 :]
    lows, highs, refs = refs[:summed], refs[summed : 2 * summed], refs[2 * summed :]
    outs, output, (sums, x, e_low) = refs[: len(plan)], refs[len(plan) : -3], refs[-3:]
    step = pl.program_id(0)

    @pl.when(step == 0)
    def _():
        sums[...] = jnp.zeros_like(sums)

    for at, (piece, _, _) in enumerate(plan):

        @pl.when(step == at)
        def _():
            x[...] = xs[piece][...]

    model = x.shape[1]
    n, scale = normed(x[...].astype(F32))
    width = d_rows[0].shape[1] // 3
    rows = jnp.concatenate([d[:, i * width : (i + 1) * width] for i in range(3) for d in d_rows], axis=1)
    d_h = dot(rows, weight[...].reshape(model, 3 * width * parts), NT)
    sums[1:2, :] += jnp.sum(d_h, axis=0, keepdims=True)
    sums[0:1, :] += jnp.sum(d_h * n, axis=0, keepdims=True)
    e = d_h * vectors[0:1, :] + to_norm[...]
    e = e - jnp.mean(e, axis=-1, keepdims=True) - n * jnp.mean(e * n, axis=-1, keepdims=True)
    e_low[...] = (e * scale).astype(LOW)
    for at in range(len(plan)):

        @pl.when(step == at)
        def _():
            outs[at][...] = e_low[...]
            if summed:
                total = x[...].astype(F32) + vectors[4:5, :] + vectors[5:6, :]
                for ref in highs if at else lows:
                    total = total + ref[...].astype(F32)
                output[0][...] = total.astype(LOW)


def call_close(order, pieces, plan, d_rows, to_norm, vectors, weight, span, cost=SHORT, low=(), high=()):
    model = pieces[0].shape[1]
    width3 = sum(d.shape[1] for d in d_rows)
    per = span // BLOCK
    steps = len(plan)

    def pick(values, i):
        value = jnp.int32(values[-1])
        for at in range(len(values) - 1):
            value = jnp.where(i == at, jnp.int32(values[at]), value)
        return value

    def block_of(piece):
        reads = [(at, start // BLOCK) for at, (index, start, _) in enumerate(plan) if index == piece]
        values = [next((b for a, b in reversed(reads) if a <= at), reads[0][1]) for at in range(steps)]
        return lambda i, o: (pick(values, i), 0)

    places = [low // BLOCK for _, _, low in plan]
    here = lambda i, o: (pick(places, i), 0)
    there = lambda i, o: (o[pick(places, i) // per] * per + pick(places, i) % per, 0)
    return pl.pallas_call(
        functools.partial(close_kernel, plan, len(pieces), len(d_rows), len(low)),
        grid_spec=pltpu.PrefetchScalarGridSpec(
            num_scalar_prefetch=1,
            grid=(steps,),
            in_specs=[pl.BlockSpec((BLOCK, model), block_of(piece)) for piece in range(len(pieces))]
            + [pl.BlockSpec((BLOCK, d.shape[1]), there) for d in d_rows]
            + [pl.BlockSpec((BLOCK, model), here), whole(vectors.shape), whole(weight.shape[:2] + (width3,))]
            + [whole((BLOCK, model))] * (2 * len(low)),
            out_specs=[whole((BLOCK, model))] * steps
            + [pl.BlockSpec((BLOCK, model), lambda i, o: (i, 0))] * bool(low)
            + [whole((8, model))],
            scratch_shapes=[pltpu.VMEM((BLOCK, model), LOW), pltpu.VMEM((BLOCK, model), LOW)],
        ),
        out_shape=[jax.ShapeDtypeStruct((BLOCK, model), LOW)] * steps
        + [jax.ShapeDtypeStruct((steps * BLOCK, model), LOW)] * bool(low)
        + [jax.ShapeDtypeStruct((8, model), F32)],
        compiler_params=params("arbitrary"),
        cost_estimate=cost,
        name="close",
    )(order, *pieces, *d_rows, to_norm, vectors, weight, *low, *high)


def finish_kernel(halves, base, shift, *refs):
    parts, out = refs[:-1], refs[-1]
    shifts = jnp.sum(shift[...], axis=0, keepdims=True)
    for at in range(2):

        @pl.when(pl.program_id(0) == at)
        def _():
            total = base[...].astype(F32) + shifts
            for part in parts[at::2]:
                total = total + part[...].astype(F32)
            out[...] = total.astype(LOW)


def call_finish(base, shift, low, high):
    rows, model = base.shape
    half = rows // 2
    arrays = [a for pair in zip(low, high) for a in pair]
    return pl.pallas_call(
        functools.partial(finish_kernel, len(low)),
        grid=(2,),
        in_specs=[pl.BlockSpec((half, model), lambda i: (i, 0)), whole(shift.shape)] + [whole((half, model))] * len(arrays),
        out_specs=pl.BlockSpec((half, model), lambda i: (i, 0)),
        out_shape=jax.ShapeDtypeStruct((rows, model), LOW),
        compiler_params=params("arbitrary"),
        cost_estimate=SHORT,
        name="finish",
    )(base, shift, *arrays)


def cut_kernel(members, member, first, second, *out):
    pieces, (down, last) = out[:members], out[members:]
    shard = last.shape[0]
    columns = first.shape[1]
    for bit, piece in enumerate(pieces):
        rows = pl.ds(pl.multiple_of((member[0] ^ bit) * shard, shard), shard)
        piece[:, :columns] = first[rows, :]
        piece[:, columns:] = second[rows, :]
    low = members * shard
    down[...] = first[low : low + down.shape[0], :].astype(F32)
    last[...] = first[low + down.shape[0] :, :]


def call_cut(member, first, second, members, shard):
    columns = first.shape[1]
    shapes = [jax.ShapeDtypeStruct((shard, columns + second.shape[1]), LOW)] * members + [
        jax.ShapeDtypeStruct((first.shape[0] - (members + 1) * shard, columns), F32),
        jax.ShapeDtypeStruct((shard, columns), LOW),
    ]
    return pl.pallas_call(
        functools.partial(cut_kernel, members),
        grid_spec=pltpu.PrefetchScalarGridSpec(
            num_scalar_prefetch=1,
            grid=(1,),
            in_specs=[whole(first.shape), whole(second.shape)],
            out_specs=[whole(a.shape) for a in shapes],
        ),
        out_shape=shapes,
        compiler_params=params("arbitrary"),
        cost_estimate=SHORT,
        name="cut",
    )(member, first, second)


def join_kernel(places, member, *refs):
    pieces, outs = refs[:-2], refs[-2:]
    for bit, piece in enumerate(pieces):
        for block, (index, column, stride) in enumerate(places):
            start = pl.multiple_of(column + (member[0] ^ bit) * stride, 128)
            outs[index][:, pl.ds(start, 128)] = piece[:, block * 128 : (block + 1) * 128].astype(F32)


def call_join(member, pieces, places, columns):
    shard = pieces[0].shape[0]
    return pl.pallas_call(
        functools.partial(join_kernel, tuple(places)),
        grid_spec=pltpu.PrefetchScalarGridSpec(
            num_scalar_prefetch=1,
            grid=(1,),
            in_specs=[whole(p.shape) for p in pieces],
            out_specs=[whole((shard, c)) for c in columns],
        ),
        out_shape=[jax.ShapeDtypeStruct((shard, c), F32) for c in columns],
        compiler_params=params("arbitrary"),
        cost_estimate=SHORT,
        name="join",
    )(member, *pieces)


def bundle_kernel(members, halves, member, two, *refs):
    *ones, out, wide = refs
    thirds, ones = ones[:halves], ones[halves:]
    groups = out.shape[0] // members
    out[...] = jnp.zeros_like(out)
    wide[...] = jnp.zeros_like(wide)
    one = functools.reduce(lambda a, b: a + b, [one[0:2, :] for one in ones])
    lines = [one[0:1, :], one[1:2, :], two[2:3, :], two[1:2, :], two[3:4, :]]
    size = thirds[0].shape[1] // 3
    per_member = halves * size // 128
    for part in range(3):
        for half, third in enumerate(thirds):
            for at in range(size // 128):
                row = (part * members + member[0]) * per_member + half * (size // 128) + at
                low = part * size + at * 128
                wide[pl.ds(row, 1), :] = third[0:1, low : low + 128]
    for group in range(groups):
        lanes = slice(group * 128, (group + 1) * 128)
        for to in range(members):
            device = group * members + to
            for row, line in enumerate(lines):
                out[device, row : row + 1, :] = line[:, lanes]
            out[device, 5:8, :] = wide[3 * group : 3 * group + 3, :]
            out[device, 8:9, :] = jnp.where(member[0] == to, two[0:1, lanes], 0.0)


def call_bundle(member, members, groups, two, thirds, ones):
    shape = (groups * members, 16, 128)
    return pl.pallas_call(
        functools.partial(bundle_kernel, members, len(thirds)),
        grid_spec=pltpu.PrefetchScalarGridSpec(
            num_scalar_prefetch=1,
            grid=(1,),
            in_specs=[whole(a.shape) for a in (two, *thirds, *ones)],
            out_specs=whole(shape),
            scratch_shapes=[pltpu.VMEM((3 * groups, 128), F32)],
        ),
        out_shape=jax.ShapeDtypeStruct(shape, F32),
        compiler_params=params("arbitrary"),
        cost_estimate=SHORT,
        name="bundle",
    )(member, two, *thirds, *ones)


def across(array, bit):
    size = lax.axis_size("fsdp")
    return lax.ppermute(array, "fsdp", [(i, i ^ bit) for i in range(size)])


def exchange(pieces):
    size = lax.axis_size("fsdp")
    if size != 4:
        return lax.all_to_all(pieces, "fsdp", split_axis=0, concat_axis=0, tiled=True)
    member = lax.axis_index("fsdp")
    out = pieces
    for bit in range(1, size):
        mine = lax.dynamic_index_in_dim(pieces, member ^ bit, 0, keepdims=False)
        out = lax.dynamic_update_index_in_dim(out, across(mine, bit), member ^ bit, 0)
    return out


def behind(array, *others):
    return lax.optimization_barrier((array, *others))[0]


def behind_all(arrays, *others):
    return tuple(behind(array, *others) for array in arrays)


def gather_rows(halves, near=None, *others):
    if lax.axis_size("fsdp") != 4:
        return [lax.all_gather(jnp.concatenate(halves, axis=0), "fsdp", axis=0, tiled=True)]
    one_low, two_high, one_high, two_low = near
    return [
        *halves, one_low, one_high, two_low, two_high,
        across(behind(one_low, *others), 2), across(behind(two_high, *others), 1),
    ]


def near_rows(halves):
    low, high = halves
    return across(low, 1), across(high, 2), across(high, 1), across(low, 2)


def hop(array, bit):
    return lax.ppermute(array, "dp", [(i, i ^ bit) for i in range(lax.axis_size("dp"))])


def scatter_relative(even, odd):
    add = lambda a, b: (a.astype(F32) + b.astype(F32)).astype(LOW)
    blocks, bit = add(even, hop(odd, 1)), 2
    while blocks.shape[0] > 1:
        blocks = add(blocks[0::2], hop(blocks[1::2], bit))
        bit *= 2
    return blocks[0]


def reduce_begin(parts):
    if len(parts) == 1:
        return ()
    _, _, one_low, _, _, two_high, three_low, three_high = parts
    return across(three_low, 1), across(three_high, 2), across(one_low, 1), across(two_high, 2)


def reduce_middle(parts, begun):
    if len(parts) == 1:
        return ()
    add = lambda a, b: (a.astype(F32) + b.astype(F32)).astype(LOW)
    return add(parts[3], begun[1]), add(parts[4], begun[0])


def reduce_last(parts, begun, middle):
    if len(parts) == 1:
        total = lax.psum_scatter(parts[0], "fsdp", scatter_dimension=0, tiled=True)
        half = total.shape[0] // 2
        return (total[:half],), (total[half:],)
    one_high, two_low = across(middle[0], 1), across(middle[1], 2)
    return (parts[0], begun[2], two_low), (parts[1], one_high, begun[3])


def total_over_all(vector):
    count = lax.axis_size("dp") * lax.axis_size("fsdp")
    step = 1
    while step < count:
        vector = vector + lax.ppermute(vector, ALL, [(i, i ^ step) for i in range(count)])
        step *= 2
    return vector


def swap_owner(array, back):
    groups, members = lax.axis_size("dp"), lax.axis_size("fsdp")
    pairs = [(m * groups + g, g * members + m) for g in range(groups) for m in range(members)]
    if back:
        pairs = [(b, a) for a, b in pairs]
    return lax.ppermute(array, ALL, pairs)


def gather_dp(array):
    return lax.all_gather(array, "dp", axis=0)


def scatter_dp(array):
    return lax.psum_scatter(array, "dp", scatter_dimension=0, tiled=True)


def rotary_tables(length):
    half = ROT // 2
    frequency = (np.float32(10000.0) ** (-(np.arange(half, dtype=np.float32) * np.float32(2.0)) / np.float32(ROT))).astype(np.float32)
    angles = (np.arange(length, dtype=np.float32)[:, None] * frequency[None, :]).astype(np.float32)
    cosine = np.cos(angles).astype(np.float32)
    sine = np.sin(angles).astype(np.float32)
    cos_row = np.ones((length, 128), np.float32)
    ahead = np.zeros((length, 128), np.float32)
    behind = np.zeros((length, 128), np.float32)
    for start in range(0, 128, HEAD):
        cos_row[:, start : start + half] = cosine
        cos_row[:, start + half : start + ROT] = cosine
        ahead[:, start : start + half] = -sine
        behind[:, start + half : start + ROT] = sine
    return jnp.asarray(np.concatenate([cos_row, ahead, behind], axis=1))


def local(
    tokens, cotangent, doc_ids, norm1_gain, norm1_bias, norm2_gain, norm2_bias, qkv_weight, qkv_bias,
    out_weight, out_bias, up_weight, up_bias, down_weight, down_bias,
):
    groups, members = lax.axis_size("dp"), lax.axis_size("fsdp")
    group, member = lax.axis_index("dp"), lax.axis_index("fsdp")
    devices = groups * members
    rows, model = tokens.shape
    stream = rows * members
    shard = qkv_weight.shape[0]
    width = model // members
    units_dev = up_bias.shape[0]
    units = groups * units_dev
    paired = members == 4 and units_dev == 128 and units == model
    me = member.astype(jnp.int32).reshape(1)
    vectors_in = [norm1_gain, norm1_bias, norm2_gain, norm2_bias, out_bias, down_bias]

    half = rows // 2
    x_halves = [tokens[:half], tokens[half:]]
    cot_halves = [cotangent[:half], cotangent[half:]]
    if paired:
        small = small_block(member, members, vectors_in, qkv_bias, up_bias)
        packed = call_pack(me, qkv_weight, up_weight, small, members)
        arrived = [packed[0]] + [across(packed[bit], bit) for bit in range(1, members)]
        x_near = near_rows(behind_all(x_halves, *arrived[1:]))
        cut = 3 * width + 128
        first_in, up_in = call_place(me, arrived, cut)
        w_first = gather_dp(first_in)
        out_own = swap_owner(behind(out_weight, first_in), False)
        out_own = behind(out_own, *x_near[:2])
        mats = (gather_dp(jnp.concatenate([up_in, down_weight, out_own], axis=0)),)
        vectors = call_vectors(me, w_first, members, cut)
    else:
        qkv_cut = qkv_weight.reshape(shard, 3, members, width).transpose(2, 0, 1, 3).reshape(members, shard, 3 * width)
        up_cut = up_weight.reshape(shard, groups, members, units_dev).transpose(2, 0, 1, 3).reshape(members, shard, units)
        arrived = exchange(jnp.concatenate([qkv_cut, up_cut], axis=2)).reshape(members * shard, -1)
        w_first = gather_dp(arrived[:, : 3 * width])
        x_near = near_rows(x_halves) if members == 4 else None
        mats = (gather_dp(arrived[:, 3 * width :]), gather_dp(down_weight), gather_dp(swap_owner(out_weight, False)))
        full = [lax.all_gather(a, ALL, axis=0, tiled=True).astype(F32) for a in vectors_in]
        shift = lax.all_gather(qkv_bias, ALL, axis=0, tiled=True).astype(F32).reshape(3, members, width)
        shift = lax.dynamic_index_in_dim(shift, member, 1, keepdims=False)
        up_all = lax.all_gather(up_bias, "dp", axis=0, tiled=True).astype(F32)
        lines = full + [jnp.pad(a, (0, model - a.shape[0])) for a in (up_all, shift[0], shift[1], shift[2])]
        vectors = jnp.pad(jnp.stack(lines), ((0, 6), (0, 0)))

    x_pieces = gather_rows(x_halves, x_near)
    sources = jnp.arange(members, dtype=jnp.int32)
    order = sources ^ member if members == 4 else sources
    doc_row = doc_ids[0]
    first = jnp.sum((doc_row[None, :] < doc_row[:, None]).astype(jnp.int32), axis=1)
    first = jnp.concatenate([first, group.astype(jnp.int32).reshape(1)])
    tables = rotary_tables(stream)

    q, k, v, normal = call_qkv(order, x_pieces, vectors, w_first, tables, rows, width)
    cot_near = near_rows(behind_all(cot_halves, *x_pieces[2:])) if members == 4 else None
    cot_pieces = gather_rows(cot_halves, cot_near, q)
    mixed, low_mixed, lse = call_fwd(first, q, k, v)
    out_sizes = [half] * (2 * members) if members == 4 else [stream]
    out_shapes = [jax.ShapeDtypeStruct((size, model), LOW) for size in out_sizes]
    results = call_mlp(
        order, x_pieces, cot_pieces, low_mixed, vectors, mats, rows, units, out_shapes
    )
    count = len(out_shapes)
    parts, (d_mixed, to_norm), grads, sums_two = results[:count], results[count : count + 2], results[count + 2 : -1], results[-1]
    scattered = scatter_dp(grads[0].reshape(-1, model)) if paired else None

    begun = reduce_begin(parts)
    halves = 2 if width % 256 == 0 else 1
    back = [call_bwd(first, q, k, v, d_mixed, mixed, lse, tables, normal, 0, halves, (), groups)]
    middle = reduce_middle(parts, behind_all(begun, back[0][0]))
    summed = reduce_last(parts, begun, middle)
    for part in range(1, halves):
        q = behind(q, *middle, *begun[2:])
        back.append(call_bwd(first, q, k, v, d_mixed, mixed, lse, tables, normal, part, halves, (back[-1][1],), groups))
    d_qkv = [b[0] for b in back]
    even, odd = back[-1][1:3]
    sums_qkv = [b[-1] for b in back]
    to_norm = behind(to_norm, *summed[0], *summed[1])
    if members == 4:
        close = lambda pieces, cost=SHORT, low=(), high=(): call_close(
            order, [x_pieces[p] for p in pieces], [(i, 0, p * half) for i, p in enumerate(pieces)],
            d_qkv, to_norm, vectors, w_first, rows, cost, low, high,
        )
        *three, ones_a = close((6, 7), LONG)
        to_norm = behind(to_norm, *three, *(() if scattered is None else (scattered,)))
        one_low, two_high, one_high, two_low, ones_b = close((2, 5, 3, 4))
        to_norm = behind(to_norm, one_low)
        own_low, own_high, output, ones_c = close((0, 1), SHORT, *summed)
        final = [own_low, own_high, one_low, one_high, two_low, two_high, *three]
        ones = [ones_a, ones_b, ones_c]
    else:
        plan = [(0, low, low) for low in range(0, stream, BLOCK)]
        *final, ones = call_close(order, x_pieces, plan, d_qkv, to_norm, vectors, w_first, rows)
        final, ones = [jnp.concatenate(final, axis=0)], [ones]
        output = call_finish(tokens, vectors[4:6, :], *summed)
    begun = reduce_begin(final)
    middle = reduce_middle(final, begun)
    grad_tokens = call_finish(cotangent, jnp.zeros((1, model), F32), *reduce_last(final, begun, middle))

    g_qkv = scatter_relative(behind(even, *final[2:4]) if members == 4 else even, odd)
    place = group * members + member
    if paired:
        *mixed_pieces, g_down, g_out = call_cut(me, scattered, g_qkv, members, shard)
        places = [(0, b * members * units_dev, units_dev) for b in range(groups)]
        places += [(1, part * model + half * (width // halves), width) for half in range(halves) for part in range(3)]
        arrived = [mixed_pieces[0]] + [across(mixed_pieces[bit], bit) for bit in range(1, members)]
        g_up, g_qkv = call_join(me, arrived, places, (up_weight.shape[1], qkv_weight.shape[1]))
        ready = behind(call_bundle(me, members, groups, sums_two, sums_qkv, ones), *middle, *begun[2:])
        totals = jnp.sum(lax.all_to_all(ready, ALL, split_axis=0, concat_axis=0), axis=0)
        g_out = swap_owner(behind(g_out, totals), True).astype(F32)
        size = model // devices
        mine = [a[0] for a in jnp.split(lax.dynamic_slice_in_dim(totals[:5], member * size, size, 1), 5)]
        mine += [lax.dynamic_slice_in_dim(totals[5:8].reshape(-1), member * 3 * size, 3 * size), totals[8]]
    else:
        g_up, g_down, g_out = [scatter_dp(g) for g in grads]
        g_down = g_down.astype(F32)
        g_out = swap_owner(g_out, True).astype(F32)
        g_up = exchange(g_up.reshape(members, shard, units))
        g_up = g_up.reshape(members, shard, groups, units_dev).transpose(1, 2, 0, 3).reshape(shard, -1).astype(F32)
        g_qkv = exchange(g_qkv.reshape(members, shard, 3 * width)).reshape(members, shard, halves, 3, width // halves)
        g_qkv = g_qkv.transpose(1, 3, 0, 2, 4).reshape(shard, -1).astype(F32)
        thirds = jnp.concatenate([a[0].reshape(3, 1, width // halves) for a in sums_qkv], axis=2)
        wide_qkv = lax.dynamic_update_index_in_dim(jnp.zeros((3, members, width), F32), thirds, member, 1)
        wide_up = lax.dynamic_update_index_in_dim(
            jnp.zeros((groups, members, units_dev), F32), sums_two[0, :units].reshape(groups, 1, units_dev), member, 1
        )
        ones = sum(ones)
        summed = total_over_all(jnp.concatenate([
            ones[0], ones[1], sums_two[2], sums_two[1], sums_two[3], wide_qkv.reshape(-1), wide_up.reshape(-1),
        ]))
        mine, start = [], 0
        for size in [model] * 5 + [3 * model, groups * members * units_dev]:
            mine.append(lax.dynamic_slice_in_dim(summed, start + place * (size // devices), size // devices))
            start += size
    gain_1, bias_1, gain_2, bias_2, end_bias, qkv_shift, up_shift = mine
    return (
        output, grad_tokens, gain_1, bias_1, gain_2, bias_2, g_qkv, qkv_shift, g_out, end_bias, g_up, up_shift, g_down, end_bias,
    )


def solution(mesh):
    row, vec = P(ALL, None), P(ALL)
    return jax.shard_map(
        local,
        mesh=mesh,
        in_specs=(row, row, P("dp", None), vec, vec, vec, vec, row, vec, row, vec, row, vec, row, vec),
        out_specs=(row, row, vec, vec, vec, vec, row, vec, row, vec, row, vec, row, vec),
        check_vma=False,
    )
```

```python
import functools

import jax
import jax.numpy as jnp
import numpy as np
from jax import lax
from jax.experimental import pallas as pl
from jax.experimental.pallas import tpu as pltpu
from jax.sharding import PartitionSpec as P

HEADS = 16
HEAD = 64
ROT = 16
BLOCK = 256
EPS = 1e-05
ALL = ("dp", "fsdp")
LONG = pl.CostEstimate(flops=2 * 10**10, bytes_accessed=10**7, transcendentals=0)
SHORT = pl.CostEstimate(flops=0, bytes_accessed=0, transcendentals=0)
F32 = jnp.float32
LOW = jnp.bfloat16


def dot(left, right, contract=((1,), (0,))):
    return lax.dot_general(left, right, (contract, ((), ())), preferred_element_type=F32)


NT = ((1,), (1,))
TN = ((0,), (0,))


def normed(x_rows):
    centre = x_rows - jnp.mean(x_rows, axis=-1, keepdims=True)
    spread = jnp.mean(centre * centre, axis=-1, keepdims=True)
    scale = lax.rsqrt(spread + EPS)
    return centre * scale, scale


def turned(z, cosine, sine, sign):
    groups = []
    for start in range(0, z.shape[1], 128):
        part = z[:, start : start + 128]
        ahead = pltpu.roll(part, 128 - ROT // 2, 1)
        behind = pltpu.roll(part, ROT // 2, 1)
        lane = lax.broadcasted_iota(jnp.int32, part.shape, 1) & (HEAD - 1)
        groups.append(part * cosine + sign * (jnp.where(lane < ROT // 2, ahead, behind) * sine))
    return groups[0] if len(groups) == 1 else jnp.concatenate(groups, axis=1)


def head_only(array, head):
    lane = lax.broadcasted_iota(jnp.int32, array.shape, 1)
    keep = (lane >= head * HEAD) & (lane < (head + 1) * HEAD)
    return jnp.where(keep, array, jnp.zeros_like(array))


def params(*order):
    return pltpu.CompilerParams(vmem_limit_bytes=60 * 1024 * 1024, dimension_semantics=order)


def whole(shape):
    return pl.BlockSpec(shape, lambda *_: (0,) * len(shape))


HBM = pl.BlockSpec(memory_space=pl.ANY)


def fetch(plan, step, refs, target, sems, begin):
    for at, pieces in enumerate(plan):

        @pl.when(step == at)
        def _():
            for index, (ref, start, put, size) in enumerate(pieces):
                copy = pltpu.make_async_copy(
                    refs[ref].at[pl.ds(start, size)], target.at[pl.ds(put, size)], sems.at[at, index]
                )
                if begin:
                    copy.start()
                else:
                    copy.wait()


def fetch_all(plan, refs, target, sems):
    for at in range(len(plan)):
        fetch(plan, at, refs, target, sems, True)


def plan_of(pieces, span):
    plan, total = [], sum(p.shape[0] for p in pieces)
    for low in range(0, total, span):
        taken, at = [], 0
        for index, piece in enumerate(pieces):
            a, b = max(low, at), min(low + span, at + piece.shape[0])
            if a < b:
                taken.append((index, a - at, a, b - a))
            at += piece.shape[0]
        plan.append(tuple(taken))
    return tuple(plan)


def store(plan, step, source, refs, sems, begin):
    for at, pieces in enumerate(plan):

        @pl.when(step == at)
        def _():
            for index, (ref, start, put, size) in enumerate(pieces):
                copy = pltpu.make_async_copy(
                    source.at[pl.ds(put, size)], refs[ref].at[pl.ds(start, size)], sems.at[at, index]
                )
                if begin:
                    copy.start()
                else:
                    copy.wait()


def pack_kernel(members, member, qkv, up, small, *out):
    width = qkv.shape[1] // 3 // members
    units_dev = 128
    groups = up.shape[1] // units_dev // members
    for bit in range(members):
        to = member[0] ^ bit
        for part in range(3):
            start = pl.multiple_of((part * members + to) * width, 128)
            out[bit][:, part * width : (part + 1) * width] = qkv[:, pl.ds(start, width)]
        out[bit][:, 3 * width : 3 * width + 128] = jnp.zeros((qkv.shape[0], 128), LOW)
        out[bit][0 : small.shape[0], 3 * width : 3 * width + 128] = small[...]
        for group in range(groups):
            start = pl.multiple_of((group * members + to) * units_dev, 128)
            low = 3 * width + 128 + group * units_dev
            out[bit][:, low : low + units_dev] = up[:, pl.ds(start, units_dev)]


def call_pack(member, qkv, up, small, members):
    shard = qkv.shape[0]
    columns = (qkv.shape[1] + up.shape[1]) // members + 128
    return pl.pallas_call(
        functools.partial(pack_kernel, members),
        grid_spec=pltpu.PrefetchScalarGridSpec(
            num_scalar_prefetch=1,
            grid=(1,),
            in_specs=[whole(qkv.shape), whole(up.shape), whole(small.shape)],
            out_specs=[whole((shard, columns))] * members,
        ),
        out_shape=[jax.ShapeDtypeStruct((shard, columns), LOW)] * members,
        compiler_params=params("arbitrary"),
        cost_estimate=SHORT,
        name="pack",
    )(member, qkv, up, small)


def place_kernel(cut, member, *refs):
    *pieces, first, second = refs
    shard = pieces[0].shape[0]
    for bit, piece in enumerate(pieces):
        rows = pl.ds(pl.multiple_of((member[0] ^ bit) * shard, shard), shard)
        first[rows, :] = piece[:, :cut]
        second[rows, :] = piece[:, cut:]


def call_place(member, pieces, cut):
    members, (shard, columns) = len(pieces), pieces[0].shape
    shapes = [(members * shard, cut), (members * shard, columns - cut)]
    return pl.pallas_call(
        functools.partial(place_kernel, cut),
        grid_spec=pltpu.PrefetchScalarGridSpec(
            num_scalar_prefetch=1,
            grid=(1,),
            in_specs=[whole(p.shape) for p in pieces],
            out_specs=[whole(a) for a in shapes],
        ),
        out_shape=[jax.ShapeDtypeStruct(a, LOW) for a in shapes],
        compiler_params=params("arbitrary"),
        cost_estimate=SHORT,
        name="place",
    )(member, *pieces)


def small_block(member, members, vectors, qkv_bias, up_bias):
    size = vectors[0].shape[0]
    wide = 128 // members * (members - 1)
    rows = jnp.pad(jnp.stack(vectors), ((0, 0), (wide, wide)))
    rows = lax.dynamic_slice_in_dim(rows, wide - member * size, 128, 1)
    wide = 3 * wide
    shift = lax.dynamic_slice_in_dim(jnp.pad(qkv_bias, (wide, wide)), wide - member * 3 * size, 384, 0)
    return jnp.concatenate([rows, shift.reshape(3, 128), up_bias[None], jnp.zeros((16 - len(vectors) - 4, 128), LOW)], axis=0)


def vectors_kernel(members, member, gathered, out, wide):
    groups, rows, _ = gathered.shape
    shard = rows // members
    model = groups * 128
    out[...] = jnp.zeros_like(out)
    for group in range(groups):
        blocks = [gathered[group, m * shard : m * shard + 16, :].astype(F32) for m in range(members)]
        block = blocks[0]
        for other in blocks[1:]:
            block = block + other
        lanes = slice(group * 128, (group + 1) * 128)
        for row in range(6):
            out[row : row + 1, lanes] = block[row : row + 1, :]
        for row in range(3):
            low = group * 384 + row * 128
            wide[0:1, low : low + 128] = block[6 + row : 7 + row, :]
        own = jnp.zeros((1, 128), F32)
        for m in range(members):
            own = own + jnp.where(member[0] == m, blocks[m][9:10, :], 0.0)
        out[6:7, lanes] = own
    width = model // members
    for part in range(3):
        start = pl.multiple_of(part * model + member[0] * width, 128)
        out[7 + part : 8 + part, :width] = wide[0:1, pl.ds(start, width)]


def call_vectors(member, gathered, members, cut):
    groups, rows, _ = gathered.shape
    model = groups * 128
    return pl.pallas_call(
        functools.partial(vectors_kernel, members),
        grid_spec=pltpu.PrefetchScalarGridSpec(
            num_scalar_prefetch=1,
            grid=(1,),
            in_specs=[pl.BlockSpec((groups, rows, 128), lambda i, o: (0, 0, cut // 128 - 1))],
            out_specs=whole((16, model)),
            scratch_shapes=[pltpu.VMEM((8, 3 * model), F32)],
        ),
        out_shape=jax.ShapeDtypeStruct((16, model), F32),
        compiler_params=params("arbitrary"),
        cost_estimate=SHORT,
        name="vectors",
    )(member, gathered)


def qkv_kernel(plan, count, order, *refs):
    pieces, rest = refs[:count], refs[count:]
    vectors, weight, turn, q, k, v, normal, x, sems = rest
    step = pl.program_id(0)
    width = q.shape[1]
    span = q.shape[0]
    model = x.shape[1]

    @pl.when(step == 0)
    def _():
        fetch_all(plan, pieces, x, sems)

    fetch(plan, step, pieces, x, sems, False)
    n, _ = normed(x[pl.ds(pl.multiple_of(step * span, span), span), :].astype(F32))
    h = (n * vectors[0:1, :] + vectors[1:2, :]).astype(LOW)
    normal[...] = h
    tables = (turn[:, :128], turn[:, 128:])
    rows = dot(h, weight[...].reshape(model, 3 * width))
    q[...] = (turned(rows[:, :width] + vectors[7:8, :width], *tables, 1.0) * 0.125).astype(LOW)
    k[...] = turned(rows[:, width : 2 * width] + vectors[8:9, :width], *tables, 1.0).astype(LOW)
    v[...] = (rows[:, 2 * width :] + vectors[9:10, :width]).astype(LOW)


def call_qkv(order, pieces, vectors, weight, tables, span, width):
    model = pieces[0].shape[1]
    plan = plan_of(pieces, span)
    rows = span * len(plan)
    there = lambda i, o: (o[i], 0)
    return pl.pallas_call(
        functools.partial(qkv_kernel, plan, len(pieces)),
        grid_spec=pltpu.PrefetchScalarGridSpec(
            num_scalar_prefetch=1,
            grid=(rows // span,),
            in_specs=[HBM] * len(pieces)
            + [whole(vectors.shape), whole(weight.shape[:2] + (3 * width,))]
            + [pl.BlockSpec((span, 256), there)],
            out_specs=[pl.BlockSpec((span, width), there)] * 3 + [pl.BlockSpec((span, model), there)],
            scratch_shapes=[pltpu.VMEM((rows, model), LOW), pltpu.SemaphoreType.DMA((len(plan), 2))],
        ),
        out_shape=[jax.ShapeDtypeStruct((rows, width), LOW)] * 3 + [jax.ShapeDtypeStruct((rows, model), LOW)],
        compiler_params=params("arbitrary"),
        cost_estimate=SHORT,
        name="qkv",
    )(order, *pieces, vectors, weight, tables)


def masked_rows(target, array):
    for head in range(array.shape[1] // HEAD):
        target[head * BLOCK : (head + 1) * BLOCK, :] = head_only(array, head)


def over_keys(first, block, tiles):
    begin = first[block]
    count = block + 1 - begin

    def pair(i, _):
        tiles(begin + 2 * i, 2)
        return 0

    def single(at, _):
        tiles(at, 1)
        return 0

    lax.fori_loop(0, count // 2, pair, 0)
    lax.fori_loop(block + 1 - count % 2, block + 1, single, 0)


def by_eight(array):
    return array.reshape(BLOCK // 8, 8, BLOCK)


def fwd_kernel(first, q, k, v, mixed, low_mixed, lse, keys, values, scores, top, total, out):
    step = pl.program_id(0)
    width = q.shape[1]
    heads = width // HEAD
    stack = heads * BLOCK
    masked_rows(keys.at[step], k[...])
    masked_rows(values.at[step], v[...])
    q_t = q[...].T
    top[...] = jnp.full_like(top, -1e30)
    total[...] = jnp.zeros_like(total)
    out[...] = jnp.zeros_like(out)

    def score(at, count):
        s = dot(keys[pl.ds(at, count)].reshape(count * stack, width), q_t)
        scores[pl.ds(at, count)] = s.reshape(count, stack, BLOCK)
        for head in range(heads):
            best = top[head]
            for tile in range(count):
                low = tile * stack + head * BLOCK
                best = jnp.maximum(best, jnp.max(by_eight(s[low : low + BLOCK]), axis=0))
            top[head] = best

    over_keys(first, step, score)
    peak = [jnp.max(top[head], axis=0, keepdims=True) for head in range(heads)]

    def mix(at, count):
        grown = []
        for tile in range(count):
            for head in range(heads):
                e = jnp.exp(scores[at + tile, head * BLOCK : (head + 1) * BLOCK] - peak[head])
                total[head] += jnp.sum(by_eight(e), axis=0)
                grown.append(e.astype(LOW))
        out[...] += dot(jnp.concatenate(grown, axis=0), values[pl.ds(at, count)].reshape(count * stack, width), TN)

    over_keys(first, step, mix)
    shares = []
    for head in range(heads):
        sums = jnp.sum(total[head], axis=0, keepdims=True)
        lse[head : head + 1, :] = peak[head] + jnp.log(sums)
        shares.append(jnp.broadcast_to(1.0 / sums, (HEAD, BLOCK)))
    result = out[...] * jnp.concatenate(shares, axis=0).T
    mixed[...] = result
    low_mixed[...] = result.astype(LOW)


def call_fwd(first, q, k, v):
    rows, width = q.shape
    heads = width // HEAD
    blocks = rows // BLOCK
    return pl.pallas_call(
        fwd_kernel,
        grid_spec=pltpu.PrefetchScalarGridSpec(
            num_scalar_prefetch=1,
            grid=(blocks,),
            in_specs=[pl.BlockSpec((BLOCK, width), lambda i, o: (i, 0))] * 3,
            out_specs=[
                pl.BlockSpec((BLOCK, width), lambda i, o: (i, 0)),
                pl.BlockSpec((BLOCK, width), lambda i, o: (i, 0)),
                pl.BlockSpec((heads, BLOCK), lambda i, o: (0, i)),
            ],
            scratch_shapes=[
                pltpu.VMEM((blocks, heads * BLOCK, width), LOW),
                pltpu.VMEM((blocks, heads * BLOCK, width), LOW),
                pltpu.VMEM((blocks, heads * BLOCK, BLOCK), F32),
                pltpu.VMEM((heads, 8, BLOCK), F32),
                pltpu.VMEM((heads, 8, BLOCK), F32),
                pltpu.VMEM((BLOCK, width), F32),
            ],
        ),
        out_shape=[
            jax.ShapeDtypeStruct((rows, width), F32),
            jax.ShapeDtypeStruct((rows, width), LOW),
            jax.ShapeDtypeStruct((heads, rows), F32),
        ],
        compiler_params=params("arbitrary"),
        cost_estimate=SHORT,
        name="attend",
    )(first, q, k, v)


def closed_rows(x, rows, to_norm, vectors, weight):
    n, scale = normed(x.astype(F32))
    d_h = dot(rows, weight, NT)
    bias = jnp.sum(d_h, axis=0, keepdims=True)
    gain = jnp.sum(d_h * n, axis=0, keepdims=True)
    e = d_h * vectors[0:1, :] + to_norm
    e = e - jnp.mean(e, axis=-1, keepdims=True) - n * jnp.mean(e * n, axis=-1, keepdims=True)
    return e * scale, gain, bias


def bwd_kernel(groups, closing, first, q, k, v, d_mixed, mixed, lse, turn, normal, *rest):
    if closing:
        (x_low, x_high, to_norm, vectors, weight), rest = rest[:5], rest[5:]
    (d_out, even, odd, sums), rest = rest[:4], rest[4:]
    if closing:
        (three_low, three_high, ones), rest = rest[:3], rest[3:]
    keys, values, sum_q, sum_k, sum_v, queries, seeds, h, d_rows, sem = rest[:10]
    step = pl.program_id(0)
    blocks = pl.num_programs(0)
    block = blocks - 1 - step
    rows, width = k.shape
    heads = width // HEAD
    stack = heads * BLOCK
    own = pl.ds(pl.multiple_of(block * BLOCK, BLOCK), BLOCK)
    loads = [pltpu.make_async_copy(normal, h, sem.at[0])]
    if closing:
        x, carried, mat = rest[10:]
        half = x_low.shape[0]
        loads += [
            pltpu.make_async_copy(x_low, x.at[pl.ds(0, half)], sem.at[1]),
            pltpu.make_async_copy(x_high, x.at[pl.ds(half, half)], sem.at[2]),
            pltpu.make_async_copy(to_norm.at[pl.ds(rows - 2 * half, 2 * half)], carried, sem.at[3]),
            pltpu.make_async_copy(weight.at[:, :, pl.ds(0, 3 * width)], mat, sem.at[4]),
        ]

    @pl.when(step == 0)
    def _():
        for load in loads:
            load.start()

        def prepare(at, _):
            here = pl.ds(pl.multiple_of(at * BLOCK, BLOCK), BLOCK)
            masked_rows(keys.at[at], k[here, :])
            masked_rows(values.at[at], v[here, :])
            sum_k[here, :] = jnp.zeros((BLOCK, width), F32)
            sum_v[here, :] = jnp.zeros((BLOCK, width), F32)
            return 0

        lax.fori_loop(0, blocks, prepare, 0)
        sums[...] = jnp.zeros_like(sums)

    q_own = q[...]
    s_own = d_mixed[...]
    masked_rows(queries, q_own)
    masked_rows(seeds, s_own)
    q_t = q_own.T
    s_t = s_own.T
    product_t = (s_own.astype(F32) * mixed[...]).T
    delta = [jnp.sum(product_t[head * HEAD : (head + 1) * HEAD, :], axis=0, keepdims=True) for head in range(heads)]
    log_total = [lse[head : head + 1, :] for head in range(heads)]
    sum_q[...] = jnp.zeros_like(sum_q)

    def tiles(at, count):
        key_rows = keys[pl.ds(at, count)].reshape(count * stack, width)
        s = dot(key_rows, q_t)
        d_p = dot(values[pl.ds(at, count)].reshape(count * stack, width), s_t)
        wide_probs, wide_scores, tall_scores = [], [], []
        for tile in range(count):
            low_probs, low_scores = [], []
            for head in range(heads):
                low = tile * stack + head * BLOCK
                probs = jnp.exp(s[low : low + BLOCK] - log_total[head])
                low_scores.append((probs * (d_p[low : low + BLOCK] - delta[head])).astype(LOW))
                low_probs.append(probs.astype(LOW))
            wide_probs.append(jnp.concatenate(low_probs, axis=1))
            wide_scores.append(jnp.concatenate(low_scores, axis=1))
            tall_scores += low_scores
        here = pl.ds(pl.multiple_of(at * BLOCK, BLOCK), count * BLOCK)
        sum_v[here, :] += dot(jnp.concatenate(wide_probs, axis=0), seeds[...])
        sum_k[here, :] += dot(jnp.concatenate(wide_scores, axis=0), queries[...])
        sum_q[...] += dot(jnp.concatenate(tall_scores, axis=0), key_rows, TN)

    over_keys(first, block, tiles)
    turns = (turn[:, :128], turn[:, 128:])
    done = jnp.concatenate(
        [
            (turned(sum_q[...], *turns, -1.0) * 0.125).astype(LOW),
            turned(sum_k[own, :], *turns, -1.0).astype(LOW),
            sum_v[own, :].astype(LOW),
        ],
        axis=1,
    )
    d_rows[own, :] = done
    d_out[...] = done
    sums[0:1, :] += jnp.sum(done.astype(F32), axis=0, keepdims=True)

    @pl.when(step == blocks - 1)
    def _():
        for load in loads:
            load.wait()
        if closing:
            start = pl.multiple_of(first[first.shape[0] - 1] * 2 * half, 2 * half)
            gain = bias = 0.0
            for low, out in ((0, three_low), (half, three_high)):
                e, a, b = closed_rows(
                    x[low : low + half, :], d_rows[pl.ds(start + low, half), :], carried[low : low + half, :], vectors,
                    mat[...].reshape(h.shape[1], 3 * width),
                )
                out[...] = e.astype(LOW)
                gain, bias = gain + a, bias + b
            ones[0:1, :] = gain
            ones[1:2, :] = bias
        group = first[first.shape[0] - 2]
        model = h.shape[1]
        grad = dot(h[...], d_rows[...], TN).astype(LOW)
        h[:model, : 3 * width] = grad
        per = model // groups
        for place in range(groups):
            to = odd if place % 2 else even
            here = pl.ds(pl.multiple_of((group ^ place) * per, per), per)
            to[place // 2] = h[here, : 3 * width]


def call_bwd(first, q, k, v, d_mixed, mixed, lse, tables, normal, groups, closing=()):
    rows, width = q.shape
    heads = width // HEAD
    blocks = rows // BLOCK
    model = normal.shape[1]
    grad = (groups // 2, model // groups, 3 * width)
    back = lambda i, o: (blocks - 1 - i, 0)
    blocked = pl.BlockSpec((BLOCK, width), back)
    outs = [((rows, 3 * width), LOW), (grad, LOW), (grad, LOW), ((8, 3 * width), F32)]
    scratch = [
        pltpu.VMEM((blocks, heads * BLOCK, width), LOW),
        pltpu.VMEM((blocks, heads * BLOCK, width), LOW),
        pltpu.VMEM((BLOCK, width), F32),
        pltpu.VMEM((rows, width), F32),
        pltpu.VMEM((rows, width), F32),
        pltpu.VMEM((heads * BLOCK, width), LOW),
        pltpu.VMEM((heads * BLOCK, width), LOW),
        pltpu.VMEM((rows, model), LOW),
        pltpu.VMEM((rows, 3 * width), LOW),
        pltpu.SemaphoreType.DMA((5,)),
    ]
    specs = []
    if closing:
        half = closing[0].shape[0]
        outs += [((half, model), LOW)] * 2 + [((8, model), F32)]
        scratch += [
            pltpu.VMEM((2 * half, model), LOW),
            pltpu.VMEM((2 * half, model), F32),
            pltpu.VMEM(closing[4].shape[:2] + (3 * width,), LOW),
        ]
        specs = [HBM] * 3 + [whole(closing[3].shape), HBM]
    return pl.pallas_call(
        functools.partial(bwd_kernel, groups, bool(closing)),
        grid_spec=pltpu.PrefetchScalarGridSpec(
            num_scalar_prefetch=1,
            grid=(blocks,),
            in_specs=[blocked, whole((rows, width)), whole((rows, width)), blocked, blocked]
            + [pl.BlockSpec((heads, BLOCK), lambda i, o: (0, blocks - 1 - i)), pl.BlockSpec((BLOCK, 256), back), HBM]
            + specs,
            out_specs=[pl.BlockSpec((BLOCK, 3 * width), back)] + [whole(a) for a, _ in outs[1:]],
            scratch_shapes=scratch,
        ),
        out_shape=[jax.ShapeDtypeStruct(a, kind) for a, kind in outs],
        compiler_params=params("arbitrary"),
        cost_estimate=SHORT,
        name="attend_back",
    )(first, q, k, v, d_mixed, mixed, lse, tables, normal, *closing)


def mlp_kernel(plan, out_plan, count, out_count, joined, chunk, order, *refs):
    x_pieces, cot_pieces, rest = refs[:count], refs[count : 2 * count], refs[2 * count :]
    mixed, vectors, rest = rest[0], rest[1], rest[2:]
    mats, rest = rest[: 1 if joined else 3], rest[1 if joined else 3 :]
    parts, rest = rest[:out_count], rest[out_count:]
    d_mixed, to_norm, rest = rest[0], rest[1], rest[2:]
    grads, rest = rest[: 1 if joined else 2], rest[1 if joined else 2 :]
    g_out, sums, normal, cot, active, d_up, own_mixed, staged, x_sems, cot_sems, out_sems = rest
    step = pl.program_id(0)
    steps = len(plan)
    span, width = own_mixed.shape[0] // steps, own_mixed.shape[1]
    model, units = normal.shape[1], active.shape[1]
    if joined:
        groups = mats[0].shape[0]
        cuts = [0, model // groups, (model + units) // groups, (model + units + width) // groups]
        w_up, w_down, w_out = (mats[0].at[:, pl.ds(cuts[i], cuts[i + 1] - cuts[i]), :] for i in range(3))
    else:
        w_up, w_down, w_out = mats
    as_up = lambda: w_up[...].reshape(model, units)
    as_down = lambda: w_down[...].reshape(units, model)
    as_out = lambda: w_out[...].reshape(width, model)

    @pl.when(step == 0)
    def _():
        fetch_all(plan, x_pieces, normal, x_sems)
        fetch_all(plan, cot_pieces, cot, cot_sems)
        sums[...] = jnp.zeros_like(sums)

    fetch(plan, step, x_pieces, normal, x_sems, False)
    fetch(plan, step, cot_pieces, cot, cot_sems, False)

    @pl.when(step < steps)
    def _():
        here = pl.ds(pl.multiple_of(step * span, span), span)
        n, _ = normed(normal[here, :].astype(F32))
        h = (n * vectors[2:3, :] + vectors[3:4, :]).astype(LOW)
        normal[here, :] = h
        dy = cot[here, :]
        own = mixed[pl.ds(pl.multiple_of(order[step] * span, span), span), :]
        own_mixed[here, :] = own
        d_mixed[...] = dot(dy, as_out(), NT).astype(LOW)
        up, down = as_up(), as_down()
        for low in range(0, units, chunk):
            cols = slice(low, low + chunk)
            u = dot(h, up[:, cols]) + vectors[6:7, cols]
            d_active = dot(dy, down[cols], NT)
            cdf = 0.5 * (1.0 + lax.erf(u * np.float32(np.sqrt(0.5))))
            slope = cdf + u * (jnp.exp(-0.5 * u * u) * np.float32(1.0 / np.sqrt(2.0 * np.pi)))
            active[here, cols] = (u * cdf).astype(LOW)
            back = (d_active * slope).astype(LOW)
            d_up[here, cols] = back
            sums[0:1, cols] += jnp.sum(back.astype(F32), axis=0, keepdims=True)
        staged[here, :] = (dot(active[here, :], down) + dot(own, as_out())).astype(LOW)
        d_h = dot(d_up[here, :], up, NT)
        sums[1:2, :model] += jnp.sum(d_h, axis=0, keepdims=True)
        sums[2:3, :model] += jnp.sum(d_h * n, axis=0, keepdims=True)
        to_norm[...] = d_h * vectors[2:3, :]

        @pl.when(step == 0)
        def _():
            sums[3:4, :model] = jnp.sum(dy.astype(F32), axis=0, keepdims=True)

    store(out_plan, step, staged, parts, out_sems, True)

    @pl.when(step >= steps)
    def _():
        at = step - steps
        many = pl.num_programs(0) - steps

        @pl.when(at == 0)
        def _():
            g_out[...] = dot(own_mixed[...], cot[...], TN).astype(LOW)

        up_cols = pl.ds(pl.multiple_of(at * (model // many), 128), model // many)
        down_cols = pl.ds(pl.multiple_of(at * (units // many), 128), units // many)
        up_grad = dot(normal[:, up_cols], d_up[...], TN).astype(LOW)
        down_grad = dot(active[:, down_cols], cot[...], TN).astype(LOW)
        if joined:
            block = grads[0].shape[0]
            grads[0][:, cuts[0] : cuts[1], :] = up_grad.reshape(block, cuts[1], units)
            grads[0][:, cuts[1] : cuts[2], :] = down_grad.reshape(block, cuts[2] - cuts[1], model)
        else:
            grads[0][...] = up_grad
            grads[1][...] = down_grad

    @pl.when(step == pl.num_programs(0) - 1)
    def _():
        for at in range(steps):
            store(out_plan, at, staged, parts, out_sems, False)


def call_mlp(order, x_pieces, cot_pieces, mixed, vectors, mats, span, units, out_shapes):
    rows, width = mixed.shape
    model = x_pieces[0].shape[1]
    joined = len(mats) == 1
    plan, out_plan = plan_of(x_pieces, span), plan_of(out_shapes, span)
    steps, many = len(plan), 4
    count = len(x_pieces)
    here = lambda i, o: (jnp.minimum(i, steps - 1), 0)
    there = lambda i, o: (o[jnp.minimum(i, steps - 1)], 0)
    later = lambda i, o: (jnp.maximum(i - steps, 0), 0)
    if joined:
        groups = mats[0].shape[0]
        grads = [(groups, (model + units) // groups, model)]
        grad_specs = [pl.BlockSpec((groups // many,) + grads[0][1:], lambda i, o: (jnp.maximum(i - steps, 0), 0, 0))]
    else:
        grads = [(model, units), (units, model)]
        grad_specs = [pl.BlockSpec((a // many, b), later) for a, b in grads]
    sums = (8, max(model, units))
    return pl.pallas_call(
        functools.partial(mlp_kernel, plan, out_plan, count, len(out_shapes), joined, 256),
        grid_spec=pltpu.PrefetchScalarGridSpec(
            num_scalar_prefetch=1,
            grid=(steps + many,),
            in_specs=[HBM] * (2 * count)
            + [whole((rows, width)), whole(vectors.shape)]
            + [pl.BlockSpec(m.shape, lambda *_: (0, 0, 0), pipeline_mode=pl.Buffered(1)) for m in mats],
            out_specs=[HBM] * len(out_shapes)
            + [pl.BlockSpec((span, width), there), pl.BlockSpec((span, model), here)]
            + grad_specs
            + [whole((width, model)), whole(sums)],
            scratch_shapes=[
                pltpu.VMEM((rows, model), LOW),
                pltpu.VMEM((rows, model), LOW),
                pltpu.VMEM((rows, units), LOW),
                pltpu.VMEM((rows, units), LOW),
                pltpu.VMEM((rows, width), LOW),
                pltpu.VMEM((rows, model), LOW),
                pltpu.SemaphoreType.DMA((steps, 2)),
                pltpu.SemaphoreType.DMA((steps, 2)),
                pltpu.SemaphoreType.DMA((steps, 2)),
            ],
        ),
        out_shape=list(out_shapes)
        + [jax.ShapeDtypeStruct((rows, width), LOW), jax.ShapeDtypeStruct((rows, model), F32)]
        + [jax.ShapeDtypeStruct(g, LOW) for g in grads + [(width, model)]]
        + [jax.ShapeDtypeStruct(sums, F32)],
        compiler_params=params("arbitrary"),
        cost_estimate=SHORT,
        name="mlp",
    )(order, *x_pieces, *cot_pieces, mixed, vectors, *mats)


def close_kernel(plan, many, parts, summed, joined, merges, order, *refs):
    xs, refs = refs[:many], refs[many:]
    d_rows, (to_norm, vectors, weight), refs = refs[:parts], refs[parts : parts + 3], refs[parts + 3 :]
    added, refs = refs[:summed], refs[summed:]
    come, refs = refs[: len(merges)], refs[len(merges) :]
    count = len(plan) // joined
    outs, output, (sums, x, e_low) = refs[:count], refs[count:-3], refs[-3:]
    step = pl.program_id(0)

    @pl.when(step == 0)
    def _():
        sums[...] = jnp.zeros_like(sums)

    for at, (piece, _, _) in enumerate(plan):

        @pl.when(step == at)
        def _():
            x[...] = xs[piece][...]

    model = x.shape[1]
    rows = d_rows[0][...]
    e, gain, bias = closed_rows(x[...], rows, to_norm[...], vectors, weight[...].reshape(model, rows.shape[1]))
    sums[0:1, :] += gain
    sums[1:2, :] += bias
    e_low[...] = e
    for at in range(len(plan)):

        @pl.when(step == at)
        def _():
            e = e_low[...]
            if at in merges:
                e = e + come[merges.index(at)][...].astype(F32)
            low = at % joined * BLOCK
            outs[at // joined][low : low + BLOCK, :] = e.astype(LOW)
            if summed and at >= len(plan) - 2:
                total = x[...].astype(F32) + vectors[4:5, :] + vectors[5:6, :]
                for ref in added:
                    total = total + ref[...].astype(F32)
                output[0][...] = total.astype(LOW)


def call_close(order, pieces, plan, d_rows, to_norm, vectors, weight, span, cost=SHORT, added=(), joined=2, merges=(), come=()):
    model = pieces[0].shape[1]
    width3 = sum(d.shape[1] for d in d_rows)
    per = span // BLOCK
    steps = len(plan)

    def pick(values, i):
        value = jnp.int32(values[-1])
        for at in range(len(values) - 1):
            value = jnp.where(i == at, jnp.int32(values[at]), value)
        return value

    def block_of(piece):
        reads = [(at, start // BLOCK) for at, (index, start, _) in enumerate(plan) if index == piece]
        values = [next((b for a, b in reversed(reads) if a <= at), reads[0][1]) for at in range(steps)]
        return lambda i, o: (pick(values, i), 0)

    places = [low // BLOCK for _, _, low in plan]
    here = lambda i, o: (pick(places, i), 0)
    there = lambda i, o: (o[pick(places, i) // per] * per + pick(places, i) % per, 0)
    return pl.pallas_call(
        functools.partial(close_kernel, plan, len(pieces), len(d_rows), len(added), joined, merges),
        grid_spec=pltpu.PrefetchScalarGridSpec(
            num_scalar_prefetch=1,
            grid=(steps,),
            in_specs=[pl.BlockSpec((BLOCK, model), block_of(piece)) for piece in range(len(pieces))]
            + [pl.BlockSpec((BLOCK, d.shape[1]), there) for d in d_rows]
            + [pl.BlockSpec((BLOCK, model), here), whole(vectors.shape), whole(weight.shape[:2] + (width3,))]
            + [pl.BlockSpec((BLOCK, model), lambda i, o: (jnp.maximum(i - (steps - 2), 0), 0))] * len(added)
            + [whole((BLOCK, model))] * len(come),
            out_specs=[whole((joined * BLOCK, model))] * (steps // joined)
            + [pl.BlockSpec((BLOCK, model), lambda i, o: (jnp.maximum(i - (steps - 2), 0), 0))] * bool(added)
            + [whole((8, model))],
            scratch_shapes=[pltpu.VMEM((BLOCK, model), LOW), pltpu.VMEM((BLOCK, model), F32)],
        ),
        out_shape=[jax.ShapeDtypeStruct((joined * BLOCK, model), LOW)] * (steps // joined)
        + [jax.ShapeDtypeStruct((2 * BLOCK, model), LOW)] * bool(added)
        + [jax.ShapeDtypeStruct((8, model), F32)],
        compiler_params=params("arbitrary"),
        cost_estimate=cost,
        name="close",
    )(order, *pieces, *d_rows, to_norm, vectors, weight, *added, *come)


def finish_kernel(base, *refs):
    *parts, out = refs
    for at in range(2):

        @pl.when(pl.program_id(0) == at)
        def _():
            total = base[...].astype(F32)
            for part in parts[at::2]:
                total = total + part[...].astype(F32)
            out[...] = total.astype(LOW)


def call_finish(base, parts):
    rows, model = base.shape
    block = pl.BlockSpec((rows // 2, model), lambda i: (i, 0))
    return pl.pallas_call(
        finish_kernel,
        grid=(2,),
        in_specs=[block] + [whole((rows // 2, model))] * len(parts),
        out_specs=block,
        out_shape=jax.ShapeDtypeStruct((rows, model), LOW),
        compiler_params=params("arbitrary"),
        cost_estimate=SHORT,
        name="finish",
    )(base, *parts)


def cut_kernel(members, member, first, second, third, *out):
    pieces, down = out[:members], out[members]
    shard = pieces[0].shape[0]
    columns = first.shape[1]
    for bit, piece in enumerate(pieces):
        rows = pl.ds(pl.multiple_of((member[0] ^ bit) * shard, shard), shard)
        piece[:, :columns] = first[rows, :]
        piece[:, columns:] = (second[rows, :].astype(F32) + third[rows, :].astype(F32)).astype(LOW)
    low = members * shard
    down[...] = first[low : low + down.shape[0], :].astype(F32)


def call_cut(member, first, second, third, members, shard):
    columns = first.shape[1]
    shapes = [jax.ShapeDtypeStruct((shard, columns + second.shape[1]), LOW)] * members + [
        jax.ShapeDtypeStruct((first.shape[0] - members * shard, columns), F32),
    ]
    return pl.pallas_call(
        functools.partial(cut_kernel, members),
        grid_spec=pltpu.PrefetchScalarGridSpec(
            num_scalar_prefetch=1,
            grid=(1,),
            in_specs=[whole(first.shape), whole(second.shape), whole(third.shape)],
            out_specs=[whole(a.shape) for a in shapes],
        ),
        out_shape=shapes,
        compiler_params=params("arbitrary"),
        cost_estimate=SHORT,
        name="cut",
    )(member, first, second, third)


def join_kernel(places, member, *refs):
    pieces, outs = refs[:-2], refs[-2:]
    for bit, piece in enumerate(pieces):
        for block, (index, column, stride) in enumerate(places):
            start = pl.multiple_of(column + (member[0] ^ bit) * stride, 128)
            outs[index][:, pl.ds(start, 128)] = piece[:, block * 128 : (block + 1) * 128].astype(F32)


def call_join(member, pieces, places, columns):
    shard = pieces[0].shape[0]
    return pl.pallas_call(
        functools.partial(join_kernel, tuple(places)),
        grid_spec=pltpu.PrefetchScalarGridSpec(
            num_scalar_prefetch=1,
            grid=(1,),
            in_specs=[whole(p.shape) for p in pieces],
            out_specs=[whole((shard, c)) for c in columns],
        ),
        out_shape=[jax.ShapeDtypeStruct((shard, c), F32) for c in columns],
        compiler_params=params("arbitrary"),
        cost_estimate=SHORT,
        name="join",
    )(member, *pieces)


def bundle_kernel(members, halves, member, two, *refs):
    *ones, out, wide = refs
    thirds, ones = ones[:halves], ones[halves:]
    groups = out.shape[0] // members
    out[...] = jnp.zeros_like(out)
    wide[...] = jnp.zeros_like(wide)
    one = functools.reduce(lambda a, b: a + b, [one[0:2, :] for one in ones])
    lines = [one[0:1, :], one[1:2, :], two[2:3, :], two[1:2, :], two[3:4, :]]
    size = thirds[0].shape[1] // 3
    per_member = halves * size // 128
    for part in range(3):
        for half, third in enumerate(thirds):
            for at in range(size // 128):
                row = (part * members + member[0]) * per_member + half * (size // 128) + at
                low = part * size + at * 128
                wide[pl.ds(row, 1), :] = third[0:1, low : low + 128]
    for group in range(groups):
        lanes = slice(group * 128, (group + 1) * 128)
        for to in range(members):
            device = group * members + to
            for row, line in enumerate(lines):
                out[device, row : row + 1, :] = line[:, lanes]
            out[device, 5:8, :] = wide[3 * group : 3 * group + 3, :]
            out[device, 8:9, :] = jnp.where(member[0] == to, two[0:1, lanes], 0.0)


def call_bundle(member, members, groups, two, thirds, ones):
    shape = (groups * members, 16, 128)
    return pl.pallas_call(
        functools.partial(bundle_kernel, members, len(thirds)),
        grid_spec=pltpu.PrefetchScalarGridSpec(
            num_scalar_prefetch=1,
            grid=(1,),
            in_specs=[whole(a.shape) for a in (two, *thirds, *ones)],
            out_specs=whole(shape),
            scratch_shapes=[pltpu.VMEM((3 * groups, 128), F32)],
        ),
        out_shape=jax.ShapeDtypeStruct(shape, F32),
        compiler_params=params("arbitrary"),
        cost_estimate=SHORT,
        name="bundle",
    )(member, two, *thirds, *ones)


def across(array, bit):
    size = lax.axis_size("fsdp")
    return lax.ppermute(array, "fsdp", [(i, i ^ bit) for i in range(size)])


def exchange(pieces):
    size = lax.axis_size("fsdp")
    if size != 4:
        return lax.all_to_all(pieces, "fsdp", split_axis=0, concat_axis=0, tiled=True)
    member = lax.axis_index("fsdp")
    out = pieces
    for bit in range(1, size):
        mine = lax.dynamic_index_in_dim(pieces, member ^ bit, 0, keepdims=False)
        out = lax.dynamic_update_index_in_dim(out, across(mine, bit), member ^ bit, 0)
    return out


def behind(array, *others):
    return lax.optimization_barrier((array, *others))[0]


def behind_all(arrays, *others):
    return tuple(behind(array, *others) for array in arrays)


def gather_rows(halves, near=None, *others):
    if lax.axis_size("fsdp") != 4:
        return [lax.all_gather(jnp.concatenate(halves, axis=0), "fsdp", axis=0, tiled=True)]
    one_low, two_high, one_high, two_low = near
    return [
        *halves, one_low, one_high, two_low, two_high,
        across(behind(one_low, *others), 2), across(behind(two_high, *others), 1),
    ]


def near_rows(halves):
    low, high = halves
    return across(low, 1), across(high, 2), across(high, 1), across(low, 2)


def hop(array, bit):
    return lax.ppermute(array, "dp", [(i, i ^ bit) for i in range(lax.axis_size("dp"))])


def scatter_step(blocks, far, bit):
    blocks = (blocks.astype(F32) + far.astype(F32)).astype(LOW)
    send = blocks[1::2]
    return blocks[0::2], hop(send, bit), send


def reduce_direct(parts):
    if len(parts) == 1:
        return (lax.psum_scatter(parts[0], "fsdp", scatter_dimension=0, tiled=True),)
    three = across(parts[3], 3)
    return parts[0], across(parts[1], 1), across(parts[2], 2), three


def total_over_all(vector):
    count = lax.axis_size("dp") * lax.axis_size("fsdp")
    step = 1
    while step < count:
        vector = vector + lax.ppermute(vector, ALL, [(i, i ^ step) for i in range(count)])
        step *= 2
    return vector


def swap_owner(array, back):
    groups, members = lax.axis_size("dp"), lax.axis_size("fsdp")
    pairs = [(m * groups + g, g * members + m) for g in range(groups) for m in range(members)]
    if back:
        pairs = [(b, a) for a, b in pairs]
    return lax.ppermute(array, ALL, pairs)


def gather_dp(array):
    return lax.all_gather(array, "dp", axis=0)


def scatter_dp(array):
    return lax.psum_scatter(array, "dp", scatter_dimension=0, tiled=True)


def rotary_tables(length):
    half = ROT // 2
    frequency = (np.float32(10000.0) ** (-(np.arange(half, dtype=np.float32) * np.float32(2.0)) / np.float32(ROT))).astype(np.float32)
    angles = (np.arange(length, dtype=np.float32)[:, None] * frequency[None, :]).astype(np.float32)
    cosine = np.cos(angles).astype(np.float32)
    sine = np.sin(angles).astype(np.float32)
    cos_row = np.ones((length, 128), np.float32)
    sine_row = np.zeros((length, 128), np.float32)
    for start in range(0, 128, HEAD):
        cos_row[:, start : start + half] = cosine
        cos_row[:, start + half : start + ROT] = cosine
        sine_row[:, start : start + half] = -sine
        sine_row[:, start + half : start + ROT] = sine
    return jnp.asarray(np.concatenate([cos_row, sine_row], axis=1))


def local(
    tokens, cotangent, doc_ids, norm1_gain, norm1_bias, norm2_gain, norm2_bias, qkv_weight, qkv_bias,
    out_weight, out_bias, up_weight, up_bias, down_weight, down_bias,
):
    groups, members = lax.axis_size("dp"), lax.axis_size("fsdp")
    group, member = lax.axis_index("dp"), lax.axis_index("fsdp")
    devices = groups * members
    rows, model = tokens.shape
    stream = rows * members
    shard = qkv_weight.shape[0]
    width = model // members
    units_dev = up_bias.shape[0]
    units = groups * units_dev
    paired = members == 4 and units_dev == 128 and units == model
    me = member.astype(jnp.int32).reshape(1)
    vectors_in = [norm1_gain, norm1_bias, norm2_gain, norm2_bias, out_bias, down_bias]

    half = rows // 2
    x_halves = [tokens[:half], tokens[half:]]
    cot_halves = [cotangent[:half], cotangent[half:]]
    if paired:
        out_own = swap_owner(out_weight, False)
        small = small_block(member, members, vectors_in, qkv_bias, up_bias)
        packed = call_pack(me, qkv_weight, up_weight, small, members)
        arrived = [packed[0]] + [across(packed[bit], bit) for bit in range(1, members)]
        x_near = near_rows(behind_all(x_halves, *arrived[1:]))
        cut = 3 * width + 128
        first_in, up_in = call_place(me, behind_all(arrived, out_own), cut)
        w_first = gather_dp(first_in)
        mats = (gather_dp(jnp.concatenate([up_in, down_weight, out_own], axis=0)),)
        vectors = call_vectors(me, w_first, members, cut)
    else:
        qkv_cut = qkv_weight.reshape(shard, 3, members, width).transpose(2, 0, 1, 3).reshape(members, shard, 3 * width)
        up_cut = up_weight.reshape(shard, groups, members, units_dev).transpose(2, 0, 1, 3).reshape(members, shard, units)
        arrived = exchange(jnp.concatenate([qkv_cut, up_cut], axis=2)).reshape(members * shard, -1)
        w_first = gather_dp(arrived[:, : 3 * width])
        x_near = near_rows(x_halves) if members == 4 else None
        mats = (gather_dp(arrived[:, 3 * width :]), gather_dp(down_weight), gather_dp(swap_owner(out_weight, False)))
        full = [lax.all_gather(a, ALL, axis=0, tiled=True).astype(F32) for a in vectors_in]
        shift = lax.all_gather(qkv_bias, ALL, axis=0, tiled=True).astype(F32).reshape(3, members, width)
        shift = lax.dynamic_index_in_dim(shift, member, 1, keepdims=False)
        up_all = lax.all_gather(up_bias, "dp", axis=0, tiled=True).astype(F32)
        lines = full + [jnp.pad(a, (0, model - a.shape[0])) for a in (up_all, shift[0], shift[1], shift[2])]
        vectors = jnp.pad(jnp.stack(lines), ((0, 6), (0, 0)))

    x_pieces = gather_rows(x_halves, x_near)
    sources = jnp.arange(members, dtype=jnp.int32)
    order = sources ^ member if members == 4 else sources
    doc_row = doc_ids[0]
    first = jnp.sum((doc_row[None, :] < doc_row[:, None]).astype(jnp.int32), axis=1)
    marks = [group, member ^ 3] if members == 4 else [group, member]
    first = jnp.concatenate([first] + [a.astype(jnp.int32).reshape(1) for a in marks])
    tables = rotary_tables(stream)

    q, k, v, normal = call_qkv(order, x_pieces, vectors, w_first, tables, rows, width)
    cot_near = near_rows(behind_all(cot_halves, *x_pieces[2:])) if members == 4 else None
    cot_pieces = gather_rows(cot_halves, cot_near, q)
    mixed, low_mixed, lse = call_fwd(first, q, k, v)
    out_sizes = [rows] * members if members == 4 else [stream]
    out_shapes = [jax.ShapeDtypeStruct((size, model), LOW) for size in out_sizes]
    results = call_mlp(
        order, x_pieces, cot_pieces, low_mixed, vectors, mats, rows, units, out_shapes
    )
    count = len(out_shapes)
    parts, (d_mixed, to_norm), grads, sums_two = results[:count], results[count : count + 2], results[count + 2 : -1], results[-1]
    *grads, g_out = grads
    scattered = scatter_dp(grads[0].reshape(-1, model)) if paired else None
    g_out = scatter_dp(g_out)

    summed = reduce_direct(parts)
    closing = (x_pieces[6], x_pieces[7], to_norm, vectors, w_first) if members == 4 else ()
    d_qkv, even, odd, sums_qkv, *three = call_bwd(first, q, k, v, d_mixed, mixed, lse, tables, normal, groups, closing)
    d_qkv, sums_qkv, halves = [d_qkv], [sums_qkv], 1
    blocks, far, bit = even, hop(odd, 1), 2
    if members == 4:
        close = lambda pieces, *more: call_close(
            order, [x_pieces[p] for p in pieces], [(i, 0, p * half) for i, p in enumerate(pieces)],
            d_qkv, to_norm, vectors, w_first, rows, *more,
        )
        three_low, three_high, ones_a = three
        come = across(three_high, 2), across(three_low, 1)
        to_norm = behind(to_norm, *summed[1:])
        one_low, two_high, ones_b = close((2, 5), LONG, (), 1)
        near = across(one_low, 1), across(two_high, 2)
        blocks, far, send = scatter_step(blocks, behind(far, one_low), bit)
        to_norm = behind(to_norm, send, one_low, *(() if scattered is None else (scattered,)))
        one_high, two_low, ones_c = close((3, 4), SHORT, (), 1, (0, 1), come)
        if groups > 4:
            blocks, far, send = scatter_step(blocks, behind(far, one_high), 2 * bit)
        near += across(behind(one_high, send), 1), across(behind(two_low, send), 2)
        to_norm = behind(to_norm, send, one_high)
        own_low, own_high, output, ones_d = close((0, 1), SHORT, summed, 1)
        ones = [ones_a, ones_b, ones_c, ones_d]
        g_out = swap_owner(behind(g_out, own_low), True)
        bit = 8 if groups > 4 else 4
    else:
        plan = [(0, low, low) for low in range(0, stream, BLOCK)]
        *final, ones = call_close(order, x_pieces, plan, d_qkv, to_norm, vectors, w_first, rows)
        ones = [ones]
        own = reduce_direct([jnp.concatenate(final, axis=0)])[0]
        own_low, own_high, near = own[:half], own[half:], None
        output = (tokens.astype(F32) + summed[0].astype(F32) + vectors[4:5, :] + vectors[5:6, :]).astype(LOW)

    while blocks.shape[0] > 1:
        (blocks, far, _), bit = scatter_step(blocks, far, bit), 2 * bit
    if near is not None:
        far = behind(far, *near[:2])
    g_qkv = blocks[0], far[0]
    if near is None:
        parts = own_low, own_high
    else:
        parts = own_low, own_high, near[0], near[2], near[3], near[1]
    place = group * members + member
    if paired:
        *mixed_pieces, g_down = call_cut(me, scattered, *g_qkv, members, shard)
        places = [(0, b * members * units_dev, units_dev) for b in range(groups)]
        places += [(1, part * model + low, width) for part in range(3) for low in range(0, width, 128)]
        arrived = [mixed_pieces[0]] + [across(mixed_pieces[bit], bit) for bit in range(1, members)]
        g_up, g_qkv = call_join(me, arrived, places, (up_weight.shape[1], qkv_weight.shape[1]))
        grad_tokens = call_finish(behind(cotangent, g_up), parts)
        ready = behind(call_bundle(me, members, groups, sums_two, sums_qkv, ones), far, *parts)
        totals = jnp.sum(lax.all_to_all(ready, ALL, split_axis=0, concat_axis=0), axis=0)
        size = model // devices
        mine = [a[0] for a in jnp.split(lax.dynamic_slice_in_dim(totals[:5], member * size, size, 1), 5)]
        mine += [lax.dynamic_slice_in_dim(totals[5:8].reshape(-1), member * 3 * size, 3 * size), totals[8]]
    else:
        g_up, g_down = [scatter_dp(g) for g in grads]
        grad_tokens = call_finish(cotangent, parts)
        g_down = g_down.astype(F32)
        g_up = exchange(g_up.reshape(members, shard, units))
        g_up = g_up.reshape(members, shard, groups, units_dev).transpose(1, 2, 0, 3).reshape(shard, -1).astype(F32)
        g_qkv = (g_qkv[0].astype(F32) + g_qkv[1].astype(F32)).astype(LOW)
        g_qkv = exchange(g_qkv.reshape(members, shard, 3 * width)).reshape(members, shard, halves, 3, width // halves)
        g_qkv = g_qkv.transpose(1, 3, 0, 2, 4).reshape(shard, -1).astype(F32)
        thirds = jnp.concatenate([a[0].reshape(3, 1, width // halves) for a in sums_qkv], axis=2)
        wide_qkv = lax.dynamic_update_index_in_dim(jnp.zeros((3, members, width), F32), thirds, member, 1)
        wide_up = lax.dynamic_update_index_in_dim(
            jnp.zeros((groups, members, units_dev), F32), sums_two[0, :units].reshape(groups, 1, units_dev), member, 1
        )
        ones = sum(ones)
        summed = total_over_all(jnp.concatenate([
            ones[0], ones[1], sums_two[2], sums_two[1], sums_two[3], wide_qkv.reshape(-1), wide_up.reshape(-1),
        ]))
        mine, start = [], 0
        for size in [model] * 5 + [3 * model, groups * members * units_dev]:
            mine.append(lax.dynamic_slice_in_dim(summed, start + place * (size // devices), size // devices))
            start += size
    gain_1, bias_1, gain_2, bias_2, end_bias, qkv_shift, up_shift = mine
    g_out = (g_out if members == 4 else swap_owner(g_out, True)).astype(F32)
    return (
        output, grad_tokens, gain_1, bias_1, gain_2, bias_2, g_qkv, qkv_shift, g_out, end_bias, g_up, up_shift, g_down, end_bias,
    )


def solution(mesh):
    row, vec = P(ALL, None), P(ALL)
    return jax.shard_map(
        local,
        mesh=mesh,
        in_specs=(row, row, P("dp", None), vec, vec, vec, vec, row, vec, row, vec, row, vec, row, vec),
        out_specs=(row, row, vec, vec, vec, vec, row, vec, row, vec, row, vec, row, vec),
        check_vma=False,
    )
```

```python
import functools

import jax
import jax.numpy as jnp
import numpy as np
from jax import lax
from jax.experimental import pallas as pl
from jax.experimental.pallas import tpu as pltpu
from jax.sharding import PartitionSpec as P

HEADS = 16
HEAD = 64
ROT = 16
BLOCK = 256
EPS = 1e-05
ALL = ("dp", "fsdp")
LONG = pl.CostEstimate(flops=2 * 10**10, bytes_accessed=10**7, transcendentals=0)
SHORT = pl.CostEstimate(flops=0, bytes_accessed=0, transcendentals=0)
F32 = jnp.float32
LOW = jnp.bfloat16


def dot(left, right, contract=((1,), (0,))):
    return lax.dot_general(left, right, (contract, ((), ())), preferred_element_type=F32)


NT = ((1,), (1,))
TN = ((0,), (0,))


def normed(x_rows):
    centre = x_rows - jnp.mean(x_rows, axis=-1, keepdims=True)
    spread = jnp.mean(centre * centre, axis=-1, keepdims=True)
    scale = lax.rsqrt(spread + EPS)
    return centre * scale, scale


def turned(z, cosine, sine, sign):
    groups = []
    for start in range(0, z.shape[1], 128):
        part = z[:, start : start + 128]
        ahead = pltpu.roll(part, 128 - ROT // 2, 1)
        behind = pltpu.roll(part, ROT // 2, 1)
        lane = lax.broadcasted_iota(jnp.int32, part.shape, 1) & (HEAD - 1)
        groups.append(part * cosine + sign * (jnp.where(lane < ROT // 2, ahead, behind) * sine))
    return groups[0] if len(groups) == 1 else jnp.concatenate(groups, axis=1)


def head_only(array, head):
    lane = lax.broadcasted_iota(jnp.int32, array.shape, 1)
    keep = (lane >= head * HEAD) & (lane < (head + 1) * HEAD)
    return jnp.where(keep, array, jnp.zeros_like(array))


def params(*order):
    return pltpu.CompilerParams(vmem_limit_bytes=60 * 1024 * 1024, dimension_semantics=order)


def whole(shape):
    return pl.BlockSpec(shape, lambda *_: (0,) * len(shape))


HBM = pl.BlockSpec(memory_space=pl.ANY)
EXTRA = 16


def fetch(plan, step, refs, target, sems, begin):
    for at, pieces in enumerate(plan):

        @pl.when(step == at)
        def _():
            for index, (ref, start, put, size) in enumerate(pieces):
                copy = pltpu.make_async_copy(
                    refs[ref].at[pl.ds(start, size)], target.at[pl.ds(put, size)], sems.at[at, index]
                )
                if begin:
                    copy.start()
                else:
                    copy.wait()


def fetch_all(plan, refs, target, sems):
    for at in range(len(plan)):
        fetch(plan, at, refs, target, sems, True)


def plan_of(pieces, span):
    plan, total = [], sum(p.shape[0] for p in pieces)
    for low in range(0, total, span):
        taken, at = [], 0
        for index, piece in enumerate(pieces):
            a, b = max(low, at), min(low + span, at + piece.shape[0])
            if a < b:
                taken.append((index, a - at, a, b - a))
            at += piece.shape[0]
        plan.append(tuple(taken))
    return tuple(plan)


def store(plan, step, source, refs, sems, begin):
    for at, pieces in enumerate(plan):

        @pl.when(step == at)
        def _():
            for index, (ref, start, put, size) in enumerate(pieces):
                copy = pltpu.make_async_copy(
                    source.at[pl.ds(put, size)], refs[ref].at[pl.ds(start, size)], sems.at[at, index]
                )
                if begin:
                    copy.start()
                else:
                    copy.wait()


def pack_kernel(members, member, qkv, up, small, *out):
    width = qkv.shape[1] // 3 // members
    units_dev = 128
    groups = up.shape[1] // units_dev // members
    for bit in range(members):
        to = member[0] ^ bit
        for part in range(3):
            start = pl.multiple_of((part * members + to) * width, 128)
            out[bit][:, part * width : (part + 1) * width] = qkv[:, pl.ds(start, width)]
        out[bit][:, 3 * width : 3 * width + 128] = jnp.zeros((qkv.shape[0], 128), LOW)
        out[bit][0 : small.shape[0], 3 * width : 3 * width + 128] = small[...]
        for group in range(groups):
            start = pl.multiple_of((group * members + to) * units_dev, 128)
            low = 3 * width + 128 + group * units_dev
            out[bit][:, low : low + units_dev] = up[:, pl.ds(start, units_dev)]


def call_pack(member, qkv, up, small, members):
    shard = qkv.shape[0]
    columns = (qkv.shape[1] + up.shape[1]) // members + 128
    return pl.pallas_call(
        functools.partial(pack_kernel, members),
        grid_spec=pltpu.PrefetchScalarGridSpec(
            num_scalar_prefetch=1,
            grid=(1,),
            in_specs=[whole(qkv.shape), whole(up.shape), whole(small.shape)],
            out_specs=[whole((shard, columns))] * members,
        ),
        out_shape=[jax.ShapeDtypeStruct((shard, columns), LOW)] * members,
        compiler_params=params("arbitrary"),
        cost_estimate=SHORT,
        name="pack",
    )(member, qkv, up, small)


def place_kernel(cut, member, *refs):
    *pieces, first, second = refs
    shard = pieces[0].shape[0]
    for bit, piece in enumerate(pieces):
        rows = pl.ds(pl.multiple_of((member[0] ^ bit) * shard, shard), shard)
        first[rows, :] = piece[:, :cut]
        second[rows, :] = piece[:, cut:]


def call_place(member, pieces, cut):
    members, (shard, columns) = len(pieces), pieces[0].shape
    shapes = [(members * shard, cut), (members * shard, columns - cut)]
    return pl.pallas_call(
        functools.partial(place_kernel, cut),
        grid_spec=pltpu.PrefetchScalarGridSpec(
            num_scalar_prefetch=1,
            grid=(1,),
            in_specs=[whole(p.shape) for p in pieces],
            out_specs=[whole(a) for a in shapes],
        ),
        out_shape=[jax.ShapeDtypeStruct(a, LOW) for a in shapes],
        compiler_params=params("arbitrary"),
        cost_estimate=SHORT,
        name="place",
    )(member, *pieces)


def small_block(member, members, vectors, qkv_bias, up_bias):
    size = vectors[0].shape[0]
    wide = 128 // members * (members - 1)
    rows = jnp.pad(jnp.stack(vectors), ((0, 0), (wide, wide)))
    rows = lax.dynamic_slice_in_dim(rows, wide - member * size, 128, 1)
    wide = 3 * wide
    shift = lax.dynamic_slice_in_dim(jnp.pad(qkv_bias, (wide, wide)), wide - member * 3 * size, 384, 0)
    return jnp.concatenate([rows, shift.reshape(3, 128), up_bias[None], jnp.zeros((16 - len(vectors) - 4, 128), LOW)], axis=0)


def vectors_kernel(members, member, gathered, out, wide):
    groups, rows, _ = gathered.shape
    shard = rows // members
    model = groups * 128
    out[...] = jnp.zeros_like(out)
    for group in range(groups):
        blocks = [gathered[group, m * shard : m * shard + 16, :].astype(F32) for m in range(members)]
        block = blocks[0]
        for other in blocks[1:]:
            block = block + other
        lanes = slice(group * 128, (group + 1) * 128)
        for row in range(6):
            out[row : row + 1, lanes] = block[row : row + 1, :]
        for row in range(3):
            low = group * 384 + row * 128
            wide[0:1, low : low + 128] = block[6 + row : 7 + row, :]
        own = jnp.zeros((1, 128), F32)
        for m in range(members):
            own = own + jnp.where(member[0] == m, blocks[m][9:10, :], 0.0)
        out[6:7, lanes] = own
    width = model // members
    for part in range(3):
        start = pl.multiple_of(part * model + member[0] * width, 128)
        out[7 + part : 8 + part, :width] = wide[0:1, pl.ds(start, width)]


def call_vectors(member, gathered, members, cut):
    groups, rows, _ = gathered.shape
    model = groups * 128
    return pl.pallas_call(
        functools.partial(vectors_kernel, members),
        grid_spec=pltpu.PrefetchScalarGridSpec(
            num_scalar_prefetch=1,
            grid=(1,),
            in_specs=[pl.BlockSpec((groups, rows, 128), lambda i, o: (0, 0, cut // 128 - 1))],
            out_specs=whole((16, model)),
            scratch_shapes=[pltpu.VMEM((8, 3 * model), F32)],
        ),
        out_shape=jax.ShapeDtypeStruct((16, model), F32),
        compiler_params=params("arbitrary"),
        cost_estimate=SHORT,
        name="vectors",
    )(member, gathered)


def qkv_kernel(plan, count, order, *refs):
    pieces, rest = refs[:count], refs[count:]
    vectors, weight, turn, q, k, v, normal, x, sems = rest
    step = pl.program_id(0)
    width = q.shape[1]
    span = q.shape[0]
    model = x.shape[1]

    @pl.when(step == 0)
    def _():
        fetch_all(plan, pieces, x, sems)

    fetch(plan, step, pieces, x, sems, False)
    n, _ = normed(x[pl.ds(pl.multiple_of(step * span, span), span), :].astype(F32))
    h = (n * vectors[0:1, :] + vectors[1:2, :]).astype(LOW)
    normal[...] = h
    tables = (turn[:, :128], turn[:, 128:])
    rows = dot(h, weight[...].reshape(model, 3 * width))
    q[...] = (turned(rows[:, :width] + vectors[7:8, :width], *tables, 1.0) * 0.125).astype(LOW)
    k[...] = turned(rows[:, width : 2 * width] + vectors[8:9, :width], *tables, 1.0).astype(LOW)
    v[...] = (rows[:, 2 * width :] + vectors[9:10, :width]).astype(LOW)


def call_qkv(order, pieces, vectors, weight, tables, span, width):
    model = pieces[0].shape[1]
    plan = plan_of(pieces, span)
    rows = span * len(plan)
    there = lambda i, o: (o[i], 0)
    return pl.pallas_call(
        functools.partial(qkv_kernel, plan, len(pieces)),
        grid_spec=pltpu.PrefetchScalarGridSpec(
            num_scalar_prefetch=1,
            grid=(rows // span,),
            in_specs=[HBM] * len(pieces)
            + [whole(vectors.shape), whole(weight.shape[:2] + (3 * width,))]
            + [pl.BlockSpec((span, 256), there)],
            out_specs=[pl.BlockSpec((span, width), there)] * 3 + [pl.BlockSpec((span, model), there)],
            scratch_shapes=[pltpu.VMEM((rows, model), LOW), pltpu.SemaphoreType.DMA((len(plan), 2))],
        ),
        out_shape=[jax.ShapeDtypeStruct((rows, width), LOW)] * 3 + [jax.ShapeDtypeStruct((rows, model), LOW)],
        compiler_params=params("arbitrary"),
        cost_estimate=SHORT,
        name="qkv",
    )(order, *pieces, vectors, weight, tables)


def masked_rows(target, array):
    for head in range(array.shape[1] // HEAD):
        target[head * BLOCK : (head + 1) * BLOCK, :] = head_only(array, head)


def over_keys(first, block, tiles):
    begin = first[block]
    count = block + 1 - begin

    def pair(i, _):
        tiles(begin + 2 * i, 2)
        return 0

    def single(at, _):
        tiles(at, 1)
        return 0

    lax.fori_loop(0, count // 2, pair, 0)
    lax.fori_loop(block + 1 - count % 2, block + 1, single, 0)


def by_eight(array):
    return array.reshape(BLOCK // 8, 8, BLOCK)


def fwd_kernel(first, q, k, v, mixed, low_mixed, lse, keys, values, scores, top, total, out):
    step = pl.program_id(0)
    width = q.shape[1]
    heads = width // HEAD
    stack = heads * BLOCK
    masked_rows(keys.at[step], k[...])
    masked_rows(values.at[step], v[...])
    q_t = q[...].T
    top[...] = jnp.full_like(top, -1e30)
    total[...] = jnp.zeros_like(total)
    out[...] = jnp.zeros_like(out)

    def score(at, count):
        s = dot(keys[pl.ds(at, count)].reshape(count * stack, width), q_t)
        scores[pl.ds(at, count)] = s.reshape(count, stack, BLOCK)
        for head in range(heads):
            best = top[head]
            for tile in range(count):
                low = tile * stack + head * BLOCK
                best = jnp.maximum(best, jnp.max(by_eight(s[low : low + BLOCK]), axis=0))
            top[head] = best

    over_keys(first, step, score)
    peak = [jnp.max(top[head], axis=0, keepdims=True) for head in range(heads)]

    def mix(at, count):
        grown = []
        for tile in range(count):
            for head in range(heads):
                e = jnp.exp(scores[at + tile, head * BLOCK : (head + 1) * BLOCK] - peak[head])
                total[head] += jnp.sum(by_eight(e), axis=0)
                grown.append(e.astype(LOW))
        out[...] += dot(jnp.concatenate(grown, axis=0), values[pl.ds(at, count)].reshape(count * stack, width), TN)

    over_keys(first, step, mix)
    shares = []
    for head in range(heads):
        sums = jnp.sum(total[head], axis=0, keepdims=True)
        lse[head : head + 1, :] = peak[head] + jnp.log(sums)
        shares.append(jnp.broadcast_to(1.0 / sums, (HEAD, BLOCK)))
    result = out[...] * jnp.concatenate(shares, axis=0).T
    mixed[...] = result
    low_mixed[...] = result.astype(LOW)


def call_fwd(first, q, k, v):
    rows, width = q.shape
    heads = width // HEAD
    blocks = rows // BLOCK
    return pl.pallas_call(
        fwd_kernel,
        grid_spec=pltpu.PrefetchScalarGridSpec(
            num_scalar_prefetch=1,
            grid=(blocks,),
            in_specs=[pl.BlockSpec((BLOCK, width), lambda i, o: (i, 0))] * 3,
            out_specs=[
                pl.BlockSpec((BLOCK, width), lambda i, o: (i, 0)),
                pl.BlockSpec((BLOCK, width), lambda i, o: (i, 0)),
                pl.BlockSpec((heads, BLOCK), lambda i, o: (0, i)),
            ],
            scratch_shapes=[
                pltpu.VMEM((blocks, heads * BLOCK, width), LOW),
                pltpu.VMEM((blocks, heads * BLOCK, width), LOW),
                pltpu.VMEM((blocks, heads * BLOCK, BLOCK), F32),
                pltpu.VMEM((heads, 8, BLOCK), F32),
                pltpu.VMEM((heads, 8, BLOCK), F32),
                pltpu.VMEM((BLOCK, width), F32),
            ],
        ),
        out_shape=[
            jax.ShapeDtypeStruct((rows, width), F32),
            jax.ShapeDtypeStruct((rows, width), LOW),
            jax.ShapeDtypeStruct((heads, rows), F32),
        ],
        compiler_params=params("arbitrary"),
        cost_estimate=SHORT,
        name="attend",
    )(first, q, k, v)


def closed_rows(x, rows, to_norm, vectors, weight):
    n, scale = normed(x.astype(F32))
    d_h = dot(rows, weight, NT)
    bias = jnp.sum(d_h, axis=0, keepdims=True)
    gain = jnp.sum(d_h * n, axis=0, keepdims=True)
    e = d_h * vectors[0:1, :] + to_norm
    e = e - jnp.mean(e, axis=-1, keepdims=True) - n * jnp.mean(e * n, axis=-1, keepdims=True)
    return e * scale, gain, bias


def bwd_kernel(plan, per, groups, extra, first, q, k, v, d_mixed, mixed, lse, turn, to_norm, vectors, normal, weight, *rest):
    many = 1 + max(piece for piece, _ in plan)
    pieces, outs, (even, odd, sums, ones), rest = rest[:many], rest[many : 2 * many], rest[2 * many : 2 * many + 4], rest[2 * many + 4 :]
    keys, values, sum_q, sum_k, sum_v, queries, seeds, h, d_rows, x, mat, wide, sem, x_sems, out_sems = rest
    step = pl.program_id(0)
    blocks = pl.num_programs(0)
    block = blocks - 1 - step
    width = k.shape[1]
    heads = width // HEAD
    stack = heads * BLOCK
    base = first.shape[0] - 1 - len(plan) // per
    group, order = first[base], lambda at: first[base + 1 + at]
    rows_of = lambda at: pl.ds(pl.multiple_of(at * BLOCK, BLOCK), BLOCK)
    own = rows_of(block)
    loads = [
        pltpu.make_async_copy(normal, h, sem.at[0]),
        pltpu.make_async_copy(weight.at[:, :, pl.ds(0, 3 * width)], mat, sem.at[1]),
    ]

    @pl.when(step == 0)
    def _():
        loads[1].start()
        for at, (piece, start) in reversed(list(enumerate(plan))):
            place = order(at // per) * per + at % per
            pltpu.make_async_copy(pieces[piece].at[pl.ds(start, BLOCK)], x.at[rows_of(place)], x_sems.at[place]).start()
        loads[0].start()

        def prepare(at, _):
            here = rows_of(at)
            masked_rows(keys.at[at], k[here, :])
            masked_rows(values.at[at], v[here, :])
            sum_k[here, :] = jnp.zeros((BLOCK, width), F32)
            sum_v[here, :] = jnp.zeros((BLOCK, width), F32)
            return 0

        lax.fori_loop(0, blocks, prepare, 0)
        sums[...] = jnp.zeros_like(sums)
        ones[...] = jnp.zeros_like(ones)

    q_own = q[...]
    s_own = d_mixed[...]
    masked_rows(queries, q_own)
    masked_rows(seeds, s_own)
    q_t = q_own.T
    s_t = s_own.T
    product_t = (s_own.astype(F32) * mixed[...]).T
    delta = [jnp.sum(product_t[head * HEAD : (head + 1) * HEAD, :], axis=0, keepdims=True) for head in range(heads)]
    log_total = [lse[head : head + 1, :] for head in range(heads)]
    sum_q[...] = jnp.zeros_like(sum_q)

    def tiles(at, count):
        key_rows = keys[pl.ds(at, count)].reshape(count * stack, width)
        s = dot(key_rows, q_t)
        d_p = dot(values[pl.ds(at, count)].reshape(count * stack, width), s_t)
        wide_probs, wide_scores, tall_scores = [], [], []
        for tile in range(count):
            low_probs, low_scores = [], []
            for head in range(heads):
                low = tile * stack + head * BLOCK
                probs = jnp.exp(s[low : low + BLOCK] - log_total[head])
                low_scores.append((probs * (d_p[low : low + BLOCK] - delta[head])).astype(LOW))
                low_probs.append(probs.astype(LOW))
            wide_probs.append(jnp.concatenate(low_probs, axis=1))
            wide_scores.append(jnp.concatenate(low_scores, axis=1))
            tall_scores += low_scores
        here = pl.ds(pl.multiple_of(at * BLOCK, BLOCK), count * BLOCK)
        sum_v[here, :] += dot(jnp.concatenate(wide_probs, axis=0), seeds[...])
        sum_k[here, :] += dot(jnp.concatenate(wide_scores, axis=0), queries[...])
        sum_q[...] += dot(jnp.concatenate(tall_scores, axis=0), key_rows, TN)

    over_keys(first, block, tiles)

    @pl.when(step == 0)
    def _():
        loads[1].wait()

    pltpu.make_async_copy(x.at[own], x.at[own], x_sems.at[block]).wait()
    turns = (turn[:, :128], turn[:, 128:])
    done = jnp.concatenate(
        [
            (turned(sum_q[...], *turns, -1.0) * 0.125).astype(LOW),
            turned(sum_k[own, :], *turns, -1.0).astype(LOW),
            sum_v[own, :].astype(LOW),
        ],
        axis=1,
    )
    d_rows[own, :] = done
    sums[0:1, :] += jnp.sum(done.astype(F32), axis=0, keepdims=True)
    n, scale = normed(x[own, :].astype(F32))
    d_h = dot(done, mat[...].reshape(h.shape[1], 3 * width), NT)
    ones[0:1, :] += jnp.sum(d_h * n, axis=0, keepdims=True)
    ones[1:2, :] += jnp.sum(d_h, axis=0, keepdims=True)
    e = d_h * vectors[0:1, :] + to_norm[...].astype(F32)
    e = e - jnp.mean(e, axis=-1, keepdims=True) - n * jnp.mean(e * n, axis=-1, keepdims=True)
    x[own, :] = (e * scale).astype(LOW)
    place = order(block // per) * per + block % per
    for at, (piece, start) in enumerate(plan):

        @pl.when(place == at)
        def _():
            pltpu.make_async_copy(x.at[own], outs[piece].at[pl.ds(start, BLOCK)], out_sems.at[block]).start()

    @pl.when(step == blocks - 1)
    def _():
        loads[0].wait()
        model = h.shape[1]
        grad = dot(h[...], d_rows[...], TN).astype(LOW)
        h[:model, : 3 * width] = grad
        size = model // groups
        for place in range(groups):
            to = odd if place % 2 else even
            to[place // 2, :size, :] = h[pl.ds(pl.multiple_of((group ^ place) * size, size), size), : 3 * width]
        if extra:
            members = len(plan) // per
            wide[...] = jnp.zeros_like(wide)
            for part in range(3):
                for at in range(width // 128):
                    row = (part * members + order(0)) * (width // 128) + at
                    low = part * width + at * 128
                    wide[pl.ds(row, 1), :] = sums[0:1, low : low + 128]
            for place in range(groups):
                to, near = odd if place % 2 else even, group ^ place
                lanes = pl.ds(pl.multiple_of(near * 128, 128), 128)
                lines = [ones[0:1, lanes], ones[1:2, lanes]] + [wide[pl.ds(3 * near + row, 1), :] for row in range(3)]
                to[place // 2, size:, :] = jnp.zeros((EXTRA, 3 * width), LOW)
                to[place // 2, size:, :128] = extra_rows(lines)
        for at in range(len(plan)):
            here = pl.ds(at * BLOCK, BLOCK)
            pltpu.make_async_copy(x.at[here], x.at[here], out_sems.at[at]).wait()


def call_bwd(first, q, k, v, d_mixed, mixed, lse, tables, to_norm, vectors, normal, weight, pieces, out_shapes, groups, span, extra):
    rows, width = q.shape
    heads = width // HEAD
    blocks = rows // BLOCK
    model = normal.shape[1]
    grad = (groups // 2, model // groups + EXTRA * extra, 3 * width)
    back = lambda i, o: (blocks - 1 - i, 0)
    blocked = pl.BlockSpec((BLOCK, width), back)
    once = lambda shape: pl.BlockSpec(shape, lambda *_: (0,) * len(shape), pipeline_mode=pl.Buffered(1))
    plan = tuple((p, start) for block in plan_of(pieces, BLOCK) for p, start, _, _ in block)
    outs = [(grad, LOW), (grad, LOW), ((8, 3 * width), F32), ((8, model), F32)]
    return pl.pallas_call(
        functools.partial(bwd_kernel, plan, span // BLOCK, groups, extra),
        grid_spec=pltpu.PrefetchScalarGridSpec(
            num_scalar_prefetch=1,
            grid=(blocks,),
            in_specs=[blocked, once((rows, width)), once((rows, width)), blocked, blocked]
            + [pl.BlockSpec((heads, BLOCK), lambda i, o: (0, blocks - 1 - i)), pl.BlockSpec((BLOCK, 256), back)]
            + [pl.BlockSpec((BLOCK, model), back), whole(vectors.shape), HBM, HBM]
            + [HBM] * len(pieces),
            out_specs=[HBM] * len(out_shapes) + [whole(a) for a, _ in outs],
            scratch_shapes=[
                pltpu.VMEM((blocks, heads * BLOCK, width), LOW),
                pltpu.VMEM((blocks, heads * BLOCK, width), LOW),
                pltpu.VMEM((BLOCK, width), F32),
                pltpu.VMEM((rows, width), F32),
                pltpu.VMEM((rows, width), F32),
                pltpu.VMEM((heads * BLOCK, width), LOW),
                pltpu.VMEM((heads * BLOCK, width), LOW),
                pltpu.VMEM((rows, model), LOW),
                pltpu.VMEM((rows, 3 * width), LOW),
                pltpu.VMEM((rows, model), LOW),
                pltpu.VMEM(weight.shape[:2] + (3 * width,), LOW),
                pltpu.VMEM((3 * groups, 128), F32),
                pltpu.SemaphoreType.DMA((2,)),
                pltpu.SemaphoreType.DMA((blocks,)),
                pltpu.SemaphoreType.DMA((blocks,)),
            ],
        ),
        out_shape=list(out_shapes) + [jax.ShapeDtypeStruct(a, kind) for a, kind in outs],
        compiler_params=params("arbitrary"),
        cost_estimate=SHORT,
        name="attend_back",
    )(first, q, k, v, d_mixed, mixed, lse, tables, to_norm, vectors, normal, weight, *pieces)


def extra_rows(lines):
    return jnp.concatenate(lines + [jnp.zeros((EXTRA - len(lines), 128), F32)], axis=0).astype(LOW)


def mlp_kernel(plan, out_plan, count, out_count, joined, chunk, order, *refs):
    x_pieces, cot_pieces, rest = refs[:count], refs[count : 2 * count], refs[2 * count :]
    mixed, vectors, rest = rest[0], rest[1], rest[2:]
    mats, rest = rest[: 1 if joined else 3], rest[1 if joined else 3 :]
    parts, rest = rest[:out_count], rest[out_count:]
    d_mixed, to_norm, rest = rest[0], rest[1], rest[2:]
    grads, rest = rest[: 1 if joined else 3], rest[1 if joined else 3 :]
    sums, normal, cot, active, d_up, own_mixed, g_out, staged, x_sems, cot_sems, out_sems = rest
    step = pl.program_id(0)
    steps = len(plan)
    span, width = own_mixed.shape[0] // steps, own_mixed.shape[1]
    model, units = normal.shape[1], active.shape[1]
    if joined:
        groups = mats[0].shape[0]
        cuts = [0, model // groups, (model + units) // groups, (model + units + width) // groups]
        w_up, w_down, w_out = (mats[0].at[:, pl.ds(cuts[i], cuts[i + 1] - cuts[i]), :] for i in range(3))
    else:
        w_up, w_down, w_out = mats
    as_up = lambda: w_up[...].reshape(model, units)
    as_down = lambda: w_down[...].reshape(units, model)
    as_out = lambda: w_out[...].reshape(width, model)

    @pl.when(step == 0)
    def _():
        fetch_all(plan, x_pieces, normal, x_sems)
        fetch_all(plan, cot_pieces, cot, cot_sems)
        sums[...] = jnp.zeros_like(sums)

    fetch(plan, step, x_pieces, normal, x_sems, False)
    fetch(plan, step, cot_pieces, cot, cot_sems, False)

    @pl.when(step < steps)
    def _():
        here = pl.ds(pl.multiple_of(step * span, span), span)
        n, _ = normed(normal[here, :].astype(F32))
        h = (n * vectors[2:3, :] + vectors[3:4, :]).astype(LOW)
        normal[here, :] = h
        dy = cot[here, :]
        own = mixed[pl.ds(pl.multiple_of(order[step] * span, span), span), :]
        own_mixed[here, :] = own
        d_mixed[...] = dot(dy, as_out(), NT).astype(LOW)
        up, down = as_up(), as_down()
        for low in range(0, units, chunk):
            cols = slice(low, low + chunk)
            u = dot(h, up[:, cols]) + vectors[6:7, cols]
            d_active = dot(dy, down[cols], NT)
            cdf = 0.5 * (1.0 + lax.erf(u * np.float32(np.sqrt(0.5))))
            slope = cdf + u * (jnp.exp(-0.5 * u * u) * np.float32(1.0 / np.sqrt(2.0 * np.pi)))
            active[here, cols] = (u * cdf).astype(LOW)
            back = (d_active * slope).astype(LOW)
            d_up[here, cols] = back
            sums[0:1, cols] += jnp.sum(back.astype(F32), axis=0, keepdims=True)
        staged[here, :] = (dot(active[here, :], down) + dot(own, as_out())).astype(LOW)
        d_h = dot(d_up[here, :], up, NT)
        sums[1:2, :model] += jnp.sum(d_h, axis=0, keepdims=True)
        sums[2:3, :model] += jnp.sum(d_h * n, axis=0, keepdims=True)
        to_norm[...] = (d_h * vectors[2:3, :]).astype(LOW)

        @pl.when(step == 0)
        def _():
            sums[3:4, :model] = jnp.sum(dy.astype(F32), axis=0, keepdims=True)

    store(out_plan, step, staged, parts, out_sems, True)

    @pl.when(step >= steps)
    def _():
        at = step - steps
        many = pl.num_programs(0) - steps

        @pl.when(at == 0)
        def _():
            g_out[...] = dot(own_mixed[...], cot[...], TN).astype(LOW)

        up_cols = pl.ds(pl.multiple_of(at * (model // many), 128), model // many)
        down_cols = pl.ds(pl.multiple_of(at * (units // many), 128), units // many)
        out_rows = pl.ds(pl.multiple_of(at * (width // many), 16), width // many)
        up_grad = dot(normal[:, up_cols], d_up[...], TN).astype(LOW)
        down_grad = dot(active[:, down_cols], cot[...], TN).astype(LOW)
        if joined:
            block = grads[0].shape[0]
            grads[0][:, cuts[0] : cuts[1], :] = up_grad.reshape(block, cuts[1], units)
            grads[0][:, cuts[1] : cuts[2], :] = down_grad.reshape(block, cuts[2] - cuts[1], model)
            grads[0][:, cuts[2] : cuts[3], :] = g_out[out_rows, :].reshape(block, cuts[3] - cuts[2], model)
            grads[0][:, cuts[3] :, :] = jnp.zeros((block, EXTRA, model), LOW)
            for place in range(block):
                lanes = pl.ds(pl.multiple_of((at * block + place) * 128, 128), 128)
                lines = [sums[row : row + 1, lanes] for row in (2, 1, 3, 0)]
                grads[0][place, cuts[3] :, :128] = extra_rows(lines)
        else:
            grads[0][...] = up_grad
            grads[1][...] = down_grad
            grads[2][...] = g_out[out_rows, :]

    @pl.when(step == pl.num_programs(0) - 1)
    def _():
        for at in range(steps):
            store(out_plan, at, staged, parts, out_sems, False)


def call_mlp(order, x_pieces, cot_pieces, mixed, vectors, mats, span, units, out_shapes):
    rows, width = mixed.shape
    model = x_pieces[0].shape[1]
    joined = len(mats) == 1
    plan, out_plan = plan_of(x_pieces, span), plan_of(out_shapes, span)
    steps, many = len(plan), 4
    count = len(x_pieces)
    there = lambda i, o: (o[jnp.minimum(i, steps - 1)], 0)
    later = lambda i, o: (jnp.maximum(i - steps, 0), 0)
    if joined:
        groups = mats[0].shape[0]
        grads = [(groups, (model + units + width) // groups + EXTRA, model)]
        grad_specs = [pl.BlockSpec((groups // many,) + grads[0][1:], lambda i, o: (jnp.maximum(i - steps, 0), 0, 0))]
    else:
        grads = [(model, units), (units, model), (width, model)]
        grad_specs = [pl.BlockSpec((a // many, b), later) for a, b in grads]
    sums = (8, max(model, units))
    return pl.pallas_call(
        functools.partial(mlp_kernel, plan, out_plan, count, len(out_shapes), joined, 256),
        grid_spec=pltpu.PrefetchScalarGridSpec(
            num_scalar_prefetch=1,
            grid=(steps + many,),
            in_specs=[HBM] * (2 * count)
            + [whole((rows, width)), whole(vectors.shape)]
            + [pl.BlockSpec(m.shape, lambda *_: (0, 0, 0), pipeline_mode=pl.Buffered(1)) for m in mats],
            out_specs=[HBM] * len(out_shapes)
            + [pl.BlockSpec((span, width), there), pl.BlockSpec((span, model), there)]
            + grad_specs
            + [whole(sums)],
            scratch_shapes=[
                pltpu.VMEM((rows, model), LOW),
                pltpu.VMEM((rows, model), LOW),
                pltpu.VMEM((rows, units), LOW),
                pltpu.VMEM((rows, units), LOW),
                pltpu.VMEM((rows, width), LOW),
                pltpu.VMEM((width, model), LOW),
                pltpu.VMEM((rows, model), LOW),
                pltpu.SemaphoreType.DMA((steps, 2)),
                pltpu.SemaphoreType.DMA((steps, 2)),
                pltpu.SemaphoreType.DMA((steps, 2)),
            ],
        ),
        out_shape=list(out_shapes)
        + [jax.ShapeDtypeStruct((rows, width), LOW), jax.ShapeDtypeStruct((rows, model), LOW)]
        + [jax.ShapeDtypeStruct(g, LOW) for g in grads]
        + [jax.ShapeDtypeStruct(sums, F32)],
        compiler_params=params("arbitrary"),
        cost_estimate=SHORT,
        name="mlp",
    )(order, *x_pieces, *cot_pieces, mixed, vectors, *mats)


def finish_kernel(shifts, wholes, base, *refs):
    refs, out = refs[:-1], refs[-1]
    shift, refs = refs[:shifts], refs[shifts:]
    common, parts = refs[:wholes], refs[wholes:]
    total = base[...].astype(F32)
    for ref in shift:
        total = total + ref[4:5, :] + ref[5:6, :]
    for ref in common:
        total = total + ref[...].astype(F32)
    if not parts:
        out[...] = total.astype(LOW)
    for at in range(2 if parts else 0):

        @pl.when(pl.program_id(0) == at)
        def _():
            more = total
            for ref in parts[at::2]:
                more = more + ref[...].astype(F32)
            out[...] = more.astype(LOW)


def call_finish(base, common, parts, vectors=(), cost=SHORT):
    rows, model = base.shape
    block = pl.BlockSpec((rows // 2, model), lambda i: (i, 0))
    return pl.pallas_call(
        functools.partial(finish_kernel, len(vectors), len(common)),
        grid=(2,),
        in_specs=[block] + [whole(v.shape) for v in vectors] + [block] * len(common) + [whole((rows // 2, model))] * len(parts),
        out_specs=block,
        out_shape=jax.ShapeDtypeStruct((rows, model), LOW),
        compiler_params=params("arbitrary"),
        cost_estimate=cost,
        name="finish",
    )(base, *vectors, *common, *parts)


def cut_kernel(members, member, first, second, third, *out):
    pieces, (down, line) = out[:members], out[members:]
    columns = first.shape[1]
    shard = pieces[0].shape[0] - EXTRA
    low = members * shard
    for bit, piece in enumerate(pieces):
        rows = pl.ds(pl.multiple_of((member[0] ^ bit) * shard, shard), shard)
        piece[:shard, :columns] = first[rows, :]
        piece[:shard, columns:] = (second[rows, :].astype(F32) + third[rows, :].astype(F32)).astype(LOW)
        piece[shard:, :columns] = first[first.shape[0] - EXTRA :, :]
        piece[shard:, columns:] = (second[low:, :].astype(F32) + third[low:, :].astype(F32)).astype(LOW)
    down[...] = first[low : low + down.shape[0], :].astype(F32)
    line[...] = first[first.shape[0] - EXTRA :, :128].astype(F32)[3:4, :]


def call_cut(member, first, second, third, members, shard):
    columns = first.shape[1]
    shapes = [jax.ShapeDtypeStruct((shard + EXTRA, columns + second.shape[1]), LOW)] * members + [
        jax.ShapeDtypeStruct((first.shape[0] - (members + 1) * shard - EXTRA, columns), F32),
        jax.ShapeDtypeStruct((1, 128), F32),
    ]
    return pl.pallas_call(
        functools.partial(cut_kernel, members),
        grid_spec=pltpu.PrefetchScalarGridSpec(
            num_scalar_prefetch=1,
            grid=(1,),
            in_specs=[whole(first.shape), whole(second.shape), whole(third.shape)],
            out_specs=[whole(a.shape) for a in shapes],
        ),
        out_shape=shapes,
        compiler_params=params("arbitrary"),
        cost_estimate=SHORT,
        name="cut",
    )(member, first, second, third)


def join_kernel(places, second, member, *refs):
    pieces, outs, total = refs[:-3], refs[-3:-1], refs[-1]
    shard = outs[0].shape[0]
    for bit, piece in enumerate(pieces):
        for block, (index, column, stride) in enumerate(places):
            start = pl.multiple_of(column + (member[0] ^ bit) * stride, 128)
            outs[index][:, pl.ds(start, 128)] = piece[:shard, block * 128 : (block + 1) * 128].astype(F32)
    for row, low in ((0, 0), (8, second)):
        total[row : row + 8, :] = sum(piece[shard:, low : low + 128].astype(F32) for piece in pieces)[:8, :]


def call_join(member, pieces, places, second, columns):
    shard = pieces[0].shape[0] - EXTRA
    shapes = [(shard, c) for c in columns] + [(16, 128)]
    return pl.pallas_call(
        functools.partial(join_kernel, tuple(places), second),
        grid_spec=pltpu.PrefetchScalarGridSpec(
            num_scalar_prefetch=1,
            grid=(1,),
            in_specs=[whole(p.shape) for p in pieces],
            out_specs=[whole(a) for a in shapes],
        ),
        out_shape=[jax.ShapeDtypeStruct(a, F32) for a in shapes],
        compiler_params=params("arbitrary"),
        cost_estimate=SHORT,
        name="join",
    )(member, *pieces)


def across(array, bit):
    size = lax.axis_size("fsdp")
    return lax.ppermute(array, "fsdp", [(i, i ^ bit) for i in range(size)])


def exchange(pieces):
    size = lax.axis_size("fsdp")
    if size != 4:
        return lax.all_to_all(pieces, "fsdp", split_axis=0, concat_axis=0, tiled=True)
    member = lax.axis_index("fsdp")
    out = pieces
    for bit in range(1, size):
        mine = lax.dynamic_index_in_dim(pieces, member ^ bit, 0, keepdims=False)
        out = lax.dynamic_update_index_in_dim(out, across(mine, bit), member ^ bit, 0)
    return out


def behind(array, *others):
    return lax.optimization_barrier((array, *others))[0]


def behind_all(arrays, *others):
    return tuple(behind(array, *others) for array in arrays)


def gather_rows(halves, near=None, *others):
    if lax.axis_size("fsdp") != 4:
        return [lax.all_gather(jnp.concatenate(halves, axis=0), "fsdp", axis=0, tiled=True)]
    one_low, two_high, one_high, two_low = near
    return [
        *halves, one_low, one_high, two_low, two_high,
        across(behind(one_low, *others), 2), across(behind(two_high, *others), 1),
    ]


def near_rows(halves):
    low, high = halves
    return across(low, 1), across(high, 2), across(high, 1), across(low, 2)


def hop(array, bit):
    return lax.ppermute(array, "dp", [(i, i ^ bit) for i in range(lax.axis_size("dp"))])


def scatter_step(blocks, far, bit):
    blocks = (blocks.astype(F32) + far.astype(F32)).astype(LOW)
    send = blocks[1::2]
    return blocks[0::2], hop(send, bit), send


def reduce_direct(parts):
    if len(parts) == 1:
        return (lax.psum_scatter(parts[0], "fsdp", scatter_dimension=0, tiled=True),)
    three = across(parts[3], 3)
    return parts[0], across(parts[1], 1), across(parts[2], 2), three


def total_over_all(vector):
    count = lax.axis_size("dp") * lax.axis_size("fsdp")
    step = 1
    while step < count:
        vector = vector + lax.ppermute(vector, ALL, [(i, i ^ step) for i in range(count)])
        step *= 2
    return vector


def swap_owner(array, back):
    groups, members = lax.axis_size("dp"), lax.axis_size("fsdp")
    pairs = [(m * groups + g, g * members + m) for g in range(groups) for m in range(members)]
    if back:
        pairs = [(b, a) for a, b in pairs]
    return lax.ppermute(array, ALL, pairs)


def gather_dp(array):
    return lax.all_gather(array, "dp", axis=0)


def scatter_dp(array):
    return lax.psum_scatter(array, "dp", scatter_dimension=0, tiled=True)


def rotary_tables(length):
    half = ROT // 2
    frequency = (np.float32(10000.0) ** (-(np.arange(half, dtype=np.float32) * np.float32(2.0)) / np.float32(ROT))).astype(np.float32)
    angles = (np.arange(length, dtype=np.float32)[:, None] * frequency[None, :]).astype(np.float32)
    cosine = np.cos(angles).astype(np.float32)
    sine = np.sin(angles).astype(np.float32)
    cos_row = np.ones((length, 128), np.float32)
    sine_row = np.zeros((length, 128), np.float32)
    for start in range(0, 128, HEAD):
        cos_row[:, start : start + half] = cosine
        cos_row[:, start + half : start + ROT] = cosine
        sine_row[:, start : start + half] = -sine
        sine_row[:, start + half : start + ROT] = sine
    return jnp.asarray(np.concatenate([cos_row, sine_row], axis=1))


def local(
    tokens, cotangent, doc_ids, norm1_gain, norm1_bias, norm2_gain, norm2_bias, qkv_weight, qkv_bias,
    out_weight, out_bias, up_weight, up_bias, down_weight, down_bias,
):
    groups, members = lax.axis_size("dp"), lax.axis_size("fsdp")
    group, member = lax.axis_index("dp"), lax.axis_index("fsdp")
    devices = groups * members
    rows, model = tokens.shape
    stream = rows * members
    shard = qkv_weight.shape[0]
    width = model // members
    units_dev = up_bias.shape[0]
    units = groups * units_dev
    paired = members == 4 and units_dev == 128 and units == model
    me = member.astype(jnp.int32).reshape(1)
    vectors_in = [norm1_gain, norm1_bias, norm2_gain, norm2_bias, out_bias, down_bias]

    half = rows // 2
    x_halves = [tokens[:half], tokens[half:]]
    cot_halves = [cotangent[:half], cotangent[half:]]
    if paired:
        out_own = swap_owner(out_weight, False)
        small = small_block(member, members, vectors_in, qkv_bias, up_bias)
        packed = call_pack(me, qkv_weight, up_weight, small, members)
        arrived = [packed[0]] + [across(packed[bit], bit) for bit in range(1, members)]
        x_near = near_rows(behind_all(x_halves, *arrived[1:]))
        cut = 3 * width + 128
        first_in, up_in = call_place(me, behind_all(arrived, out_own), cut)
        w_first = gather_dp(first_in)
        mats = (gather_dp(jnp.concatenate([up_in, down_weight, out_own], axis=0)),)
        vectors = call_vectors(me, w_first, members, cut)
    else:
        qkv_cut = qkv_weight.reshape(shard, 3, members, width).transpose(2, 0, 1, 3).reshape(members, shard, 3 * width)
        up_cut = up_weight.reshape(shard, groups, members, units_dev).transpose(2, 0, 1, 3).reshape(members, shard, units)
        arrived = exchange(jnp.concatenate([qkv_cut, up_cut], axis=2)).reshape(members * shard, -1)
        w_first = gather_dp(arrived[:, : 3 * width])
        x_near = near_rows(x_halves) if members == 4 else None
        mats = (gather_dp(arrived[:, 3 * width :]), gather_dp(down_weight), gather_dp(swap_owner(out_weight, False)))
        full = [lax.all_gather(a, ALL, axis=0, tiled=True).astype(F32) for a in vectors_in]
        shift = lax.all_gather(qkv_bias, ALL, axis=0, tiled=True).astype(F32).reshape(3, members, width)
        shift = lax.dynamic_index_in_dim(shift, member, 1, keepdims=False)
        up_all = lax.all_gather(up_bias, "dp", axis=0, tiled=True).astype(F32)
        lines = full + [jnp.pad(a, (0, model - a.shape[0])) for a in (up_all, shift[0], shift[1], shift[2])]
        vectors = jnp.pad(jnp.stack(lines), ((0, 6), (0, 0)))

    x_pieces = gather_rows(x_halves, x_near)
    sources = jnp.arange(members, dtype=jnp.int32)
    order = sources ^ member if members == 4 else sources
    doc_row = doc_ids[0]
    first = jnp.sum((doc_row[None, :] < doc_row[:, None]).astype(jnp.int32), axis=1)
    first = jnp.concatenate([first, group.astype(jnp.int32).reshape(1), order])
    tables = rotary_tables(stream)

    q, k, v, normal = call_qkv(order, x_pieces, vectors, w_first, tables, rows, width)
    cot_near = near_rows(behind_all(cot_halves, *x_pieces[2:])) if members == 4 else None
    cot_pieces = gather_rows(cot_halves, cot_near, q)
    mixed, low_mixed, lse = call_fwd(first, q, k, v)
    out_sizes = [rows] * members if members == 4 else [stream]
    out_shapes = [jax.ShapeDtypeStruct((size, model), LOW) for size in out_sizes]
    results = call_mlp(
        order, x_pieces, cot_pieces, low_mixed, vectors, mats, rows, units, out_shapes
    )
    count = len(out_shapes)
    parts, (d_mixed, to_norm), grads, sums_two = results[:count], results[count : count + 2], results[count + 2 : -1], results[-1]
    scattered = scatter_dp(grads[0].reshape(-1, model)) if paired else None

    summed = reduce_direct(parts)
    sizes = [half] * (2 * members) if members == 4 else [stream]
    *pieces, even, odd, sums_qkv, ones = call_bwd(
        first, q, k, v, d_mixed, mixed, lse, tables, to_norm, vectors, normal, w_first, x_pieces,
        [jax.ShapeDtypeStruct((size, model), LOW) for size in sizes], groups, rows, paired,
    )
    far, bit = hop(odd, 1), 2
    if members == 4:
        add = lambda a, b: (a.astype(F32) + b.astype(F32)).astype(LOW)
        own_low, own_high, one_low, one_high, two_low, two_high, three_low, three_high = pieces
        come = across(three_high, 2), across(three_low, 1)
        near = across(one_low, 1), across(two_high, 2)
        output = call_finish(tokens, summed, (), (vectors,), LONG)
        blocks, far, send = scatter_step(even, behind(far, output), bit)
        come = behind_all(come, send)
        one_high, two_low = add(one_high, come[0]), add(two_low, come[1])
        near += across(one_high, 1), across(two_low, 2)
        parts = own_low, own_high, near[0], near[2], near[3], near[1]
        blocks, far, send = scatter_step(blocks, behind(far, one_high, two_low), 2 * bit)
        bit = 8
    if members != 4:
        blocks, far, _ = scatter_step(even, far, bit)
        bit = 4
        output = call_finish(tokens, summed, (), (vectors,))
        total = reduce_direct(pieces)[0]
        parts = total[:half], total[half:]
    while blocks.shape[0] > 1:
        (blocks, far, _), bit = scatter_step(blocks, far, bit), 2 * bit
    g_qkv = blocks[0], far[0]
    place = group * members + member
    if paired:
        *mixed_pieces, g_down, up_shift = call_cut(me, scattered, *g_qkv, members, shard)
        g_out = scattered[scattered.shape[0] - shard - EXTRA : scattered.shape[0] - EXTRA]
        g_out = swap_owner(behind(g_out, g_down), True)
        grad_tokens = call_finish(behind(cotangent, g_down), (), parts)
        places = [(0, b * members * units_dev, units_dev) for b in range(groups)]
        places += [(1, part * model + low, width) for part in range(3) for low in range(0, width, 128)]
        arrived = [mixed_pieces[0]] + [across(mixed_pieces[bit], bit) for bit in range(1, members)]
        g_up, g_qkv, totals = call_join(me, arrived, places, model, (up_weight.shape[1], qkv_weight.shape[1]))
        size = model // devices
        lines = lax.dynamic_slice_in_dim(totals, member * size, size, 1)
        mine = [lines[row] for row in (8, 9, 0, 1, 2)]
        mine += [lax.dynamic_slice_in_dim(totals[10:13].reshape(-1), member * 3 * size, 3 * size), up_shift[0]]
    else:
        grad_tokens = call_finish(cotangent, (), parts)
        g_up, g_down, g_out = [scatter_dp(g) for g in grads]
        g_down = g_down.astype(F32)
        g_up = exchange(g_up.reshape(members, shard, units))
        g_up = g_up.reshape(members, shard, groups, units_dev).transpose(1, 2, 0, 3).reshape(shard, -1).astype(F32)
        g_qkv = (g_qkv[0].astype(F32) + g_qkv[1].astype(F32)).astype(LOW)
        g_qkv = exchange(g_qkv.reshape(members, shard, 3 * width)).reshape(members, shard, 1, 3, width)
        g_qkv = g_qkv.transpose(1, 3, 0, 2, 4).reshape(shard, -1).astype(F32)
        thirds = jnp.concatenate([a[0].reshape(3, 1, width) for a in [sums_qkv]], axis=2)
        wide_qkv = lax.dynamic_update_index_in_dim(jnp.zeros((3, members, width), F32), thirds, member, 1)
        wide_up = lax.dynamic_update_index_in_dim(
            jnp.zeros((groups, members, units_dev), F32), sums_two[0, :units].reshape(groups, 1, units_dev), member, 1
        )
        summed = total_over_all(jnp.concatenate([
            ones[0], ones[1], sums_two[2], sums_two[1], sums_two[3], wide_qkv.reshape(-1), wide_up.reshape(-1),
        ]))
        mine, start = [], 0
        for size in [model] * 5 + [3 * model, groups * members * units_dev]:
            mine.append(lax.dynamic_slice_in_dim(summed, start + place * (size // devices), size // devices))
            start += size
    gain_1, bias_1, gain_2, bias_2, end_bias, qkv_shift, up_shift = mine
    g_out = (g_out if paired else swap_owner(g_out, True)).astype(F32)
    return (
        output, grad_tokens, gain_1, bias_1, gain_2, bias_2, g_qkv, qkv_shift, g_out, end_bias, g_up, up_shift, g_down, end_bias,
    )


def solution(mesh):
    row, vec = P(ALL, None), P(ALL)
    return jax.shard_map(
        local,
        mesh=mesh,
        in_specs=(row, row, P("dp", None), vec, vec, vec, vec, row, vec, row, vec, row, vec, row, vec),
        out_specs=(row, row, vec, vec, vec, vec, row, vec, row, vec, row, vec, row, vec),
        check_vma=False,
    )
```

```python
import functools

import jax
import jax.numpy as jnp
import numpy as np
from jax import lax
from jax.experimental import pallas as pl
from jax.experimental.pallas import tpu as pltpu
from jax.sharding import PartitionSpec as P

HEADS = 16
HEAD = 64
ROT = 16
BLOCK = 256
EPS = 1e-05
ALL = ("dp", "fsdp")
LONG = pl.CostEstimate(flops=2 * 10**10, bytes_accessed=10**7, transcendentals=0)
SHORT = pl.CostEstimate(flops=0, bytes_accessed=0, transcendentals=0)
F32 = jnp.float32
LOW = jnp.bfloat16


def dot(left, right, contract=((1,), (0,))):
    return lax.dot_general(left, right, (contract, ((), ())), preferred_element_type=F32)


NT = ((1,), (1,))
TN = ((0,), (0,))


def normed(x_rows):
    centre = x_rows - jnp.mean(x_rows, axis=-1, keepdims=True)
    spread = jnp.mean(centre * centre, axis=-1, keepdims=True)
    scale = lax.rsqrt(spread + EPS)
    return centre * scale, scale


def turned(z, cosine, sine, sign):
    groups = []
    for start in range(0, z.shape[1], 128):
        part = z[:, start : start + 128]
        ahead = pltpu.roll(part, 128 - ROT // 2, 1)
        behind = pltpu.roll(part, ROT // 2, 1)
        lane = lax.broadcasted_iota(jnp.int32, part.shape, 1) & (HEAD - 1)
        groups.append(part * cosine + sign * (jnp.where(lane < ROT // 2, ahead, behind) * sine))
    return groups[0] if len(groups) == 1 else jnp.concatenate(groups, axis=1)


def head_only(array, head):
    lane = lax.broadcasted_iota(jnp.int32, array.shape, 1)
    keep = (lane >= head * HEAD) & (lane < (head + 1) * HEAD)
    return jnp.where(keep, array, jnp.zeros_like(array))


def params(*order):
    return pltpu.CompilerParams(vmem_limit_bytes=60 * 1024 * 1024, dimension_semantics=order)


def whole(shape):
    return pl.BlockSpec(shape, lambda *_: (0,) * len(shape))


HBM = pl.BlockSpec(memory_space=pl.ANY)
EXTRA = 16


def fetch(plan, step, refs, target, sems, begin):
    for at, pieces in enumerate(plan):

        @pl.when(step == at)
        def _():
            for index, (ref, start, put, size) in enumerate(pieces):
                copy = pltpu.make_async_copy(
                    refs[ref].at[pl.ds(start, size)], target.at[pl.ds(put, size)], sems.at[at, index]
                )
                if begin:
                    copy.start()
                else:
                    copy.wait()


def fetch_all(plan, refs, target, sems):
    for at in range(len(plan)):
        fetch(plan, at, refs, target, sems, True)


def plan_of(pieces, span):
    plan, total = [], sum(p.shape[0] for p in pieces)
    for low in range(0, total, span):
        taken, at = [], 0
        for index, piece in enumerate(pieces):
            a, b = max(low, at), min(low + span, at + piece.shape[0])
            if a < b:
                taken.append((index, a - at, a, b - a))
            at += piece.shape[0]
        plan.append(tuple(taken))
    return tuple(plan)


def store(plan, step, source, refs, sems, begin):
    for at, pieces in enumerate(plan):

        @pl.when(step == at)
        def _():
            for index, (ref, start, put, size) in enumerate(pieces):
                copy = pltpu.make_async_copy(
                    source.at[pl.ds(put, size)], refs[ref].at[pl.ds(start, size)], sems.at[at, index]
                )
                if begin:
                    copy.start()
                else:
                    copy.wait()


def pack_kernel(members, member, qkv, up, small, *out):
    width = qkv.shape[1] // 3 // members
    units_dev = 128
    groups = up.shape[1] // units_dev // members
    for bit in range(members):
        to = member[0] ^ bit
        for part in range(3):
            start = pl.multiple_of((part * members + to) * width, 128)
            out[bit][:, part * width : (part + 1) * width] = qkv[:, pl.ds(start, width)]
        out[bit][:, 3 * width : 3 * width + 128] = jnp.zeros((qkv.shape[0], 128), LOW)
        out[bit][0 : small.shape[0], 3 * width : 3 * width + 128] = small[...]
        for group in range(groups):
            start = pl.multiple_of((group * members + to) * units_dev, 128)
            low = 3 * width + 128 + group * units_dev
            out[bit][:, low : low + units_dev] = up[:, pl.ds(start, units_dev)]


def call_pack(member, qkv, up, small, members):
    shard = qkv.shape[0]
    columns = (qkv.shape[1] + up.shape[1]) // members + 128
    return pl.pallas_call(
        functools.partial(pack_kernel, members),
        grid_spec=pltpu.PrefetchScalarGridSpec(
            num_scalar_prefetch=1,
            grid=(1,),
            in_specs=[whole(qkv.shape), whole(up.shape), whole(small.shape)],
            out_specs=[whole((shard, columns))] * members,
        ),
        out_shape=[jax.ShapeDtypeStruct((shard, columns), LOW)] * members,
        compiler_params=params("arbitrary"),
        cost_estimate=SHORT,
        name="pack",
    )(member, qkv, up, small)


def place_kernel(cut, member, *refs):
    *pieces, first, second = refs
    shard = pieces[0].shape[0]
    for bit, piece in enumerate(pieces):
        rows = pl.ds(pl.multiple_of((member[0] ^ bit) * shard, shard), shard)
        first[rows, :] = piece[:, :cut]
        second[rows, :] = piece[:, cut:]


def call_place(member, pieces, cut):
    members, (shard, columns) = len(pieces), pieces[0].shape
    shapes = [(members * shard, cut), (members * shard, columns - cut)]
    return pl.pallas_call(
        functools.partial(place_kernel, cut),
        grid_spec=pltpu.PrefetchScalarGridSpec(
            num_scalar_prefetch=1,
            grid=(1,),
            in_specs=[whole(p.shape) for p in pieces],
            out_specs=[whole(a) for a in shapes],
        ),
        out_shape=[jax.ShapeDtypeStruct(a, LOW) for a in shapes],
        compiler_params=params("arbitrary"),
        cost_estimate=SHORT,
        name="place",
    )(member, *pieces)


def small_block(member, members, vectors, qkv_bias, up_bias):
    size = vectors[0].shape[0]
    wide = 128 // members * (members - 1)
    rows = jnp.pad(jnp.stack(vectors), ((0, 0), (wide, wide)))
    rows = lax.dynamic_slice_in_dim(rows, wide - member * size, 128, 1)
    wide = 3 * wide
    shift = lax.dynamic_slice_in_dim(jnp.pad(qkv_bias, (wide, wide)), wide - member * 3 * size, 384, 0)
    return jnp.concatenate([rows, shift.reshape(3, 128), up_bias[None], jnp.zeros((16 - len(vectors) - 4, 128), LOW)], axis=0)


def vectors_kernel(members, member, gathered, out, wide):
    groups, rows, _ = gathered.shape
    shard = rows // members
    model = groups * 128
    out[...] = jnp.zeros_like(out)
    for group in range(groups):
        blocks = [gathered[group, m * shard : m * shard + 16, :].astype(F32) for m in range(members)]
        block = blocks[0]
        for other in blocks[1:]:
            block = block + other
        lanes = slice(group * 128, (group + 1) * 128)
        for row in range(6):
            out[row : row + 1, lanes] = block[row : row + 1, :]
        for row in range(3):
            low = group * 384 + row * 128
            wide[0:1, low : low + 128] = block[6 + row : 7 + row, :]
        own = jnp.zeros((1, 128), F32)
        for m in range(members):
            own = own + jnp.where(member[0] == m, blocks[m][9:10, :], 0.0)
        out[6:7, lanes] = own
    width = model // members
    for part in range(3):
        start = pl.multiple_of(part * model + member[0] * width, 128)
        out[7 + part : 8 + part, :width] = wide[0:1, pl.ds(start, width)]


def call_vectors(member, gathered, members, cut):
    groups, rows, _ = gathered.shape
    model = groups * 128
    return pl.pallas_call(
        functools.partial(vectors_kernel, members),
        grid_spec=pltpu.PrefetchScalarGridSpec(
            num_scalar_prefetch=1,
            grid=(1,),
            in_specs=[pl.BlockSpec((groups, rows, 128), lambda i, o: (0, 0, cut // 128 - 1))],
            out_specs=whole((16, model)),
            scratch_shapes=[pltpu.VMEM((8, 3 * model), F32)],
        ),
        out_shape=jax.ShapeDtypeStruct((16, model), F32),
        compiler_params=params("arbitrary"),
        cost_estimate=SHORT,
        name="vectors",
    )(member, gathered)


def qkv_kernel(plan, count, order, *refs):
    pieces, rest = refs[:count], refs[count:]
    vectors, weight, turn, q, k, v, x, sems = rest
    step = pl.program_id(0)
    width = q.shape[1]
    span = q.shape[0]
    model = x.shape[1]

    @pl.when(step == 0)
    def _():
        fetch_all(plan, pieces, x, sems)

    fetch(plan, step, pieces, x, sems, False)
    n, _ = normed(x[pl.ds(pl.multiple_of(step * span, span), span), :].astype(F32))
    h = (n * vectors[0:1, :] + vectors[1:2, :]).astype(LOW)
    tables = (turn[:, :128], turn[:, 128:])
    rows = dot(h, weight[...].reshape(model, 3 * width))
    q[...] = (turned(rows[:, :width] + vectors[7:8, :width], *tables, 1.0) * 0.125).astype(LOW)
    k[...] = turned(rows[:, width : 2 * width] + vectors[8:9, :width], *tables, 1.0).astype(LOW)
    v[...] = (rows[:, 2 * width :] + vectors[9:10, :width]).astype(LOW)


def call_qkv(order, pieces, vectors, weight, tables, span, width):
    model = pieces[0].shape[1]
    plan = plan_of(pieces, span)
    rows = span * len(plan)
    there = lambda i, o: (o[i], 0)
    return pl.pallas_call(
        functools.partial(qkv_kernel, plan, len(pieces)),
        grid_spec=pltpu.PrefetchScalarGridSpec(
            num_scalar_prefetch=1,
            grid=(rows // span,),
            in_specs=[HBM] * len(pieces)
            + [whole(vectors.shape), whole(weight.shape[:2] + (3 * width,))]
            + [pl.BlockSpec((span, 256), there)],
            out_specs=[pl.BlockSpec((span, width), there)] * 3,
            scratch_shapes=[pltpu.VMEM((rows, model), LOW), pltpu.SemaphoreType.DMA((len(plan), 2))],
        ),
        out_shape=[jax.ShapeDtypeStruct((rows, width), LOW)] * 3,
        compiler_params=params("arbitrary"),
        cost_estimate=SHORT,
        name="qkv",
    )(order, *pieces, vectors, weight, tables)


def masked_rows(target, array):
    for head in range(array.shape[1] // HEAD):
        target[head * BLOCK : (head + 1) * BLOCK, :] = head_only(array, head)


def over_keys(first, block, tiles):
    begin = first[block]
    count = block + 1 - begin

    def pair(i, _):
        tiles(begin + 2 * i, 2)
        return 0

    def single(at, _):
        tiles(at, 1)
        return 0

    lax.fori_loop(0, count // 2, pair, 0)
    lax.fori_loop(block + 1 - count % 2, block + 1, single, 0)


def by_eight(array):
    return array.reshape(BLOCK // 8, 8, BLOCK)


def fwd_kernel(first, q, k, v, mixed, low_mixed, lse, keys, values, scores, top, total, out):
    step = pl.program_id(0)
    width = q.shape[1]
    heads = width // HEAD
    stack = heads * BLOCK
    masked_rows(keys.at[step], k[...])
    masked_rows(values.at[step], v[...])
    q_t = q[...].T
    top[...] = jnp.full_like(top, -1e30)
    total[...] = jnp.zeros_like(total)
    out[...] = jnp.zeros_like(out)

    def score(at, count):
        s = dot(keys[pl.ds(at, count)].reshape(count * stack, width), q_t)
        scores[pl.ds(at, count)] = s.reshape(count, stack, BLOCK)
        for head in range(heads):
            best = top[head]
            for tile in range(count):
                low = tile * stack + head * BLOCK
                best = jnp.maximum(best, jnp.max(by_eight(s[low : low + BLOCK]), axis=0))
            top[head] = best

    over_keys(first, step, score)
    peak = [jnp.max(top[head], axis=0, keepdims=True) for head in range(heads)]

    def mix(at, count):
        grown = []
        for tile in range(count):
            for head in range(heads):
                e = jnp.exp(scores[at + tile, head * BLOCK : (head + 1) * BLOCK] - peak[head])
                total[head] += jnp.sum(by_eight(e), axis=0)
                grown.append(e.astype(LOW))
        out[...] += dot(jnp.concatenate(grown, axis=0), values[pl.ds(at, count)].reshape(count * stack, width), TN)

    over_keys(first, step, mix)
    shares = []
    for head in range(heads):
        sums = jnp.sum(total[head], axis=0, keepdims=True)
        lse[head : head + 1, :] = peak[head] + jnp.log(sums)
        shares.append(jnp.broadcast_to(1.0 / sums, (HEAD, BLOCK)))
    result = out[...] * jnp.concatenate(shares, axis=0).T
    mixed[...] = result
    low_mixed[...] = result.astype(LOW)


def call_fwd(first, q, k, v):
    rows, width = q.shape
    heads = width // HEAD
    blocks = rows // BLOCK
    return pl.pallas_call(
        fwd_kernel,
        grid_spec=pltpu.PrefetchScalarGridSpec(
            num_scalar_prefetch=1,
            grid=(blocks,),
            in_specs=[pl.BlockSpec((BLOCK, width), lambda i, o: (i, 0))] * 3,
            out_specs=[
                pl.BlockSpec((BLOCK, width), lambda i, o: (i, 0)),
                pl.BlockSpec((BLOCK, width), lambda i, o: (i, 0)),
                pl.BlockSpec((heads, BLOCK), lambda i, o: (0, i)),
            ],
            scratch_shapes=[
                pltpu.VMEM((blocks, heads * BLOCK, width), LOW),
                pltpu.VMEM((blocks, heads * BLOCK, width), LOW),
                pltpu.VMEM((blocks, heads * BLOCK, BLOCK), F32),
                pltpu.VMEM((heads, 8, BLOCK), F32),
                pltpu.VMEM((heads, 8, BLOCK), F32),
                pltpu.VMEM((BLOCK, width), F32),
            ],
        ),
        out_shape=[
            jax.ShapeDtypeStruct((rows, width), F32),
            jax.ShapeDtypeStruct((rows, width), LOW),
            jax.ShapeDtypeStruct((heads, rows), F32),
        ],
        compiler_params=params("arbitrary"),
        cost_estimate=SHORT,
        name="attend",
    )(first, q, k, v)


def closed_rows(x, rows, to_norm, vectors, weight):
    n, scale = normed(x.astype(F32))
    d_h = dot(rows, weight, NT)
    bias = jnp.sum(d_h, axis=0, keepdims=True)
    gain = jnp.sum(d_h * n, axis=0, keepdims=True)
    e = d_h * vectors[0:1, :] + to_norm
    e = e - jnp.mean(e, axis=-1, keepdims=True) - n * jnp.mean(e * n, axis=-1, keepdims=True)
    return e * scale, gain, bias


def bwd_kernel(plan, per, groups, extra, first, q, k, v, d_mixed, mixed, lse, turn, to_norm, vectors, weight, *rest):
    many = 1 + max(piece for piece, _ in plan)
    pieces, outs, (even, odd, sums, ones), rest = rest[:many], rest[many : 2 * many], rest[2 * many : 2 * many + 4], rest[2 * many + 4 :]
    keys, values, sum_q, sum_k, sum_v, queries, seeds, h, d_rows, x, mat, wide, sem, x_sems, out_sems = rest
    step = pl.program_id(0)
    blocks = pl.num_programs(0)
    block = blocks - 1 - step
    width = k.shape[1]
    heads = width // HEAD
    stack = heads * BLOCK
    base = first.shape[0] - 1 - len(plan) // per
    group, order = first[base], lambda at: first[base + 1 + at]
    rows_of = lambda at: pl.ds(pl.multiple_of(at * BLOCK, BLOCK), BLOCK)
    own = rows_of(block)
    load = pltpu.make_async_copy(weight.at[:, :, pl.ds(0, 3 * width)], mat, sem.at[0])

    @pl.when(step == 0)
    def _():
        load.start()
        for at, (piece, start) in reversed(list(enumerate(plan))):
            place = order(at // per) * per + at % per
            pltpu.make_async_copy(pieces[piece].at[pl.ds(start, BLOCK)], x.at[rows_of(place)], x_sems.at[place]).start()

        def prepare(at, _):
            here = rows_of(at)
            masked_rows(keys.at[at], k[here, :])
            masked_rows(values.at[at], v[here, :])
            sum_k[here, :] = jnp.zeros((BLOCK, width), F32)
            sum_v[here, :] = jnp.zeros((BLOCK, width), F32)
            return 0

        lax.fori_loop(0, blocks, prepare, 0)
        sums[...] = jnp.zeros_like(sums)
        ones[...] = jnp.zeros_like(ones)

    q_own = q[...]
    s_own = d_mixed[...]
    masked_rows(queries, q_own)
    masked_rows(seeds, s_own)
    q_t = q_own.T
    s_t = s_own.T
    product_t = (s_own.astype(F32) * mixed[...]).T
    delta = [jnp.sum(product_t[head * HEAD : (head + 1) * HEAD, :], axis=0, keepdims=True) for head in range(heads)]
    log_total = [lse[head : head + 1, :] for head in range(heads)]
    sum_q[...] = jnp.zeros_like(sum_q)

    def tiles(at, count):
        key_rows = keys[pl.ds(at, count)].reshape(count * stack, width)
        s = dot(key_rows, q_t)
        d_p = dot(values[pl.ds(at, count)].reshape(count * stack, width), s_t)
        wide_probs, wide_scores, tall_scores = [], [], []
        for tile in range(count):
            low_probs, low_scores = [], []
            for head in range(heads):
                low = tile * stack + head * BLOCK
                probs = jnp.exp(s[low : low + BLOCK] - log_total[head])
                low_scores.append((probs * (d_p[low : low + BLOCK] - delta[head])).astype(LOW))
                low_probs.append(probs.astype(LOW))
            wide_probs.append(jnp.concatenate(low_probs, axis=1))
            wide_scores.append(jnp.concatenate(low_scores, axis=1))
            tall_scores += low_scores
        here = pl.ds(pl.multiple_of(at * BLOCK, BLOCK), count * BLOCK)
        sum_v[here, :] += dot(jnp.concatenate(wide_probs, axis=0), seeds[...])
        sum_k[here, :] += dot(jnp.concatenate(wide_scores, axis=0), queries[...])
        sum_q[...] += dot(jnp.concatenate(tall_scores, axis=0), key_rows, TN)

    over_keys(first, block, tiles)

    @pl.when(step == 0)
    def _():
        load.wait()

    pltpu.make_async_copy(x.at[own], x.at[own], x_sems.at[block]).wait()
    turns = (turn[:, :128], turn[:, 128:])
    done = jnp.concatenate(
        [
            (turned(sum_q[...], *turns, -1.0) * 0.125).astype(LOW),
            turned(sum_k[own, :], *turns, -1.0).astype(LOW),
            sum_v[own, :].astype(LOW),
        ],
        axis=1,
    )
    d_rows[own, :] = done
    sums[0:1, :] += jnp.sum(done.astype(F32), axis=0, keepdims=True)
    n, scale = normed(x[own, :].astype(F32))
    h[own, :] = (n * vectors[0:1, :] + vectors[1:2, :]).astype(LOW)
    d_h = dot(done, mat[...].reshape(h.shape[1], 3 * width), NT)
    ones[0:1, :] += jnp.sum(d_h * n, axis=0, keepdims=True)
    ones[1:2, :] += jnp.sum(d_h, axis=0, keepdims=True)
    e = d_h * vectors[0:1, :] + to_norm[...].astype(F32)
    e = e - jnp.mean(e, axis=-1, keepdims=True) - n * jnp.mean(e * n, axis=-1, keepdims=True)
    x[own, :] = (e * scale).astype(LOW)
    place = order(block // per) * per + block % per
    for at, (piece, start) in enumerate(plan):

        @pl.when(place == at)
        def _():
            pltpu.make_async_copy(x.at[own], outs[piece].at[pl.ds(start, BLOCK)], out_sems.at[block]).start()

    @pl.when(step == blocks - 1)
    def _():
        model = h.shape[1]
        grad = dot(h[...], d_rows[...], TN).astype(LOW)
        h[:model, : 3 * width] = grad
        size = model // groups
        for place in range(groups):
            to = odd if place % 2 else even
            to[place // 2, :size, :] = h[pl.ds(pl.multiple_of((group ^ place) * size, size), size), : 3 * width]
        if extra:
            members = len(plan) // per
            wide[...] = jnp.zeros_like(wide)
            for part in range(3):
                for at in range(width // 128):
                    row = (part * members + order(0)) * (width // 128) + at
                    low = part * width + at * 128
                    wide[pl.ds(row, 1), :] = sums[0:1, low : low + 128]
            for place in range(groups):
                to, near = odd if place % 2 else even, group ^ place
                lanes = pl.ds(pl.multiple_of(near * 128, 128), 128)
                lines = [ones[0:1, lanes], ones[1:2, lanes]] + [wide[pl.ds(3 * near + row, 1), :] for row in range(3)]
                to[place // 2, size:, :] = jnp.zeros((EXTRA, 3 * width), LOW)
                to[place // 2, size:, :128] = extra_rows(lines)
        for at in range(len(plan)):
            here = pl.ds(at * BLOCK, BLOCK)
            pltpu.make_async_copy(x.at[here], x.at[here], out_sems.at[at]).wait()


def call_bwd(first, q, k, v, d_mixed, mixed, lse, tables, to_norm, vectors, weight, pieces, out_shapes, groups, span, extra):
    rows, width = q.shape
    heads = width // HEAD
    blocks = rows // BLOCK
    model = to_norm.shape[1]
    grad = (groups // 2, model // groups + EXTRA * extra, 3 * width)
    back = lambda i, o: (blocks - 1 - i, 0)
    blocked = pl.BlockSpec((BLOCK, width), back)
    once = lambda shape: pl.BlockSpec(shape, lambda *_: (0,) * len(shape), pipeline_mode=pl.Buffered(1))
    plan = tuple((p, start) for block in plan_of(pieces, BLOCK) for p, start, _, _ in block)
    outs = [(grad, LOW), (grad, LOW), ((8, 3 * width), F32), ((8, model), F32)]
    return pl.pallas_call(
        functools.partial(bwd_kernel, plan, span // BLOCK, groups, extra),
        grid_spec=pltpu.PrefetchScalarGridSpec(
            num_scalar_prefetch=1,
            grid=(blocks,),
            in_specs=[blocked, once((rows, width)), once((rows, width)), blocked, blocked]
            + [pl.BlockSpec((heads, BLOCK), lambda i, o: (0, blocks - 1 - i)), pl.BlockSpec((BLOCK, 256), back)]
            + [pl.BlockSpec((BLOCK, model), back), whole(vectors.shape), HBM]
            + [HBM] * len(pieces),
            out_specs=[HBM] * len(out_shapes) + [whole(a) for a, _ in outs],
            scratch_shapes=[
                pltpu.VMEM((blocks, heads * BLOCK, width), LOW),
                pltpu.VMEM((blocks, heads * BLOCK, width), LOW),
                pltpu.VMEM((BLOCK, width), F32),
                pltpu.VMEM((rows, width), F32),
                pltpu.VMEM((rows, width), F32),
                pltpu.VMEM((heads * BLOCK, width), LOW),
                pltpu.VMEM((heads * BLOCK, width), LOW),
                pltpu.VMEM((rows, model), LOW),
                pltpu.VMEM((rows, 3 * width), LOW),
                pltpu.VMEM((rows, model), LOW),
                pltpu.VMEM(weight.shape[:2] + (3 * width,), LOW),
                pltpu.VMEM((3 * groups, 128), F32),
                pltpu.SemaphoreType.DMA((1,)),
                pltpu.SemaphoreType.DMA((blocks,)),
                pltpu.SemaphoreType.DMA((blocks,)),
            ],
        ),
        out_shape=list(out_shapes) + [jax.ShapeDtypeStruct(a, kind) for a, kind in outs],
        compiler_params=params("arbitrary"),
        cost_estimate=SHORT,
        name="attend_back",
    )(first, q, k, v, d_mixed, mixed, lse, tables, to_norm, vectors, weight, *pieces)


def extra_rows(lines):
    return jnp.concatenate(lines + [jnp.zeros((EXTRA - len(lines), 128), F32)], axis=0).astype(LOW)


def mlp_kernel(plan, out_plan, count, out_count, joined, chunk, order, *refs):
    x_pieces, cot_pieces, rest = refs[:count], refs[count : 2 * count], refs[2 * count :]
    mixed, vectors, rest = rest[0], rest[1], rest[2:]
    mats, rest = rest[: 1 if joined else 3], rest[1 if joined else 3 :]
    parts, rest = rest[:out_count], rest[out_count:]
    d_mixed, to_norm, rest = rest[0], rest[1], rest[2:]
    grads, rest = rest[: 1 if joined else 3], rest[1 if joined else 3 :]
    sums, normal, cot, active, d_up, own_mixed, g_out, staged, x_sems, cot_sems, out_sems = rest
    step = pl.program_id(0)
    steps = len(plan)
    span, width = own_mixed.shape[0] // steps, own_mixed.shape[1]
    model, units = normal.shape[1], active.shape[1]
    if joined:
        groups = mats[0].shape[0]
        cuts = [0, model // groups, (model + units) // groups, (model + units + width) // groups]
        w_up, w_down, w_out = (mats[0].at[:, pl.ds(cuts[i], cuts[i + 1] - cuts[i]), :] for i in range(3))
    else:
        w_up, w_down, w_out = mats
    as_up = lambda: w_up[...].reshape(model, units)
    as_down = lambda: w_down[...].reshape(units, model)
    as_out = lambda: w_out[...].reshape(width, model)

    @pl.when(step == 0)
    def _():
        fetch_all(plan, x_pieces, normal, x_sems)
        fetch_all(plan, cot_pieces, cot, cot_sems)
        sums[...] = jnp.zeros_like(sums)

    fetch(plan, step, x_pieces, normal, x_sems, False)
    fetch(plan, step, cot_pieces, cot, cot_sems, False)

    @pl.when(step < steps)
    def _():
        here = pl.ds(pl.multiple_of(step * span, span), span)
        n, _ = normed(normal[here, :].astype(F32))
        h = (n * vectors[2:3, :] + vectors[3:4, :]).astype(LOW)
        normal[here, :] = h
        dy = cot[here, :]
        own = mixed[pl.ds(pl.multiple_of(order[step] * span, span), span), :]
        own_mixed[here, :] = own
        d_mixed[...] = dot(dy, as_out(), NT).astype(LOW)
        up, down = as_up(), as_down()
        for low in range(0, units, chunk):
            cols = slice(low, low + chunk)
            u = dot(h, up[:, cols]) + vectors[6:7, cols]
            d_active = dot(dy, down[cols], NT)
            cdf = 0.5 * (1.0 + lax.erf(u * np.float32(np.sqrt(0.5))))
            slope = cdf + u * (jnp.exp(-0.5 * u * u) * np.float32(1.0 / np.sqrt(2.0 * np.pi)))
            active[here, cols] = (u * cdf).astype(LOW)
            back = (d_active * slope).astype(LOW)
            d_up[here, cols] = back
            sums[0:1, cols] += jnp.sum(back.astype(F32), axis=0, keepdims=True)
        staged[here, :] = (dot(active[here, :], down) + dot(own, as_out())).astype(LOW)
        d_h = dot(d_up[here, :], up, NT)
        sums[1:2, :model] += jnp.sum(d_h, axis=0, keepdims=True)
        sums[2:3, :model] += jnp.sum(d_h * n, axis=0, keepdims=True)
        to_norm[...] = (d_h * vectors[2:3, :]).astype(LOW)

        @pl.when(step == 0)
        def _():
            sums[3:4, :model] = jnp.sum(dy.astype(F32), axis=0, keepdims=True)

    store(out_plan, step, staged, parts, out_sems, True)

    @pl.when(step >= steps)
    def _():
        at = step - steps
        many = pl.num_programs(0) - steps

        @pl.when(at == 0)
        def _():
            g_out[...] = dot(own_mixed[...], cot[...], TN).astype(LOW)

        up_cols = pl.ds(pl.multiple_of(at * (model // many), 128), model // many)
        down_cols = pl.ds(pl.multiple_of(at * (units // many), 128), units // many)
        out_rows = pl.ds(pl.multiple_of(at * (width // many), 16), width // many)
        up_grad = dot(normal[:, up_cols], d_up[...], TN).astype(LOW)
        down_grad = dot(active[:, down_cols], cot[...], TN).astype(LOW)
        if joined:
            block = grads[0].shape[0]
            grads[0][:, cuts[0] : cuts[1], :] = up_grad.reshape(block, cuts[1], units)
            grads[0][:, cuts[1] : cuts[2], :] = down_grad.reshape(block, cuts[2] - cuts[1], model)
            grads[0][:, cuts[2] : cuts[3], :] = g_out[out_rows, :].reshape(block, cuts[3] - cuts[2], model)
            grads[0][:, cuts[3] :, :] = jnp.zeros((block, EXTRA, model), LOW)
            for place in range(block):
                lanes = pl.ds(pl.multiple_of((at * block + place) * 128, 128), 128)
                lines = [sums[row : row + 1, lanes] for row in (2, 1, 3, 0)]
                grads[0][place, cuts[3] :, :128] = extra_rows(lines)
        else:
            grads[0][...] = up_grad
            grads[1][...] = down_grad
            grads[2][...] = g_out[out_rows, :]

    @pl.when(step == pl.num_programs(0) - 1)
    def _():
        for at in range(steps):
            store(out_plan, at, staged, parts, out_sems, False)


def call_mlp(order, x_pieces, cot_pieces, mixed, vectors, mats, span, units, out_shapes):
    rows, width = mixed.shape
    model = x_pieces[0].shape[1]
    joined = len(mats) == 1
    plan, out_plan = plan_of(x_pieces, span), plan_of(out_shapes, span)
    steps, many = len(plan), 4
    count = len(x_pieces)
    there = lambda i, o: (o[jnp.minimum(i, steps - 1)], 0)
    later = lambda i, o: (jnp.maximum(i - steps, 0), 0)
    if joined:
        groups = mats[0].shape[0]
        grads = [(groups, (model + units + width) // groups + EXTRA, model)]
        grad_specs = [pl.BlockSpec((groups // many,) + grads[0][1:], lambda i, o: (jnp.maximum(i - steps, 0), 0, 0))]
    else:
        grads = [(model, units), (units, model), (width, model)]
        grad_specs = [pl.BlockSpec((a // many, b), later) for a, b in grads]
    sums = (8, max(model, units))
    return pl.pallas_call(
        functools.partial(mlp_kernel, plan, out_plan, count, len(out_shapes), joined, 256),
        grid_spec=pltpu.PrefetchScalarGridSpec(
            num_scalar_prefetch=1,
            grid=(steps + many,),
            in_specs=[HBM] * (2 * count)
            + [whole((rows, width)), whole(vectors.shape)]
            + [pl.BlockSpec(m.shape, lambda *_: (0, 0, 0), pipeline_mode=pl.Buffered(1)) for m in mats],
            out_specs=[HBM] * len(out_shapes)
            + [pl.BlockSpec((span, width), there), pl.BlockSpec((span, model), there)]
            + grad_specs
            + [whole(sums)],
            scratch_shapes=[
                pltpu.VMEM((rows, model), LOW),
                pltpu.VMEM((rows, model), LOW),
                pltpu.VMEM((rows, units), LOW),
                pltpu.VMEM((rows, units), LOW),
                pltpu.VMEM((rows, width), LOW),
                pltpu.VMEM((width, model), LOW),
                pltpu.VMEM((rows, model), LOW),
                pltpu.SemaphoreType.DMA((steps, 2)),
                pltpu.SemaphoreType.DMA((steps, 2)),
                pltpu.SemaphoreType.DMA((steps, 2)),
            ],
        ),
        out_shape=list(out_shapes)
        + [jax.ShapeDtypeStruct((rows, width), LOW), jax.ShapeDtypeStruct((rows, model), LOW)]
        + [jax.ShapeDtypeStruct(g, LOW) for g in grads]
        + [jax.ShapeDtypeStruct(sums, F32)],
        compiler_params=params("arbitrary"),
        cost_estimate=SHORT,
        name="mlp",
    )(order, *x_pieces, *cot_pieces, mixed, vectors, *mats)


def finish_kernel(shifts, wholes, base, *refs):
    refs, out = refs[:-1], refs[-1]
    shift, refs = refs[:shifts], refs[shifts:]
    common, parts = refs[:wholes], refs[wholes:]
    total = base[...].astype(F32)
    for ref in shift:
        total = total + ref[4:5, :] + ref[5:6, :]
    for ref in common:
        total = total + ref[...].astype(F32)
    if not parts:
        out[...] = total.astype(LOW)
    for at in range(2 if parts else 0):

        @pl.when(pl.program_id(0) == at)
        def _():
            more = total
            for ref in parts[at::2]:
                more = more + ref[...].astype(F32)
            out[...] = more.astype(LOW)


def call_finish(base, common, parts, vectors=(), cost=SHORT):
    rows, model = base.shape
    block = pl.BlockSpec((rows // 2, model), lambda i: (i, 0))
    return pl.pallas_call(
        functools.partial(finish_kernel, len(vectors), len(common)),
        grid=(2,),
        in_specs=[block] + [whole(v.shape) for v in vectors] + [block] * len(common) + [whole((rows // 2, model))] * len(parts),
        out_specs=block,
        out_shape=jax.ShapeDtypeStruct((rows, model), LOW),
        compiler_params=params("arbitrary"),
        cost_estimate=cost,
        name="finish",
    )(base, *vectors, *common, *parts)


def cut_kernel(members, member, first, second, third, *out):
    pieces, (down, line) = out[:members], out[members:]
    columns = first.shape[1]
    shard = pieces[0].shape[0] - EXTRA
    low = members * shard
    for bit, piece in enumerate(pieces):
        rows = pl.ds(pl.multiple_of((member[0] ^ bit) * shard, shard), shard)
        piece[:shard, :columns] = first[rows, :]
        piece[:shard, columns:] = (second[rows, :].astype(F32) + third[rows, :].astype(F32)).astype(LOW)
        piece[shard:, :columns] = first[first.shape[0] - EXTRA :, :]
        piece[shard:, columns:] = (second[low:, :].astype(F32) + third[low:, :].astype(F32)).astype(LOW)
    down[...] = first[low : low + down.shape[0], :].astype(F32)
    line[...] = first[first.shape[0] - EXTRA :, :128].astype(F32)[3:4, :]


def call_cut(member, first, second, third, members, shard):
    columns = first.shape[1]
    shapes = [jax.ShapeDtypeStruct((shard + EXTRA, columns + second.shape[1]), LOW)] * members + [
        jax.ShapeDtypeStruct((first.shape[0] - (members + 1) * shard - EXTRA, columns), F32),
        jax.ShapeDtypeStruct((1, 128), F32),
    ]
    return pl.pallas_call(
        functools.partial(cut_kernel, members),
        grid_spec=pltpu.PrefetchScalarGridSpec(
            num_scalar_prefetch=1,
            grid=(1,),
            in_specs=[whole(first.shape), whole(second.shape), whole(third.shape)],
            out_specs=[whole(a.shape) for a in shapes],
        ),
        out_shape=shapes,
        compiler_params=params("arbitrary"),
        cost_estimate=SHORT,
        name="cut",
    )(member, first, second, third)


def join_kernel(places, second, member, *refs):
    pieces, outs, total = refs[:-3], refs[-3:-1], refs[-1]
    shard = outs[0].shape[0]
    for bit, piece in enumerate(pieces):
        for block, (index, column, stride) in enumerate(places):
            start = pl.multiple_of(column + (member[0] ^ bit) * stride, 128)
            outs[index][:, pl.ds(start, 128)] = piece[:shard, block * 128 : (block + 1) * 128].astype(F32)
    for row, low in ((0, 0), (8, second)):
        total[row : row + 8, :] = sum(piece[shard:, low : low + 128].astype(F32) for piece in pieces)[:8, :]


def call_join(member, pieces, places, second, columns):
    shard = pieces[0].shape[0] - EXTRA
    shapes = [(shard, c) for c in columns] + [(16, 128)]
    return pl.pallas_call(
        functools.partial(join_kernel, tuple(places), second),
        grid_spec=pltpu.PrefetchScalarGridSpec(
            num_scalar_prefetch=1,
            grid=(1,),
            in_specs=[whole(p.shape) for p in pieces],
            out_specs=[whole(a) for a in shapes],
        ),
        out_shape=[jax.ShapeDtypeStruct(a, F32) for a in shapes],
        compiler_params=params("arbitrary"),
        cost_estimate=SHORT,
        name="join",
    )(member, *pieces)


def across(array, bit):
    size = lax.axis_size("fsdp")
    return lax.ppermute(array, "fsdp", [(i, i ^ bit) for i in range(size)])


def exchange(pieces):
    size = lax.axis_size("fsdp")
    if size != 4:
        return lax.all_to_all(pieces, "fsdp", split_axis=0, concat_axis=0, tiled=True)
    member = lax.axis_index("fsdp")
    out = pieces
    for bit in range(1, size):
        mine = lax.dynamic_index_in_dim(pieces, member ^ bit, 0, keepdims=False)
        out = lax.dynamic_update_index_in_dim(out, across(mine, bit), member ^ bit, 0)
    return out


def behind(array, *others):
    return lax.optimization_barrier((array, *others))[0]


def behind_all(arrays, *others):
    return tuple(behind(array, *others) for array in arrays)


def gather_rows(halves, near=None, *others):
    if lax.axis_size("fsdp") != 4:
        return [lax.all_gather(jnp.concatenate(halves, axis=0), "fsdp", axis=0, tiled=True)]
    one_low, two_high, one_high, two_low = near
    return [
        *halves, one_low, one_high, two_low, two_high,
        across(behind(one_low, *others), 2), across(behind(two_high, *others), 1),
    ]


def near_rows(halves):
    low, high = halves
    return across(low, 1), across(high, 2), across(high, 1), across(low, 2)


def hop(array, bit):
    return lax.ppermute(array, "dp", [(i, i ^ bit) for i in range(lax.axis_size("dp"))])


def scatter_step(blocks, far, bit):
    blocks = (blocks.astype(F32) + far.astype(F32)).astype(LOW)
    send = blocks[1::2]
    return blocks[0::2], hop(send, bit), send


def reduce_direct(parts):
    if len(parts) == 1:
        return (lax.psum_scatter(parts[0], "fsdp", scatter_dimension=0, tiled=True),)
    three = across(parts[3], 3)
    return parts[0], across(parts[1], 1), across(parts[2], 2), three


def total_over_all(vector):
    count = lax.axis_size("dp") * lax.axis_size("fsdp")
    step = 1
    while step < count:
        vector = vector + lax.ppermute(vector, ALL, [(i, i ^ step) for i in range(count)])
        step *= 2
    return vector


def swap_owner(array, back):
    groups, members = lax.axis_size("dp"), lax.axis_size("fsdp")
    pairs = [(m * groups + g, g * members + m) for g in range(groups) for m in range(members)]
    if back:
        pairs = [(b, a) for a, b in pairs]
    return lax.ppermute(array, ALL, pairs)


def gather_dp(array):
    return lax.all_gather(array, "dp", axis=0)


def scatter_dp(array):
    return lax.psum_scatter(array, "dp", scatter_dimension=0, tiled=True)


def rotary_tables(length):
    half = ROT // 2
    frequency = (np.float32(10000.0) ** (-(np.arange(half, dtype=np.float32) * np.float32(2.0)) / np.float32(ROT))).astype(np.float32)
    angles = (np.arange(length, dtype=np.float32)[:, None] * frequency[None, :]).astype(np.float32)
    cosine = np.cos(angles).astype(np.float32)
    sine = np.sin(angles).astype(np.float32)
    cos_row = np.ones((length, 128), np.float32)
    sine_row = np.zeros((length, 128), np.float32)
    for start in range(0, 128, HEAD):
        cos_row[:, start : start + half] = cosine
        cos_row[:, start + half : start + ROT] = cosine
        sine_row[:, start : start + half] = -sine
        sine_row[:, start + half : start + ROT] = sine
    return jnp.asarray(np.concatenate([cos_row, sine_row], axis=1))


def local(
    tokens, cotangent, doc_ids, norm1_gain, norm1_bias, norm2_gain, norm2_bias, qkv_weight, qkv_bias,
    out_weight, out_bias, up_weight, up_bias, down_weight, down_bias,
):
    groups, members = lax.axis_size("dp"), lax.axis_size("fsdp")
    group, member = lax.axis_index("dp"), lax.axis_index("fsdp")
    devices = groups * members
    rows, model = tokens.shape
    stream = rows * members
    shard = qkv_weight.shape[0]
    width = model // members
    units_dev = up_bias.shape[0]
    units = groups * units_dev
    paired = members == 4 and units_dev == 128 and units == model
    me = member.astype(jnp.int32).reshape(1)
    vectors_in = [norm1_gain, norm1_bias, norm2_gain, norm2_bias, out_bias, down_bias]

    half = rows // 2
    x_halves = [tokens[:half], tokens[half:]]
    cot_halves = [cotangent[:half], cotangent[half:]]
    if paired:
        small = small_block(member, members, vectors_in, qkv_bias, up_bias)
        packed = call_pack(me, qkv_weight, up_weight, small, members)
        arrived = [packed[0]] + [across(packed[bit], bit) for bit in range(1, members)]
        x_near = near_rows(behind_all(x_halves, *arrived[1:]))
        cut = 3 * width + 128
        first_in, up_in = call_place(me, arrived, cut)
        w_first = gather_dp(first_in)
        out_own = behind(swap_owner(behind(out_weight, first_in), False), *x_near[:2])
        mats = (gather_dp(jnp.concatenate([up_in, down_weight, out_own], axis=0)),)
        vectors = call_vectors(me, w_first, members, cut)
    else:
        qkv_cut = qkv_weight.reshape(shard, 3, members, width).transpose(2, 0, 1, 3).reshape(members, shard, 3 * width)
        up_cut = up_weight.reshape(shard, groups, members, units_dev).transpose(2, 0, 1, 3).reshape(members, shard, units)
        arrived = exchange(jnp.concatenate([qkv_cut, up_cut], axis=2)).reshape(members * shard, -1)
        w_first = gather_dp(arrived[:, : 3 * width])
        x_near = near_rows(x_halves) if members == 4 else None
        mats = (gather_dp(arrived[:, 3 * width :]), gather_dp(down_weight), gather_dp(swap_owner(out_weight, False)))
        full = [lax.all_gather(a, ALL, axis=0, tiled=True).astype(F32) for a in vectors_in]
        shift = lax.all_gather(qkv_bias, ALL, axis=0, tiled=True).astype(F32).reshape(3, members, width)
        shift = lax.dynamic_index_in_dim(shift, member, 1, keepdims=False)
        up_all = lax.all_gather(up_bias, "dp", axis=0, tiled=True).astype(F32)
        lines = full + [jnp.pad(a, (0, model - a.shape[0])) for a in (up_all, shift[0], shift[1], shift[2])]
        vectors = jnp.pad(jnp.stack(lines), ((0, 6), (0, 0)))

    x_pieces = gather_rows(x_halves, x_near)
    sources = jnp.arange(members, dtype=jnp.int32)
    order = sources ^ member if members == 4 else sources
    doc_row = doc_ids[0]
    first = jnp.sum((doc_row[None, :] < doc_row[:, None]).astype(jnp.int32), axis=1)
    first = jnp.concatenate([first, group.astype(jnp.int32).reshape(1), order])
    tables = rotary_tables(stream)

    q, k, v = call_qkv(order, x_pieces, vectors, w_first, tables, rows, width)
    cot_near = near_rows(behind_all(cot_halves, *x_near)) if members == 4 else None
    cot_pieces = gather_rows(cot_halves, cot_near, q)
    mixed, low_mixed, lse = call_fwd(first, q, k, v)
    out_sizes = [rows] * members if members == 4 else [stream]
    out_shapes = [jax.ShapeDtypeStruct((size, model), LOW) for size in out_sizes]
    results = call_mlp(
        order, x_pieces, cot_pieces, low_mixed, vectors, mats, rows, units, out_shapes
    )
    count = len(out_shapes)
    parts, (d_mixed, to_norm), grads, sums_two = results[:count], results[count : count + 2], results[count + 2 : -1], results[-1]
    scattered = scatter_dp(grads[0].reshape(-1, model)) if paired else None

    summed = reduce_direct(parts)
    sizes = [half] * (2 * members) if members == 4 else [stream]
    *pieces, even, odd, sums_qkv, ones = call_bwd(
        first, q, k, v, d_mixed, mixed, lse, tables, to_norm, vectors, w_first, x_pieces,
        [jax.ShapeDtypeStruct((size, model), LOW) for size in sizes], groups, rows, paired,
    )
    far, bit = hop(odd, 1), 2
    if members == 4:
        add = lambda a, b: (a.astype(F32) + b.astype(F32)).astype(LOW)
        own_low, own_high, one_low, one_high, two_low, two_high, three_low, three_high = pieces
        come = across(three_high, 2), across(three_low, 1)
        near = across(one_low, 1), across(two_high, 2)
        output = call_finish(tokens, summed, (), (vectors,), LONG)
        blocks, far, send = scatter_step(even, behind(far, output), bit)
        come = behind_all(come, send)
        one_high, two_low = add(one_high, come[0]), add(two_low, come[1])
        near += across(one_high, 1), across(two_low, 2)
        parts = own_low, own_high, near[0], near[2], near[3], near[1]
        blocks, far, send = scatter_step(blocks, behind(far, one_high, two_low), 2 * bit)
        bit = 8
    if members != 4:
        blocks, far, _ = scatter_step(even, far, bit)
        bit = 4
        output = call_finish(tokens, summed, (), (vectors,))
        total = reduce_direct(pieces)[0]
        parts = total[:half], total[half:]
    while blocks.shape[0] > 1:
        (blocks, far, _), bit = scatter_step(blocks, far, bit), 2 * bit
    g_qkv = blocks[0], far[0]
    place = group * members + member
    if paired:
        *mixed_pieces, g_down, up_shift = call_cut(me, scattered, *g_qkv, members, shard)
        g_out = scattered[scattered.shape[0] - shard - EXTRA : scattered.shape[0] - EXTRA]
        g_out = swap_owner(behind(g_out, g_down), True)
        grad_tokens = call_finish(behind(cotangent, g_down), (), parts)
        places = [(0, b * members * units_dev, units_dev) for b in range(groups)]
        places += [(1, part * model + low, width) for part in range(3) for low in range(0, width, 128)]
        arrived = [mixed_pieces[0]] + [across(mixed_pieces[bit], bit) for bit in range(1, members)]
        g_up, g_qkv, totals = call_join(me, arrived, places, model, (up_weight.shape[1], qkv_weight.shape[1]))
        size = model // devices
        lines = lax.dynamic_slice_in_dim(totals, member * size, size, 1)
        mine = [lines[row] for row in (8, 9, 0, 1, 2)]
        mine += [lax.dynamic_slice_in_dim(totals[10:13].reshape(-1), member * 3 * size, 3 * size), up_shift[0]]
    else:
        grad_tokens = call_finish(cotangent, (), parts)
        g_up, g_down, g_out = [scatter_dp(g) for g in grads]
        g_down = g_down.astype(F32)
        g_up = exchange(g_up.reshape(members, shard, units))
        g_up = g_up.reshape(members, shard, groups, units_dev).transpose(1, 2, 0, 3).reshape(shard, -1).astype(F32)
        g_qkv = (g_qkv[0].astype(F32) + g_qkv[1].astype(F32)).astype(LOW)
        g_qkv = exchange(g_qkv.reshape(members, shard, 3 * width)).reshape(members, shard, 1, 3, width)
        g_qkv = g_qkv.transpose(1, 3, 0, 2, 4).reshape(shard, -1).astype(F32)
        thirds = jnp.concatenate([a[0].reshape(3, 1, width) for a in [sums_qkv]], axis=2)
        wide_qkv = lax.dynamic_update_index_in_dim(jnp.zeros((3, members, width), F32), thirds, member, 1)
        wide_up = lax.dynamic_update_index_in_dim(
            jnp.zeros((groups, members, units_dev), F32), sums_two[0, :units].reshape(groups, 1, units_dev), member, 1
        )
        summed = total_over_all(jnp.concatenate([
            ones[0], ones[1], sums_two[2], sums_two[1], sums_two[3], wide_qkv.reshape(-1), wide_up.reshape(-1),
        ]))
        mine, start = [], 0
        for size in [model] * 5 + [3 * model, groups * members * units_dev]:
            mine.append(lax.dynamic_slice_in_dim(summed, start + place * (size // devices), size // devices))
            start += size
    gain_1, bias_1, gain_2, bias_2, end_bias, qkv_shift, up_shift = mine
    g_out = (g_out if paired else swap_owner(g_out, True)).astype(F32)
    return (
        output, grad_tokens, gain_1, bias_1, gain_2, bias_2, g_qkv, qkv_shift, g_out, end_bias, g_up, up_shift, g_down, end_bias,
    )


def solution(mesh):
    row, vec = P(ALL, None), P(ALL)
    return jax.shard_map(
        local,
        mesh=mesh,
        in_specs=(row, row, P("dp", None), vec, vec, vec, vec, row, vec, row, vec, row, vec, row, vec),
        out_specs=(row, row, vec, vec, vec, vec, row, vec, row, vec, row, vec, row, vec),
        check_vma=False,
    )
```

```python
import functools

import jax
import jax.numpy as jnp
import numpy as np
from jax import lax
from jax.experimental import pallas as pl
from jax.experimental.pallas import tpu as pltpu
from jax.sharding import PartitionSpec as P

HEADS = 16
HEAD = 64
ROT = 16
BLOCK = 256
EPS = 1e-05
ALL = ("dp", "fsdp")
LONG = pl.CostEstimate(flops=2 * 10**10, bytes_accessed=10**7, transcendentals=0)
SHORT = pl.CostEstimate(flops=0, bytes_accessed=0, transcendentals=0)
F32 = jnp.float32
LOW = jnp.bfloat16


def dot(left, right, contract=((1,), (0,))):
    return lax.dot_general(left, right, (contract, ((), ())), preferred_element_type=F32)


NT = ((1,), (1,))
TN = ((0,), (0,))


def normed(x_rows):
    centre = x_rows - jnp.mean(x_rows, axis=-1, keepdims=True)
    spread = jnp.mean(centre * centre, axis=-1, keepdims=True)
    scale = lax.rsqrt(spread + EPS)
    return centre * scale, scale


def turned(z, cosine, sine, sign):
    groups = []
    for start in range(0, z.shape[1], 128):
        part = z[:, start : start + 128]
        ahead = pltpu.roll(part, 128 - ROT // 2, 1)
        behind = pltpu.roll(part, ROT // 2, 1)
        lane = lax.broadcasted_iota(jnp.int32, part.shape, 1) & (HEAD - 1)
        groups.append(part * cosine + sign * (jnp.where(lane < ROT // 2, ahead, behind) * sine))
    return groups[0] if len(groups) == 1 else jnp.concatenate(groups, axis=1)


def head_only(array, head):
    lane = lax.broadcasted_iota(jnp.int32, array.shape, 1)
    keep = (lane >= head * HEAD) & (lane < (head + 1) * HEAD)
    return jnp.where(keep, array, jnp.zeros_like(array))


def params(*order):
    return pltpu.CompilerParams(vmem_limit_bytes=60 * 1024 * 1024, dimension_semantics=order)


def whole(shape):
    return pl.BlockSpec(shape, lambda *_: (0,) * len(shape))


HBM = pl.BlockSpec(memory_space=pl.ANY)
EXTRA = 16


def fetch(plan, step, refs, target, sems, begin):
    for at, pieces in enumerate(plan):

        @pl.when(step == at)
        def _():
            for index, (ref, start, put, size) in enumerate(pieces):
                copy = pltpu.make_async_copy(
                    refs[ref].at[pl.ds(start, size)], target.at[pl.ds(put, size)], sems.at[at, index]
                )
                if begin:
                    copy.start()
                else:
                    copy.wait()


def fetch_all(plan, refs, target, sems):
    for at in range(len(plan)):
        fetch(plan, at, refs, target, sems, True)


def plan_of(pieces, span):
    plan, total = [], sum(p.shape[0] for p in pieces)
    for low in range(0, total, span):
        taken, at = [], 0
        for index, piece in enumerate(pieces):
            a, b = max(low, at), min(low + span, at + piece.shape[0])
            if a < b:
                taken.append((index, a - at, a, b - a))
            at += piece.shape[0]
        plan.append(tuple(taken))
    return tuple(plan)


def store(plan, step, source, refs, sems, begin):
    for at, pieces in enumerate(plan):

        @pl.when(step == at)
        def _():
            for index, (ref, start, put, size) in enumerate(pieces):
                copy = pltpu.make_async_copy(
                    source.at[pl.ds(put, size)], refs[ref].at[pl.ds(start, size)], sems.at[at, index]
                )
                if begin:
                    copy.start()
                else:
                    copy.wait()


def pack_kernel(members, member, qkv, up, *refs):
    vectors, (qkv_bias, up_bias), out, (small, wide) = refs[:6], refs[6:8], refs[8:-2], refs[-2:]
    width = qkv.shape[1] // 3 // members
    units_dev = up_bias.shape[0]
    groups = up.shape[1] // units_dev // members
    size = 128 // members
    small[...] = jnp.zeros_like(small)
    wide[...] = jnp.zeros_like(wide)
    for at in range(members):

        @pl.when(member[0] == at)
        def _():
            for row, vector in enumerate(vectors):
                small[row, at * size : (at + 1) * size] = vector[...].astype(F32)
            wide[0, 3 * at * size : 3 * (at + 1) * size] = qkv_bias[...].astype(F32)

    for row in range(3):
        small[6 + row : 7 + row, :] = wide[0:1, row * 128 : (row + 1) * 128]
    small[9, :] = up_bias[...].astype(F32)
    block = small[...].astype(LOW)
    for bit in range(members):
        to = member[0] ^ bit
        for part in range(3):
            start = pl.multiple_of((part * members + to) * width, 128)
            out[bit][:, part * width : (part + 1) * width] = qkv[:, pl.ds(start, width)]
        out[bit][:, 3 * width : 3 * width + 128] = jnp.zeros((qkv.shape[0], 128), LOW)
        out[bit][0:16, 3 * width : 3 * width + 128] = block
        for group in range(groups):
            start = pl.multiple_of((group * members + to) * units_dev, 128)
            low = 3 * width + 128 + group * units_dev
            out[bit][:, low : low + units_dev] = up[:, pl.ds(start, units_dev)]


def call_pack(member, qkv, up, vectors, members):
    shard = qkv.shape[0]
    columns = (qkv.shape[1] + up.shape[1]) // members + 128
    return pl.pallas_call(
        functools.partial(pack_kernel, members),
        grid_spec=pltpu.PrefetchScalarGridSpec(
            num_scalar_prefetch=1,
            grid=(1,),
            in_specs=[whole(a.shape) for a in (qkv, up, *vectors)],
            out_specs=[whole((shard, columns))] * members,
            scratch_shapes=[pltpu.VMEM((16, 128), F32), pltpu.VMEM((8, 384), F32)],
        ),
        out_shape=[jax.ShapeDtypeStruct((shard, columns), LOW)] * members,
        compiler_params=params("arbitrary"),
        cost_estimate=SHORT,
        name="pack",
    )(member, qkv, up, *vectors)


def place_kernel(cut, member, *refs):
    *pieces, first, second = refs
    shard = pieces[0].shape[0]
    for bit, piece in enumerate(pieces):
        rows = pl.ds(pl.multiple_of((member[0] ^ bit) * shard, shard), shard)
        first[rows, :] = piece[:, :cut]
        second[rows, :] = piece[:, cut:]


def call_place(member, pieces, cut):
    members, (shard, columns) = len(pieces), pieces[0].shape
    shapes = [(members * shard, cut), (members * shard, columns - cut)]
    return pl.pallas_call(
        functools.partial(place_kernel, cut),
        grid_spec=pltpu.PrefetchScalarGridSpec(
            num_scalar_prefetch=1,
            grid=(1,),
            in_specs=[whole(p.shape) for p in pieces],
            out_specs=[whole(a) for a in shapes],
        ),
        out_shape=[jax.ShapeDtypeStruct(a, LOW) for a in shapes],
        compiler_params=params("arbitrary"),
        cost_estimate=SHORT,
        name="place",
    )(member, *pieces)


def vectors_kernel(members, member, gathered, out, wide):
    groups, rows, _ = gathered.shape
    shard = rows // members
    model = groups * 128
    out[...] = jnp.zeros_like(out)
    for group in range(groups):
        blocks = [gathered[group, m * shard : m * shard + 16, :].astype(F32) for m in range(members)]
        block = blocks[0]
        for other in blocks[1:]:
            block = block + other
        lanes = slice(group * 128, (group + 1) * 128)
        for row in range(6):
            out[row : row + 1, lanes] = block[row : row + 1, :]
        for row in range(3):
            low = group * 384 + row * 128
            wide[0:1, low : low + 128] = block[6 + row : 7 + row, :]
        own = jnp.zeros((1, 128), F32)
        for m in range(members):
            own = own + jnp.where(member[0] == m, blocks[m][9:10, :], 0.0)
        out[6:7, lanes] = own
    width = model // members
    for part in range(3):
        start = pl.multiple_of(part * model + member[0] * width, 128)
        out[7 + part : 8 + part, :width] = wide[0:1, pl.ds(start, width)]


def call_vectors(member, gathered, members, cut):
    groups, rows, _ = gathered.shape
    model = groups * 128
    return pl.pallas_call(
        functools.partial(vectors_kernel, members),
        grid_spec=pltpu.PrefetchScalarGridSpec(
            num_scalar_prefetch=1,
            grid=(1,),
            in_specs=[pl.BlockSpec((groups, rows, 128), lambda i, o: (0, 0, cut // 128 - 1))],
            out_specs=whole((16, model)),
            scratch_shapes=[pltpu.VMEM((8, 3 * model), F32)],
        ),
        out_shape=jax.ShapeDtypeStruct((16, model), F32),
        compiler_params=params("arbitrary"),
        cost_estimate=SHORT,
        name="vectors",
    )(member, gathered)


def qkv_kernel(plan, count, order, *refs):
    pieces, rest = refs[:count], refs[count:]
    vectors, weight, turn, q, k, v, x, sems = rest
    step = pl.program_id(0)
    width = q.shape[1]
    span = q.shape[0]
    model = x.shape[1]

    @pl.when(step == 0)
    def _():
        fetch_all(plan, pieces, x, sems)

    fetch(plan, step, pieces, x, sems, False)
    n, _ = normed(x[pl.ds(pl.multiple_of(step * span, span), span), :].astype(F32))
    h = (n * vectors[0:1, :] + vectors[1:2, :]).astype(LOW)
    tables = (turn[:, :128], turn[:, 128:])
    rows = dot(h, weight[...].reshape(model, 3 * width))
    q[...] = (turned(rows[:, :width] + vectors[7:8, :width], *tables, 1.0) * 0.125).astype(LOW)
    k[...] = turned(rows[:, width : 2 * width] + vectors[8:9, :width], *tables, 1.0).astype(LOW)
    v[...] = (rows[:, 2 * width :] + vectors[9:10, :width]).astype(LOW)


def call_qkv(order, pieces, vectors, weight, tables, span, width):
    model = pieces[0].shape[1]
    plan = plan_of(pieces, span)
    rows = span * len(plan)
    there = lambda i, o: (o[i], 0)
    return pl.pallas_call(
        functools.partial(qkv_kernel, plan, len(pieces)),
        grid_spec=pltpu.PrefetchScalarGridSpec(
            num_scalar_prefetch=1,
            grid=(rows // span,),
            in_specs=[HBM] * len(pieces)
            + [whole(vectors.shape), whole(weight.shape[:2] + (3 * width,))]
            + [pl.BlockSpec((span, 256), there)],
            out_specs=[pl.BlockSpec((span, width), there)] * 3,
            scratch_shapes=[pltpu.VMEM((rows, model), LOW), pltpu.SemaphoreType.DMA((len(plan), 2))],
        ),
        out_shape=[jax.ShapeDtypeStruct((rows, width), LOW)] * 3,
        compiler_params=params("arbitrary"),
        cost_estimate=SHORT,
        name="qkv",
    )(order, *pieces, vectors, weight, tables)


def masked_rows(target, array):
    for head in range(array.shape[1] // HEAD):
        target[head * BLOCK : (head + 1) * BLOCK, :] = head_only(array, head)


def over_keys(first, block, tiles):
    begin = first[block]
    count = block + 1 - begin

    def pair(i, _):
        tiles(begin + 2 * i, 2)
        return 0

    def single(at, _):
        tiles(at, 1)
        return 0

    lax.fori_loop(0, count // 2, pair, 0)
    lax.fori_loop(block + 1 - count % 2, block + 1, single, 0)


def by_eight(array):
    return array.reshape(BLOCK // 8, 8, BLOCK)


def fwd_kernel(first, q, k, v, mixed, low_mixed, lse, keys, values, scores, top, total, out):
    step = pl.program_id(0)
    width = q.shape[1]
    heads = width // HEAD
    stack = heads * BLOCK
    masked_rows(keys.at[step], k[...])
    masked_rows(values.at[step], v[...])
    q_t = q[...].T
    top[...] = jnp.full_like(top, -1e30)
    total[...] = jnp.zeros_like(total)
    out[...] = jnp.zeros_like(out)

    def score(at, count):
        s = dot(keys[pl.ds(at, count)].reshape(count * stack, width), q_t)
        scores[pl.ds(at, count)] = s.reshape(count, stack, BLOCK)
        for head in range(heads):
            best = top[head]
            for tile in range(count):
                low = tile * stack + head * BLOCK
                best = jnp.maximum(best, jnp.max(by_eight(s[low : low + BLOCK]), axis=0))
            top[head] = best

    over_keys(first, step, score)
    peak = [jnp.max(top[head], axis=0, keepdims=True) for head in range(heads)]

    def mix(at, count):
        grown = []
        for tile in range(count):
            for head in range(heads):
                e = jnp.exp(scores[at + tile, head * BLOCK : (head + 1) * BLOCK] - peak[head])
                total[head] += jnp.sum(by_eight(e), axis=0)
                grown.append(e.astype(LOW))
        out[...] += dot(jnp.concatenate(grown, axis=0), values[pl.ds(at, count)].reshape(count * stack, width), TN)

    over_keys(first, step, mix)
    shares = []
    for head in range(heads):
        sums = jnp.sum(total[head], axis=0, keepdims=True)
        lse[head : head + 1, :] = peak[head] + jnp.log(sums)
        shares.append(jnp.broadcast_to(1.0 / sums, (HEAD, BLOCK)))
    result = out[...] * jnp.concatenate(shares, axis=0).T
    mixed[...] = result
    low_mixed[...] = result.astype(LOW)


def call_fwd(first, q, k, v):
    rows, width = q.shape
    heads = width // HEAD
    blocks = rows // BLOCK
    return pl.pallas_call(
        fwd_kernel,
        grid_spec=pltpu.PrefetchScalarGridSpec(
            num_scalar_prefetch=1,
            grid=(blocks,),
            in_specs=[pl.BlockSpec((BLOCK, width), lambda i, o: (i, 0))] * 3,
            out_specs=[
                pl.BlockSpec((BLOCK, width), lambda i, o: (i, 0)),
                pl.BlockSpec((BLOCK, width), lambda i, o: (i, 0)),
                pl.BlockSpec((heads, BLOCK), lambda i, o: (0, i)),
            ],
            scratch_shapes=[
                pltpu.VMEM((blocks, heads * BLOCK, width), LOW),
                pltpu.VMEM((blocks, heads * BLOCK, width), LOW),
                pltpu.VMEM((blocks, heads * BLOCK, BLOCK), F32),
                pltpu.VMEM((heads, 8, BLOCK), F32),
                pltpu.VMEM((heads, 8, BLOCK), F32),
                pltpu.VMEM((BLOCK, width), F32),
            ],
        ),
        out_shape=[
            jax.ShapeDtypeStruct((rows, width), F32),
            jax.ShapeDtypeStruct((rows, width), LOW),
            jax.ShapeDtypeStruct((heads, rows), F32),
        ],
        compiler_params=params("arbitrary"),
        cost_estimate=SHORT,
        name="attend",
    )(first, q, k, v)


def closed_rows(x, rows, to_norm, vectors, weight):
    n, scale = normed(x.astype(F32))
    d_h = dot(rows, weight, NT)
    bias = jnp.sum(d_h, axis=0, keepdims=True)
    gain = jnp.sum(d_h * n, axis=0, keepdims=True)
    e = d_h * vectors[0:1, :] + to_norm
    e = e - jnp.mean(e, axis=-1, keepdims=True) - n * jnp.mean(e * n, axis=-1, keepdims=True)
    return e * scale, gain, bias


def bwd_kernel(plan, per, groups, extra, first, q, k, v, d_mixed, mixed, lse, turn, to_norm, vectors, weight, *rest):
    many = 1 + max(piece for piece, _ in plan)
    pieces, outs, (even, odd, sums, ones), rest = rest[:many], rest[many : 2 * many], rest[2 * many : 2 * many + 4], rest[2 * many + 4 :]
    keys, values, sum_q, sum_k, sum_v, queries, seeds, h, d_rows, x, mat, wide, sem, x_sems, out_sems = rest
    step = pl.program_id(0)
    blocks = pl.num_programs(0)
    block = blocks - 1 - step
    width = k.shape[1]
    heads = width // HEAD
    stack = heads * BLOCK
    base = first.shape[0] - 1 - len(plan) // per
    group, order = first[base], lambda at: first[base + 1 + at]
    rows_of = lambda at: pl.ds(pl.multiple_of(at * BLOCK, BLOCK), BLOCK)
    own = rows_of(block)
    load = pltpu.make_async_copy(weight.at[:, :, pl.ds(0, 3 * width)], mat, sem.at[0])

    @pl.when(step == 0)
    def _():
        load.start()
        for at, (piece, start) in reversed(list(enumerate(plan))):
            place = order(at // per) * per + at % per
            pltpu.make_async_copy(pieces[piece].at[pl.ds(start, BLOCK)], x.at[rows_of(place)], x_sems.at[place]).start()

        def prepare(at, _):
            here = rows_of(at)
            masked_rows(keys.at[at], k[here, :])
            masked_rows(values.at[at], v[here, :])
            sum_k[here, :] = jnp.zeros((BLOCK, width), F32)
            sum_v[here, :] = jnp.zeros((BLOCK, width), F32)
            return 0

        lax.fori_loop(0, blocks, prepare, 0)
        sums[...] = jnp.zeros_like(sums)
        ones[...] = jnp.zeros_like(ones)

    q_own = q[...]
    s_own = d_mixed[...]
    masked_rows(queries, q_own)
    masked_rows(seeds, s_own)
    q_t = q_own.T
    s_t = s_own.T
    product_t = (s_own.astype(F32) * mixed[...]).T
    delta = [jnp.sum(product_t[head * HEAD : (head + 1) * HEAD, :], axis=0, keepdims=True) for head in range(heads)]
    log_total = [lse[head : head + 1, :] for head in range(heads)]
    sum_q[...] = jnp.zeros_like(sum_q)

    def tiles(at, count):
        key_rows = keys[pl.ds(at, count)].reshape(count * stack, width)
        s = dot(key_rows, q_t)
        d_p = dot(values[pl.ds(at, count)].reshape(count * stack, width), s_t)
        wide_probs, wide_scores, tall_scores = [], [], []
        for tile in range(count):
            low_probs, low_scores = [], []
            for head in range(heads):
                low = tile * stack + head * BLOCK
                probs = jnp.exp(s[low : low + BLOCK] - log_total[head])
                low_scores.append((probs * (d_p[low : low + BLOCK] - delta[head])).astype(LOW))
                low_probs.append(probs.astype(LOW))
            wide_probs.append(jnp.concatenate(low_probs, axis=1))
            wide_scores.append(jnp.concatenate(low_scores, axis=1))
            tall_scores += low_scores
        here = pl.ds(pl.multiple_of(at * BLOCK, BLOCK), count * BLOCK)
        sum_v[here, :] += dot(jnp.concatenate(wide_probs, axis=0), seeds[...])
        sum_k[here, :] += dot(jnp.concatenate(wide_scores, axis=0), queries[...])
        sum_q[...] += dot(jnp.concatenate(tall_scores, axis=0), key_rows, TN)

    over_keys(first, block, tiles)

    @pl.when(step == 0)
    def _():
        load.wait()

    pltpu.make_async_copy(x.at[own], x.at[own], x_sems.at[block]).wait()
    turns = (turn[:, :128], turn[:, 128:])
    done = jnp.concatenate(
        [
            (turned(sum_q[...], *turns, -1.0) * 0.125).astype(LOW),
            turned(sum_k[own, :], *turns, -1.0).astype(LOW),
            sum_v[own, :].astype(LOW),
        ],
        axis=1,
    )
    d_rows[own, :] = done
    sums[0:1, :] += jnp.sum(done.astype(F32), axis=0, keepdims=True)
    n, scale = normed(x[own, :].astype(F32))
    h[own, :] = (n * vectors[0:1, :] + vectors[1:2, :]).astype(LOW)
    d_h = dot(done, mat[...].reshape(h.shape[1], 3 * width), NT)
    ones[0:1, :] += jnp.sum(d_h * n, axis=0, keepdims=True)
    ones[1:2, :] += jnp.sum(d_h, axis=0, keepdims=True)
    e = d_h * vectors[0:1, :] + to_norm[...].astype(F32)
    e = e - jnp.mean(e, axis=-1, keepdims=True) - n * jnp.mean(e * n, axis=-1, keepdims=True)
    x[own, :] = (e * scale).astype(LOW)
    place = order(block // per) * per + block % per
    for at, (piece, start) in enumerate(plan):

        @pl.when(place == at)
        def _():
            pltpu.make_async_copy(x.at[own], outs[piece].at[pl.ds(start, BLOCK)], out_sems.at[block]).start()

    @pl.when(step == blocks - 1)
    def _():
        model = h.shape[1]
        grad = dot(h[...], d_rows[...], TN).astype(LOW)
        h[:model, : 3 * width] = grad
        size = model // groups
        for place in range(groups):
            to = odd if place % 2 else even
            to[place // 2, :size, :] = h[pl.ds(pl.multiple_of((group ^ place) * size, size), size), : 3 * width]
        if extra:
            members = len(plan) // per
            wide[...] = jnp.zeros_like(wide)
            for part in range(3):
                for at in range(width // 128):
                    row = (part * members + order(0)) * (width // 128) + at
                    low = part * width + at * 128
                    wide[pl.ds(row, 1), :] = sums[0:1, low : low + 128]
            for place in range(groups):
                to, near = odd if place % 2 else even, group ^ place
                lanes = pl.ds(pl.multiple_of(near * 128, 128), 128)
                lines = [ones[0:1, lanes], ones[1:2, lanes]] + [wide[pl.ds(3 * near + row, 1), :] for row in range(3)]
                to[place // 2, size:, :] = jnp.zeros((EXTRA, 3 * width), LOW)
                to[place // 2, size:, :128] = extra_rows(lines)
        for at in range(len(plan)):
            here = pl.ds(at * BLOCK, BLOCK)
            pltpu.make_async_copy(x.at[here], x.at[here], out_sems.at[at]).wait()


def call_bwd(first, q, k, v, d_mixed, mixed, lse, tables, to_norm, vectors, weight, pieces, out_shapes, groups, span, extra):
    rows, width = q.shape
    heads = width // HEAD
    blocks = rows // BLOCK
    model = to_norm.shape[1]
    grad = (groups // 2, model // groups + EXTRA * extra, 3 * width)
    back = lambda i, o: (blocks - 1 - i, 0)
    blocked = pl.BlockSpec((BLOCK, width), back)
    once = lambda shape: pl.BlockSpec(shape, lambda *_: (0,) * len(shape), pipeline_mode=pl.Buffered(1))
    plan = tuple((p, start) for block in plan_of(pieces, BLOCK) for p, start, _, _ in block)
    outs = [(grad, LOW), (grad, LOW), ((8, 3 * width), F32), ((8, model), F32)]
    return pl.pallas_call(
        functools.partial(bwd_kernel, plan, span // BLOCK, groups, extra),
        grid_spec=pltpu.PrefetchScalarGridSpec(
            num_scalar_prefetch=1,
            grid=(blocks,),
            in_specs=[blocked, once((rows, width)), once((rows, width)), blocked, blocked]
            + [pl.BlockSpec((heads, BLOCK), lambda i, o: (0, blocks - 1 - i)), pl.BlockSpec((BLOCK, 256), back)]
            + [pl.BlockSpec((BLOCK, model), back), whole(vectors.shape), HBM]
            + [HBM] * len(pieces),
            out_specs=[HBM] * len(out_shapes) + [whole(a) for a, _ in outs],
            scratch_shapes=[
                pltpu.VMEM((blocks, heads * BLOCK, width), LOW),
                pltpu.VMEM((blocks, heads * BLOCK, width), LOW),
                pltpu.VMEM((BLOCK, width), F32),
                pltpu.VMEM((rows, width), F32),
                pltpu.VMEM((rows, width), F32),
                pltpu.VMEM((heads * BLOCK, width), LOW),
                pltpu.VMEM((heads * BLOCK, width), LOW),
                pltpu.VMEM((rows, model), LOW),
                pltpu.VMEM((rows, 3 * width), LOW),
                pltpu.VMEM((rows, model), LOW),
                pltpu.VMEM(weight.shape[:2] + (3 * width,), LOW),
                pltpu.VMEM((3 * groups, 128), F32),
                pltpu.SemaphoreType.DMA((1,)),
                pltpu.SemaphoreType.DMA((blocks,)),
                pltpu.SemaphoreType.DMA((blocks,)),
            ],
        ),
        out_shape=list(out_shapes) + [jax.ShapeDtypeStruct(a, kind) for a, kind in outs],
        compiler_params=params("arbitrary"),
        cost_estimate=SHORT,
        name="attend_back",
    )(first, q, k, v, d_mixed, mixed, lse, tables, to_norm, vectors, weight, *pieces)


def extra_rows(lines):
    return jnp.concatenate(lines + [jnp.zeros((EXTRA - len(lines), 128), F32)], axis=0).astype(LOW)


def mlp_kernel(plan, out_plan, count, out_count, joined, chunk, order, *refs):
    x_pieces, cot_pieces, rest = refs[:count], refs[count : 2 * count], refs[2 * count :]
    mixed, vectors, rest = rest[0], rest[1], rest[2:]
    mats, rest = rest[: 1 if joined else 3], rest[1 if joined else 3 :]
    parts, rest = rest[:out_count], rest[out_count:]
    d_mixed, to_norm, rest = rest[0], rest[1], rest[2:]
    grads, rest = rest[: 1 if joined else 3], rest[1 if joined else 3 :]
    sums, normal, cot, active, d_up, own_mixed, g_out, staged, x_sems, cot_sems, out_sems = rest
    step = pl.program_id(0)
    steps = len(plan)
    span, width = own_mixed.shape[0] // steps, own_mixed.shape[1]
    model, units = normal.shape[1], active.shape[1]
    if joined:
        groups = mats[0].shape[0]
        cuts = [0, model // groups, (model + units) // groups, (model + units + width) // groups]
        w_up, w_down, w_out = (mats[0].at[:, pl.ds(cuts[i], cuts[i + 1] - cuts[i]), :] for i in range(3))
    else:
        w_up, w_down, w_out = mats
    as_up = lambda: w_up[...].reshape(model, units)
    as_down = lambda: w_down[...].reshape(units, model)
    as_out = lambda: w_out[...].reshape(width, model)

    @pl.when(step == 0)
    def _():
        fetch_all(plan, x_pieces, normal, x_sems)
        fetch_all(plan, cot_pieces, cot, cot_sems)
        sums[...] = jnp.zeros_like(sums)

    fetch(plan, step, x_pieces, normal, x_sems, False)
    fetch(plan, step, cot_pieces, cot, cot_sems, False)

    @pl.when(step < steps)
    def _():
        here = pl.ds(pl.multiple_of(step * span, span), span)
        n, _ = normed(normal[here, :].astype(F32))
        h = (n * vectors[2:3, :] + vectors[3:4, :]).astype(LOW)
        normal[here, :] = h
        dy = cot[here, :]
        own = mixed[pl.ds(pl.multiple_of(order[step] * span, span), span), :]
        own_mixed[here, :] = own
        d_mixed[...] = dot(dy, as_out(), NT).astype(LOW)
        up, down = as_up(), as_down()
        for low in range(0, units, chunk):
            cols = slice(low, low + chunk)
            u = dot(h, up[:, cols]) + vectors[6:7, cols]
            d_active = dot(dy, down[cols], NT)
            cdf = 0.5 * (1.0 + lax.erf(u * np.float32(np.sqrt(0.5))))
            slope = cdf + u * (jnp.exp(-0.5 * u * u) * np.float32(1.0 / np.sqrt(2.0 * np.pi)))
            active[here, cols] = (u * cdf).astype(LOW)
            back = (d_active * slope).astype(LOW)
            d_up[here, cols] = back
            sums[0:1, cols] += jnp.sum(back.astype(F32), axis=0, keepdims=True)
        staged[here, :] = (dot(active[here, :], down) + dot(own, as_out())).astype(LOW)
        d_h = dot(d_up[here, :], up, NT)
        sums[1:2, :model] += jnp.sum(d_h, axis=0, keepdims=True)
        sums[2:3, :model] += jnp.sum(d_h * n, axis=0, keepdims=True)
        to_norm[...] = (d_h * vectors[2:3, :]).astype(LOW)

        @pl.when(step == 0)
        def _():
            sums[3:4, :model] = jnp.sum(dy.astype(F32), axis=0, keepdims=True)

    store(out_plan, step, staged, parts, out_sems, True)

    @pl.when(step >= steps)
    def _():
        at = step - steps
        many = pl.num_programs(0) - steps

        @pl.when(at == 0)
        def _():
            g_out[...] = dot(own_mixed[...], cot[...], TN).astype(LOW)

        up_cols = pl.ds(pl.multiple_of(at * (model // many), 128), model // many)
        down_cols = pl.ds(pl.multiple_of(at * (units // many), 128), units // many)
        out_rows = pl.ds(pl.multiple_of(at * (width // many), 16), width // many)
        up_grad = dot(normal[:, up_cols], d_up[...], TN).astype(LOW)
        down_grad = dot(active[:, down_cols], cot[...], TN).astype(LOW)
        if joined:
            block = grads[0].shape[0]
            grads[0][:, cuts[0] : cuts[1], :] = up_grad.reshape(block, cuts[1], units)
            grads[0][:, cuts[1] : cuts[2], :] = down_grad.reshape(block, cuts[2] - cuts[1], model)
            grads[0][:, cuts[2] : cuts[3], :] = g_out[out_rows, :].reshape(block, cuts[3] - cuts[2], model)
            grads[0][:, cuts[3] :, :] = jnp.zeros((block, EXTRA, model), LOW)
            for place in range(block):
                lanes = pl.ds(pl.multiple_of((at * block + place) * 128, 128), 128)
                lines = [sums[row : row + 1, lanes] for row in (2, 1, 3, 0)]
                grads[0][place, cuts[3] :, :128] = extra_rows(lines)
        else:
            grads[0][...] = up_grad
            grads[1][...] = down_grad
            grads[2][...] = g_out[out_rows, :]

    @pl.when(step == pl.num_programs(0) - 1)
    def _():
        for at in range(steps):
            store(out_plan, at, staged, parts, out_sems, False)


def call_mlp(order, x_pieces, cot_pieces, mixed, vectors, mats, span, units, out_shapes):
    rows, width = mixed.shape
    model = x_pieces[0].shape[1]
    joined = len(mats) == 1
    plan, out_plan = plan_of(x_pieces, span), plan_of(out_shapes, span)
    steps, many = len(plan), 4
    count = len(x_pieces)
    there = lambda i, o: (o[jnp.minimum(i, steps - 1)], 0)
    later = lambda i, o: (jnp.maximum(i - steps, 0), 0)
    if joined:
        groups = mats[0].shape[0]
        grads = [(groups, (model + units + width) // groups + EXTRA, model)]
        grad_specs = [pl.BlockSpec((groups // many,) + grads[0][1:], lambda i, o: (jnp.maximum(i - steps, 0), 0, 0))]
    else:
        grads = [(model, units), (units, model), (width, model)]
        grad_specs = [pl.BlockSpec((a // many, b), later) for a, b in grads]
    sums = (8, max(model, units))
    return pl.pallas_call(
        functools.partial(mlp_kernel, plan, out_plan, count, len(out_shapes), joined, 256),
        grid_spec=pltpu.PrefetchScalarGridSpec(
            num_scalar_prefetch=1,
            grid=(steps + many,),
            in_specs=[HBM] * (2 * count)
            + [whole((rows, width)), whole(vectors.shape)]
            + [pl.BlockSpec(m.shape, lambda *_: (0, 0, 0), pipeline_mode=pl.Buffered(1)) for m in mats],
            out_specs=[HBM] * len(out_shapes)
            + [pl.BlockSpec((span, width), there), pl.BlockSpec((span, model), there)]
            + grad_specs
            + [whole(sums)],
            scratch_shapes=[
                pltpu.VMEM((rows, model), LOW),
                pltpu.VMEM((rows, model), LOW),
                pltpu.VMEM((rows, units), LOW),
                pltpu.VMEM((rows, units), LOW),
                pltpu.VMEM((rows, width), LOW),
                pltpu.VMEM((width, model), LOW),
                pltpu.VMEM((rows, model), LOW),
                pltpu.SemaphoreType.DMA((steps, 2)),
                pltpu.SemaphoreType.DMA((steps, 2)),
                pltpu.SemaphoreType.DMA((steps, 2)),
            ],
        ),
        out_shape=list(out_shapes)
        + [jax.ShapeDtypeStruct((rows, width), LOW), jax.ShapeDtypeStruct((rows, model), LOW)]
        + [jax.ShapeDtypeStruct(g, LOW) for g in grads]
        + [jax.ShapeDtypeStruct(sums, F32)],
        compiler_params=params("arbitrary"),
        cost_estimate=SHORT,
        name="mlp",
    )(order, *x_pieces, *cot_pieces, mixed, vectors, *mats)


def finish_kernel(shifts, wholes, base, *refs):
    refs, out = refs[:-1], refs[-1]
    shift, refs = refs[:shifts], refs[shifts:]
    common, parts = refs[:wholes], refs[wholes:]
    total = base[...].astype(F32)
    for ref in shift:
        total = total + ref[4:5, :] + ref[5:6, :]
    for ref in common:
        total = total + ref[...].astype(F32)
    if not parts:
        out[...] = total.astype(LOW)
    for at in range(2 if parts else 0):

        @pl.when(pl.program_id(0) == at)
        def _():
            more = total
            for ref in parts[at::2]:
                more = more + ref[...].astype(F32)
            out[...] = more.astype(LOW)


def call_finish(base, common, parts, vectors=(), cost=SHORT):
    rows, model = base.shape
    block = pl.BlockSpec((rows // 2, model), lambda i: (i, 0))
    return pl.pallas_call(
        functools.partial(finish_kernel, len(vectors), len(common)),
        grid=(2,),
        in_specs=[block] + [whole(v.shape) for v in vectors] + [block] * len(common) + [whole((rows // 2, model))] * len(parts),
        out_specs=block,
        out_shape=jax.ShapeDtypeStruct((rows, model), LOW),
        compiler_params=params("arbitrary"),
        cost_estimate=cost,
        name="finish",
    )(base, *vectors, *common, *parts)


def cut_kernel(members, member, first, second, third, *out):
    pieces, (down, line) = out[:members], out[members:]
    columns = first.shape[1]
    shard = pieces[0].shape[0] - EXTRA
    low = members * shard
    for bit, piece in enumerate(pieces):
        rows = pl.ds(pl.multiple_of((member[0] ^ bit) * shard, shard), shard)
        piece[:shard, :columns] = first[rows, :]
        piece[:shard, columns:] = (second[rows, :].astype(F32) + third[rows, :].astype(F32)).astype(LOW)
        piece[shard:, :columns] = first[first.shape[0] - EXTRA :, :]
        piece[shard:, columns:] = (second[low:, :].astype(F32) + third[low:, :].astype(F32)).astype(LOW)
    down[...] = first[low : low + down.shape[0], :].astype(F32)
    line[...] = first[first.shape[0] - EXTRA :, :128].astype(F32)[3, :]


def call_cut(member, first, second, third, members, shard):
    columns = first.shape[1]
    shapes = [jax.ShapeDtypeStruct((shard + EXTRA, columns + second.shape[1]), LOW)] * members + [
        jax.ShapeDtypeStruct((first.shape[0] - (members + 1) * shard - EXTRA, columns), F32),
        jax.ShapeDtypeStruct((128,), F32),
    ]
    return pl.pallas_call(
        functools.partial(cut_kernel, members),
        grid_spec=pltpu.PrefetchScalarGridSpec(
            num_scalar_prefetch=1,
            grid=(1,),
            in_specs=[whole(first.shape), whole(second.shape), whole(third.shape)],
            out_specs=[whole(a.shape) for a in shapes],
        ),
        out_shape=shapes,
        compiler_params=params("arbitrary"),
        cost_estimate=SHORT,
        name="cut",
    )(member, first, second, third)


def join_kernel(places, second, count, member, *refs):
    base, parts, refs, total = refs[0], refs[1 : 1 + count], refs[1 + count : -1], refs[-1]
    finish_kernel(0, 0, base, *parts, total)

    @pl.when(pl.program_id(0) == 0)
    def _():
        join_pieces(places, second, member, *refs)


def join_pieces(places, second, member, *refs):
    *pieces, last, up, qkv, out, gain_1, bias_1, gain_2, bias_2, end_bias, end_bias_2, shift = refs
    outs = up, qkv
    shard = up.shape[0]
    for bit, piece in enumerate(pieces):
        for block, (index, column, stride) in enumerate(places):
            start = pl.multiple_of(column + (member[0] ^ bit) * stride, 128)
            outs[index][:, pl.ds(start, 128)] = piece[:shard, block * 128 : (block + 1) * 128].astype(F32)
    out[...] = last[...].astype(F32)
    size = gain_1.shape[0]
    two, one = (sum(piece[shard:, low : low + 128].astype(F32) for piece in pieces) for low in (0, second))
    wide = jnp.concatenate([one[2:3, :], one[3:4, :], one[4:5, :]], axis=1)
    for at in range(len(pieces)):

        @pl.when(member[0] == at)
        def _():
            lanes = slice(at * size, (at + 1) * size)
            for ref, rows, row in ((gain_1, one, 0), (bias_1, one, 1), (gain_2, two, 0), (bias_2, two, 1), (end_bias, two, 2), (end_bias_2, two, 2)):
                ref[...] = rows[row, lanes]
            shift[...] = wide[0, 3 * at * size : 3 * (at + 1) * size]


def call_join(member, base, parts, pieces, last, places, second, columns):
    shard = pieces[0].shape[0] - EXTRA
    size = 128 // len(pieces)
    shapes = [(shard, c) for c in columns] + [last.shape] + [(size,)] * 6 + [(3 * size,)]
    block = pl.BlockSpec((base.shape[0] // 2, base.shape[1]), lambda i, o: (i, 0))
    return pl.pallas_call(
        functools.partial(join_kernel, tuple(places), second, len(parts)),
        grid_spec=pltpu.PrefetchScalarGridSpec(
            num_scalar_prefetch=1,
            grid=(2,),
            in_specs=[block] + [whole(p.shape) for p in (*parts, *pieces, last)],
            out_specs=[whole(a) for a in shapes] + [block],
        ),
        out_shape=[jax.ShapeDtypeStruct(a, F32) for a in shapes] + [jax.ShapeDtypeStruct(base.shape, LOW)],
        compiler_params=params("arbitrary"),
        cost_estimate=SHORT,
        name="join",
    )(member, base, *parts, *pieces, last)


def across(array, bit):
    size = lax.axis_size("fsdp")
    return lax.ppermute(array, "fsdp", [(i, i ^ bit) for i in range(size)])


def exchange(pieces):
    size = lax.axis_size("fsdp")
    if size != 4:
        return lax.all_to_all(pieces, "fsdp", split_axis=0, concat_axis=0, tiled=True)
    member = lax.axis_index("fsdp")
    out = pieces
    for bit in range(1, size):
        mine = lax.dynamic_index_in_dim(pieces, member ^ bit, 0, keepdims=False)
        out = lax.dynamic_update_index_in_dim(out, across(mine, bit), member ^ bit, 0)
    return out


def behind(array, *others):
    return lax.optimization_barrier((array, *others))[0]


def behind_all(arrays, *others):
    return tuple(behind(array, *others) for array in arrays)


def gather_rows(halves, near=None, *others):
    if lax.axis_size("fsdp") != 4:
        return [lax.all_gather(jnp.concatenate(halves, axis=0), "fsdp", axis=0, tiled=True)]
    one_low, two_high, one_high, two_low = near
    return [
        *halves, one_low, one_high, two_low, two_high,
        across(behind(one_low, *others), 2), across(behind(two_high, *others), 1),
    ]


def near_rows(halves):
    low, high = halves
    return across(low, 1), across(high, 2), across(high, 1), across(low, 2)


def hop(array, bit):
    return lax.ppermute(array, "dp", [(i, i ^ bit) for i in range(lax.axis_size("dp"))])


def scatter_step(blocks, far, bit):
    blocks = (blocks.astype(F32) + far.astype(F32)).astype(LOW)
    send = blocks[1::2]
    return blocks[0::2], hop(send, bit), send


def reduce_direct(parts):
    if len(parts) == 1:
        return (lax.psum_scatter(parts[0], "fsdp", scatter_dimension=0, tiled=True),)
    three = across(parts[3], 3)
    return parts[0], across(parts[1], 1), across(parts[2], 2), three


def total_over_all(vector):
    count = lax.axis_size("dp") * lax.axis_size("fsdp")
    step = 1
    while step < count:
        vector = vector + lax.ppermute(vector, ALL, [(i, i ^ step) for i in range(count)])
        step *= 2
    return vector


def swap_owner(array, back):
    groups, members = lax.axis_size("dp"), lax.axis_size("fsdp")
    pairs = [(m * groups + g, g * members + m) for g in range(groups) for m in range(members)]
    if back:
        pairs = [(b, a) for a, b in pairs]
    return lax.ppermute(array, ALL, pairs)


def gather_dp(array):
    return lax.all_gather(array, "dp", axis=0)


def scatter_dp(array):
    return lax.psum_scatter(array, "dp", scatter_dimension=0, tiled=True)


def rotary_tables(length):
    half = ROT // 2
    frequency = (np.float32(10000.0) ** (-(np.arange(half, dtype=np.float32) * np.float32(2.0)) / np.float32(ROT))).astype(np.float32)
    angles = (np.arange(length, dtype=np.float32)[:, None] * frequency[None, :]).astype(np.float32)
    cosine = np.cos(angles).astype(np.float32)
    sine = np.sin(angles).astype(np.float32)
    cos_row = np.ones((length, 128), np.float32)
    sine_row = np.zeros((length, 128), np.float32)
    for start in range(0, 128, HEAD):
        cos_row[:, start : start + half] = cosine
        cos_row[:, start + half : start + ROT] = cosine
        sine_row[:, start : start + half] = -sine
        sine_row[:, start + half : start + ROT] = sine
    return jnp.asarray(np.concatenate([cos_row, sine_row], axis=1))


def local(
    tokens, cotangent, doc_ids, norm1_gain, norm1_bias, norm2_gain, norm2_bias, qkv_weight, qkv_bias,
    out_weight, out_bias, up_weight, up_bias, down_weight, down_bias,
):
    groups, members = lax.axis_size("dp"), lax.axis_size("fsdp")
    group, member = lax.axis_index("dp"), lax.axis_index("fsdp")
    devices = groups * members
    rows, model = tokens.shape
    stream = rows * members
    shard = qkv_weight.shape[0]
    width = model // members
    units_dev = up_bias.shape[0]
    units = groups * units_dev
    paired = members == 4 and units_dev == 128 and units == model
    me = member.astype(jnp.int32).reshape(1)
    vectors_in = [norm1_gain, norm1_bias, norm2_gain, norm2_bias, out_bias, down_bias]

    half = rows // 2
    x_halves = [tokens[:half], tokens[half:]]
    cot_halves = [cotangent[:half], cotangent[half:]]
    if paired:
        packed = call_pack(me, qkv_weight, up_weight, (*vectors_in, qkv_bias, up_bias), members)
        arrived = [packed[0]] + [across(packed[bit], bit) for bit in range(1, members)]
        x_near = near_rows(behind_all(x_halves, *arrived[1:]))
        cut = 3 * width + 128
        first_in, up_in = call_place(me, arrived, cut)
        w_first = gather_dp(first_in)
        out_own = behind(swap_owner(behind(out_weight, first_in), False), *x_near[:2])
        mats = (gather_dp(jnp.concatenate([up_in, down_weight, out_own], axis=0)),)
        vectors = call_vectors(me, w_first, members, cut)
    else:
        qkv_cut = qkv_weight.reshape(shard, 3, members, width).transpose(2, 0, 1, 3).reshape(members, shard, 3 * width)
        up_cut = up_weight.reshape(shard, groups, members, units_dev).transpose(2, 0, 1, 3).reshape(members, shard, units)
        arrived = exchange(jnp.concatenate([qkv_cut, up_cut], axis=2)).reshape(members * shard, -1)
        w_first = gather_dp(arrived[:, : 3 * width])
        x_near = near_rows(x_halves) if members == 4 else None
        mats = (gather_dp(arrived[:, 3 * width :]), gather_dp(down_weight), gather_dp(swap_owner(out_weight, False)))
        full = [lax.all_gather(a, ALL, axis=0, tiled=True).astype(F32) for a in vectors_in]
        shift = lax.all_gather(qkv_bias, ALL, axis=0, tiled=True).astype(F32).reshape(3, members, width)
        shift = lax.dynamic_index_in_dim(shift, member, 1, keepdims=False)
        up_all = lax.all_gather(up_bias, "dp", axis=0, tiled=True).astype(F32)
        lines = full + [jnp.pad(a, (0, model - a.shape[0])) for a in (up_all, shift[0], shift[1], shift[2])]
        vectors = jnp.pad(jnp.stack(lines), ((0, 6), (0, 0)))

    x_pieces = gather_rows(x_halves, x_near)
    sources = jnp.arange(members, dtype=jnp.int32)
    order = sources ^ member if members == 4 else sources
    doc_row = doc_ids[0]
    first = jnp.sum((doc_row[None, :] < doc_row[:, None]).astype(jnp.int32), axis=1)
    first = jnp.concatenate([first, group.astype(jnp.int32).reshape(1), order])
    tables = rotary_tables(stream)

    q, k, v = call_qkv(order, x_pieces, vectors, w_first, tables, rows, width)
    cot_near = near_rows(behind_all(cot_halves, *x_near)) if members == 4 else None
    cot_pieces = gather_rows(cot_halves, cot_near, q)
    mixed, low_mixed, lse = call_fwd(first, q, k, v)
    out_sizes = [rows] * members if members == 4 else [stream]
    out_shapes = [jax.ShapeDtypeStruct((size, model), LOW) for size in out_sizes]
    results = call_mlp(
        order, x_pieces, cot_pieces, low_mixed, vectors, mats, rows, units, out_shapes
    )
    count = len(out_shapes)
    parts, (d_mixed, to_norm), grads, sums_two = results[:count], results[count : count + 2], results[count + 2 : -1], results[-1]
    scattered = scatter_dp(grads[0].reshape(-1, model)) if paired else None

    summed = reduce_direct(parts)
    sizes = [half] * (2 * members) if members == 4 else [stream]
    *pieces, even, odd, sums_qkv, ones = call_bwd(
        first, q, k, v, d_mixed, mixed, lse, tables, to_norm, vectors, w_first, x_pieces,
        [jax.ShapeDtypeStruct((size, model), LOW) for size in sizes], groups, rows, paired,
    )
    far, bit = hop(odd, 1), 2
    if members == 4:
        add = lambda a, b: (a.astype(F32) + b.astype(F32)).astype(LOW)
        own_low, own_high, one_low, one_high, two_low, two_high, three_low, three_high = pieces
        come = across(three_high, 2), across(three_low, 1)
        output = call_finish(tokens, summed, (), (vectors,), LONG)
        one_low, two_high = behind_all((one_low, two_high), output)
        near = across(one_low, 1), across(two_high, 2)
        blocks, far, send = scatter_step(even, behind(far, output), bit)
        come = behind_all(come, send)
        one_high, two_low = add(one_high, come[0]), add(two_low, come[1])
        near += across(one_high, 1), across(two_low, 2)
        parts = own_low, own_high, near[0], near[2], near[3], near[1]
        blocks, far, send = scatter_step(blocks, behind(far, one_high, two_low), 2 * bit)
        bit = 8
    if members != 4:
        blocks, far, _ = scatter_step(even, far, bit)
        bit = 4
        output = call_finish(tokens, summed, (), (vectors,))
        total = reduce_direct(pieces)[0]
        parts = total[:half], total[half:]
    while blocks.shape[0] > 1:
        (blocks, far, _), bit = scatter_step(blocks, far, bit), 2 * bit
    g_qkv = blocks[0], far[0]
    place = group * members + member
    if paired:
        *mixed_pieces, g_down, up_shift = call_cut(me, scattered, *g_qkv, members, shard)
        g_out = scattered[scattered.shape[0] - shard - EXTRA : scattered.shape[0] - EXTRA]
        g_out = swap_owner(behind(g_out, g_down), True)
        places = [(0, b * members * units_dev, units_dev) for b in range(groups)]
        places += [(1, part * model + low, width) for part in range(3) for low in range(0, width, 128)]
        arrived = [mixed_pieces[0]] + [across(mixed_pieces[bit], bit) for bit in range(1, members)]
        g_up, g_qkv, g_out, *mine, grad_tokens = call_join(
            me, cotangent, parts, arrived, g_out, places, model, (up_weight.shape[1], qkv_weight.shape[1])
        )
        mine.append(up_shift)
    else:
        grad_tokens = call_finish(cotangent, (), parts)
        g_up, g_down, g_out = [scatter_dp(g) for g in grads]
        g_down = g_down.astype(F32)
        g_up = exchange(g_up.reshape(members, shard, units))
        g_up = g_up.reshape(members, shard, groups, units_dev).transpose(1, 2, 0, 3).reshape(shard, -1).astype(F32)
        g_qkv = (g_qkv[0].astype(F32) + g_qkv[1].astype(F32)).astype(LOW)
        g_qkv = exchange(g_qkv.reshape(members, shard, 3 * width)).reshape(members, shard, 1, 3, width)
        g_qkv = g_qkv.transpose(1, 3, 0, 2, 4).reshape(shard, -1).astype(F32)
        thirds = jnp.concatenate([a[0].reshape(3, 1, width) for a in [sums_qkv]], axis=2)
        wide_qkv = lax.dynamic_update_index_in_dim(jnp.zeros((3, members, width), F32), thirds, member, 1)
        wide_up = lax.dynamic_update_index_in_dim(
            jnp.zeros((groups, members, units_dev), F32), sums_two[0, :units].reshape(groups, 1, units_dev), member, 1
        )
        summed = total_over_all(jnp.concatenate([
            ones[0], ones[1], sums_two[2], sums_two[1], sums_two[3], wide_qkv.reshape(-1), wide_up.reshape(-1),
        ]))
        mine, start = [], 0
        for size in [model] * 5 + [3 * model, groups * members * units_dev]:
            mine.append(lax.dynamic_slice_in_dim(summed, start + place * (size // devices), size // devices))
            start += size
        mine.insert(5, mine[4])
    gain_1, bias_1, gain_2, bias_2, end_bias, end_bias_2, qkv_shift, up_shift = mine
    if not paired:
        g_out = swap_owner(g_out, True).astype(F32)
    return (
        output, grad_tokens, gain_1, bias_1, gain_2, bias_2, g_qkv, qkv_shift, g_out, end_bias, g_up, up_shift, g_down, end_bias_2,
    )


def solution(mesh):
    row, vec = P(ALL, None), P(ALL)
    return jax.shard_map(
        local,
        mesh=mesh,
        in_specs=(row, row, P("dp", None), vec, vec, vec, vec, row, vec, row, vec, row, vec, row, vec),
        out_specs=(row, row, vec, vec, vec, vec, row, vec, row, vec, row, vec, row, vec),
        check_vma=False,
    )
```

```python
import functools

import jax
import jax.numpy as jnp
import numpy as np
from jax import lax
from jax.experimental import pallas as pl
from jax.experimental.pallas import tpu as pltpu
from jax.sharding import PartitionSpec as P

HEADS = 16
HEAD = 64
ROT = 16
BLOCK = 256
EPS = 1e-05
ALL = ("dp", "fsdp")
LONG = pl.CostEstimate(flops=2 * 10**10, bytes_accessed=10**7, transcendentals=0)
SHORT = pl.CostEstimate(flops=0, bytes_accessed=0, transcendentals=0)
F32 = jnp.float32
LOW = jnp.bfloat16


def dot(left, right, contract=((1,), (0,))):
    return lax.dot_general(left, right, (contract, ((), ())), preferred_element_type=F32)


NT = ((1,), (1,))
TN = ((0,), (0,))


def normed(x_rows):
    centre = x_rows - jnp.mean(x_rows, axis=-1, keepdims=True)
    spread = jnp.mean(centre * centre, axis=-1, keepdims=True)
    scale = lax.rsqrt(spread + EPS)
    return centre * scale, scale


def turned(z, cosine, sine, sign):
    groups = []
    for start in range(0, z.shape[1], 128):
        part = z[:, start : start + 128]
        ahead = pltpu.roll(part, 128 - ROT // 2, 1)
        behind = pltpu.roll(part, ROT // 2, 1)
        lane = lax.broadcasted_iota(jnp.int32, part.shape, 1) & (HEAD - 1)
        groups.append(part * cosine + sign * (jnp.where(lane < ROT // 2, ahead, behind) * sine))
    return groups[0] if len(groups) == 1 else jnp.concatenate(groups, axis=1)


def head_only(array, head):
    lane = lax.broadcasted_iota(jnp.int32, array.shape, 1)
    keep = (lane >= head * HEAD) & (lane < (head + 1) * HEAD)
    return jnp.where(keep, array, jnp.zeros_like(array))


def params(*order):
    return pltpu.CompilerParams(vmem_limit_bytes=60 * 1024 * 1024, dimension_semantics=order)


def whole(shape):
    return pl.BlockSpec(shape, lambda *_: (0,) * len(shape))


HBM = pl.BlockSpec(memory_space=pl.ANY)
EXTRA = 16


def fetch(plan, step, refs, target, sems, begin):
    for at, pieces in enumerate(plan):

        @pl.when(step == at)
        def _():
            for index, (ref, start, put, size) in enumerate(pieces):
                copy = pltpu.make_async_copy(
                    refs[ref].at[pl.ds(start, size)], target.at[pl.ds(put, size)], sems.at[at, index]
                )
                if begin:
                    copy.start()
                else:
                    copy.wait()


def fetch_all(plan, refs, target, sems):
    for at in range(len(plan)):
        fetch(plan, at, refs, target, sems, True)


def plan_of(pieces, span):
    plan, total = [], sum(p.shape[0] for p in pieces)
    for low in range(0, total, span):
        taken, at = [], 0
        for index, piece in enumerate(pieces):
            a, b = max(low, at), min(low + span, at + piece.shape[0])
            if a < b:
                taken.append((index, a - at, a, b - a))
            at += piece.shape[0]
        plan.append(tuple(taken))
    return tuple(plan)


def store(plan, step, source, refs, sems, begin):
    for at, pieces in enumerate(plan):

        @pl.when(step == at)
        def _():
            for index, (ref, start, put, size) in enumerate(pieces):
                copy = pltpu.make_async_copy(
                    source.at[pl.ds(put, size)], refs[ref].at[pl.ds(start, size)], sems.at[at, index]
                )
                if begin:
                    copy.start()
                else:
                    copy.wait()


def pack_kernel(members, member, qkv, up, *refs):
    vectors, (qkv_bias, up_bias), out, (small, wide) = refs[:6], refs[6:8], refs[8:-2], refs[-2:]
    width = qkv.shape[1] // 3 // members
    units_dev = up_bias.shape[0]
    groups = up.shape[1] // units_dev // members
    size = 128 // members
    small[...] = jnp.zeros_like(small)
    wide[...] = jnp.zeros_like(wide)
    for at in range(members):

        @pl.when(member[0] == at)
        def _():
            for row, vector in enumerate(vectors):
                small[row, at * size : (at + 1) * size] = vector[...].astype(F32)
            wide[0, 3 * at * size : 3 * (at + 1) * size] = qkv_bias[...].astype(F32)

    for row in range(3):
        small[6 + row : 7 + row, :] = wide[0:1, row * 128 : (row + 1) * 128]
    small[9, :] = up_bias[...].astype(F32)
    block = small[...].astype(LOW)
    for bit in range(members):
        to = member[0] ^ bit
        for part in range(3):
            start = pl.multiple_of((part * members + to) * width, 128)
            out[bit][:, part * width : (part + 1) * width] = qkv[:, pl.ds(start, width)]
        out[bit][:, 3 * width : 3 * width + 128] = jnp.zeros((qkv.shape[0], 128), LOW)
        out[bit][0:16, 3 * width : 3 * width + 128] = block
        for group in range(groups):
            start = pl.multiple_of((group * members + to) * units_dev, 128)
            low = 3 * width + 128 + group * units_dev
            out[bit][:, low : low + units_dev] = up[:, pl.ds(start, units_dev)]


def call_pack(member, qkv, up, vectors, members):
    shard = qkv.shape[0]
    columns = (qkv.shape[1] + up.shape[1]) // members + 128
    return pl.pallas_call(
        functools.partial(pack_kernel, members),
        grid_spec=pltpu.PrefetchScalarGridSpec(
            num_scalar_prefetch=1,
            grid=(1,),
            in_specs=[whole(a.shape) for a in (qkv, up, *vectors)],
            out_specs=[whole((shard, columns))] * members,
            scratch_shapes=[pltpu.VMEM((16, 128), F32), pltpu.VMEM((8, 384), F32)],
        ),
        out_shape=[jax.ShapeDtypeStruct((shard, columns), LOW)] * members,
        compiler_params=params("arbitrary"),
        cost_estimate=SHORT,
        name="pack",
    )(member, qkv, up, *vectors)


def place_kernel(cut, member, *refs):
    *pieces, first, second = refs
    shard = pieces[0].shape[0]
    for bit, piece in enumerate(pieces):
        rows = pl.ds(pl.multiple_of((member[0] ^ bit) * shard, shard), shard)
        first[rows, :] = piece[:, :cut]
        second[rows, :] = piece[:, cut:]


def call_place(member, pieces, cut):
    members, (shard, columns) = len(pieces), pieces[0].shape
    shapes = [(members * shard, cut), (members * shard, columns - cut)]
    return pl.pallas_call(
        functools.partial(place_kernel, cut),
        grid_spec=pltpu.PrefetchScalarGridSpec(
            num_scalar_prefetch=1,
            grid=(1,),
            in_specs=[whole(p.shape) for p in pieces],
            out_specs=[whole(a) for a in shapes],
        ),
        out_shape=[jax.ShapeDtypeStruct(a, LOW) for a in shapes],
        compiler_params=params("arbitrary"),
        cost_estimate=SHORT,
        name="place",
    )(member, *pieces)


def vectors_kernel(members, member, gathered, out, wide):
    groups, rows, _ = gathered.shape
    shard = rows // members
    model = groups * 128
    out[...] = jnp.zeros_like(out)
    for group in range(groups):
        blocks = [gathered[group, m * shard : m * shard + 16, :].astype(F32) for m in range(members)]
        block = blocks[0]
        for other in blocks[1:]:
            block = block + other
        lanes = slice(group * 128, (group + 1) * 128)
        for row in range(6):
            out[row : row + 1, lanes] = block[row : row + 1, :]
        for row in range(3):
            low = group * 384 + row * 128
            wide[0:1, low : low + 128] = block[6 + row : 7 + row, :]
        own = jnp.zeros((1, 128), F32)
        for m in range(members):
            own = own + jnp.where(member[0] == m, blocks[m][9:10, :], 0.0)
        out[6:7, lanes] = own
    width = model // members
    for part in range(3):
        start = pl.multiple_of(part * model + member[0] * width, 128)
        out[7 + part : 8 + part, :width] = wide[0:1, pl.ds(start, width)]


def call_vectors(member, gathered, members, cut):
    groups, rows, _ = gathered.shape
    model = groups * 128
    return pl.pallas_call(
        functools.partial(vectors_kernel, members),
        grid_spec=pltpu.PrefetchScalarGridSpec(
            num_scalar_prefetch=1,
            grid=(1,),
            in_specs=[pl.BlockSpec((groups, rows, 128), lambda i, o: (0, 0, cut // 128 - 1))],
            out_specs=whole((16, model)),
            scratch_shapes=[pltpu.VMEM((8, 3 * model), F32)],
        ),
        out_shape=jax.ShapeDtypeStruct((16, model), F32),
        compiler_params=params("arbitrary"),
        cost_estimate=SHORT,
        name="vectors",
    )(member, gathered)


def qkv_kernel(plan, count, order, *refs):
    pieces, rest = refs[:count], refs[count:]
    vectors, weight, turn, q, k, v, x, sems = rest
    step = pl.program_id(0)
    width = q.shape[1]
    span = q.shape[0]
    model = x.shape[1]

    @pl.when(step == 0)
    def _():
        fetch_all(plan, pieces, x, sems)

    fetch(plan, step, pieces, x, sems, False)
    n, _ = normed(x[pl.ds(pl.multiple_of(step * span, span), span), :].astype(F32))
    h = (n * vectors[0:1, :] + vectors[1:2, :]).astype(LOW)
    tables = (turn[:, :128], turn[:, 128:])
    rows = dot(h, weight[...].reshape(model, 3 * width))
    q[...] = (turned(rows[:, :width] + vectors[7:8, :width], *tables, 1.0) * 0.125).astype(LOW)
    k[...] = turned(rows[:, width : 2 * width] + vectors[8:9, :width], *tables, 1.0).astype(LOW)
    v[...] = (rows[:, 2 * width :] + vectors[9:10, :width]).astype(LOW)


def call_qkv(order, pieces, vectors, weight, tables, span, width):
    model = pieces[0].shape[1]
    plan = plan_of(pieces, span)
    rows = span * len(plan)
    there = lambda i, o: (o[i], 0)
    return pl.pallas_call(
        functools.partial(qkv_kernel, plan, len(pieces)),
        grid_spec=pltpu.PrefetchScalarGridSpec(
            num_scalar_prefetch=1,
            grid=(rows // span,),
            in_specs=[HBM] * len(pieces)
            + [whole(vectors.shape), whole(weight.shape[:2] + (3 * width,))]
            + [pl.BlockSpec((span, 256), there)],
            out_specs=[pl.BlockSpec((span, width), there)] * 3,
            scratch_shapes=[pltpu.VMEM((rows, model), LOW), pltpu.SemaphoreType.DMA((len(plan), 2))],
        ),
        out_shape=[jax.ShapeDtypeStruct((rows, width), LOW)] * 3,
        compiler_params=params("arbitrary"),
        cost_estimate=SHORT,
        name="qkv",
    )(order, *pieces, vectors, weight, tables)


def masked_rows(target, array):
    for head in range(array.shape[1] // HEAD):
        target[head * BLOCK : (head + 1) * BLOCK, :] = head_only(array, head)


def over_keys(first, block, tiles):
    begin = first[block]
    count = block + 1 - begin

    def pair(i, _):
        tiles(begin + 2 * i, 2)
        return 0

    def single(at, _):
        tiles(at, 1)
        return 0

    lax.fori_loop(0, count // 2, pair, 0)
    lax.fori_loop(block + 1 - count % 2, block + 1, single, 0)


def by_eight(array):
    return array.reshape(BLOCK // 8, 8, BLOCK)


def fwd_kernel(first, q, k, v, mixed, low_mixed, lse, keys, values, scores, top, total, out):
    step = pl.program_id(0)
    width = q.shape[1]
    heads = width // HEAD
    stack = heads * BLOCK
    masked_rows(keys.at[step], k[...])
    masked_rows(values.at[step], v[...])
    q_t = q[...].T
    top[...] = jnp.full_like(top, -1e30)
    total[...] = jnp.zeros_like(total)
    out[...] = jnp.zeros_like(out)

    def score(at, count):
        s = dot(keys[pl.ds(at, count)].reshape(count * stack, width), q_t)
        scores[pl.ds(at, count)] = s.reshape(count, stack, BLOCK)
        for head in range(heads):
            best = top[head]
            for tile in range(count):
                low = tile * stack + head * BLOCK
                best = jnp.maximum(best, jnp.max(by_eight(s[low : low + BLOCK]), axis=0))
            top[head] = best

    over_keys(first, step, score)
    peak = [jnp.max(top[head], axis=0, keepdims=True) for head in range(heads)]

    def mix(at, count):
        grown = []
        for tile in range(count):
            for head in range(heads):
                e = jnp.exp(scores[at + tile, head * BLOCK : (head + 1) * BLOCK] - peak[head])
                total[head] += jnp.sum(by_eight(e), axis=0)
                grown.append(e.astype(LOW))
        out[...] += dot(jnp.concatenate(grown, axis=0), values[pl.ds(at, count)].reshape(count * stack, width), TN)

    over_keys(first, step, mix)
    shares = []
    for head in range(heads):
        sums = jnp.sum(total[head], axis=0, keepdims=True)
        lse[head : head + 1, :] = peak[head] + jnp.log(sums)
        shares.append(jnp.broadcast_to(1.0 / sums, (HEAD, BLOCK)))
    result = out[...] * jnp.concatenate(shares, axis=0).T
    mixed[...] = result
    low_mixed[...] = result.astype(LOW)


def call_fwd(first, q, k, v):
    rows, width = q.shape
    heads = width // HEAD
    blocks = rows // BLOCK
    return pl.pallas_call(
        fwd_kernel,
        grid_spec=pltpu.PrefetchScalarGridSpec(
            num_scalar_prefetch=1,
            grid=(blocks,),
            in_specs=[pl.BlockSpec((BLOCK, width), lambda i, o: (i, 0))] * 3,
            out_specs=[
                pl.BlockSpec((BLOCK, width), lambda i, o: (i, 0)),
                pl.BlockSpec((BLOCK, width), lambda i, o: (i, 0)),
                pl.BlockSpec((heads, BLOCK), lambda i, o: (0, i)),
            ],
            scratch_shapes=[
                pltpu.VMEM((blocks, heads * BLOCK, width), LOW),
                pltpu.VMEM((blocks, heads * BLOCK, width), LOW),
                pltpu.VMEM((blocks, heads * BLOCK, BLOCK), F32),
                pltpu.VMEM((heads, 8, BLOCK), F32),
                pltpu.VMEM((heads, 8, BLOCK), F32),
                pltpu.VMEM((BLOCK, width), F32),
            ],
        ),
        out_shape=[
            jax.ShapeDtypeStruct((rows, width), F32),
            jax.ShapeDtypeStruct((rows, width), LOW),
            jax.ShapeDtypeStruct((heads, rows), F32),
        ],
        compiler_params=params("arbitrary"),
        cost_estimate=SHORT,
        name="attend",
    )(first, q, k, v)


def closed_rows(x, rows, to_norm, vectors, weight):
    n, scale = normed(x.astype(F32))
    d_h = dot(rows, weight, NT)
    bias = jnp.sum(d_h, axis=0, keepdims=True)
    gain = jnp.sum(d_h * n, axis=0, keepdims=True)
    e = d_h * vectors[0:1, :] + to_norm
    e = e - jnp.mean(e, axis=-1, keepdims=True) - n * jnp.mean(e * n, axis=-1, keepdims=True)
    return e * scale, gain, bias


def bwd_kernel(plan, per, groups, extra, first, q, k, v, d_mixed, mixed, lse, turn, to_norm, vectors, weight, *rest):
    many = 1 + max(piece for piece, _ in plan)
    pieces, outs, (even, odd, sums, ones), rest = rest[:many], rest[many : 2 * many], rest[2 * many : 2 * many + 4], rest[2 * many + 4 :]
    keys, values, sum_q, sum_k, sum_v, queries, seeds, h, d_rows, x, mat, wide, sem, x_sems, out_sems = rest
    step = pl.program_id(0)
    blocks = pl.num_programs(0)
    block = blocks - 1 - step
    width = k.shape[1]
    heads = width // HEAD
    stack = heads * BLOCK
    base = first.shape[0] - 1 - len(plan) // per
    group, order = first[base], lambda at: first[base + 1 + at]
    rows_of = lambda at: pl.ds(pl.multiple_of(at * BLOCK, BLOCK), BLOCK)
    own = rows_of(block)
    load = pltpu.make_async_copy(weight.at[:, :, pl.ds(0, 3 * width)], mat, sem.at[0])

    @pl.when(step == 0)
    def _():
        load.start()
        for at, (piece, start) in reversed(list(enumerate(plan))):
            place = order(at // per) * per + at % per
            pltpu.make_async_copy(pieces[piece].at[pl.ds(start, BLOCK)], x.at[rows_of(place)], x_sems.at[place]).start()

        def prepare(at, _):
            here = rows_of(at)
            masked_rows(keys.at[at], k[here, :])
            masked_rows(values.at[at], v[here, :])
            sum_k[here, :] = jnp.zeros((BLOCK, width), F32)
            sum_v[here, :] = jnp.zeros((BLOCK, width), F32)
            return 0

        lax.fori_loop(0, blocks, prepare, 0)
        sums[...] = jnp.zeros_like(sums)
        ones[...] = jnp.zeros_like(ones)

    q_own = q[...]
    s_own = d_mixed[...]
    masked_rows(queries, q_own)
    masked_rows(seeds, s_own)
    q_t = q_own.T
    s_t = s_own.T
    product_t = (s_own.astype(F32) * mixed[...]).T
    delta = [jnp.sum(product_t[head * HEAD : (head + 1) * HEAD, :], axis=0, keepdims=True) for head in range(heads)]
    log_total = [lse[head : head + 1, :] for head in range(heads)]
    sum_q[...] = jnp.zeros_like(sum_q)

    def tiles(at, count):
        key_rows = keys[pl.ds(at, count)].reshape(count * stack, width)
        s = dot(key_rows, q_t)
        d_p = dot(values[pl.ds(at, count)].reshape(count * stack, width), s_t)
        wide_probs, wide_scores, tall_scores = [], [], []
        for tile in range(count):
            low_probs, low_scores = [], []
            for head in range(heads):
                low = tile * stack + head * BLOCK
                probs = jnp.exp(s[low : low + BLOCK] - log_total[head])
                low_scores.append((probs * (d_p[low : low + BLOCK] - delta[head])).astype(LOW))
                low_probs.append(probs.astype(LOW))
            wide_probs.append(jnp.concatenate(low_probs, axis=1))
            wide_scores.append(jnp.concatenate(low_scores, axis=1))
            tall_scores += low_scores
        here = pl.ds(pl.multiple_of(at * BLOCK, BLOCK), count * BLOCK)
        sum_v[here, :] += dot(jnp.concatenate(wide_probs, axis=0), seeds[...])
        sum_k[here, :] += dot(jnp.concatenate(wide_scores, axis=0), queries[...])
        sum_q[...] += dot(jnp.concatenate(tall_scores, axis=0), key_rows, TN)

    over_keys(first, block, tiles)

    @pl.when(step == 0)
    def _():
        load.wait()

    pltpu.make_async_copy(x.at[own], x.at[own], x_sems.at[block]).wait()
    turns = (turn[:, :128], turn[:, 128:])
    done = jnp.concatenate(
        [
            (turned(sum_q[...], *turns, -1.0) * 0.125).astype(LOW),
            turned(sum_k[own, :], *turns, -1.0).astype(LOW),
            sum_v[own, :].astype(LOW),
        ],
        axis=1,
    )
    d_rows[own, :] = done
    sums[0:1, :] += jnp.sum(done.astype(F32), axis=0, keepdims=True)
    n, scale = normed(x[own, :].astype(F32))
    h[own, :] = (n * vectors[0:1, :] + vectors[1:2, :]).astype(LOW)
    d_h = dot(done, mat[...].reshape(h.shape[1], 3 * width), NT)
    ones[0:1, :] += jnp.sum(d_h * n, axis=0, keepdims=True)
    ones[1:2, :] += jnp.sum(d_h, axis=0, keepdims=True)
    e = d_h * vectors[0:1, :] + to_norm[...].astype(F32)
    e = e - jnp.mean(e, axis=-1, keepdims=True) - n * jnp.mean(e * n, axis=-1, keepdims=True)
    x[own, :] = (e * scale).astype(LOW)
    place = order(block // per) * per + block % per
    for at, (piece, start) in enumerate(plan):

        @pl.when(place == at)
        def _():
            pltpu.make_async_copy(x.at[own], outs[piece].at[pl.ds(start, BLOCK)], out_sems.at[block]).start()

    @pl.when(step == blocks - 1)
    def _():
        model = h.shape[1]
        grad = dot(h[...], d_rows[...], TN).astype(LOW)
        h[:model, : 3 * width] = grad
        size = model // groups
        for place in range(groups):
            to = odd if place % 2 else even
            to[place // 2, :size, :] = h[pl.ds(pl.multiple_of((group ^ place) * size, size), size), : 3 * width]
        if extra:
            members = len(plan) // per
            wide[...] = jnp.zeros_like(wide)
            for part in range(3):
                for at in range(width // 128):
                    row = (part * members + order(0)) * (width // 128) + at
                    low = part * width + at * 128
                    wide[pl.ds(row, 1), :] = sums[0:1, low : low + 128]
            for place in range(groups):
                to, near = odd if place % 2 else even, group ^ place
                lanes = pl.ds(pl.multiple_of(near * 128, 128), 128)
                lines = [ones[0:1, lanes], ones[1:2, lanes]] + [wide[pl.ds(3 * near + row, 1), :] for row in range(3)]
                to[place // 2, size:, :] = jnp.zeros((EXTRA, 3 * width), LOW)
                to[place // 2, size:, :128] = extra_rows(lines)
        for at in range(len(plan)):
            here = pl.ds(at * BLOCK, BLOCK)
            pltpu.make_async_copy(x.at[here], x.at[here], out_sems.at[at]).wait()


def call_bwd(first, q, k, v, d_mixed, mixed, lse, tables, to_norm, vectors, weight, pieces, out_shapes, groups, span, extra):
    rows, width = q.shape
    heads = width // HEAD
    blocks = rows // BLOCK
    model = to_norm.shape[1]
    grad = (groups // 2, model // groups + EXTRA * extra, 3 * width)
    back = lambda i, o: (blocks - 1 - i, 0)
    blocked = pl.BlockSpec((BLOCK, width), back)
    once = lambda shape: pl.BlockSpec(shape, lambda *_: (0,) * len(shape), pipeline_mode=pl.Buffered(1))
    plan = tuple((p, start) for block in plan_of(pieces, BLOCK) for p, start, _, _ in block)
    outs = [(grad, LOW), (grad, LOW), ((8, 3 * width), F32), ((8, model), F32)]
    return pl.pallas_call(
        functools.partial(bwd_kernel, plan, span // BLOCK, groups, extra),
        grid_spec=pltpu.PrefetchScalarGridSpec(
            num_scalar_prefetch=1,
            grid=(blocks,),
            in_specs=[blocked, once((rows, width)), once((rows, width)), blocked, blocked]
            + [pl.BlockSpec((heads, BLOCK), lambda i, o: (0, blocks - 1 - i)), pl.BlockSpec((BLOCK, 256), back)]
            + [pl.BlockSpec((BLOCK, model), back), whole(vectors.shape), HBM]
            + [HBM] * len(pieces),
            out_specs=[HBM] * len(out_shapes) + [whole(a) for a, _ in outs],
            scratch_shapes=[
                pltpu.VMEM((blocks, heads * BLOCK, width), LOW),
                pltpu.VMEM((blocks, heads * BLOCK, width), LOW),
                pltpu.VMEM((BLOCK, width), F32),
                pltpu.VMEM((rows, width), F32),
                pltpu.VMEM((rows, width), F32),
                pltpu.VMEM((heads * BLOCK, width), LOW),
                pltpu.VMEM((heads * BLOCK, width), LOW),
                pltpu.VMEM((rows, model), LOW),
                pltpu.VMEM((rows, 3 * width), LOW),
                pltpu.VMEM((rows, model), LOW),
                pltpu.VMEM(weight.shape[:2] + (3 * width,), LOW),
                pltpu.VMEM((3 * groups, 128), F32),
                pltpu.SemaphoreType.DMA((1,)),
                pltpu.SemaphoreType.DMA((blocks,)),
                pltpu.SemaphoreType.DMA((blocks,)),
            ],
        ),
        out_shape=list(out_shapes) + [jax.ShapeDtypeStruct(a, kind) for a, kind in outs],
        compiler_params=params("arbitrary"),
        cost_estimate=SHORT,
        name="attend_back",
    )(first, q, k, v, d_mixed, mixed, lse, tables, to_norm, vectors, weight, *pieces)


def extra_rows(lines):
    return jnp.concatenate(lines + [jnp.zeros((EXTRA - len(lines), 128), F32)], axis=0).astype(LOW)


def mlp_kernel(plan, out_plan, count, out_count, joined, chunk, order, *refs):
    x_pieces, cot_pieces, rest = refs[:count], refs[count : 2 * count], refs[2 * count :]
    mixed, vectors, rest = rest[0], rest[1], rest[2:]
    mats, rest = rest[: 1 if joined else 3], rest[1 if joined else 3 :]
    parts, rest = rest[:out_count], rest[out_count:]
    d_mixed, to_norm, rest = rest[0], rest[1], rest[2:]
    grads, rest = rest[: 1 if joined else 3], rest[1 if joined else 3 :]
    sums, normal, cot, active, d_up, own_mixed, g_out, staged, x_sems, cot_sems, out_sems = rest
    step = pl.program_id(0)
    steps = len(plan)
    span, width = own_mixed.shape[0] // steps, own_mixed.shape[1]
    model, units = normal.shape[1], active.shape[1]
    if joined:
        groups = mats[0].shape[0]
        cuts = [0, model // groups, (model + units) // groups, (model + units + width) // groups]
        w_up, w_down, w_out = (mats[0].at[:, pl.ds(cuts[i], cuts[i + 1] - cuts[i]), :] for i in range(3))
    else:
        w_up, w_down, w_out = mats
    as_up = lambda: w_up[...].reshape(model, units)
    as_down = lambda: w_down[...].reshape(units, model)
    as_out = lambda: w_out[...].reshape(width, model)

    @pl.when(step == 0)
    def _():
        fetch_all(plan, x_pieces, normal, x_sems)
        fetch_all(plan, cot_pieces, cot, cot_sems)
        sums[...] = jnp.zeros_like(sums)

    fetch(plan, step, x_pieces, normal, x_sems, False)
    fetch(plan, step, cot_pieces, cot, cot_sems, False)

    @pl.when(step < steps)
    def _():
        here = pl.ds(pl.multiple_of(step * span, span), span)
        n, _ = normed(normal[here, :].astype(F32))
        h = (n * vectors[2:3, :] + vectors[3:4, :]).astype(LOW)
        normal[here, :] = h
        dy = cot[here, :]
        own = mixed[pl.ds(pl.multiple_of(order[step] * span, span), span), :]
        own_mixed[here, :] = own
        d_mixed[...] = dot(dy, as_out(), NT).astype(LOW)
        up, down = as_up(), as_down()
        for low in range(0, units, chunk):
            cols = slice(low, low + chunk)
            u = dot(h, up[:, cols]) + vectors[6:7, cols]
            d_active = dot(dy, down[cols], NT)
            cdf = 0.5 * (1.0 + lax.erf(u * np.float32(np.sqrt(0.5))))
            slope = cdf + u * (jnp.exp(-0.5 * u * u) * np.float32(1.0 / np.sqrt(2.0 * np.pi)))
            active[here, cols] = (u * cdf).astype(LOW)
            back = (d_active * slope).astype(LOW)
            d_up[here, cols] = back
            sums[0:1, cols] += jnp.sum(back.astype(F32), axis=0, keepdims=True)
        staged[here, :] = (dot(active[here, :], down) + dot(own, as_out())).astype(LOW)
        d_h = dot(d_up[here, :], up, NT)
        sums[1:2, :model] += jnp.sum(d_h, axis=0, keepdims=True)
        sums[2:3, :model] += jnp.sum(d_h * n, axis=0, keepdims=True)
        to_norm[...] = (d_h * vectors[2:3, :]).astype(LOW)

        @pl.when(step == 0)
        def _():
            sums[3:4, :model] = jnp.sum(dy.astype(F32), axis=0, keepdims=True)

    store(out_plan, step, staged, parts, out_sems, True)

    @pl.when(step >= steps)
    def _():
        at = step - steps
        many = pl.num_programs(0) - steps

        @pl.when(at == 0)
        def _():
            g_out[...] = dot(own_mixed[...], cot[...], TN).astype(LOW)

        up_cols = pl.ds(pl.multiple_of(at * (model // many), 128), model // many)
        down_cols = pl.ds(pl.multiple_of(at * (units // many), 128), units // many)
        out_rows = pl.ds(pl.multiple_of(at * (width // many), 16), width // many)
        up_grad = dot(normal[:, up_cols], d_up[...], TN).astype(LOW)
        down_grad = dot(active[:, down_cols], cot[...], TN).astype(LOW)
        if joined:
            block = grads[0].shape[0]
            grads[0][:, cuts[0] : cuts[1], :] = up_grad.reshape(block, cuts[1], units)
            grads[0][:, cuts[1] : cuts[2], :] = down_grad.reshape(block, cuts[2] - cuts[1], model)
            grads[0][:, cuts[2] : cuts[3], :] = g_out[out_rows, :].reshape(block, cuts[3] - cuts[2], model)
            grads[0][:, cuts[3] :, :] = jnp.zeros((block, EXTRA, model), LOW)
            for place in range(block):
                lanes = pl.ds(pl.multiple_of((at * block + place) * 128, 128), 128)
                lines = [sums[row : row + 1, lanes] for row in (2, 1, 3, 0)]
                grads[0][place, cuts[3] :, :128] = extra_rows(lines)
        else:
            grads[0][...] = up_grad
            grads[1][...] = down_grad
            grads[2][...] = g_out[out_rows, :]

    @pl.when(step == pl.num_programs(0) - 1)
    def _():
        for at in range(steps):
            store(out_plan, at, staged, parts, out_sems, False)


def call_mlp(order, x_pieces, cot_pieces, mixed, vectors, mats, span, units, out_shapes):
    rows, width = mixed.shape
    model = x_pieces[0].shape[1]
    joined = len(mats) == 1
    plan, out_plan = plan_of(x_pieces, span), plan_of(out_shapes, span)
    steps, many = len(plan), 4
    count = len(x_pieces)
    there = lambda i, o: (o[jnp.minimum(i, steps - 1)], 0)
    later = lambda i, o: (jnp.maximum(i - steps, 0), 0)
    if joined:
        groups = mats[0].shape[0]
        grads = [(groups, (model + units + width) // groups + EXTRA, model)]
        grad_specs = [pl.BlockSpec((groups // many,) + grads[0][1:], lambda i, o: (jnp.maximum(i - steps, 0), 0, 0))]
    else:
        grads = [(model, units), (units, model), (width, model)]
        grad_specs = [pl.BlockSpec((a // many, b), later) for a, b in grads]
    sums = (8, max(model, units))
    return pl.pallas_call(
        functools.partial(mlp_kernel, plan, out_plan, count, len(out_shapes), joined, 256),
        grid_spec=pltpu.PrefetchScalarGridSpec(
            num_scalar_prefetch=1,
            grid=(steps + many,),
            in_specs=[HBM] * (2 * count)
            + [whole((rows, width)), whole(vectors.shape)]
            + [pl.BlockSpec(m.shape, lambda *_: (0, 0, 0), pipeline_mode=pl.Buffered(1)) for m in mats],
            out_specs=[HBM] * len(out_shapes)
            + [pl.BlockSpec((span, width), there), pl.BlockSpec((span, model), there)]
            + grad_specs
            + [whole(sums)],
            scratch_shapes=[
                pltpu.VMEM((rows, model), LOW),
                pltpu.VMEM((rows, model), LOW),
                pltpu.VMEM((rows, units), LOW),
                pltpu.VMEM((rows, units), LOW),
                pltpu.VMEM((rows, width), LOW),
                pltpu.VMEM((width, model), LOW),
                pltpu.VMEM((rows, model), LOW),
                pltpu.SemaphoreType.DMA((steps, 2)),
                pltpu.SemaphoreType.DMA((steps, 2)),
                pltpu.SemaphoreType.DMA((steps, 2)),
            ],
        ),
        out_shape=list(out_shapes)
        + [jax.ShapeDtypeStruct((rows, width), LOW), jax.ShapeDtypeStruct((rows, model), LOW)]
        + [jax.ShapeDtypeStruct(g, LOW) for g in grads]
        + [jax.ShapeDtypeStruct(sums, F32)],
        compiler_params=params("arbitrary"),
        cost_estimate=SHORT,
        name="mlp",
    )(order, *x_pieces, *cot_pieces, mixed, vectors, *mats)


def finish_kernel(shifts, wholes, base, *refs):
    refs, out = refs[:-1], refs[-1]
    shift, refs = refs[:shifts], refs[shifts:]
    common, parts = refs[:wholes], refs[wholes:]
    total = base[...].astype(F32)
    for ref in shift:
        total = total + ref[4:5, :] + ref[5:6, :]
    for ref in common:
        total = total + ref[...].astype(F32)
    if not parts:
        out[...] = total.astype(LOW)
    for at in range(2 if parts else 0):

        @pl.when(pl.program_id(0) == at)
        def _():
            more = total
            for ref in parts[at::2]:
                more = more + ref[...].astype(F32)
            out[...] = more.astype(LOW)


def call_finish(base, common, parts, vectors=(), cost=SHORT):
    rows, model = base.shape
    block = pl.BlockSpec((rows // 2, model), lambda i: (i, 0))
    return pl.pallas_call(
        functools.partial(finish_kernel, len(vectors), len(common)),
        grid=(2,),
        in_specs=[block] + [whole(v.shape) for v in vectors] + [block] * len(common) + [whole((rows // 2, model))] * len(parts),
        out_specs=block,
        out_shape=jax.ShapeDtypeStruct((rows, model), LOW),
        compiler_params=params("arbitrary"),
        cost_estimate=cost,
        name="finish",
    )(base, *vectors, *common, *parts)


def cut_kernel(first, second, third, pieces, down, line):
    columns = first.shape[1]
    members, shard, _ = pieces.shape
    low = members * shard
    both = columns + second.shape[1]
    for at in range(members):
        rows = slice(at * shard, (at + 1) * shard)
        pieces[at, :, :columns] = first[rows, :]
        pieces[at, :, columns:both] = (second[rows, :].astype(F32) + third[rows, :].astype(F32)).astype(LOW)
        pieces[at, :EXTRA, both:] = first[first.shape[0] - EXTRA :, :128]
        pieces[at, EXTRA:, both:] = (second[low:, :128].astype(F32) + third[low:, :128].astype(F32)).astype(LOW)
    down[...] = first[low : low + down.shape[0], :].astype(F32)
    line[...] = first[first.shape[0] - EXTRA :, :128].astype(F32)[3, :]


def call_cut(first, second, third, members, shard):
    columns = first.shape[1]
    shapes = [
        jax.ShapeDtypeStruct((members, shard, columns + second.shape[1] + 128), LOW),
        jax.ShapeDtypeStruct((first.shape[0] - (members + 1) * shard - EXTRA, columns), F32),
        jax.ShapeDtypeStruct((128,), F32),
    ]
    return pl.pallas_call(
        cut_kernel,
        grid=(1,),
        in_specs=[whole(first.shape), whole(second.shape), whole(third.shape)],
        out_specs=[whole(a.shape) for a in shapes],
        out_shape=shapes,
        compiler_params=params("arbitrary"),
        cost_estimate=SHORT,
        name="cut",
    )(first, second, third)


def join_kernel(places, count, member, *refs):
    base, parts, refs, total = refs[0], refs[1 : 1 + count], refs[1 + count : -1], refs[-1]
    finish_kernel(0, 0, base, *parts, total)

    @pl.when(pl.program_id(0) == 0)
    def _():
        join_pieces(places, member, *refs)


def join_pieces(places, member, *refs):
    pieces, last, up, qkv, out, gain_1, bias_1, gain_2, bias_2, end_bias, end_bias_2, shift = refs
    outs = up, qkv
    members = pieces.shape[0]
    for at in range(members):
        for block, (index, column, stride) in enumerate(places):
            start = column + at * stride
            outs[index][:, start : start + 128] = pieces[at, :, block * 128 : (block + 1) * 128].astype(F32)
    out[...] = last[...].astype(F32)
    size = gain_1.shape[0]
    low = len(places) * 128
    two, one = (sum(pieces[at, row : row + EXTRA, low:].astype(F32) for at in range(members)) for row in (0, EXTRA))
    wide = jnp.concatenate([one[2:3, :], one[3:4, :], one[4:5, :]], axis=1)
    for at in range(members):

        @pl.when(member[0] == at)
        def _():
            lanes = slice(at * size, (at + 1) * size)
            for ref, rows, row in ((gain_1, one, 0), (bias_1, one, 1), (gain_2, two, 0), (bias_2, two, 1), (end_bias, two, 2), (end_bias_2, two, 2)):
                ref[...] = rows[row, lanes]
            shift[...] = wide[0, 3 * at * size : 3 * (at + 1) * size]


def call_join(member, base, parts, pieces, last, places, columns):
    members, shard, _ = pieces.shape
    size = 128 // members
    shapes = [(shard, c) for c in columns] + [last.shape] + [(size,)] * 6 + [(3 * size,)]
    block = pl.BlockSpec((base.shape[0] // 2, base.shape[1]), lambda i, o: (i, 0))
    return pl.pallas_call(
        functools.partial(join_kernel, tuple(places), len(parts)),
        grid_spec=pltpu.PrefetchScalarGridSpec(
            num_scalar_prefetch=1,
            grid=(2,),
            in_specs=[block] + [whole(p.shape) for p in (*parts, pieces, last)],
            out_specs=[whole(a) for a in shapes] + [block],
        ),
        out_shape=[jax.ShapeDtypeStruct(a, F32) for a in shapes] + [jax.ShapeDtypeStruct(base.shape, LOW)],
        compiler_params=params("arbitrary"),
        cost_estimate=SHORT,
        name="join",
    )(member, base, *parts, pieces, last)


def across(array, bit):
    size = lax.axis_size("fsdp")
    return lax.ppermute(array, "fsdp", [(i, i ^ bit) for i in range(size)])


def exchange(pieces):
    size = lax.axis_size("fsdp")
    if size != 4:
        return lax.all_to_all(pieces, "fsdp", split_axis=0, concat_axis=0, tiled=True)
    member = lax.axis_index("fsdp")
    out = pieces
    for bit in range(1, size):
        mine = lax.dynamic_index_in_dim(pieces, member ^ bit, 0, keepdims=False)
        out = lax.dynamic_update_index_in_dim(out, across(mine, bit), member ^ bit, 0)
    return out


def behind(array, *others):
    return lax.optimization_barrier((array, *others))[0]


def behind_all(arrays, *others):
    return tuple(behind(array, *others) for array in arrays)


def gather_rows(halves, near=None, *others):
    if lax.axis_size("fsdp") != 4:
        return [lax.all_gather(jnp.concatenate(halves, axis=0), "fsdp", axis=0, tiled=True)]
    one_low, two_high, one_high, two_low = near
    return [
        *halves, one_low, one_high, two_low, two_high,
        across(behind(one_low, *others), 2), across(behind(two_high, *others), 1),
    ]


def near_rows(halves):
    low, high = halves
    return across(low, 1), across(high, 2), across(high, 1), across(low, 2)


def hop(array, bit):
    return lax.ppermute(array, "dp", [(i, i ^ bit) for i in range(lax.axis_size("dp"))])


def scatter_step(blocks, far, bit):
    blocks = (blocks.astype(F32) + far.astype(F32)).astype(LOW)
    send = blocks[1::2]
    return blocks[0::2], hop(send, bit), send


def reduce_direct(parts):
    if len(parts) == 1:
        return (lax.psum_scatter(parts[0], "fsdp", scatter_dimension=0, tiled=True),)
    three = across(parts[3], 3)
    return parts[0], across(parts[1], 1), across(parts[2], 2), three


def total_over_all(vector):
    count = lax.axis_size("dp") * lax.axis_size("fsdp")
    step = 1
    while step < count:
        vector = vector + lax.ppermute(vector, ALL, [(i, i ^ step) for i in range(count)])
        step *= 2
    return vector


def swap_owner(array, back):
    groups, members = lax.axis_size("dp"), lax.axis_size("fsdp")
    pairs = [(m * groups + g, g * members + m) for g in range(groups) for m in range(members)]
    if back:
        pairs = [(b, a) for a, b in pairs]
    return lax.ppermute(array, ALL, pairs)


def gather_dp(array):
    return lax.all_gather(array, "dp", axis=0)


def scatter_dp(array):
    return lax.psum_scatter(array, "dp", scatter_dimension=0, tiled=True)


def rotary_tables(length):
    half = ROT // 2
    frequency = (np.float32(10000.0) ** (-(np.arange(half, dtype=np.float32) * np.float32(2.0)) / np.float32(ROT))).astype(np.float32)
    angles = (np.arange(length, dtype=np.float32)[:, None] * frequency[None, :]).astype(np.float32)
    cosine = np.cos(angles).astype(np.float32)
    sine = np.sin(angles).astype(np.float32)
    cos_row = np.ones((length, 128), np.float32)
    sine_row = np.zeros((length, 128), np.float32)
    for start in range(0, 128, HEAD):
        cos_row[:, start : start + half] = cosine
        cos_row[:, start + half : start + ROT] = cosine
        sine_row[:, start : start + half] = -sine
        sine_row[:, start + half : start + ROT] = sine
    return jnp.asarray(np.concatenate([cos_row, sine_row], axis=1))


def local(
    tokens, cotangent, doc_ids, norm1_gain, norm1_bias, norm2_gain, norm2_bias, qkv_weight, qkv_bias,
    out_weight, out_bias, up_weight, up_bias, down_weight, down_bias,
):
    groups, members = lax.axis_size("dp"), lax.axis_size("fsdp")
    group, member = lax.axis_index("dp"), lax.axis_index("fsdp")
    devices = groups * members
    rows, model = tokens.shape
    stream = rows * members
    shard = qkv_weight.shape[0]
    width = model // members
    units_dev = up_bias.shape[0]
    units = groups * units_dev
    paired = members == 4 and units_dev == 128 and units == model and shard == 2 * EXTRA
    me = member.astype(jnp.int32).reshape(1)
    vectors_in = [norm1_gain, norm1_bias, norm2_gain, norm2_bias, out_bias, down_bias]

    half = rows // 2
    x_halves = [tokens[:half], tokens[half:]]
    cot_halves = [cotangent[:half], cotangent[half:]]
    if paired:
        packed = call_pack(me, qkv_weight, up_weight, (*vectors_in, qkv_bias, up_bias), members)
        arrived = [packed[0]] + [across(packed[bit], bit) for bit in range(1, members)]
        x_near = near_rows(behind_all(x_halves, *arrived[1:]))
        cut = 3 * width + 128
        first_in, up_in = call_place(me, arrived, cut)
        w_first = gather_dp(first_in)
        out_own = behind(swap_owner(behind(out_weight, first_in), False), *x_near[:2])
        mats = (gather_dp(jnp.concatenate([up_in, down_weight, out_own], axis=0)),)
        vectors = call_vectors(me, w_first, members, cut)
    else:
        qkv_cut = qkv_weight.reshape(shard, 3, members, width).transpose(2, 0, 1, 3).reshape(members, shard, 3 * width)
        up_cut = up_weight.reshape(shard, groups, members, units_dev).transpose(2, 0, 1, 3).reshape(members, shard, units)
        arrived = exchange(jnp.concatenate([qkv_cut, up_cut], axis=2)).reshape(members * shard, -1)
        w_first = gather_dp(arrived[:, : 3 * width])
        x_near = near_rows(x_halves) if members == 4 else None
        mats = (gather_dp(arrived[:, 3 * width :]), gather_dp(down_weight), gather_dp(swap_owner(out_weight, False)))
        full = [lax.all_gather(a, ALL, axis=0, tiled=True).astype(F32) for a in vectors_in]
        shift = lax.all_gather(qkv_bias, ALL, axis=0, tiled=True).astype(F32).reshape(3, members, width)
        shift = lax.dynamic_index_in_dim(shift, member, 1, keepdims=False)
        up_all = lax.all_gather(up_bias, "dp", axis=0, tiled=True).astype(F32)
        lines = full + [jnp.pad(a, (0, model - a.shape[0])) for a in (up_all, shift[0], shift[1], shift[2])]
        vectors = jnp.pad(jnp.stack(lines), ((0, 6), (0, 0)))

    x_pieces = gather_rows(x_halves, x_near)
    sources = jnp.arange(members, dtype=jnp.int32)
    order = sources ^ member if members == 4 else sources
    doc_row = doc_ids[0]
    first = jnp.sum((doc_row[None, :] < doc_row[:, None]).astype(jnp.int32), axis=1)
    first = jnp.concatenate([first, group.astype(jnp.int32).reshape(1), order])
    tables = rotary_tables(stream)

    q, k, v = call_qkv(order, x_pieces, vectors, w_first, tables, rows, width)
    cot_near = near_rows(behind_all(cot_halves, *x_near)) if members == 4 else None
    cot_pieces = gather_rows(cot_halves, cot_near, q)
    mixed, low_mixed, lse = call_fwd(first, q, k, v)
    out_sizes = [rows] * members if members == 4 else [stream]
    out_shapes = [jax.ShapeDtypeStruct((size, model), LOW) for size in out_sizes]
    results = call_mlp(
        order, x_pieces, cot_pieces, low_mixed, vectors, mats, rows, units, out_shapes
    )
    count = len(out_shapes)
    parts, (d_mixed, to_norm), grads, sums_two = results[:count], results[count : count + 2], results[count + 2 : -1], results[-1]
    scattered = scatter_dp(grads[0].reshape(-1, model)) if paired else None

    summed = reduce_direct(parts)
    sizes = [half] * (2 * members) if members == 4 else [stream]
    *pieces, even, odd, sums_qkv, ones = call_bwd(
        first, q, k, v, d_mixed, mixed, lse, tables, to_norm, vectors, w_first, x_pieces,
        [jax.ShapeDtypeStruct((size, model), LOW) for size in sizes], groups, rows, paired,
    )
    far, bit = hop(odd, 1), 2
    if members == 4:
        add = lambda a, b: (a.astype(F32) + b.astype(F32)).astype(LOW)
        own_low, own_high, one_low, one_high, two_low, two_high, three_low, three_high = pieces
        come = across(three_high, 2), across(three_low, 1)
        output = call_finish(tokens, summed, (), (vectors,), LONG)
        one_low, two_high = behind_all((one_low, two_high), output)
        near = across(one_low, 1), across(two_high, 2)
        blocks, far, send = scatter_step(even, behind(far, output), bit)
        come = behind_all(come, send)
        one_high, two_low = add(one_high, come[0]), add(two_low, come[1])
        near += across(one_high, 1), across(two_low, 2)
        parts = own_low, own_high, near[0], near[2], near[3], near[1]
        blocks, far, send = scatter_step(blocks, behind(far, one_high, two_low), 2 * bit)
        bit = 8
    if members != 4:
        blocks, far, _ = scatter_step(even, far, bit)
        bit = 4
        output = call_finish(tokens, summed, (), (vectors,))
        total = reduce_direct(pieces)[0]
        parts = total[:half], total[half:]
    while blocks.shape[0] > 1:
        (blocks, far, _), bit = scatter_step(blocks, far, bit), 2 * bit
    if members == 4:
        far = behind(far, *near[2:])
    g_qkv = blocks[0], far[0]
    place = group * members + member
    if paired:
        mixed_pieces, g_down, up_shift = call_cut(scattered, *g_qkv, members, shard)
        g_out = scattered[scattered.shape[0] - shard - EXTRA : scattered.shape[0] - EXTRA]
        g_out = swap_owner(behind(g_out, g_down), True)
        places = [(0, b * members * units_dev, units_dev) for b in range(groups)]
        places += [(1, part * model + low, width) for part in range(3) for low in range(0, width, 128)]
        arrived = lax.all_to_all(mixed_pieces, "fsdp", split_axis=0, concat_axis=0)
        g_up, g_qkv, g_out, *mine, grad_tokens = call_join(
            me, cotangent, parts, arrived, g_out, places, (up_weight.shape[1], qkv_weight.shape[1])
        )
        mine.append(up_shift)
    else:
        grad_tokens = call_finish(cotangent, (), parts)
        g_up, g_down, g_out = [scatter_dp(g) for g in grads]
        g_down = g_down.astype(F32)
        g_up = exchange(g_up.reshape(members, shard, units))
        g_up = g_up.reshape(members, shard, groups, units_dev).transpose(1, 2, 0, 3).reshape(shard, -1).astype(F32)
        g_qkv = (g_qkv[0].astype(F32) + g_qkv[1].astype(F32)).astype(LOW)
        g_qkv = exchange(g_qkv.reshape(members, shard, 3 * width)).reshape(members, shard, 1, 3, width)
        g_qkv = g_qkv.transpose(1, 3, 0, 2, 4).reshape(shard, -1).astype(F32)
        thirds = jnp.concatenate([a[0].reshape(3, 1, width) for a in [sums_qkv]], axis=2)
        wide_qkv = lax.dynamic_update_index_in_dim(jnp.zeros((3, members, width), F32), thirds, member, 1)
        wide_up = lax.dynamic_update_index_in_dim(
            jnp.zeros((groups, members, units_dev), F32), sums_two[0, :units].reshape(groups, 1, units_dev), member, 1
        )
        summed = total_over_all(jnp.concatenate([
            ones[0], ones[1], sums_two[2], sums_two[1], sums_two[3], wide_qkv.reshape(-1), wide_up.reshape(-1),
        ]))
        mine, start = [], 0
        for size in [model] * 5 + [3 * model, groups * members * units_dev]:
            mine.append(lax.dynamic_slice_in_dim(summed, start + place * (size // devices), size // devices))
            start += size
        mine.insert(5, mine[4])
    gain_1, bias_1, gain_2, bias_2, end_bias, end_bias_2, qkv_shift, up_shift = mine
    if not paired:
        g_out = swap_owner(g_out, True).astype(F32)
    return (
        output, grad_tokens, gain_1, bias_1, gain_2, bias_2, g_qkv, qkv_shift, g_out, end_bias, g_up, up_shift, g_down, end_bias_2,
    )


def solution(mesh):
    row, vec = P(ALL, None), P(ALL)
    return jax.shard_map(
        local,
        mesh=mesh,
        in_specs=(row, row, P("dp", None), vec, vec, vec, vec, row, vec, row, vec, row, vec, row, vec),
        out_specs=(row, row, vec, vec, vec, vec, row, vec, row, vec, row, vec, row, vec),
        check_vma=False,
    )
```

```python
import functools

import jax
import jax.numpy as jnp
import numpy as np
from jax import lax
from jax.experimental import pallas as pl
from jax.experimental.pallas import tpu as pltpu
from jax.sharding import PartitionSpec as P

HEADS = 16
HEAD = 64
ROT = 16
BLOCK = 256
EPS = 1e-05
ALL = ("dp", "fsdp")
LONG = pl.CostEstimate(flops=2 * 10**10, bytes_accessed=10**7, transcendentals=0)
SHORT = pl.CostEstimate(flops=0, bytes_accessed=0, transcendentals=0)
F32 = jnp.float32
LOW = jnp.bfloat16


def dot(left, right, contract=((1,), (0,))):
    return lax.dot_general(left, right, (contract, ((), ())), preferred_element_type=F32)


NT = ((1,), (1,))
TN = ((0,), (0,))


def normed(x_rows):
    centre = x_rows - jnp.mean(x_rows, axis=-1, keepdims=True)
    spread = jnp.mean(centre * centre, axis=-1, keepdims=True)
    scale = lax.rsqrt(spread + EPS)
    return centre * scale, scale


def turned(z, cosine, sine, sign):
    groups = []
    for start in range(0, z.shape[1], 128):
        part = z[:, start : start + 128]
        ahead = pltpu.roll(part, 128 - ROT // 2, 1)
        behind = pltpu.roll(part, ROT // 2, 1)
        lane = lax.broadcasted_iota(jnp.int32, part.shape, 1) & (HEAD - 1)
        groups.append(part * cosine + sign * (jnp.where(lane < ROT // 2, ahead, behind) * sine))
    return groups[0] if len(groups) == 1 else jnp.concatenate(groups, axis=1)


def head_only(array, head):
    lane = lax.broadcasted_iota(jnp.int32, array.shape, 1)
    keep = (lane >= head * HEAD) & (lane < (head + 1) * HEAD)
    return jnp.where(keep, array, jnp.zeros_like(array))


def params(*order):
    return pltpu.CompilerParams(vmem_limit_bytes=60 * 1024 * 1024, dimension_semantics=order)


def whole(shape):
    return pl.BlockSpec(shape, lambda *_: (0,) * len(shape))


HBM = pl.BlockSpec(memory_space=pl.ANY)
EXTRA = 16


def fetch(plan, step, refs, target, sems, begin):
    for at, pieces in enumerate(plan):

        @pl.when(step == at)
        def _():
            for index, (ref, start, put, size) in enumerate(pieces):
                copy = pltpu.make_async_copy(
                    refs[ref].at[pl.ds(start, size)], target.at[pl.ds(put, size)], sems.at[at, index]
                )
                if begin:
                    copy.start()
                else:
                    copy.wait()


def fetch_all(plan, refs, target, sems):
    for at in range(len(plan)):
        fetch(plan, at, refs, target, sems, True)


def plan_of(pieces, span):
    plan, total = [], sum(p.shape[0] for p in pieces)
    for low in range(0, total, span):
        taken, at = [], 0
        for index, piece in enumerate(pieces):
            a, b = max(low, at), min(low + span, at + piece.shape[0])
            if a < b:
                taken.append((index, a - at, a, b - a))
            at += piece.shape[0]
        plan.append(tuple(taken))
    return tuple(plan)


def store(plan, step, source, refs, sems, begin):
    for at, pieces in enumerate(plan):

        @pl.when(step == at)
        def _():
            for index, (ref, start, put, size) in enumerate(pieces):
                copy = pltpu.make_async_copy(
                    source.at[pl.ds(put, size)], refs[ref].at[pl.ds(start, size)], sems.at[at, index]
                )
                if begin:
                    copy.start()
                else:
                    copy.wait()


def pack_kernel(members, member, qkv, up, *refs):
    vectors, (qkv_bias, up_bias), out, (small, wide) = refs[:6], refs[6:8], refs[8:-2], refs[-2:]
    width = qkv.shape[1] // 3 // members
    units_dev = up_bias.shape[0]
    groups = up.shape[1] // units_dev // members
    size = 128 // members
    small[...] = jnp.zeros_like(small)
    wide[...] = jnp.zeros_like(wide)
    for at in range(members):

        @pl.when(member[0] == at)
        def _():
            for row, vector in enumerate(vectors):
                small[row, at * size : (at + 1) * size] = vector[...].astype(F32)
            wide[0, 3 * at * size : 3 * (at + 1) * size] = qkv_bias[...].astype(F32)

    for row in range(3):
        small[6 + row : 7 + row, :] = wide[0:1, row * 128 : (row + 1) * 128]
    small[9, :] = up_bias[...].astype(F32)
    block = small[...].astype(LOW)
    for bit in range(members):
        to = member[0] ^ bit
        for part in range(3):
            start = pl.multiple_of((part * members + to) * width, 128)
            out[bit][:, part * width : (part + 1) * width] = qkv[:, pl.ds(start, width)]
        out[bit][:, 3 * width : 3 * width + 128] = jnp.zeros((qkv.shape[0], 128), LOW)
        out[bit][0:16, 3 * width : 3 * width + 128] = block
        for group in range(groups):
            start = pl.multiple_of((group * members + to) * units_dev, 128)
            low = 3 * width + 128 + group * units_dev
            out[bit][:, low : low + units_dev] = up[:, pl.ds(start, units_dev)]


def call_pack(member, qkv, up, vectors, members):
    shard = qkv.shape[0]
    columns = (qkv.shape[1] + up.shape[1]) // members + 128
    return pl.pallas_call(
        functools.partial(pack_kernel, members),
        grid_spec=pltpu.PrefetchScalarGridSpec(
            num_scalar_prefetch=1,
            grid=(1,),
            in_specs=[whole(a.shape) for a in (qkv, up, *vectors)],
            out_specs=[whole((shard, columns))] * members,
            scratch_shapes=[pltpu.VMEM((16, 128), F32), pltpu.VMEM((8, 384), F32)],
        ),
        out_shape=[jax.ShapeDtypeStruct((shard, columns), LOW)] * members,
        compiler_params=params("arbitrary"),
        cost_estimate=SHORT,
        name="pack",
    )(member, qkv, up, *vectors)


def place_kernel(cut, member, *refs):
    *pieces, first, second = refs
    shard = pieces[0].shape[0]
    for bit, piece in enumerate(pieces):
        rows = pl.ds(pl.multiple_of((member[0] ^ bit) * shard, shard), shard)
        first[rows, :] = piece[:, :cut]
        second[rows, :] = piece[:, cut:]


def call_place(member, pieces, cut):
    members, (shard, columns) = len(pieces), pieces[0].shape
    shapes = [(members * shard, cut), (members * shard, columns - cut)]
    return pl.pallas_call(
        functools.partial(place_kernel, cut),
        grid_spec=pltpu.PrefetchScalarGridSpec(
            num_scalar_prefetch=1,
            grid=(1,),
            in_specs=[whole(p.shape) for p in pieces],
            out_specs=[whole(a) for a in shapes],
        ),
        out_shape=[jax.ShapeDtypeStruct(a, LOW) for a in shapes],
        compiler_params=params("arbitrary"),
        cost_estimate=SHORT,
        name="place",
    )(member, *pieces)


def vectors_kernel(members, member, gathered, out, wide):
    groups, rows, _ = gathered.shape
    shard = rows // members
    model = groups * 128
    out[...] = jnp.zeros_like(out)
    for group in range(groups):
        blocks = [gathered[group, m * shard : m * shard + 16, :].astype(F32) for m in range(members)]
        block = blocks[0]
        for other in blocks[1:]:
            block = block + other
        lanes = slice(group * 128, (group + 1) * 128)
        for row in range(6):
            out[row : row + 1, lanes] = block[row : row + 1, :]
        for row in range(3):
            low = group * 384 + row * 128
            wide[0:1, low : low + 128] = block[6 + row : 7 + row, :]
        own = jnp.zeros((1, 128), F32)
        for m in range(members):
            own = own + jnp.where(member[0] == m, blocks[m][9:10, :], 0.0)
        out[6:7, lanes] = own
    width = model // members
    for part in range(3):
        start = pl.multiple_of(part * model + member[0] * width, 128)
        out[7 + part : 8 + part, :width] = wide[0:1, pl.ds(start, width)]


def call_vectors(member, gathered, members, cut):
    groups, rows, _ = gathered.shape
    model = groups * 128
    return pl.pallas_call(
        functools.partial(vectors_kernel, members),
        grid_spec=pltpu.PrefetchScalarGridSpec(
            num_scalar_prefetch=1,
            grid=(1,),
            in_specs=[pl.BlockSpec((groups, rows, 128), lambda i, o: (0, 0, cut // 128 - 1))],
            out_specs=whole((16, model)),
            scratch_shapes=[pltpu.VMEM((8, 3 * model), F32)],
        ),
        out_shape=jax.ShapeDtypeStruct((16, model), F32),
        compiler_params=params("arbitrary"),
        cost_estimate=SHORT,
        name="vectors",
    )(member, gathered)


def qkv_kernel(plan, count, order, *refs):
    pieces, rest = refs[:count], refs[count:]
    vectors, weight, turn, q, k, v, x, sems = rest
    step = pl.program_id(0)
    width = q.shape[1]
    span = q.shape[0]
    model = x.shape[1]

    @pl.when(step == 0)
    def _():
        fetch_all(plan, pieces, x, sems)

    fetch(plan, step, pieces, x, sems, False)
    n, _ = normed(x[pl.ds(pl.multiple_of(step * span, span), span), :].astype(F32))
    h = (n * vectors[0:1, :] + vectors[1:2, :]).astype(LOW)
    tables = (turn[:, :128], turn[:, 128:])
    rows = dot(h, weight[...].reshape(model, 3 * width))
    q[...] = (turned(rows[:, :width] + vectors[7:8, :width], *tables, 1.0) * 0.125).astype(LOW)
    k[...] = turned(rows[:, width : 2 * width] + vectors[8:9, :width], *tables, 1.0).astype(LOW)
    v[...] = (rows[:, 2 * width :] + vectors[9:10, :width]).astype(LOW)


def call_qkv(order, pieces, vectors, weight, tables, span, width):
    model = pieces[0].shape[1]
    plan = plan_of(pieces, span)
    rows = span * len(plan)
    there = lambda i, o: (o[i], 0)
    return pl.pallas_call(
        functools.partial(qkv_kernel, plan, len(pieces)),
        grid_spec=pltpu.PrefetchScalarGridSpec(
            num_scalar_prefetch=1,
            grid=(rows // span,),
            in_specs=[HBM] * len(pieces)
            + [whole(vectors.shape), whole(weight.shape[:2] + (3 * width,))]
            + [pl.BlockSpec((span, 256), there)],
            out_specs=[pl.BlockSpec((span, width), there)] * 3,
            scratch_shapes=[pltpu.VMEM((rows, model), LOW), pltpu.SemaphoreType.DMA((len(plan), 2))],
        ),
        out_shape=[jax.ShapeDtypeStruct((rows, width), LOW)] * 3,
        compiler_params=params("arbitrary"),
        cost_estimate=SHORT,
        name="qkv",
    )(order, *pieces, vectors, weight, tables)


def masked_rows(target, array):
    for head in range(array.shape[1] // HEAD):
        target[head * BLOCK : (head + 1) * BLOCK, :] = head_only(array, head)


def over_keys(first, block, tiles):
    begin = first[block]
    count = block + 1 - begin

    def pair(i, _):
        tiles(begin + 2 * i, 2)
        return 0

    def single(at, _):
        tiles(at, 1)
        return 0

    lax.fori_loop(0, count // 2, pair, 0)
    lax.fori_loop(block + 1 - count % 2, block + 1, single, 0)


def by_eight(array):
    return array.reshape(BLOCK // 8, 8, BLOCK)


def fwd_kernel(first, q, k, v, mixed, low_mixed, lse, keys, values, scores, top, total, out):
    step = pl.program_id(0)
    width = q.shape[1]
    heads = width // HEAD
    stack = heads * BLOCK
    masked_rows(keys.at[step], k[...])
    masked_rows(values.at[step], v[...])
    q_t = q[...].T
    top[...] = jnp.full_like(top, -1e30)
    total[...] = jnp.zeros_like(total)
    out[...] = jnp.zeros_like(out)

    def score(at, count):
        s = dot(keys[pl.ds(at, count)].reshape(count * stack, width), q_t)
        scores[pl.ds(at, count)] = s.reshape(count, stack, BLOCK)
        for head in range(heads):
            best = top[head]
            for tile in range(count):
                low = tile * stack + head * BLOCK
                best = jnp.maximum(best, jnp.max(by_eight(s[low : low + BLOCK]), axis=0))
            top[head] = best

    over_keys(first, step, score)
    peak = [jnp.max(top[head], axis=0, keepdims=True) for head in range(heads)]

    def mix(at, count):
        grown = []
        for tile in range(count):
            for head in range(heads):
                e = jnp.exp(scores[at + tile, head * BLOCK : (head + 1) * BLOCK] - peak[head])
                total[head] += jnp.sum(by_eight(e), axis=0)
                grown.append(e.astype(LOW))
        out[...] += dot(jnp.concatenate(grown, axis=0), values[pl.ds(at, count)].reshape(count * stack, width), TN)

    over_keys(first, step, mix)
    shares = []
    for head in range(heads):
        sums = jnp.sum(total[head], axis=0, keepdims=True)
        lse[head : head + 1, :] = peak[head] + jnp.log(sums)
        shares.append(jnp.broadcast_to(1.0 / sums, (HEAD, BLOCK)))
    result = out[...] * jnp.concatenate(shares, axis=0).T
    mixed[...] = result
    low_mixed[...] = result.astype(LOW)


def call_fwd(first, q, k, v):
    rows, width = q.shape
    heads = width // HEAD
    blocks = rows // BLOCK
    return pl.pallas_call(
        fwd_kernel,
        grid_spec=pltpu.PrefetchScalarGridSpec(
            num_scalar_prefetch=1,
            grid=(blocks,),
            in_specs=[pl.BlockSpec((BLOCK, width), lambda i, o: (i, 0))] * 3,
            out_specs=[
                pl.BlockSpec((BLOCK, width), lambda i, o: (i, 0)),
                pl.BlockSpec((BLOCK, width), lambda i, o: (i, 0)),
                pl.BlockSpec((heads, BLOCK), lambda i, o: (0, i)),
            ],
            scratch_shapes=[
                pltpu.VMEM((blocks, heads * BLOCK, width), LOW),
                pltpu.VMEM((blocks, heads * BLOCK, width), LOW),
                pltpu.VMEM((blocks, heads * BLOCK, BLOCK), F32),
                pltpu.VMEM((heads, 8, BLOCK), F32),
                pltpu.VMEM((heads, 8, BLOCK), F32),
                pltpu.VMEM((BLOCK, width), F32),
            ],
        ),
        out_shape=[
            jax.ShapeDtypeStruct((rows, width), F32),
            jax.ShapeDtypeStruct((rows, width), LOW),
            jax.ShapeDtypeStruct((heads, rows), F32),
        ],
        compiler_params=params("arbitrary"),
        cost_estimate=SHORT,
        name="attend",
    )(first, q, k, v)


def closed_rows(x, rows, to_norm, vectors, weight):
    n, scale = normed(x.astype(F32))
    d_h = dot(rows, weight, NT)
    bias = jnp.sum(d_h, axis=0, keepdims=True)
    gain = jnp.sum(d_h * n, axis=0, keepdims=True)
    e = d_h * vectors[0:1, :] + to_norm
    e = e - jnp.mean(e, axis=-1, keepdims=True) - n * jnp.mean(e * n, axis=-1, keepdims=True)
    return e * scale, gain, bias


def bwd_kernel(plan, per, groups, extra, first, q, k, v, d_mixed, mixed, lse, turn, to_norm, vectors, weight, *rest):
    many = 1 + max(piece for piece, _ in plan)
    pieces, outs, (even, odd, sums, ones), rest = rest[:many], rest[many : 2 * many], rest[2 * many : 2 * many + 4], rest[2 * many + 4 :]
    keys, values, sum_q, sum_k, sum_v, queries, seeds, h, d_rows, x, mat, wide, sem, x_sems, out_sems = rest
    step = pl.program_id(0)
    blocks = pl.num_programs(0)
    block = blocks - 1 - step
    width = k.shape[1]
    heads = width // HEAD
    stack = heads * BLOCK
    base = first.shape[0] - 1 - len(plan) // per
    group, order = first[base], lambda at: first[base + 1 + at]
    rows_of = lambda at: pl.ds(pl.multiple_of(at * BLOCK, BLOCK), BLOCK)
    own = rows_of(block)
    load = pltpu.make_async_copy(weight.at[:, :, pl.ds(0, 3 * width)], mat, sem.at[0])

    @pl.when(step == 0)
    def _():
        load.start()
        for at, (piece, start) in reversed(list(enumerate(plan))):
            place = order(at // per) * per + at % per
            pltpu.make_async_copy(pieces[piece].at[pl.ds(start, BLOCK)], x.at[rows_of(place)], x_sems.at[place]).start()

        def prepare(at, _):
            here = rows_of(at)
            masked_rows(keys.at[at], k[here, :])
            masked_rows(values.at[at], v[here, :])
            sum_k[here, :] = jnp.zeros((BLOCK, width), F32)
            sum_v[here, :] = jnp.zeros((BLOCK, width), F32)
            return 0

        lax.fori_loop(0, blocks, prepare, 0)
        sums[...] = jnp.zeros_like(sums)
        ones[...] = jnp.zeros_like(ones)

    q_own = q[...]
    s_own = d_mixed[...]
    masked_rows(queries, q_own)
    masked_rows(seeds, s_own)
    q_t = q_own.T
    s_t = s_own.T
    product_t = (s_own.astype(F32) * mixed[...]).T
    delta = [jnp.sum(product_t[head * HEAD : (head + 1) * HEAD, :], axis=0, keepdims=True) for head in range(heads)]
    log_total = [lse[head : head + 1, :] for head in range(heads)]
    sum_q[...] = jnp.zeros_like(sum_q)

    def tiles(at, count):
        key_rows = keys[pl.ds(at, count)].reshape(count * stack, width)
        s = dot(key_rows, q_t)
        d_p = dot(values[pl.ds(at, count)].reshape(count * stack, width), s_t)
        wide_probs, wide_scores, tall_scores = [], [], []
        for tile in range(count):
            low_probs, low_scores = [], []
            for head in range(heads):
                low = tile * stack + head * BLOCK
                probs = jnp.exp(s[low : low + BLOCK] - log_total[head])
                low_scores.append((probs * (d_p[low : low + BLOCK] - delta[head])).astype(LOW))
                low_probs.append(probs.astype(LOW))
            wide_probs.append(jnp.concatenate(low_probs, axis=1))
            wide_scores.append(jnp.concatenate(low_scores, axis=1))
            tall_scores += low_scores
        here = pl.ds(pl.multiple_of(at * BLOCK, BLOCK), count * BLOCK)
        sum_v[here, :] += dot(jnp.concatenate(wide_probs, axis=0), seeds[...])
        sum_k[here, :] += dot(jnp.concatenate(wide_scores, axis=0), queries[...])
        sum_q[...] += dot(jnp.concatenate(tall_scores, axis=0), key_rows, TN)

    over_keys(first, block, tiles)

    @pl.when(step == 0)
    def _():
        load.wait()

    pltpu.make_async_copy(x.at[own], x.at[own], x_sems.at[block]).wait()
    turns = (turn[:, :128], turn[:, 128:])
    done = jnp.concatenate(
        [
            (turned(sum_q[...], *turns, -1.0) * 0.125).astype(LOW),
            turned(sum_k[own, :], *turns, -1.0).astype(LOW),
            sum_v[own, :].astype(LOW),
        ],
        axis=1,
    )
    d_rows[own, :] = done
    sums[0:1, :] += jnp.sum(done.astype(F32), axis=0, keepdims=True)
    n, scale = normed(x[own, :].astype(F32))
    h[own, :] = (n * vectors[0:1, :] + vectors[1:2, :]).astype(LOW)
    d_h = dot(done, mat[...].reshape(h.shape[1], 3 * width), NT)
    ones[0:1, :] += jnp.sum(d_h * n, axis=0, keepdims=True)
    ones[1:2, :] += jnp.sum(d_h, axis=0, keepdims=True)
    e = d_h * vectors[0:1, :] + to_norm[...].astype(F32)
    e = e - jnp.mean(e, axis=-1, keepdims=True) - n * jnp.mean(e * n, axis=-1, keepdims=True)
    x[own, :] = (e * scale).astype(LOW)
    place = order(block // per) * per + block % per
    for at, (piece, start) in enumerate(plan):

        @pl.when(place == at)
        def _():
            pltpu.make_async_copy(x.at[own], outs[piece].at[pl.ds(start, BLOCK)], out_sems.at[block]).start()

    @pl.when(step == blocks - 1)
    def _():
        model = h.shape[1]
        grad = dot(h[...], d_rows[...], TN).astype(LOW)
        h[:model, : 3 * width] = grad
        size = model // groups
        for place in range(groups):
            to = odd if place % 2 else even
            to[place // 2, :size, :] = h[pl.ds(pl.multiple_of((group ^ place) * size, size), size), : 3 * width]
        if extra:
            members = len(plan) // per
            wide[...] = jnp.zeros_like(wide)
            for part in range(3):
                for at in range(width // 128):
                    row = (part * members + order(0)) * (width // 128) + at
                    low = part * width + at * 128
                    wide[pl.ds(row, 1), :] = sums[0:1, low : low + 128]
            for place in range(groups):
                to, near = odd if place % 2 else even, group ^ place
                lanes = pl.ds(pl.multiple_of(near * 128, 128), 128)
                lines = [ones[0:1, lanes], ones[1:2, lanes]] + [wide[pl.ds(3 * near + row, 1), :] for row in range(3)]
                to[place // 2, size:, :] = jnp.zeros((EXTRA, 3 * width), LOW)
                to[place // 2, size:, :128] = extra_rows(lines)
        for at in range(len(plan)):
            here = pl.ds(at * BLOCK, BLOCK)
            pltpu.make_async_copy(x.at[here], x.at[here], out_sems.at[at]).wait()


def call_bwd(first, q, k, v, d_mixed, mixed, lse, tables, to_norm, vectors, weight, pieces, out_shapes, groups, span, extra):
    rows, width = q.shape
    heads = width // HEAD
    blocks = rows // BLOCK
    model = to_norm.shape[1]
    grad = (groups // 2, model // groups + EXTRA * extra, 3 * width)
    back = lambda i, o: (blocks - 1 - i, 0)
    blocked = pl.BlockSpec((BLOCK, width), back)
    once = lambda shape: pl.BlockSpec(shape, lambda *_: (0,) * len(shape), pipeline_mode=pl.Buffered(1))
    plan = tuple((p, start) for block in plan_of(pieces, BLOCK) for p, start, _, _ in block)
    outs = [(grad, LOW), (grad, LOW), ((8, 3 * width), F32), ((8, model), F32)]
    return pl.pallas_call(
        functools.partial(bwd_kernel, plan, span // BLOCK, groups, extra),
        grid_spec=pltpu.PrefetchScalarGridSpec(
            num_scalar_prefetch=1,
            grid=(blocks,),
            in_specs=[blocked, once((rows, width)), once((rows, width)), blocked, blocked]
            + [pl.BlockSpec((heads, BLOCK), lambda i, o: (0, blocks - 1 - i)), pl.BlockSpec((BLOCK, 256), back)]
            + [pl.BlockSpec((BLOCK, model), back), whole(vectors.shape), HBM]
            + [HBM] * len(pieces),
            out_specs=[HBM] * len(out_shapes) + [whole(a) for a, _ in outs],
            scratch_shapes=[
                pltpu.VMEM((blocks, heads * BLOCK, width), LOW),
                pltpu.VMEM((blocks, heads * BLOCK, width), LOW),
                pltpu.VMEM((BLOCK, width), F32),
                pltpu.VMEM((rows, width), F32),
                pltpu.VMEM((rows, width), F32),
                pltpu.VMEM((heads * BLOCK, width), LOW),
                pltpu.VMEM((heads * BLOCK, width), LOW),
                pltpu.VMEM((rows, model), LOW),
                pltpu.VMEM((rows, 3 * width), LOW),
                pltpu.VMEM((rows, model), LOW),
                pltpu.VMEM(weight.shape[:2] + (3 * width,), LOW),
                pltpu.VMEM((3 * groups, 128), F32),
                pltpu.SemaphoreType.DMA((1,)),
                pltpu.SemaphoreType.DMA((blocks,)),
                pltpu.SemaphoreType.DMA((blocks,)),
            ],
        ),
        out_shape=list(out_shapes) + [jax.ShapeDtypeStruct(a, kind) for a, kind in outs],
        compiler_params=params("arbitrary"),
        cost_estimate=SHORT,
        name="attend_back",
    )(first, q, k, v, d_mixed, mixed, lse, tables, to_norm, vectors, weight, *pieces)


def extra_rows(lines):
    return jnp.concatenate(lines + [jnp.zeros((EXTRA - len(lines), 128), F32)], axis=0).astype(LOW)


def mlp_kernel(plan, out_plan, count, out_count, joined, chunk, order, *refs):
    x_pieces, cot_pieces, rest = refs[:count], refs[count : 2 * count], refs[2 * count :]
    mixed, vectors, rest = rest[0], rest[1], rest[2:]
    mats, rest = rest[: 1 if joined else 3], rest[1 if joined else 3 :]
    parts, rest = rest[:out_count], rest[out_count:]
    d_mixed, to_norm, rest = rest[0], rest[1], rest[2:]
    grads, rest = rest[: 1 if joined else 3], rest[1 if joined else 3 :]
    sums, normal, cot, active, d_up, own_mixed, g_out, staged, x_sems, cot_sems, out_sems = rest
    step = pl.program_id(0)
    steps = len(plan)
    span, width = own_mixed.shape[0] // steps, own_mixed.shape[1]
    model, units = normal.shape[1], active.shape[1]
    if joined:
        groups = mats[0].shape[0]
        cuts = [0, model // groups, (model + units) // groups, (model + units + width) // groups]
        w_up, w_down, w_out = (mats[0].at[:, pl.ds(cuts[i], cuts[i + 1] - cuts[i]), :] for i in range(3))
    else:
        w_up, w_down, w_out = mats
    as_up = lambda: w_up[...].reshape(model, units)
    as_down = lambda: w_down[...].reshape(units, model)
    as_out = lambda: w_out[...].reshape(width, model)

    @pl.when(step == 0)
    def _():
        fetch_all(plan, x_pieces, normal, x_sems)
        fetch_all(plan, cot_pieces, cot, cot_sems)
        sums[...] = jnp.zeros_like(sums)

    fetch(plan, step, x_pieces, normal, x_sems, False)
    fetch(plan, step, cot_pieces, cot, cot_sems, False)

    @pl.when(step < steps)
    def _():
        here = pl.ds(pl.multiple_of(step * span, span), span)
        n, _ = normed(normal[here, :].astype(F32))
        h = (n * vectors[2:3, :] + vectors[3:4, :]).astype(LOW)
        normal[here, :] = h
        dy = cot[here, :]
        own = mixed[pl.ds(pl.multiple_of(order[step] * span, span), span), :]
        own_mixed[here, :] = own
        d_mixed[...] = dot(dy, as_out(), NT).astype(LOW)
        up, down = as_up(), as_down()
        for low in range(0, units, chunk):
            cols = slice(low, low + chunk)
            u = dot(h, up[:, cols]) + vectors[6:7, cols]
            d_active = dot(dy, down[cols], NT)
            cdf = 0.5 * (1.0 + lax.erf(u * np.float32(np.sqrt(0.5))))
            slope = cdf + u * (jnp.exp(-0.5 * u * u) * np.float32(1.0 / np.sqrt(2.0 * np.pi)))
            active[here, cols] = (u * cdf).astype(LOW)
            back = (d_active * slope).astype(LOW)
            d_up[here, cols] = back
            sums[0:1, cols] += jnp.sum(back.astype(F32), axis=0, keepdims=True)
        staged[here, :] = (dot(active[here, :], down) + dot(own, as_out())).astype(LOW)
        d_h = dot(d_up[here, :], up, NT)
        sums[1:2, :model] += jnp.sum(d_h, axis=0, keepdims=True)
        sums[2:3, :model] += jnp.sum(d_h * n, axis=0, keepdims=True)
        to_norm[...] = (d_h * vectors[2:3, :]).astype(LOW)

        @pl.when(step == 0)
        def _():
            sums[3:4, :model] = jnp.sum(dy.astype(F32), axis=0, keepdims=True)

    store(out_plan, step, staged, parts, out_sems, True)

    @pl.when(step >= steps)
    def _():
        at = step - steps
        many = pl.num_programs(0) - steps

        @pl.when(at == 0)
        def _():
            g_out[...] = dot(own_mixed[...], cot[...], TN).astype(LOW)

        up_cols = pl.ds(pl.multiple_of(at * (model // many), 128), model // many)
        down_cols = pl.ds(pl.multiple_of(at * (units // many), 128), units // many)
        out_rows = pl.ds(pl.multiple_of(at * (width // many), 16), width // many)
        up_grad = dot(normal[:, up_cols], d_up[...], TN).astype(LOW)
        down_grad = dot(active[:, down_cols], cot[...], TN).astype(LOW)
        if joined:
            block = grads[0].shape[0]
            grads[0][:, cuts[0] : cuts[1], :] = up_grad.reshape(block, cuts[1], units)
            grads[0][:, cuts[1] : cuts[2], :] = down_grad.reshape(block, cuts[2] - cuts[1], model)
            grads[0][:, cuts[2] : cuts[3], :] = g_out[out_rows, :].reshape(block, cuts[3] - cuts[2], model)
            grads[0][:, cuts[3] :, :] = jnp.zeros((block, EXTRA, model), LOW)
            for place in range(block):
                lanes = pl.ds(pl.multiple_of((at * block + place) * 128, 128), 128)
                lines = [sums[row : row + 1, lanes] for row in (2, 1, 3, 0)]
                grads[0][place, cuts[3] :, :128] = extra_rows(lines)
        else:
            grads[0][...] = up_grad
            grads[1][...] = down_grad
            grads[2][...] = g_out[out_rows, :]

    @pl.when(step == pl.num_programs(0) - 1)
    def _():
        for at in range(steps):
            store(out_plan, at, staged, parts, out_sems, False)


def call_mlp(order, x_pieces, cot_pieces, mixed, vectors, mats, span, units, out_shapes):
    rows, width = mixed.shape
    model = x_pieces[0].shape[1]
    joined = len(mats) == 1
    plan, out_plan = plan_of(x_pieces, span), plan_of(out_shapes, span)
    steps, many = len(plan), 2
    count = len(x_pieces)
    there = lambda i, o: (o[jnp.minimum(i, steps - 1)], 0)
    later = lambda i, o: (jnp.maximum(i - steps, 0), 0)
    if joined:
        groups = mats[0].shape[0]
        grads = [(groups, (model + units + width) // groups + EXTRA, model)]
        grad_specs = [pl.BlockSpec((groups // many,) + grads[0][1:], lambda i, o: (jnp.maximum(i - steps, 0), 0, 0))]
    else:
        grads = [(model, units), (units, model), (width, model)]
        grad_specs = [pl.BlockSpec((a // many, b), later) for a, b in grads]
    sums = (8, max(model, units))
    return pl.pallas_call(
        functools.partial(mlp_kernel, plan, out_plan, count, len(out_shapes), joined, 256),
        grid_spec=pltpu.PrefetchScalarGridSpec(
            num_scalar_prefetch=1,
            grid=(steps + many,),
            in_specs=[HBM] * (2 * count)
            + [whole((rows, width)), whole(vectors.shape)]
            + [pl.BlockSpec(m.shape, lambda *_: (0, 0, 0), pipeline_mode=pl.Buffered(1)) for m in mats],
            out_specs=[HBM] * len(out_shapes)
            + [pl.BlockSpec((span, width), there), pl.BlockSpec((span, model), there)]
            + grad_specs
            + [whole(sums)],
            scratch_shapes=[
                pltpu.VMEM((rows, model), LOW),
                pltpu.VMEM((rows, model), LOW),
                pltpu.VMEM((rows, units), LOW),
                pltpu.VMEM((rows, units), LOW),
                pltpu.VMEM((rows, width), LOW),
                pltpu.VMEM((width, model), LOW),
                pltpu.VMEM((rows, model), LOW),
                pltpu.SemaphoreType.DMA((steps, 2)),
                pltpu.SemaphoreType.DMA((steps, 2)),
                pltpu.SemaphoreType.DMA((steps, 2)),
            ],
        ),
        out_shape=list(out_shapes)
        + [jax.ShapeDtypeStruct((rows, width), LOW), jax.ShapeDtypeStruct((rows, model), LOW)]
        + [jax.ShapeDtypeStruct(g, LOW) for g in grads]
        + [jax.ShapeDtypeStruct(sums, F32)],
        compiler_params=params("arbitrary"),
        cost_estimate=SHORT,
        name="mlp",
    )(order, *x_pieces, *cot_pieces, mixed, vectors, *mats)


def finish_kernel(shifts, wholes, base, *refs):
    refs, out = refs[:-1], refs[-1]
    shift, refs = refs[:shifts], refs[shifts:]
    common, parts = refs[:wholes], refs[wholes:]
    total = base[...].astype(F32)
    for ref in shift:
        total = total + ref[4:5, :] + ref[5:6, :]
    for ref in common:
        total = total + ref[...].astype(F32)
    if not parts:
        out[...] = total.astype(LOW)
    for at in range(2 if parts else 0):

        @pl.when(pl.program_id(0) == at)
        def _():
            more = total
            for ref in parts[at::2]:
                more = more + ref[...].astype(F32)
            out[...] = more.astype(LOW)


def call_finish(base, common, parts, vectors=(), cost=SHORT):
    rows, model = base.shape
    block = pl.BlockSpec((rows // 2, model), lambda i: (i, 0))
    return pl.pallas_call(
        functools.partial(finish_kernel, len(vectors), len(common)),
        grid=(2,),
        in_specs=[block] + [whole(v.shape) for v in vectors] + [block] * len(common) + [whole((rows // 2, model))] * len(parts),
        out_specs=block,
        out_shape=jax.ShapeDtypeStruct((rows, model), LOW),
        compiler_params=params("arbitrary"),
        cost_estimate=cost,
        name="finish",
    )(base, *vectors, *common, *parts)


def cut_kernel(first, second, third, pieces, down, line, out):
    columns = first.shape[1]
    members, shard, _ = pieces.shape
    low = members * shard
    both = columns + second.shape[1]
    for at in range(members):
        rows = slice(at * shard, (at + 1) * shard)
        pieces[at, :, :columns] = first[rows, :]
        pieces[at, :, columns:both] = (second[rows, :].astype(F32) + third[rows, :].astype(F32)).astype(LOW)
        pieces[at, :EXTRA, both:] = first[first.shape[0] - EXTRA :, :128]
        pieces[at, EXTRA:, both:] = (second[low:, :128].astype(F32) + third[low:, :128].astype(F32)).astype(LOW)
    down[...] = first[low : low + down.shape[0], :].astype(F32)
    line[...] = first[first.shape[0] - EXTRA :, :128].astype(F32)[3, :]
    out[...] = first[low + down.shape[0] : low + down.shape[0] + shard, :]


def call_cut(first, second, third, members, shard):
    columns = first.shape[1]
    shapes = [
        jax.ShapeDtypeStruct((members, shard, columns + second.shape[1] + 128), LOW),
        jax.ShapeDtypeStruct((first.shape[0] - (members + 1) * shard - EXTRA, columns), F32),
        jax.ShapeDtypeStruct((128,), F32),
        jax.ShapeDtypeStruct((shard, columns), LOW),
    ]
    return pl.pallas_call(
        cut_kernel,
        grid=(1,),
        in_specs=[whole(first.shape), whole(second.shape), whole(third.shape)],
        out_specs=[whole(a.shape) for a in shapes],
        out_shape=shapes,
        compiler_params=params("arbitrary"),
        cost_estimate=SHORT,
        name="cut",
    )(first, second, third)


def join_kernel(places, count, member, *refs):
    base, parts, refs, total = refs[0], refs[1 : 1 + count], refs[1 + count : -1], refs[-1]
    finish_kernel(0, 0, base, *parts, total)

    @pl.when(pl.program_id(0) == 0)
    def _():
        join_pieces(places, member, *refs)


def join_pieces(places, member, *refs):
    pieces, last, up, qkv, out, gain_1, bias_1, gain_2, bias_2, end_bias, end_bias_2, shift = refs
    outs = up, qkv
    members = pieces.shape[0]
    for at in range(members):
        for block, (index, column, stride) in enumerate(places):
            start = column + at * stride
            outs[index][:, start : start + 128] = pieces[at, :, block * 128 : (block + 1) * 128].astype(F32)
    out[...] = last[...].astype(F32)
    size = gain_1.shape[0]
    low = len(places) * 128
    two, one = (sum(pieces[at, row : row + EXTRA, low:].astype(F32) for at in range(members)) for row in (0, EXTRA))
    wide = jnp.concatenate([one[2:3, :], one[3:4, :], one[4:5, :]], axis=1)
    for at in range(members):

        @pl.when(member[0] == at)
        def _():
            lanes = slice(at * size, (at + 1) * size)
            for ref, rows, row in ((gain_1, one, 0), (bias_1, one, 1), (gain_2, two, 0), (bias_2, two, 1), (end_bias, two, 2), (end_bias_2, two, 2)):
                ref[...] = rows[row, lanes]
            shift[...] = wide[0, 3 * at * size : 3 * (at + 1) * size]


def call_join(member, base, parts, pieces, last, places, columns):
    members, shard, _ = pieces.shape
    size = 128 // members
    shapes = [(shard, c) for c in columns] + [last.shape] + [(size,)] * 6 + [(3 * size,)]
    block = pl.BlockSpec((base.shape[0] // 2, base.shape[1]), lambda i, o: (i, 0))
    return pl.pallas_call(
        functools.partial(join_kernel, tuple(places), len(parts)),
        grid_spec=pltpu.PrefetchScalarGridSpec(
            num_scalar_prefetch=1,
            grid=(2,),
            in_specs=[block] + [whole(p.shape) for p in (*parts, pieces, last)],
            out_specs=[whole(a) for a in shapes] + [block],
        ),
        out_shape=[jax.ShapeDtypeStruct(a, F32) for a in shapes] + [jax.ShapeDtypeStruct(base.shape, LOW)],
        compiler_params=params("arbitrary"),
        cost_estimate=SHORT,
        name="join",
    )(member, base, *parts, pieces, last)


def across(array, bit):
    size = lax.axis_size("fsdp")
    return lax.ppermute(array, "fsdp", [(i, i ^ bit) for i in range(size)])


def exchange(pieces):
    size = lax.axis_size("fsdp")
    if size != 4:
        return lax.all_to_all(pieces, "fsdp", split_axis=0, concat_axis=0, tiled=True)
    member = lax.axis_index("fsdp")
    out = pieces
    for bit in range(1, size):
        mine = lax.dynamic_index_in_dim(pieces, member ^ bit, 0, keepdims=False)
        out = lax.dynamic_update_index_in_dim(out, across(mine, bit), member ^ bit, 0)
    return out


def behind(array, *others):
    return lax.optimization_barrier((array, *others))[0]


def behind_all(arrays, *others):
    return tuple(behind(array, *others) for array in arrays)


def gather_rows(halves, near=None, *others):
    if lax.axis_size("fsdp") != 4:
        return [lax.all_gather(jnp.concatenate(halves, axis=0), "fsdp", axis=0, tiled=True)]
    one_low, two_high, one_high, two_low = near
    return [
        *halves, one_low, one_high, two_low, two_high,
        across(behind(one_low, *others), 2), across(behind(two_high, *others), 1),
    ]


def near_rows(halves):
    low, high = halves
    return across(low, 1), across(high, 2), across(high, 1), across(low, 2)


def hop(array, bit):
    return lax.ppermute(array, "dp", [(i, i ^ bit) for i in range(lax.axis_size("dp"))])


def scatter_step(blocks, far, bit):
    blocks = (blocks.astype(F32) + far.astype(F32)).astype(LOW)
    send = blocks[1::2]
    return blocks[0::2], hop(send, bit), send


def reduce_direct(parts):
    if len(parts) == 1:
        return (lax.psum_scatter(parts[0], "fsdp", scatter_dimension=0, tiled=True),)
    three = across(parts[3], 3)
    return parts[0], across(parts[1], 1), across(parts[2], 2), three


def total_over_all(vector):
    count = lax.axis_size("dp") * lax.axis_size("fsdp")
    step = 1
    while step < count:
        vector = vector + lax.ppermute(vector, ALL, [(i, i ^ step) for i in range(count)])
        step *= 2
    return vector


def swap_owner(array, back):
    groups, members = lax.axis_size("dp"), lax.axis_size("fsdp")
    pairs = [(m * groups + g, g * members + m) for g in range(groups) for m in range(members)]
    if back:
        pairs = [(b, a) for a, b in pairs]
    return lax.ppermute(array, ALL, pairs)


def gather_dp(array):
    return lax.all_gather(array, "dp", axis=0)


def scatter_dp(array):
    return lax.psum_scatter(array, "dp", scatter_dimension=0, tiled=True)


def rotary_tables(length):
    half = ROT // 2
    frequency = (np.float32(10000.0) ** (-(np.arange(half, dtype=np.float32) * np.float32(2.0)) / np.float32(ROT))).astype(np.float32)
    angles = (np.arange(length, dtype=np.float32)[:, None] * frequency[None, :]).astype(np.float32)
    cosine = np.cos(angles).astype(np.float32)
    sine = np.sin(angles).astype(np.float32)
    cos_row = np.ones((length, 128), np.float32)
    sine_row = np.zeros((length, 128), np.float32)
    for start in range(0, 128, HEAD):
        cos_row[:, start : start + half] = cosine
        cos_row[:, start + half : start + ROT] = cosine
        sine_row[:, start : start + half] = -sine
        sine_row[:, start + half : start + ROT] = sine
    return jnp.asarray(np.concatenate([cos_row, sine_row], axis=1))


def local(
    tokens, cotangent, doc_ids, norm1_gain, norm1_bias, norm2_gain, norm2_bias, qkv_weight, qkv_bias,
    out_weight, out_bias, up_weight, up_bias, down_weight, down_bias,
):
    groups, members = lax.axis_size("dp"), lax.axis_size("fsdp")
    group, member = lax.axis_index("dp"), lax.axis_index("fsdp")
    devices = groups * members
    rows, model = tokens.shape
    stream = rows * members
    shard = qkv_weight.shape[0]
    width = model // members
    units_dev = up_bias.shape[0]
    units = groups * units_dev
    paired = members == 4 and units_dev == 128 and units == model and shard == 2 * EXTRA
    me = member.astype(jnp.int32).reshape(1)
    vectors_in = [norm1_gain, norm1_bias, norm2_gain, norm2_bias, out_bias, down_bias]

    half = rows // 2
    x_halves = [tokens[:half], tokens[half:]]
    cot_halves = [cotangent[:half], cotangent[half:]]
    if paired:
        packed = call_pack(me, qkv_weight, up_weight, (*vectors_in, qkv_bias, up_bias), members)
        arrived = [packed[0]] + [across(packed[bit], bit) for bit in range(1, members)]
        x_near = near_rows(behind_all(x_halves, *arrived[1:]))
        cut = 3 * width + 128
        first_in, up_in = call_place(me, arrived, cut)
        w_first = gather_dp(first_in)
        out_own = behind(swap_owner(behind(out_weight, first_in), False), *x_near[:2])
        mats = (gather_dp(jnp.concatenate([up_in, down_weight, out_own], axis=0)),)
        vectors = call_vectors(me, w_first, members, cut)
    else:
        qkv_cut = qkv_weight.reshape(shard, 3, members, width).transpose(2, 0, 1, 3).reshape(members, shard, 3 * width)
        up_cut = up_weight.reshape(shard, groups, members, units_dev).transpose(2, 0, 1, 3).reshape(members, shard, units)
        arrived = exchange(jnp.concatenate([qkv_cut, up_cut], axis=2)).reshape(members * shard, -1)
        w_first = gather_dp(arrived[:, : 3 * width])
        x_near = near_rows(x_halves) if members == 4 else None
        mats = (gather_dp(arrived[:, 3 * width :]), gather_dp(down_weight), gather_dp(swap_owner(out_weight, False)))
        full = [lax.all_gather(a, ALL, axis=0, tiled=True).astype(F32) for a in vectors_in]
        shift = lax.all_gather(qkv_bias, ALL, axis=0, tiled=True).astype(F32).reshape(3, members, width)
        shift = lax.dynamic_index_in_dim(shift, member, 1, keepdims=False)
        up_all = lax.all_gather(up_bias, "dp", axis=0, tiled=True).astype(F32)
        lines = full + [jnp.pad(a, (0, model - a.shape[0])) for a in (up_all, shift[0], shift[1], shift[2])]
        vectors = jnp.pad(jnp.stack(lines), ((0, 6), (0, 0)))

    x_pieces = gather_rows(x_halves, x_near)
    sources = jnp.arange(members, dtype=jnp.int32)
    order = sources ^ member if members == 4 else sources
    doc_row = doc_ids[0]
    first = jnp.sum((doc_row[None, :] < doc_row[:, None]).astype(jnp.int32), axis=1)
    first = jnp.concatenate([first, group.astype(jnp.int32).reshape(1), order])
    tables = rotary_tables(stream)

    q, k, v = call_qkv(order, x_pieces, vectors, w_first, tables, rows, width)
    cot_near = near_rows(behind_all(cot_halves, *x_near)) if members == 4 else None
    cot_pieces = gather_rows(cot_halves, cot_near, q)
    mixed, low_mixed, lse = call_fwd(first, q, k, v)
    out_sizes = [rows] * members if members == 4 else [stream]
    out_shapes = [jax.ShapeDtypeStruct((size, model), LOW) for size in out_sizes]
    results = call_mlp(
        order, x_pieces, cot_pieces, low_mixed, vectors, mats, rows, units, out_shapes
    )
    count = len(out_shapes)
    parts, (d_mixed, to_norm), grads, sums_two = results[:count], results[count : count + 2], results[count + 2 : -1], results[-1]
    scattered = scatter_dp(grads[0].reshape(-1, model)) if paired else None

    summed = reduce_direct(parts)
    sizes = [half] * (2 * members) if members == 4 else [stream]
    *pieces, even, odd, sums_qkv, ones = call_bwd(
        first, q, k, v, d_mixed, mixed, lse, tables, to_norm, vectors, w_first, x_pieces,
        [jax.ShapeDtypeStruct((size, model), LOW) for size in sizes], groups, rows, paired,
    )
    far, bit = hop(odd, 1), 2
    if members == 4:
        add = lambda a, b: (a.astype(F32) + b.astype(F32)).astype(LOW)
        own_low, own_high, one_low, one_high, two_low, two_high, three_low, three_high = pieces
        come = across(three_high, 2), across(three_low, 1)
        output = call_finish(tokens, summed, (), (vectors,), LONG)
        one_low, two_high = behind_all((one_low, two_high), output)
        near = across(one_low, 1), across(two_high, 2)
        blocks, far, send = scatter_step(even, behind(far, output), bit)
        come = behind_all(come, send)
        one_high, two_low = add(one_high, come[0]), add(two_low, come[1])
        near += across(one_high, 1), across(two_low, 2)
        parts = own_low, own_high, near[0], near[2], near[3], near[1]
        blocks, far, send = scatter_step(blocks, behind(far, one_high, two_low), 2 * bit)
        bit = 8
    if members != 4:
        blocks, far, _ = scatter_step(even, far, bit)
        bit = 4
        output = call_finish(tokens, summed, (), (vectors,))
        total = reduce_direct(pieces)[0]
        parts = total[:half], total[half:]
    while blocks.shape[0] > 1:
        (blocks, far, _), bit = scatter_step(blocks, far, bit), 2 * bit
    if members == 4:
        far = behind(far, *near[2:])
    g_qkv = blocks[0], far[0]
    place = group * members + member
    if paired:
        mixed_pieces, g_down, up_shift, g_out = call_cut(scattered, *g_qkv, members, shard)
        g_out = swap_owner(g_out, True)
        places = [(0, b * members * units_dev, units_dev) for b in range(groups)]
        places += [(1, part * model + low, width) for part in range(3) for low in range(0, width, 128)]
        arrived = lax.all_to_all(mixed_pieces, "fsdp", split_axis=0, concat_axis=0)
        g_up, g_qkv, g_out, *mine, grad_tokens = call_join(
            me, cotangent, parts, arrived, g_out, places, (up_weight.shape[1], qkv_weight.shape[1])
        )
        mine.append(up_shift)
    else:
        grad_tokens = call_finish(cotangent, (), parts)
        g_up, g_down, g_out = [scatter_dp(g) for g in grads]
        g_down = g_down.astype(F32)
        g_up = exchange(g_up.reshape(members, shard, units))
        g_up = g_up.reshape(members, shard, groups, units_dev).transpose(1, 2, 0, 3).reshape(shard, -1).astype(F32)
        g_qkv = (g_qkv[0].astype(F32) + g_qkv[1].astype(F32)).astype(LOW)
        g_qkv = exchange(g_qkv.reshape(members, shard, 3 * width)).reshape(members, shard, 1, 3, width)
        g_qkv = g_qkv.transpose(1, 3, 0, 2, 4).reshape(shard, -1).astype(F32)
        thirds = jnp.concatenate([a[0].reshape(3, 1, width) for a in [sums_qkv]], axis=2)
        wide_qkv = lax.dynamic_update_index_in_dim(jnp.zeros((3, members, width), F32), thirds, member, 1)
        wide_up = lax.dynamic_update_index_in_dim(
            jnp.zeros((groups, members, units_dev), F32), sums_two[0, :units].reshape(groups, 1, units_dev), member, 1
        )
        summed = total_over_all(jnp.concatenate([
            ones[0], ones[1], sums_two[2], sums_two[1], sums_two[3], wide_qkv.reshape(-1), wide_up.reshape(-1),
        ]))
        mine, start = [], 0
        for size in [model] * 5 + [3 * model, groups * members * units_dev]:
            mine.append(lax.dynamic_slice_in_dim(summed, start + place * (size // devices), size // devices))
            start += size
        mine.insert(5, mine[4])
    gain_1, bias_1, gain_2, bias_2, end_bias, end_bias_2, qkv_shift, up_shift = mine
    if not paired:
        g_out = swap_owner(g_out, True).astype(F32)
    return (
        output, grad_tokens, gain_1, bias_1, gain_2, bias_2, g_qkv, qkv_shift, g_out, end_bias, g_up, up_shift, g_down, end_bias_2,
    )


def solution(mesh):
    row, vec = P(ALL, None), P(ALL)
    return jax.shard_map(
        local,
        mesh=mesh,
        in_specs=(row, row, P("dp", None), vec, vec, vec, vec, row, vec, row, vec, row, vec, row, vec),
        out_specs=(row, row, vec, vec, vec, vec, row, vec, row, vec, row, vec, row, vec),
        check_vma=False,
    )
```
